32 devices in a mesh: batch: 8 (over z, x), narrow: 4 (over y, core).
Axes of the slice: x: 2, y: 2, z: 4, core: 2. Of those that a mesh axis runs over, the one named last changes fastest.
Arguments:
- inputs: bfloat16 [128, 16, 16, 1024], P('batch', 'narrow'), may hold values from -6 to 6
- image_class: int32 [128], P('batch'), may hold values from 0 to 2
- weight_reduce: bfloat16 [1024, 256], replicated, may hold values from -0.1875 to 0.1875
- gain_reduce: float32 [256], replicated, may hold values from 0.5 to 1.5
- shift_reduce: float32 [256], replicated, may hold values from -3 to 3
- weight_split: bfloat16 [3, 3, 2, 128, 256], replicated, may hold values from -0.1875 to 0.1875
- gain_split: float32 [512], replicated, may hold values from 0.5 to 1.5
- shift_split: float32 [512], replicated, may hold values from -3 to 3
- weight_squeeze: float32 [256, 128], replicated, may hold values from -0.375 to 0.375
- gain_squeeze: float32 [128], replicated, may hold values from 0.5 to 1.5
- shift_squeeze: float32 [128], replicated, may hold values from -3 to 3
- weight_excite: float32 [128, 512], replicated, may hold values from -0.5 to 0.5
- bias_excite: float32 [512], replicated, may hold values from -4 to 4
- weight_expand: bfloat16 [256, 1024], replicated, may hold values from -0.375 to 0.375
- gain_expand: float32 [1024], replicated, may hold values from 0.5 to 1.5
- shift_expand: float32 [1024], replicated, may hold values from -3 to 3
- cotangent: bfloat16 [128, 16, 16, 1024], P('batch', 'narrow'), may hold values from -6 to 6
Outputs:
- block_output: bfloat16 [128, 16, 16, 1024], P('batch', 'narrow')
- input_grad: bfloat16 [128, 16, 16, 1024], P('batch', 'narrow')
- grad_weight_reduce: float32 [1024, 256], replicated
- grad_gain_reduce: float32 [256], replicated
- grad_shift_reduce: float32 [256], replicated
- grad_weight_split: float32 [3, 3, 2, 128, 256], replicated
- grad_gain_split: float32 [512], replicated
- grad_shift_split: float32 [512], replicated
- grad_weight_squeeze: float32 [256, 128], replicated
- grad_gain_squeeze: float32 [128], replicated
- grad_shift_squeeze: float32 [128], replicated
- grad_weight_excite: float32 [128, 512], replicated
- grad_bias_excite: float32 [512], replicated
- grad_weight_expand: float32 [256, 1024], replicated
- grad_gain_expand: float32 [1024], replicated
- grad_shift_expand: float32 [1024], replicated
The draws below stay inside these ranges and needn't reach their ends.
Inputs may be any that keep to these rules, and one draw needn't show every extreme that they name: `image_class`: an image's side is 12 + 2 times its class; rows and columns from that side up to 16 lie outside it.
All inputs are finite; a program needn't handle non-finite values.
Results may differ from the reference program's by a relative error of at most 0.011.
Values may be sent and summed in bfloat16 or wider, within the bound.
No kernel may reach another device: no remote copies, remote signals or barrier semaphores. Data moves between devices by JAX's collectives and lax.ppermute only.
A program may use at most 128 MiB of HBM per device.

```python
import jax
import jax.numpy as jnp
from jax import lax

CH = 1024
MID = 256
INTER = 128
RADIX = 2
SIDE = 16
IMAGES = 128


def touch_ends(values, stream_key, low, largest):
    index_at = [jax.random.randint(jax.random.fold_in(stream_key, axis), (), 0, length) for axis, length in enumerate(values.shape)]
    widest = values.shape.index(max(values.shape))
    neighbour = index_at[:widest] + [(index_at[widest] + 1) % values.shape[widest]] + index_at[widest + 1:]
    return values.at[tuple(index_at)].set(low).at[tuple(neighbour)].set(largest)


def level_of(rng, shape, pieces, smallest, largest):
    def one(dim, parts):
        steps = jax.random.uniform(jax.random.fold_in(jax.random.fold_in(rng, 6), dim), (parts,), jnp.float32, smallest / len(pieces), largest / len(pieces))
        return jnp.repeat(jnp.exp(steps), shape[dim] // parts).reshape((-1,) + (1,) * (len(shape) - dim - 1))

    loudness = one(*pieces[0])
    for cut in pieces[1:]:
        loudness = loudness * one(*cut)
    return loudness


def centred(stream_key, extent, width, bound, split=(), kind=jnp.bfloat16):
    gain = level_of(stream_key, extent, split, -0.22, 0.18) if split else 1.0
    array = jax.random.normal(stream_key, extent, jnp.float32) * width * gain
    return jnp.minimum(jnp.maximum(array, -bound), bound).astype(kind)


def setup_inputs(seed: int = 0) -> dict:
    key_of = jax.random.split(jax.random.key(seed), 18)
    inputs = centred(key_of[0], (IMAGES, SIDE, SIDE, CH), 1.0, 6.0, ((0, 8), (1, 4)))
    image_class = touch_ends(jax.random.randint(key_of[1], (IMAGES,), 0, 3), jax.random.fold_in(key_of[1], 1), 0, 2).astype(jnp.int32)
    weight_reduce = centred(key_of[2], (CH, MID), CH ** -0.5, 0.1875)
    gain_reduce = jnp.clip(1.0 + 0.1 * jax.random.normal(key_of[3], (MID,), jnp.float32), 0.5, 1.5)
    shift_reduce = centred(key_of[4], (MID,), 0.5, 3.0, (), jnp.float32)
    weight_split = centred(key_of[5], (3, 3, RADIX, MID // RADIX, MID), (9 * (MID // RADIX)) ** -0.5, 0.1875)
    gain_split = jnp.clip(1.0 + 0.1 * jax.random.normal(key_of[6], (RADIX * MID,), jnp.float32), 0.5, 1.5)
    shift_split = centred(key_of[7], (RADIX * MID,), 0.5, 3.0, (), jnp.float32)
    weight_squeeze = centred(key_of[8], (MID, INTER), MID ** -0.5, 0.375, (), jnp.float32)
    gain_squeeze = jnp.clip(1.0 + 0.1 * jax.random.normal(key_of[9], (INTER,), jnp.float32), 0.5, 1.5)
    shift_squeeze = centred(key_of[10], (INTER,), 0.5, 3.0, (), jnp.float32)
    weight_excite = centred(key_of[11], (INTER, RADIX * MID), INTER ** -0.5, 0.5, (), jnp.float32)
    bias_excite = centred(key_of[12], (RADIX * MID,), 1.0, 4.0, (), jnp.float32)
    weight_expand = centred(key_of[13], (MID, CH), MID ** -0.5, 0.375)
    gain_expand = jnp.clip(1.0 + 0.1 * jax.random.normal(key_of[14], (CH,), jnp.float32), 0.5, 1.5)
    shift_expand = centred(key_of[15], (CH,), 0.5, 3.0, (), jnp.float32)
    cotangent = centred(key_of[16], (IMAGES, SIDE, SIDE, CH), 1.0, 6.0, ((0, 8), (1, 4)))
    return {"inputs": inputs, "image_class": image_class, "weight_reduce": weight_reduce, "gain_reduce": gain_reduce, "shift_reduce": shift_reduce, "weight_split": weight_split, "gain_split": gain_split, "shift_split": shift_split, "weight_squeeze": weight_squeeze, "gain_squeeze": gain_squeeze, "shift_squeeze": shift_squeeze, "weight_excite": weight_excite, "bias_excite": bias_excite, "weight_expand": weight_expand, "gain_expand": gain_expand, "shift_expand": shift_expand, "cotangent": cotangent}


EPSILON = 1e-05
HIGHEST = lax.Precision.HIGHEST

@jax.custom_vjp
def low(v):
    return lax.optimization_barrier(v.astype(jnp.bfloat16)).astype(jnp.float32)

@jax.custom_vjp
def low_back(v):
    return v

def low_keep(v):
    return (low(v), None)

def low_pass(kept, grad):
    return (grad,)

def back_keep(v):
    return (v, None)

def back_low(kept, grad):
    return (low(grad),)
low.defvjp(low_keep, low_pass)
low_back.defvjp(back_keep, back_low)

def batch_norm(values, valid, pixel_count, gains, shifts):
    center = lax.optimization_barrier(jnp.sum(values * valid, axis=(0, 1, 2))) / pixel_count
    moment = lax.optimization_barrier(jnp.sum(values * values * valid, axis=(0, 1, 2))) / pixel_count
    inv_std = lax.rsqrt(moment - center * center + EPSILON)
    return (values - center) * inv_std * gains + shifts

def block_forward(valid, image_area, pixel_count, inputs, weight_reduce, gain_reduce, shift_reduce, weight_split, gain_split, shift_split, weight_squeeze, gain_squeeze, shift_squeeze, weight_excite, bias_excite, weight_expand, gain_expand, shift_expand):
    masked = inputs * valid
    pre_reduce = low_back(jnp.einsum('ihwc,cd->ihwd', masked, weight_reduce, precision=HIGHEST))
    hidden_reduce = low(jax.nn.silu(batch_norm(pre_reduce, valid, pixel_count, gain_reduce, shift_reduce)) * valid)
    kernel = jnp.transpose(weight_split, (0, 1, 3, 2, 4)).reshape(3, 3, MID // RADIX, RADIX * MID)
    pre_split = low_back(lax.conv_general_dilated(hidden_reduce, kernel, (1, 1), ((1, 1), (1, 1)), dimension_numbers=('NHWC', 'HWIO', 'NHWC'), feature_group_count=RADIX, precision=HIGHEST))
    hidden_split = low_back(low(jax.nn.silu(batch_norm(pre_split, valid, pixel_count, gain_split, shift_split)) * valid))
    first_half = hidden_split[..., :MID]
    second_half = hidden_split[..., MID:]
    pooled = lax.optimization_barrier(jnp.sum(first_half + second_half, axis=(1, 2))) / image_area[:, None]
    pre_squeeze = jnp.dot(pooled, weight_squeeze, precision=HIGHEST)
    center = lax.optimization_barrier(jnp.mean(pre_squeeze, axis=0))
    moment = lax.optimization_barrier(jnp.mean(pre_squeeze * pre_squeeze, axis=0))
    z_squeeze = (pre_squeeze - center) * lax.rsqrt(moment - center * center + EPSILON) * gain_squeeze + shift_squeeze
    logits = jnp.dot(jax.nn.silu(z_squeeze), weight_excite, precision=HIGHEST) + bias_excite
    attention = jax.nn.softmax(logits.reshape(-1, RADIX, MID), axis=1)
    mixture = attention[:, 0][:, None, None, :] * first_half + attention[:, 1][:, None, None, :] * second_half
    mixture = low_back(low(mixture))
    pre_expand = low_back(low(jnp.einsum('ihwc,cd->ihwd', mixture, weight_expand, precision=HIGHEST)))
    residual = batch_norm(pre_expand, valid, pixel_count, gain_expand, shift_expand) + masked
    return jax.nn.silu(residual) * valid

def reference(inputs, image_class, weight_reduce, gain_reduce, shift_reduce, weight_split, gain_split, shift_split, weight_squeeze, gain_squeeze, shift_squeeze, weight_excite, bias_excite, weight_expand, gain_expand, shift_expand, cotangent):
    image_side = 12 + 2 * image_class
    positions = jnp.arange(SIDE, dtype=jnp.int32)
    inside = (positions[None, :] < image_side[:, None]).astype(jnp.float32)
    valid = (inside[:, :, None] * inside[:, None, :])[..., None]
    image_area = (image_side * image_side).astype(jnp.float32)
    pixel_count = jnp.sum(valid)

    def forward(inputs, weight_reduce, gain_reduce, shift_reduce, weight_split, gain_split, shift_split, weight_squeeze, gain_squeeze, shift_squeeze, weight_excite, bias_excite, weight_expand, gain_expand, shift_expand):
        return block_forward(valid, image_area, pixel_count, inputs, weight_reduce, gain_reduce, shift_reduce, weight_split, gain_split, shift_split, weight_squeeze, gain_squeeze, shift_squeeze, weight_excite, bias_excite, weight_expand, gain_expand, shift_expand)
    output, pullback = jax.vjp(forward, inputs.astype(jnp.float32), weight_reduce.astype(jnp.float32), gain_reduce.astype(jnp.float32), shift_reduce.astype(jnp.float32), weight_split.astype(jnp.float32), gain_split.astype(jnp.float32), shift_split.astype(jnp.float32), weight_squeeze.astype(jnp.float32), gain_squeeze.astype(jnp.float32), shift_squeeze.astype(jnp.float32), weight_excite.astype(jnp.float32), bias_excite.astype(jnp.float32), weight_expand.astype(jnp.float32), gain_expand.astype(jnp.float32), shift_expand.astype(jnp.float32))
    gradients = pullback(cotangent.astype(jnp.float32))
    return (output.astype(jnp.bfloat16), gradients[0].astype(jnp.bfloat16), gradients[1], gradients[2], gradients[3], gradients[4], gradients[5], gradients[6], gradients[7], gradients[8], gradients[9], gradients[10], gradients[11], gradients[12], gradients[13], gradients[14])
```

```python
import jax
import jax.numpy as jnp
from jax import lax
from jax.sharding import PartitionSpec as P

EPSILON = 1e-05
HIGHEST = lax.Precision.HIGHEST
ALL = ("batch", "narrow")


def device_count():
    return lax.axis_size("batch") * lax.axis_size("narrow")


def gather_all(block):
    count = device_count()
    return lax.all_to_all(jnp.broadcast_to(block[None], (count,) + block.shape), ALL, 0, 0)


def sum_all(*vectors):
    flat = jnp.concatenate(vectors)
    size = flat.shape[0]
    rows = -(-size // 128)
    flat = jnp.pad(flat, (0, rows * 128 - size)).reshape(rows, 128)
    total = jnp.sum(gather_all(flat), 0).reshape(-1)
    outs, start = [], 0
    for vector in vectors:
        outs.append(total[start : start + vector.shape[0]])
        start += vector.shape[0]
    return outs


def sum_weights(*parts):
    count = device_count()
    flat = jnp.concatenate([part.astype(jnp.bfloat16).reshape(-1, 128) for part in parts])
    rows = flat.shape[0]
    per = -(-rows // (count * 16)) * 16
    flat = jnp.pad(flat, ((0, per * count - rows), (0, 0))).reshape(count, per, 128)
    mine = jnp.sum(lax.all_to_all(flat, ALL, 0, 0).astype(jnp.float32), 0)
    full = gather_all(mine.astype(jnp.bfloat16)).reshape(-1, 128)
    outs, start = [], 0
    for part in parts:
        length = part.size // 128
        outs.append(full[start : start + length].astype(jnp.float32).reshape(part.shape))
        start += length
    return outs


def halo(block):
    count = lax.axis_size("narrow")
    forward = [(i, i + 1) for i in range(count - 1)]
    backward = [(i + 1, i) for i in range(count - 1)]
    low = lax.ppermute(block[:, -1:], "narrow", forward)
    high = lax.ppermute(block[:, :1], "narrow", backward)
    return low, high


def silu_slope(values):
    sigmoid_part = jax.nn.sigmoid(values)
    return sigmoid_part * (1.0 + values * (1.0 - sigmoid_part))


def side_mask(classes, first_row, row_count, col_count):
    image_side = 12 + 2 * classes
    row_ids = first_row + jnp.arange(row_count, dtype=jnp.int32)
    col_ids = jnp.arange(col_count, dtype=jnp.int32)
    row_inside = (row_ids[None, :] < image_side[:, None]) & (row_ids >= 0)[None, :]
    col_inside = col_ids[None, :] < image_side[:, None]
    return (row_inside[:, :, None] & col_inside[:, None, :]).astype(jnp.float32)[..., None]


def moments(totals, squares, counted):
    center = totals / counted
    return center, lax.rsqrt(squares / counted - center * center + EPSILON)


def conv_forward(padded, kernel, row_count, col_count):
    blocks = padded.shape[0]
    groups = kernel.shape[2]
    group_width = kernel.shape[3]
    accum = None
    for row_off in range(3):
        for col_off in range(3):
            window = padded[
                :, row_off : row_off + row_count, col_off : col_off + col_count, :
            ].reshape(blocks * row_count * col_count, groups, group_width)
            partial_value = jnp.einsum(
                "pgc,gco->pgo", window, kernel[row_off, col_off], preferred_element_type=jnp.float32
            )
            accum = partial_value if accum is None else accum + partial_value
    return accum.reshape(blocks, row_count, col_count, -1)


def conv_weight_grad(padded, grad_out, row_count, col_count, groups):
    blocks = padded.shape[0]
    group_width = padded.shape[3] // groups
    pieces = []
    for row_off in range(3):
        for col_off in range(3):
            window = padded[
                :, row_off : row_off + row_count, col_off : col_off + col_count, :
            ].reshape(blocks * row_count * col_count, groups, group_width)
            pieces.append(
                jnp.einsum("pgc,pgo->gco", window, grad_out, preferred_element_type=jnp.float32)
            )
    stacked = jnp.stack(pieces)
    return stacked.reshape(3, 3, groups, group_width, -1)


def conv_input_grad(padded_grad, kernel, row_count, col_count):
    blocks = padded_grad.shape[0]
    groups = kernel.shape[2]
    out_width = kernel.shape[4]
    accum = None
    for row_off in range(3):
        for col_off in range(3):
            window = padded_grad[
                :, 2 - row_off : 2 - row_off + row_count, 2 - col_off : 2 - col_off + col_count, :
            ].reshape(blocks * row_count * col_count, groups, out_width)
            partial_value = jnp.einsum(
                "pgo,gco->pgc", window, kernel[row_off, col_off], preferred_element_type=jnp.float32
            )
            accum = partial_value if accum is None else accum + partial_value
    return accum.reshape(blocks, row_count, col_count, -1)


def body(
    inputs,
    image_class,
    weight_reduce,
    gain_reduce,
    shift_reduce,
    weight_split,
    gain_split,
    shift_split,
    weight_squeeze,
    gain_squeeze,
    shift_squeeze,
    weight_excite,
    bias_excite,
    weight_expand,
    gain_expand,
    shift_expand,
    cotangent,
):
    blocks, row_count, col_count, channels = inputs.shape
    bottleneck = weight_reduce.shape[1]
    groups = weight_split.shape[2]
    parts = lax.axis_size("narrow")
    bands = lax.axis_size("batch")
    pixels = blocks * row_count * col_count
    first_row = lax.axis_index("narrow") * row_count
    tall = side_mask(image_class, first_row - 1, row_count + 2, col_count)
    valid = tall[:, 1:-1]
    flat_valid = valid.reshape(pixels, 1)
    side = (12 + 2 * image_class).astype(jnp.float32)
    image_area = side * side
    masked = inputs * valid.astype(jnp.bfloat16)
    flat_masked = masked.reshape(pixels, channels)

    pre_reduce = jnp.dot(flat_masked, weight_reduce, preferred_element_type=jnp.float32)
    low, high = halo(pre_reduce.reshape(blocks, row_count, col_count, bottleneck))
    sum_reduce, square_reduce, pixel_count = sum_all(
        jnp.sum(pre_reduce * flat_valid, 0),
        jnp.sum(pre_reduce * pre_reduce * flat_valid, 0),
        jnp.sum(flat_valid)[None],
    )
    center_reduce, inv_reduce = moments(sum_reduce, square_reduce, pixel_count)
    tall_reduce = jnp.concatenate(
        [low, pre_reduce.reshape(blocks, row_count, col_count, bottleneck), high], axis=1
    )
    tall_norm = (tall_reduce - center_reduce) * inv_reduce
    tall_z = tall_norm * gain_reduce + shift_reduce
    padded_reduce = jnp.pad(
        (jax.nn.silu(tall_z) * tall).astype(jnp.bfloat16), ((0, 0), (0, 0), (1, 1), (0, 0))
    )
    norm_reduce = tall_norm[:, 1:-1].reshape(pixels, -1)
    z_reduce = tall_z[:, 1:-1].reshape(pixels, -1)

    pre_split = conv_forward(padded_reduce, weight_split, row_count, col_count)
    low_split, high_split = halo(pre_split)
    flat_split = pre_split.reshape(pixels, -1)
    sum_split, square_split = sum_all(
        jnp.sum(flat_split * flat_valid, 0), jnp.sum(flat_split * flat_split * flat_valid, 0)
    )
    center_split, inv_split = moments(sum_split, square_split, pixel_count)
    tall_norm_split = (
        jnp.concatenate([low_split, pre_split, high_split], axis=1) - center_split
    ) * inv_split
    tall_z_split = tall_norm_split * gain_split + shift_split
    hidden_split = (jax.nn.silu(tall_z_split[:, 1:-1]) * valid).astype(jnp.bfloat16)
    first_half = hidden_split[..., :bottleneck]
    second_half = hidden_split[..., bottleneck:]
    summed = jnp.sum(hidden_split, axis=(1, 2), dtype=jnp.float32)
    pooled = (summed[:, :bottleneck] + summed[:, bottleneck:]) / image_area[:, None]
    squeeze_part = jnp.dot(pooled, weight_squeeze, precision=HIGHEST)
    all_squeeze = jnp.sum(
        gather_all(squeeze_part).reshape(bands, parts, blocks, -1), 1
    )
    image_count = bands * blocks
    center_squeeze, inv_squeeze = moments(
        jnp.sum(all_squeeze, (0, 1)), jnp.sum(all_squeeze * all_squeeze, (0, 1)), image_count
    )
    all_norm_squeeze = (all_squeeze - center_squeeze) * inv_squeeze
    all_z_squeeze = all_norm_squeeze * gain_squeeze + shift_squeeze
    band = lax.axis_index("batch")
    z_squeeze = lax.dynamic_index_in_dim(all_z_squeeze, band, keepdims=False)
    hidden_squeeze = jax.nn.silu(z_squeeze)
    logits = jnp.dot(hidden_squeeze, weight_excite, precision=HIGHEST) + bias_excite
    logit_first = logits[:, :bottleneck]
    logit_second = logits[:, bottleneck:]
    ceiling = jnp.maximum(logit_first, logit_second)
    exp_first = jnp.exp(logit_first - ceiling)
    exp_second = jnp.exp(logit_second - ceiling)
    att_first = exp_first / (exp_first + exp_second)
    att_second = exp_second / (exp_first + exp_second)
    mixture = (
        att_first[:, None, None, :] * first_half + att_second[:, None, None, :] * second_half
    ).astype(jnp.bfloat16)
    flat_mix = mixture.reshape(pixels, bottleneck)
    pre_expand = jnp.dot(flat_mix, weight_expand, preferred_element_type=jnp.float32).astype(
        jnp.bfloat16
    )
    expand_values = pre_expand.astype(jnp.float32)
    sum_expand, square_expand = sum_all(
        jnp.sum(expand_values * flat_valid, 0),
        jnp.sum(expand_values * expand_values * flat_valid, 0),
    )
    center_expand, inv_expand = moments(sum_expand, square_expand, pixel_count)
    norm_expand = (expand_values - center_expand) * inv_expand
    residual = norm_expand * gain_expand + shift_expand + flat_masked
    block_output = (
        (jax.nn.silu(residual) * flat_valid)
        .astype(jnp.bfloat16)
        .reshape(blocks, row_count, col_count, channels)
    )
    grad_residual = cotangent.reshape(pixels, channels) * flat_valid * silu_slope(residual)
    shift_expand_grad, gain_expand_grad = sum_all(
        jnp.sum(grad_residual, 0), jnp.sum(grad_residual * norm_expand, 0)
    )
    grad_expand = (
        flat_valid
        * gain_expand
        * inv_expand
        * (
            grad_residual
            - shift_expand_grad / pixel_count
            - norm_expand * gain_expand_grad / pixel_count
        )
    ).astype(jnp.bfloat16)
    expand_part = jnp.einsum("pc,pd->cd", flat_mix, grad_expand, preferred_element_type=jnp.float32)
    grad_mixture = (
        jnp.einsum("pd,cd->pc", grad_expand, weight_expand, preferred_element_type=jnp.float32)
        .astype(jnp.bfloat16)
        .reshape(blocks, row_count, col_count, bottleneck)
    )
    low_mix, high_mix = halo(grad_mixture)
    grad_att_first = jnp.einsum(
        "ihwc,ihwc->ic", grad_mixture, first_half, preferred_element_type=jnp.float32
    )
    grad_att_second = jnp.einsum(
        "ihwc,ihwc->ic", grad_mixture, second_half, preferred_element_type=jnp.float32
    )
    inner = att_first * grad_att_first + att_second * grad_att_second
    grad_logits = jnp.concatenate(
        [att_first * (grad_att_first - inner), att_second * (grad_att_second - inner)], axis=1
    )
    bias_part = jnp.sum(grad_logits, 0)
    excite_part = jnp.einsum("ik,ic->kc", hidden_squeeze, grad_logits, precision=HIGHEST)
    hidden_part = jnp.einsum("ic,kc->ik", grad_logits, weight_excite, precision=HIGHEST)
    all_hidden = jnp.sum(gather_all(hidden_part).reshape(bands, parts, blocks, -1), 1)
    all_grad_z = all_hidden * silu_slope(all_z_squeeze)
    shift_squeeze_grad = jnp.sum(all_grad_z, (0, 1))
    gain_squeeze_grad = jnp.sum(all_grad_z * all_norm_squeeze, (0, 1))
    grad_z_squeeze = lax.dynamic_index_in_dim(all_grad_z, band, keepdims=False)
    norm_squeeze = lax.dynamic_index_in_dim(all_norm_squeeze, band, keepdims=False)
    grad_pre_squeeze = (
        gain_squeeze
        * inv_squeeze
        * (
            grad_z_squeeze
            - shift_squeeze_grad / image_count
            - norm_squeeze * gain_squeeze_grad / image_count
        )
    )
    squeeze_grad_part = jnp.einsum("ic,ik->ck", pooled, grad_pre_squeeze, precision=HIGHEST)
    grad_pooled = (
        jnp.einsum("ik,ck->ic", grad_pre_squeeze, weight_squeeze, precision=HIGHEST)
        / image_area[:, None]
    )
    tall_mix = jnp.concatenate([low_mix, grad_mixture, high_mix], axis=1)
    spread = grad_pooled[:, None, None, :] * tall
    tall_hidden = jnp.concatenate(
        [
            tall_mix * att_first[:, None, None, :] + spread,
            tall_mix * att_second[:, None, None, :] + spread,
        ],
        axis=-1,
    ).astype(jnp.bfloat16)
    tall_grad_z = tall_hidden * tall * silu_slope(tall_z_split)
    own_grad_z = tall_grad_z[:, 1:-1].reshape(pixels, -1)
    own_norm_split = tall_norm_split[:, 1:-1].reshape(pixels, -1)
    shift_split_grad, gain_split_grad = sum_all(
        jnp.sum(own_grad_z, 0), jnp.sum(own_grad_z * own_norm_split, 0)
    )
    tall_grad_split = (
        tall
        * gain_split
        * inv_split
        * (
            tall_grad_z
            - shift_split_grad / pixel_count
            - tall_norm_split * gain_split_grad / pixel_count
        )
    ).astype(jnp.bfloat16)
    grad_split = tall_grad_split[:, 1:-1].reshape(-1, groups, bottleneck)
    split_part = conv_weight_grad(padded_reduce, grad_split, row_count, col_count, groups)
    padded_grad = jnp.pad(tall_grad_split, ((0, 0), (0, 0), (1, 1), (0, 0)))
    grad_hidden_reduce = conv_input_grad(padded_grad, weight_split, row_count, col_count).reshape(
        pixels, -1
    )
    grad_z_reduce = grad_hidden_reduce * flat_valid * silu_slope(z_reduce)
    shift_reduce_grad, gain_reduce_grad, bias_total = sum_all(
        jnp.sum(grad_z_reduce, 0), jnp.sum(grad_z_reduce * norm_reduce, 0), bias_part
    )
    grad_reduce = (
        flat_valid
        * gain_reduce
        * inv_reduce
        * (
            grad_z_reduce
            - shift_reduce_grad / pixel_count
            - norm_reduce * gain_reduce_grad / pixel_count
        )
    ).astype(jnp.bfloat16)
    reduce_part = jnp.einsum(
        "pc,pd->cd", flat_masked, grad_reduce, preferred_element_type=jnp.float32
    )
    grad_input = (
        jnp.einsum("pd,cd->pc", grad_reduce, weight_reduce, preferred_element_type=jnp.float32)
        + grad_residual
    )
    input_grad = (
        (grad_input * flat_valid)
        .astype(jnp.bfloat16)
        .reshape(blocks, row_count, col_count, channels)
    )
    expand_total, squeeze_total, excite_total = sum_weights(
        expand_part, squeeze_grad_part, excite_part
    )
    (split_total,) = sum_weights(split_part)
    (reduce_total,) = sum_weights(reduce_part)
    return (
        block_output,
        input_grad,
        reduce_total,
        gain_reduce_grad,
        shift_reduce_grad,
        split_total,
        gain_split_grad,
        shift_split_grad,
        squeeze_total,
        gain_squeeze_grad,
        shift_squeeze_grad,
        excite_total,
        bias_total,
        expand_total,
        gain_expand_grad,
        shift_expand_grad,
    )


def solution(mesh):
    rows = P("batch", "narrow", None, None)
    return jax.shard_map(
        body,
        mesh=mesh,
        in_specs=(rows, P("batch")) + (P(),) * 14 + (rows,),
        out_specs=(rows, rows) + (P(),) * 14,
        check_vma=False,
    )
```

```python
import functools

import jax
import jax.numpy as jnp
from jax import lax
from jax.experimental import pallas as pl
from jax.experimental.pallas import tpu as pltpu
from jax.sharding import PartitionSpec as P

EPSILON = 1e-05
HIGHEST = lax.Precision.HIGHEST
ALL = ("batch", "narrow")
F32 = jnp.float32
BF16 = jnp.bfloat16
COLS = 16
LANES = 128


def device_count():
    return lax.axis_size("batch") * lax.axis_size("narrow")


def halo(top, bottom):
    count = lax.axis_size("narrow")
    low = lax.ppermute(bottom, "narrow", [(i, i + 1) for i in range(count - 1)])
    high = lax.ppermute(top, "narrow", [(i + 1, i) for i in range(count - 1)])
    return low, high


def exchange(block):
    return lax.all_to_all(block, ALL, 0, 0)


def sum_weights(*parts):
    count = device_count()
    flat = jnp.concatenate([part.astype(BF16).reshape(-1, LANES) for part in parts])
    rows = flat.shape[0]
    per = -(-rows // (count * 16)) * 16
    flat = jnp.pad(flat, ((0, per * count - rows), (0, 0))).reshape(count, per, LANES)
    mine = jnp.sum(exchange(flat).astype(F32), 0).astype(BF16)
    full = exchange(jnp.broadcast_to(mine[None], (count,) + mine.shape)).reshape(-1, LANES)
    outs, start = [], 0
    for part in parts:
        length = part.size // LANES
        outs.append(full[start : start + length].astype(F32).reshape(part.shape))
        start += length
    return outs


def sigmoid(values):
    return 0.5 * jnp.tanh(0.5 * values) + 0.5


def wide(mask, width):
    return jnp.concatenate([mask] * (width // LANES), axis=1) if width > LANES else mask


def inside(meta, image, start, count):
    pixel = lax.broadcasted_iota(jnp.int32, (count * COLS, LANES), 0)
    row = (pixel >> 4) + (meta[0] + start)
    col = pixel & (COLS - 1)
    side = 12 + 2 * meta[2 + image]
    return jnp.where((row < side) & (row >= 0) & (col < side), 1.0, 0.0).astype(F32)


def area_of(meta, image):
    side = (12 + 2 * meta[2 + image]).astype(F32)
    return side * side


def row_of(block, first, count):
    return jnp.concatenate([block[first + k : first + k + 1] for k in range(count)], axis=1)


def put_row(ref, first, vector):
    for k in range(vector.shape[1] // LANES):
        ref[0, first + k : first + k + 1, :] = vector[:, k * LANES : (k + 1) * LANES]


def spread(ref):
    block = ref[0]

    def step(k, carry):
        ref[k] = block
        return carry

    lax.fori_loop(1, ref.shape[0], step, 0)


def fold(values):
    return jnp.sum(values.reshape(-1, 8, values.shape[-1]), 0)


def total(block):
    return jnp.sum(block, 0, keepdims=True)


def stats(totals, squares, counted):
    center = totals / counted
    return center, lax.rsqrt(squares / counted - center * center + EPSILON)


def shifted(values):
    count, width = values.shape
    col = lax.broadcasted_iota(jnp.int32, (count, LANES), 0) & (COLS - 1)
    has_left = wide(jnp.where(col > 0, 1.0, 0.0).astype(F32), width)
    has_right = wide(jnp.where(col < COLS - 1, 1.0, 0.0).astype(F32), width)
    left = pltpu.roll(values, 1, 0) * has_left
    right = pltpu.roll(values, count - 1, 0) * has_right
    return left.astype(BF16), values.astype(BF16), right.astype(BF16)


def dot(a, b, dims=((1,), (0,)), precision=None):
    return lax.dot_general(a, b, (dims, ((), ())), precision=precision, preferred_element_type=F32)


def call(kernel, outs, args, scratch=(), megabytes=32, flops=0, **sizes):
    moved = sum(a.size * a.dtype.itemsize for a in args) + sum(
        functools.reduce(lambda x, y: x * y, s) * jnp.dtype(t).itemsize for s, t in outs
    )
    return pl.pallas_call(
        functools.partial(kernel, **sizes),
        out_shape=[jax.ShapeDtypeStruct(s, t) for s, t in outs],
        in_specs=[pl.BlockSpec(memory_space=pltpu.SMEM)]
        + [pl.BlockSpec(memory_space=pltpu.VMEM)] * (len(args) - 1),
        out_specs=[pl.BlockSpec(memory_space=pltpu.VMEM)] * len(outs),
        scratch_shapes=[pltpu.VMEM(s, t) for s, t in scratch],
        compiler_params=pltpu.CompilerParams(vmem_limit_bytes=megabytes << 20),
        cost_estimate=pl.CostEstimate(flops=flops, bytes_accessed=moved, transcendentals=0),
    )(*args)


def reduce_kernel(meta, x, w, pre, top, bottom, pay, acc, *, blocks, rows):
    slab = rows * COLS
    acc[...] = jnp.zeros_like(acc)
    group = 4

    def step(g, carry):
        base = pl.multiple_of(g * group * slab, group * slab)
        out = dot(x[pl.ds(base, group * slab), :], w[...])
        for j in range(group):
            image = g * group + j
            mask = inside(meta, image, 0, rows)
            part = out[j * slab : (j + 1) * slab] * wide(mask, out.shape[1])
            pre[pl.ds(pl.multiple_of(image * slab, slab), slab), :] = part
            edge = pl.ds(pl.multiple_of(image * COLS, COLS), COLS)
            top[edge, :] = part[:COLS]
            bottom[edge, :] = part[slab - COLS :]
            acc[0] += fold(part)
            acc[1] += fold(part * part)
            acc[2, :, :LANES] += fold(mask)
        return carry

    lax.fori_loop(0, blocks // group, step, 0)
    put_row(pay, 0, total(acc[0]))
    put_row(pay, 2, total(acc[1]))
    put_row(pay, 4, total(acc[2, :, :LANES]))
    pay[0, 5:8, :] = jnp.zeros((3, LANES), F32)
    spread(pay)


def split_kernel(
    meta, got, pre, low, high, gain, shift, w, hid, out, top, bottom, pay, stat, acc, *, blocks, rows
):
    slab = rows * COLS
    sums = jnp.sum(got[...], 0)
    counted = row_of(jnp.concatenate([sums[4:5]] * 2, 0), 0, 2)
    center, inv = stats(row_of(sums, 0, 2), row_of(sums, 2, 2), counted)
    stat[...] = jnp.zeros_like(stat)
    stat[0:1] = center
    stat[1:2] = inv
    stat[2:3] = counted
    scale = inv * gain[...]
    offset = shift[...]

    def prepare(i, carry):
        edge = pl.ds(pl.multiple_of(i * COLS, COLS), COLS)
        own = pl.ds(pl.multiple_of(i * slab, slab), slab)
        tall = jnp.concatenate([low[edge, :], pre[own, :], high[edge, :]], axis=0)
        z = (tall - center) * scale + offset
        mask = wide(inside(meta, i, -1, rows + 2), z.shape[1])
        left, middle, right = shifted(z * sigmoid(z) * mask)
        hid[0, i] = left
        hid[1, i] = middle
        hid[2, i] = right
        return carry

    lax.fori_loop(0, blocks, prepare, 0)
    acc[...] = jnp.zeros_like(acc)
    group = 4

    def step(g, carry):
        for half in range(2):
            lanes = slice(half * 128, half * 128 + 128)
            outs = slice(half * 256, half * 256 + 256)
            lhs = jnp.concatenate(
                [
                    hid[dx, pl.ds(g * group, group), dy * COLS : dy * COLS + slab, lanes].reshape(
                        group * slab, 128
                    )
                    for dy in range(3)
                    for dx in range(3)
                ],
                axis=1,
            )
            value = dot(lhs, w[:, :, half].reshape(9 * 128, 256))
            for j in range(group):
                image = g * group + j
                mask = inside(meta, image, 0, rows)
                part = value[j * slab : (j + 1) * slab] * wide(mask, 256)
                out[pl.ds(pl.multiple_of(image * slab, slab), slab), outs] = part
                edge = pl.ds(pl.multiple_of(image * COLS, COLS), COLS)
                top[edge, outs] = part[:COLS]
                bottom[edge, outs] = part[slab - COLS :]
                acc[0, :, outs] += fold(part)
                acc[1, :, outs] += fold(part * part)
        return carry

    lax.fori_loop(0, blocks // group, step, 0)
    put_row(pay, 0, total(acc[0]))
    put_row(pay, 4, total(acc[1]))
    spread(pay)


def pool_kernel(
    meta, got, stat, pre, gain, shift, w, hid, pooled, pay, stat2, *, blocks, rows
):
    slab = rows * COLS
    sums = jnp.sum(got[...], 0)
    counted = jnp.concatenate([stat[2:3]] * 2, axis=1)
    center, inv = stats(row_of(sums, 0, 4), row_of(sums, 4, 4), counted)
    stat2[...] = jnp.zeros_like(stat2)
    stat2[0:1] = center
    stat2[1:2] = inv
    stat2[2:3] = counted
    scale = inv * gain[...]
    offset = shift[...]

    def step(i, carry):
        own = pl.ds(pl.multiple_of(i * slab, slab), slab)
        mask = wide(inside(meta, i, 0, rows), 256)
        summed = None
        for half in range(2):
            lanes = slice(half * 256, half * 256 + 256)
            z = (pre[own, lanes] - center[:, lanes]) * scale[:, lanes] + offset[:, lanes]
            value = (z * sigmoid(z) * mask).astype(BF16)
            hid[own, lanes] = value
            part = fold(value.astype(F32))
            summed = part if summed is None else summed + part
        pooled[pl.ds(i, 1), :] = total(summed) / area_of(meta, i)
        return carry

    lax.fori_loop(0, blocks, step, 0)
    pay[0] = dot(pooled[...], w[...], precision=HIGHEST)
    spread(pay)


def squeeze_stats(block):
    return stats(total(block), total(block * block), float(block.shape[0]))


def expand_kernel(
    meta, got, hid, gain, shift, we, bias, w, mix, pre, att, hsq, znorm, zall, pay, stat_sq, acc, *, blocks, rows, parts
):
    slab = rows * COLS
    bands = got.shape[0] // parts
    for b in range(bands):
        block = got[b * parts]
        for k in range(1, parts):
            block = block + got[b * parts + k]
        znorm[b * blocks : (b + 1) * blocks, :] = block
    center, inv = squeeze_stats(znorm[...])
    stat_sq[...] = jnp.zeros_like(stat_sq)
    stat_sq[0:1] = center
    stat_sq[1:2] = inv
    normed = (znorm[...] - center) * inv
    znorm[...] = normed
    zall[...] = normed * gain[...] + shift[...]
    own_z = zall[pl.ds(pl.multiple_of(meta[1] * blocks, blocks), blocks), :]
    hidden = own_z * jax.nn.sigmoid(own_z)
    hsq[...] = hidden
    logits = dot(hidden, we[...], precision=HIGHEST) + bias[...]
    first = logits[:, :256]
    second = logits[:, 256:]
    ceiling = jnp.maximum(first, second)
    exp_first = jnp.exp(first - ceiling)
    exp_second = jnp.exp(second - ceiling)
    att[:, :256] = exp_first / (exp_first + exp_second)
    att[:, 256:] = exp_second / (exp_first + exp_second)
    acc[...] = jnp.zeros_like(acc)
    group = 4

    def step(g, carry):
        for j in range(group):
            image = g * group + j
            own = pl.ds(pl.multiple_of(image * slab, slab), slab)
            weights = att[pl.ds(image, 1), :]
            mix[own, :] = (
                weights[:, :256] * hid[own, :256].astype(F32)
                + weights[:, 256:] * hid[own, 256:].astype(F32)
            ).astype(BF16)
        many = pl.ds(pl.multiple_of(g * group * slab, group * slab), group * slab)
        for k in range(4):
            lanes = slice(k * 256, k * 256 + 256)
            value = dot(mix[many, :], w[:, lanes]).astype(BF16)
            pre[many, lanes] = value
            value = value.astype(F32)
            acc[0, :, lanes] += fold(value)
            acc[1, :, lanes] += fold(value * value)
        return carry

    lax.fori_loop(0, blocks // group, step, 0)
    put_row(pay, 0, total(acc[0]))
    put_row(pay, 8, total(acc[1]))
    spread(pay)


def residual_kernel(
    meta, got, stat, x, pre, cot, gain, shift, out, grad, pay, stat3, acc, *, blocks, rows
):
    slab = rows * COLS
    sums = jnp.sum(got[...], 0)
    counted = jnp.concatenate([stat[2:3]] * 4, axis=1)
    center, inv = stats(row_of(sums, 0, 8), row_of(sums, 8, 8), counted)
    stat3[...] = jnp.zeros_like(stat3)
    stat3[0:1] = center
    stat3[1:2] = inv
    stat3[2:3] = counted
    acc[...] = jnp.zeros_like(acc)

    def step(i, carry):
        own = pl.ds(pl.multiple_of(i * slab, slab), slab)
        mask = wide(inside(meta, i, 0, rows), 256)
        for k in range(4):
            lanes = slice(k * 256, k * 256 + 256)
            normed = (pre[own, lanes].astype(F32) - center[:, lanes]) * inv[:, lanes]
            value = normed * gain[:, lanes] + shift[:, lanes] + x[own, lanes].astype(F32)
            part = sigmoid(value)
            silu = value * part
            out[own, lanes] = (silu * mask).astype(BF16)
            slope = part + silu * (1.0 - part)
            back = cot[own, lanes].astype(F32) * mask * slope
            grad[own, lanes] = back
            acc[0, :, lanes] += fold(back)
            acc[1, :, lanes] += fold(back * normed)
        return carry

    lax.fori_loop(0, blocks, step, 0)
    put_row(pay, 0, total(acc[0]))
    put_row(pay, 8, total(acc[1]))
    spread(pay)


def back_terms(stat, gain, shift_sum, gain_sum):
    center, inv, counted = stat[0:1], stat[1:2], stat[2:3]
    a = gain * inv
    d = -a * inv * (gain_sum / counted)
    b = -a * (shift_sum / counted) - d * center
    return a, b, d


def mixture_kernel(
    meta, got, stat3, pre, grad, gain, w, hid, att, we, gexp, gmix, top, bottom, glog, pay, sums_out, *, blocks, rows
):
    slab = rows * COLS
    sums = jnp.sum(got[...], 0)
    shift_sum, gain_sum = row_of(sums, 0, 8), row_of(sums, 8, 8)
    sums_out[0:1] = shift_sum
    sums_out[1:2] = gain_sum
    a, b, d = back_terms(stat3, gain[...], shift_sum, gain_sum)
    group = 4

    def step(g, carry):
        many = pl.ds(pl.multiple_of(g * group * slab, group * slab), group * slab)
        for j in range(group):
            image = g * group + j
            own = pl.ds(pl.multiple_of(image * slab, slab), slab)
            mask = wide(inside(meta, image, 0, rows), 256)
            for k in range(4):
                lanes = slice(k * 256, k * 256 + 256)
                gexp[own, lanes] = (
                    mask
                    * (
                        a[:, lanes] * grad[own, lanes]
                        + b[:, lanes]
                        + d[:, lanes] * pre[own, lanes].astype(F32)
                    )
                ).astype(BF16)
        value = dot(gexp[many, :], w[...], ((1,), (1,))).astype(BF16)
        gmix[many, :] = value
        value = value.astype(F32)
        for j in range(group):
            image = g * group + j
            own = pl.ds(pl.multiple_of(image * slab, slab), slab)
            edge = pl.ds(pl.multiple_of(image * COLS, COLS), COLS)
            part = value[j * slab : (j + 1) * slab]
            top[edge, :] = part[:COLS].astype(BF16)
            bottom[edge, :] = part[slab - COLS :].astype(BF16)
            for half in range(2):
                lanes = slice(half * 256, half * 256 + 256)
                glog[pl.ds(image, 1), lanes] = total(fold(part * hid[own, lanes].astype(F32)))
        return carry

    lax.fori_loop(0, blocks // group, step, 0)
    first, second = att[:, :256], att[:, 256:]
    inner = first * glog[:, :256] + second * glog[:, 256:]
    logits = jnp.concatenate(
        [first * (glog[:, :256] - inner), second * (glog[:, 256:] - inner)], axis=1
    )
    glog[...] = logits
    pay[0] = dot(logits, we[...], ((1,), (1,)), HIGHEST)
    spread(pay)


def expand_grad_kernel(meta, mix, gexp, hsq, glog, out, excite, bias):
    for k in range(4):
        lanes = slice(k * 256, k * 256 + 256)
        out[:, lanes] = dot(mix[...], gexp[:, lanes], ((0,), (0,))).astype(BF16)
    excite[...] = dot(hsq[...], glog[...], ((0,), (0,)), HIGHEST)
    bias[...] = jnp.zeros_like(bias)
    put = total(glog[...])
    for k in range(4):
        bias[k : k + 1, :] = put[:, k * LANES : (k + 1) * LANES]


def hidden_kernel(
    meta, got, znorm, zall, hsq_gain, stat_sq, pooled, wsq, att, gmix, pre, stat2, gain, shift,
    dz, gpool, squeeze, pay, sums_out, acc, full, *, blocks, rows, parts
):
    slab = rows * COLS
    bands = got.shape[0] // parts
    for b in range(bands):
        block = got[b * parts]
        for k in range(1, parts):
            block = block + got[b * parts + k]
        full[b * blocks : (b + 1) * blocks, :] = block
    z = zall[...]
    part = jax.nn.sigmoid(z)
    grad_z = full[...] * (part * (1.0 + z * (1.0 - part)))
    full[...] = grad_z
    images = float(bands * blocks)
    shift_sum = total(grad_z)
    gain_sum = total(grad_z * znorm[...])
    sums_out[...] = jnp.zeros_like(sums_out)
    sums_out[0:1] = shift_sum
    sums_out[1:2] = gain_sum
    mine = pl.ds(pl.multiple_of(meta[1] * blocks, blocks), blocks)
    grad_pre = (
        hsq_gain[...]
        * stat_sq[1:2]
        * (full[mine, :] - shift_sum / images - znorm[mine, :] * (gain_sum / images))
    )
    squeeze[...] = dot(pooled[...], grad_pre, ((0,), (0,)), HIGHEST)
    gpool[...] = dot(grad_pre, wsq[...], ((1,), (1,)), HIGHEST)
    for i in range(blocks):
        gpool[i : i + 1, :] = gpool[i : i + 1, :] / area_of(meta, i)
    center, inv = stat2[0:1], stat2[1:2]
    acc[...] = jnp.zeros_like(acc)

    def step(i, carry):
        own = pl.ds(pl.multiple_of(i * slab, slab), slab)
        mask = wide(inside(meta, i, 0, rows), 256)
        mixed = gmix[own, :].astype(F32)
        pool = gpool[pl.ds(i, 1), :]
        for half in range(2):
            lanes = slice(half * 256, half * 256 + 256)
            normed = (pre[own, lanes] - center[:, lanes]) * inv[:, lanes]
            value = normed * gain[:, lanes] + shift[:, lanes]
            sig = sigmoid(value)
            slope = sig * (1.0 + value * (1.0 - sig))
            hidden = (mixed * att[pl.ds(i, 1), lanes] + pool).astype(BF16).astype(F32)
            back = hidden * mask * slope
            dz[own, lanes] = back
            acc[0, :, lanes] += fold(back)
            acc[1, :, lanes] += fold(back * normed)
        return carry

    lax.fori_loop(0, blocks, step, 0)
    put_row(pay, 0, total(acc[0]))
    put_row(pay, 4, total(acc[1]))
    spread(pay)


def conv_kernel(
    meta, got, stat2, gain2, shift2, dz, pre2, low2, high2, lowm, highm, att, gpool, w, pre, stat, gain, shift,
    gsplit, out, pay, sums_out, tall, acc, *, blocks, rows
):
    slab = rows * COLS
    sums = jnp.sum(got[...], 0)
    shift_sum, gain_sum = row_of(sums, 0, 4), row_of(sums, 4, 4)
    sums_out[0:1] = shift_sum
    sums_out[1:2] = gain_sum
    a, b, d = back_terms(stat2, gain2[...], shift_sum, gain_sum)
    center2, inv2 = stat2[0:1], stat2[1:2]

    def prepare(i, carry):
        own = pl.ds(pl.multiple_of(i * slab, slab), slab)
        edge = pl.ds(pl.multiple_of(i * COLS, COLS), COLS)
        mask = inside(meta, i, -1, rows + 2)
        for half in range(2):
            lanes = slice(half * 256, half * 256 + 256)

            def edge_grad(values, mixed, keep):
                z = (values[edge, lanes] - center2[:, lanes]) * inv2[:, lanes]
                z = z * gain2[:, lanes] + shift2[:, lanes]
                sig = sigmoid(z)
                slope = sig * (1.0 + z * (1.0 - sig))
                hidden = (
                    mixed[edge, :].astype(F32) * att[pl.ds(i, 1), lanes] + gpool[pl.ds(i, 1), :]
                ).astype(BF16)
                return hidden.astype(F32) * keep * slope

            keep_low = wide(mask[:COLS], 256)
            keep_high = wide(mask[slab + COLS :], 256)
            grads = jnp.concatenate(
                [edge_grad(low2, lowm, keep_low), dz[own, lanes], edge_grad(high2, highm, keep_high)],
                axis=0,
            )
            values = jnp.concatenate([low2[edge, lanes], pre2[own, lanes], high2[edge, lanes]], axis=0)
            back = wide(mask, 256) * (a[:, lanes] * grads + b[:, lanes] + d[:, lanes] * values)
            left, middle, right = shifted(back)
            tall[0, i, :, lanes] = left
            tall[1, i, :, lanes] = middle
            tall[2, i, :, lanes] = right
            gsplit[own, lanes] = middle[COLS : COLS + slab]
        return carry

    lax.fori_loop(0, blocks, prepare, 0)
    acc[...] = jnp.zeros_like(acc)
    center, inv = stat[0:1], stat[1:2]
    group = 4

    def step(g, carry):
        for half in range(2):
            lanes = slice(half * 256, half * 256 + 256)
            outs = slice(half * 128, half * 128 + 128)
            value = None
            for dy in range(3):
                for dx in range(3):
                    lhs = tall[
                        2 - dx, pl.ds(g * group, group), (2 - dy) * COLS : (2 - dy) * COLS + slab, lanes
                    ].reshape(group * slab, 256)
                    part = dot(lhs, w[dy, dx, half], ((1,), (1,)))
                    value = part if value is None else value + part
            for j in range(group):
                image = g * group + j
                own = pl.ds(pl.multiple_of(image * slab, slab), slab)
                mask = inside(meta, image, 0, rows)
                normed = (pre[own, outs] - center[:, outs]) * inv[:, outs]
                z = normed * gain[:, outs] + shift[:, outs]
                sig = sigmoid(z)
                slope = sig * (1.0 + z * (1.0 - sig))
                back = value[j * slab : (j + 1) * slab] * mask * slope
                out[own, outs] = back
                acc[0, :, outs] += fold(back)
                acc[1, :, outs] += fold(back * normed)
        return carry

    lax.fori_loop(0, blocks // group, step, 0)
    put_row(pay, 0, total(acc[0]))
    put_row(pay, 2, total(acc[1]))
    pay[0, 4:8, :] = jnp.zeros((4, LANES), F32)
    spread(pay)


def split_grad_kernel(meta, hid, gsplit, out, *, blocks, rows):
    slab = rows * COLS
    for half in range(2):
        lanes = slice(half * 128, half * 128 + 128)
        grads = gsplit[:, half * 256 : half * 256 + 256]
        for dy in range(3):
            lhs = jnp.concatenate(
                [
                    hid[dx, :, dy * COLS : dy * COLS + slab, lanes].reshape(blocks * slab, 128)
                    for dx in range(3)
                ],
                axis=1,
            )
            value = dot(lhs, grads, ((0,), (0,))).astype(BF16)
            for dx in range(3):
                out[dy, dx, half] = value[dx * 128 : (dx + 1) * 128]


def input_kernel(meta, got, stat, gain, dz, pre, w, x, grad, out, wgrad, sums_out, small, *, blocks, rows):
    slab = rows * COLS
    sums = jnp.sum(got[...], 0)
    shift_sum, gain_sum = row_of(sums, 0, 2), row_of(sums, 2, 2)
    sums_out[0:1] = shift_sum
    sums_out[1:2] = gain_sum
    a, b, d = back_terms(stat, gain[...], shift_sum, gain_sum)
    group = 4

    def step(g, carry):
        many = pl.ds(pl.multiple_of(g * group * slab, group * slab), group * slab)
        for j in range(group):
            image = g * group + j
            own = pl.ds(pl.multiple_of(image * slab, slab), slab)
            mask = wide(inside(meta, image, 0, rows), 256)
            small[own, :] = (mask * (a * dz[own, :] + b + d * pre[own, :])).astype(BF16)
        for k in range(4):
            lanes = slice(k * 256, k * 256 + 256)
            value = dot(small[many, :], w[lanes, :], ((1,), (1,)))
            for j in range(group):
                image = g * group + j
                own = pl.ds(pl.multiple_of(image * slab, slab), slab)
                mask = wide(inside(meta, image, 0, rows), 256)
                out[own, lanes] = (
                    (value[j * slab : (j + 1) * slab] + grad[own, lanes]) * mask
                ).astype(BF16)
        return carry

    lax.fori_loop(0, blocks // group, step, 0)
    wgrad[...] = dot(x[...], small[...], ((0,), (0,))).astype(BF16)


def body(
    inputs,
    image_class,
    weight_reduce,
    gain_reduce,
    shift_reduce,
    weight_split,
    gain_split,
    shift_split,
    weight_squeeze,
    gain_squeeze,
    shift_squeeze,
    weight_excite,
    bias_excite,
    weight_expand,
    gain_expand,
    shift_expand,
    cotangent,
):
    blocks, rows, cols, channels = inputs.shape
    mid = weight_reduce.shape[1]
    inter = weight_squeeze.shape[1]
    parts = lax.axis_size("narrow")
    count = device_count()
    pixels = blocks * rows * cols
    slab = rows * cols
    edge = blocks * cols
    images = blocks * lax.axis_size("batch")
    meta = jnp.concatenate(
        [
            (lax.axis_index("narrow") * rows).astype(jnp.int32)[None],
            lax.axis_index("batch").astype(jnp.int32)[None],
            image_class,
        ]
    )
    x = inputs.reshape(pixels, channels)
    cot = cotangent.reshape(pixels, channels)
    row = lambda v: v.reshape(1, -1)
    gain1, shift1 = row(gain_reduce), row(shift_reduce)
    gain2, shift2 = row(gain_split), row(shift_split)
    gain3, shift3 = row(gain_expand), row(shift_expand)
    gain_sq, shift_sq = row(gain_squeeze), row(shift_squeeze)
    sizes = dict(blocks=blocks, rows=rows)
    small = 2 * pixels * channels * mid
    large = 2 * pixels * 9 * 128 * 512

    pre1, top, bottom, pay = call(
        reduce_kernel,
        [((pixels, mid), F32), ((edge, mid), F32), ((edge, mid), F32), ((count, 8, LANES), F32)],
        [meta, x, weight_reduce],
        [((3, 8, mid), F32)],
        flops=small,
        **sizes,
    )
    low, high = halo(top, bottom)
    hid1, pre2, top, bottom, pay, stat1 = call(
        split_kernel,
        [
            ((3, blocks, slab + 2 * cols, mid), BF16),
            ((pixels, 2 * mid), F32),
            ((edge, 2 * mid), F32),
            ((edge, 2 * mid), F32),
            ((count, 8, LANES), F32),
            ((8, mid), F32),
        ],
        [meta, exchange(pay), pre1, low, high, gain1, shift1, weight_split],
        [((2, 8, 2 * mid), F32)],
        flops=large,
        **sizes,
    )
    low2, high2 = halo(top, bottom)
    hid2, pooled, pay, stat2 = call(
        pool_kernel,
        [
            ((pixels, 2 * mid), BF16),
            ((blocks, mid), F32),
            ((count, blocks, inter), F32),
            ((8, 2 * mid), F32),
        ],
        [meta, exchange(pay), stat1, pre2, gain2, shift2, weight_squeeze],
        **sizes,
    )
    mix, pre3, att, hsq, znorm, zall, pay, stat_sq = call(
        expand_kernel,
        [
            ((pixels, mid), BF16),
            ((pixels, channels), BF16),
            ((blocks, 2 * mid), F32),
            ((blocks, inter), F32),
            ((images, inter), F32),
            ((images, inter), F32),
            ((count, 16, LANES), F32),
            ((8, inter), F32),
        ],
        [
            meta,
            exchange(pay),
            hid2,
            gain_sq,
            shift_sq,
            weight_excite,
            row(bias_excite),
            weight_expand,
        ],
        [((2, 8, channels), F32)],
        flops=small,
        parts=parts,
        **sizes,
    )
    out, grad_res, pay, stat3 = call(
        residual_kernel,
        [
            ((pixels, channels), BF16),
            ((pixels, channels), F32),
            ((count, 16, LANES), F32),
            ((8, channels), F32),
        ],
        [meta, exchange(pay), stat1, x, pre3, cot, gain3, shift3],
        [((2, 8, channels), F32)],
        **sizes,
    )
    gexp, gmix, top, bottom, glog, pay, sums3 = call(
        mixture_kernel,
        [
            ((pixels, channels), BF16),
            ((pixels, mid), BF16),
            ((edge, mid), BF16),
            ((edge, mid), BF16),
            ((blocks, 2 * mid), F32),
            ((count, blocks, inter), F32),
            ((2, channels), F32),
        ],
        [meta, exchange(pay), stat3, pre3, grad_res, gain3, weight_expand, hid2, att, weight_excite],
        flops=small,
        **sizes,
    )
    lowm, highm = halo(top, bottom)
    expand_part, excite_part, bias_part = call(
        expand_grad_kernel,
        [((mid, channels), BF16), ((inter, 2 * mid), F32), ((8, LANES), F32)],
        [meta, mix, gexp, hsq, glog],
        flops=small,
    )
    dz2, gpool, squeeze_part, pay, sums_sq = call(
        hidden_kernel,
        [
            ((pixels, 2 * mid), F32),
            ((blocks, mid), F32),
            ((mid, inter), F32),
            ((count, 8, LANES), F32),
            ((8, inter), F32),
        ],
        [
            meta,
            exchange(pay),
            znorm,
            zall,
            gain_sq,
            stat_sq,
            pooled,
            weight_squeeze,
            att,
            gmix,
            pre2,
            stat2,
            gain2,
            shift2,
        ],
        [((2, 8, 2 * mid), F32), ((images, inter), F32)],
        parts=parts,
        **sizes,
    )
    gsplit, dz1, pay, sums2 = call(
        conv_kernel,
        [
            ((pixels, 2 * mid), BF16),
            ((pixels, mid), F32),
            ((count, 8, LANES), F32),
            ((2, 2 * mid), F32),
        ],
        [
            meta,
            exchange(pay),
            stat2,
            gain2,
            shift2,
            dz2,
            pre2,
            low2,
            high2,
            lowm,
            highm,
            att,
            gpool,
            weight_split,
            pre1,
            stat1,
            gain1,
            shift1,
        ],
        [((3, blocks, slab + 2 * cols, 2 * mid), BF16), ((2, 8, mid), F32)],
        flops=large,
        **sizes,
    )
    (split_part,) = call(
        split_grad_kernel,
        [(weight_split.shape, BF16)],
        [meta, hid1, gsplit],
        flops=large,
        **sizes,
    )
    input_grad, reduce_part, sums1 = call(
        input_kernel,
        [((pixels, channels), BF16), ((channels, mid), BF16), ((2, mid), F32)],
        [meta, exchange(pay), stat1, gain1, dz1, pre1, weight_reduce, x, grad_res],
        [((pixels, mid), BF16)],
        flops=2 * small,
        **sizes,
    )
    per = -(-(squeeze_part.size // LANES + 8) // count)
    flat = jnp.concatenate([squeeze_part, bias_part])
    flat = jnp.pad(flat, ((0, per * count - flat.shape[0]), (0, 0))).reshape(count, per, LANES)
    mine = jnp.sum(exchange(flat), 0)
    full = exchange(jnp.broadcast_to(mine[None], (count,) + mine.shape)).reshape(-1, LANES)
    squeeze_total = full[:mid]
    bias_total = full[mid : mid + 4].reshape(-1)
    expand_total, excite_total = sum_weights(expand_part, excite_part)
    (split_total,) = sum_weights(split_part)
    (reduce_total,) = sum_weights(reduce_part)
    return (
        out.reshape(inputs.shape),
        input_grad.reshape(inputs.shape),
        reduce_total,
        sums1[1],
        sums1[0],
        split_total,
        sums2[1],
        sums2[0],
        squeeze_total,
        sums_sq[1],
        sums_sq[0],
        excite_total,
        bias_total,
        expand_total,
        sums3[1],
        sums3[0],
    )


def solution(mesh):
    rows = P("batch", "narrow", None, None)
    return jax.shard_map(
        body,
        mesh=mesh,
        in_specs=(rows, P("batch")) + (P(),) * 14 + (rows,),
        out_specs=(rows, rows) + (P(),) * 14,
        check_vma=False,
    )
```

```python
import functools

import jax
import jax.numpy as jnp
from jax import lax
from jax.experimental import pallas as pl
from jax.experimental.pallas import tpu as pltpu
from jax.sharding import PartitionSpec as P

EPSILON = 1e-05
HIGHEST = lax.Precision.HIGHEST
ALL = ("batch", "narrow")
F32 = jnp.float32
BF16 = jnp.bfloat16
COLS = 16
LANES = 128


def device_count():
    return lax.axis_size("batch") * lax.axis_size("narrow")


def halo(top, bottom):
    count = lax.axis_size("narrow")
    low = lax.ppermute(bottom, "narrow", [(i, i + 1) for i in range(count - 1)])
    high = lax.ppermute(top, "narrow", [(i + 1, i) for i in range(count - 1)])
    return low, high


def exchange(block):
    return lax.all_to_all(block, ALL, 0, 0)


def swap_cores(block):
    count = lax.axis_size("narrow")
    return lax.ppermute(block, "narrow", [(i, i ^ 1) for i in range(count)])


def exchange_chips(block):
    count = device_count()
    groups = [[i for i in range(count) if i % 2 == core] for core in range(2)]
    return lax.all_to_all(block, ALL, 0, 0, axis_index_groups=groups)


def sigmoid(values):
    return 0.5 * jnp.tanh(0.5 * values) + 0.5


def wide(mask, width):
    return jnp.concatenate([mask] * (width // LANES), axis=1) if width > LANES else mask


def inside(meta, image, start, count):
    pixel = lax.broadcasted_iota(jnp.int32, (count * COLS, LANES), 0)
    row = (pixel >> 4) + (meta[0] + start)
    col = pixel & (COLS - 1)
    side = 12 + 2 * meta[3 + image]
    return jnp.where((row < side) & (row >= 0) & (col < side), 1.0, 0.0).astype(F32)


def area_of(meta, image):
    side = (12 + 2 * meta[3 + image]).astype(F32)
    return side * side


def row_of(block, first, count):
    return jnp.concatenate([block[first + k : first + k + 1] for k in range(count)], axis=1)


def put_row(ref, first, vector):
    for k in range(vector.shape[1] // LANES):
        ref[0, first + k : first + k + 1, :] = vector[:, k * LANES : (k + 1) * LANES]


def spread(ref):
    block = ref[0]

    def step(k, carry):
        ref[k] = block
        return carry

    lax.fori_loop(1, ref.shape[0], step, 0)


def fold(values):
    return jnp.sum(values.reshape(-1, 8, values.shape[-1]), 0)


def total(block):
    return jnp.sum(block, 0, keepdims=True)


def stats(totals, squares, counted):
    center = totals / counted
    return center, lax.rsqrt(squares / counted - center * center + EPSILON)


def shifted(values):
    count, width = values.shape
    col = lax.broadcasted_iota(jnp.int32, (count, LANES), 0) & (COLS - 1)
    has_left = wide(jnp.where(col > 0, 1.0, 0.0).astype(F32), width)
    has_right = wide(jnp.where(col < COLS - 1, 1.0, 0.0).astype(F32), width)
    left = pltpu.roll(values, 1, 0) * has_left
    right = pltpu.roll(values, count - 1, 0) * has_right
    return left.astype(BF16), values.astype(BF16), right.astype(BF16)


def dot(a, b, dims=((1,), (0,)), precision=None):
    return lax.dot_general(a, b, (dims, ((), ())), precision=precision, preferred_element_type=F32)


def whole(shape):
    return pl.BlockSpec(shape, lambda step: (0,) * len(shape))


def call(kernel, outs, args, scratch=(), megabytes=56, flops=0, after=(), local="", **sizes):
    moved = sum(a.size * a.dtype.itemsize for a in args) + sum(
        functools.reduce(lambda x, y: x * y, s) * jnp.dtype(t).itemsize for s, t in outs
    )
    count = len(args)
    vmem = pl.BlockSpec(memory_space=pltpu.VMEM)

    def run(*refs):
        kernel(*refs[:count], *refs[count + len(after) :], **sizes)

    return pl.pallas_call(
        run,
        grid=() if local == "in out" else (1,),
        out_shape=[jax.ShapeDtypeStruct(s, t) for s, t in outs],
        in_specs=[pl.BlockSpec(memory_space=pltpu.SMEM)]
        + [vmem if "in" in local else whole(a.shape) for a in args[1:]]
        + [pl.BlockSpec(memory_space=pl.ANY)] * len(after),
        out_specs=[vmem if "out" in local else whole(s) for s, _ in outs],
        scratch_shapes=[pltpu.VMEM(s, t) for s, t in scratch],
        compiler_params=pltpu.CompilerParams(vmem_limit_bytes=(24 if local else megabytes) << 20),
        cost_estimate=pl.CostEstimate(flops=flops, bytes_accessed=moved, transcendentals=0),
    )(*args, *after)


def reduce_kernel(meta, x, w, pre, top, bottom, pay, acc, *, blocks, rows):
    slab = rows * COLS
    acc[...] = jnp.zeros_like(acc)
    group = 4

    def step(g, carry):
        base = pl.multiple_of(g * group * slab, group * slab)
        out = dot(x[pl.ds(base, group * slab), :], w[...])
        for j in range(group):
            image = g * group + j
            mask = inside(meta, image, 0, rows)
            part = out[j * slab : (j + 1) * slab] * wide(mask, out.shape[1])
            pre[pl.ds(pl.multiple_of(image * slab, slab), slab), :] = part
            edge = pl.ds(pl.multiple_of(image * COLS, COLS), COLS)
            top[edge, :] = part[:COLS]
            bottom[edge, :] = part[slab - COLS :]
            acc[0] += fold(part)
            acc[1] += fold(part * part)
            acc[2, :, :LANES] += fold(mask)
        return carry

    lax.fori_loop(0, blocks // group, step, 0)
    put_row(pay, 0, total(acc[0]))
    put_row(pay, 2, total(acc[1]))
    put_row(pay, 4, total(acc[2, :, :LANES]))
    pay[0, 5:8, :] = jnp.zeros((3, LANES), F32)
    spread(pay)


def split_kernel(
    meta, got, pre, low, high, gain, shift, w, hid, out, top, bottom, pay, stat, acc, *, blocks, rows
):
    slab = rows * COLS
    sums = jnp.sum(got[...], 0)
    counted = row_of(jnp.concatenate([sums[4:5]] * 2, 0), 0, 2)
    center, inv = stats(row_of(sums, 0, 2), row_of(sums, 2, 2), counted)
    stat[...] = jnp.zeros_like(stat)
    stat[0:1] = center
    stat[1:2] = inv
    stat[2:3] = counted
    scale = inv * gain[...]
    offset = shift[...]

    def prepare(i, carry):
        edge = pl.ds(pl.multiple_of(i * COLS, COLS), COLS)
        own = pl.ds(pl.multiple_of(i * slab, slab), slab)
        tall = jnp.concatenate([low[edge, :], pre[own, :], high[edge, :]], axis=0)
        z = (tall - center) * scale + offset
        mask = wide(inside(meta, i, -1, rows + 2), z.shape[1])
        left, middle, right = shifted(z * sigmoid(z) * mask)
        hid[0, i] = left
        hid[1, i] = middle
        hid[2, i] = right
        return carry

    lax.fori_loop(0, blocks, prepare, 0)
    acc[...] = jnp.zeros_like(acc)
    group = 4

    def step(g, carry):
        for half in range(2):
            lanes = slice(half * 128, half * 128 + 128)
            outs = slice(half * 256, half * 256 + 256)
            lhs = jnp.concatenate(
                [
                    hid[dx, pl.ds(g * group, group), dy * COLS : dy * COLS + slab, lanes].reshape(
                        group * slab, 128
                    )
                    for dy in range(3)
                    for dx in range(3)
                ],
                axis=1,
            )
            value = dot(lhs, w[:, :, half].reshape(9 * 128, 256))
            for j in range(group):
                image = g * group + j
                mask = inside(meta, image, 0, rows)
                part = value[j * slab : (j + 1) * slab] * wide(mask, 256)
                out[pl.ds(pl.multiple_of(image * slab, slab), slab), outs] = part
                edge = pl.ds(pl.multiple_of(image * COLS, COLS), COLS)
                top[edge, outs] = part[:COLS]
                bottom[edge, outs] = part[slab - COLS :]
                acc[0, :, outs] += fold(part)
                acc[1, :, outs] += fold(part * part)
        return carry

    lax.fori_loop(0, blocks // group, step, 0)
    put_row(pay, 0, total(acc[0]))
    put_row(pay, 4, total(acc[1]))
    spread(pay)


def pool_kernel(
    meta, got, stat, pre, gain, shift, w, hid, pooled, pay, stat2, *, blocks, rows
):
    slab = rows * COLS
    sums = jnp.sum(got[...], 0)
    counted = jnp.concatenate([stat[2:3]] * 2, axis=1)
    center, inv = stats(row_of(sums, 0, 4), row_of(sums, 4, 4), counted)
    stat2[...] = jnp.zeros_like(stat2)
    stat2[0:1] = center
    stat2[1:2] = inv
    stat2[2:3] = counted
    scale = inv * gain[...]
    offset = shift[...]

    def step(i, carry):
        own = pl.ds(pl.multiple_of(i * slab, slab), slab)
        mask = wide(inside(meta, i, 0, rows), 256)
        summed = None
        for half in range(2):
            lanes = slice(half * 256, half * 256 + 256)
            z = (pre[own, lanes] - center[:, lanes]) * scale[:, lanes] + offset[:, lanes]
            value = (z * sigmoid(z) * mask).astype(BF16)
            hid[own, lanes] = value
            part = fold(value.astype(F32))
            summed = part if summed is None else summed + part
        pooled[pl.ds(i, 1), :] = total(summed) / area_of(meta, i)
        return carry

    lax.fori_loop(0, blocks, step, 0)
    pay[0] = dot(pooled[...], w[...], precision=HIGHEST)
    spread(pay)


def squeeze_stats(block):
    return stats(total(block), total(block * block), float(block.shape[0]))


def expand_kernel(
    meta, got, hid, gain, shift, we, bias, w, mix, pre, att, hsq, znorm, zall, pay, stat_sq, acc, *, blocks, rows, parts
):
    slab = rows * COLS
    bands = got.shape[0] // parts
    for b in range(bands):
        block = got[b * parts]
        for k in range(1, parts):
            block = block + got[b * parts + k]
        znorm[b * blocks : (b + 1) * blocks, :] = block
    center, inv = squeeze_stats(znorm[...])
    stat_sq[...] = jnp.zeros_like(stat_sq)
    stat_sq[0:1] = center
    stat_sq[1:2] = inv
    normed = (znorm[...] - center) * inv
    znorm[...] = normed
    zall[...] = normed * gain[...] + shift[...]
    own_z = zall[pl.ds(pl.multiple_of(meta[1] * blocks, blocks), blocks), :]
    hidden = own_z * jax.nn.sigmoid(own_z)
    hsq[...] = hidden
    logits = dot(hidden, we[...], precision=HIGHEST) + bias[...]
    first = logits[:, :256]
    second = logits[:, 256:]
    ceiling = jnp.maximum(first, second)
    exp_first = jnp.exp(first - ceiling)
    exp_second = jnp.exp(second - ceiling)
    att[:, :256] = exp_first / (exp_first + exp_second)
    att[:, 256:] = exp_second / (exp_first + exp_second)
    acc[...] = jnp.zeros_like(acc)
    group = 4

    def step(g, carry):
        for j in range(group):
            image = g * group + j
            own = pl.ds(pl.multiple_of(image * slab, slab), slab)
            weights = att[pl.ds(image, 1), :]
            mix[own, :] = (
                weights[:, :256] * hid[own, :256].astype(F32)
                + weights[:, 256:] * hid[own, 256:].astype(F32)
            ).astype(BF16)
        many = pl.ds(pl.multiple_of(g * group * slab, group * slab), group * slab)
        for k in range(4):
            lanes = slice(k * 256, k * 256 + 256)
            value = dot(mix[many, :], w[:, lanes]).astype(BF16)
            pre[many, lanes] = value
            value = value.astype(F32)
            acc[0, :, lanes] += fold(value)
            acc[1, :, lanes] += fold(value * value)
        return carry

    lax.fori_loop(0, blocks // group, step, 0)
    put_row(pay, 0, total(acc[0]))
    put_row(pay, 8, total(acc[1]))
    spread(pay)


def residual_kernel(
    meta, got, stat, x, pre, cot, gain, shift, out, grad, pay, stat3, acc, *, blocks, rows
):
    slab = rows * COLS
    sums = jnp.sum(got[...], 0)
    counted = jnp.concatenate([stat[2:3]] * 4, axis=1)
    center, inv = stats(row_of(sums, 0, 8), row_of(sums, 8, 8), counted)
    stat3[...] = jnp.zeros_like(stat3)
    stat3[0:1] = center
    stat3[1:2] = inv
    stat3[2:3] = counted
    acc[...] = jnp.zeros_like(acc)

    def step(i, carry):
        own = pl.ds(pl.multiple_of(i * slab, slab), slab)
        mask = wide(inside(meta, i, 0, rows), 256)
        for k in range(4):
            lanes = slice(k * 256, k * 256 + 256)
            normed = (pre[own, lanes].astype(F32) - center[:, lanes]) * inv[:, lanes]
            value = normed * gain[:, lanes] + shift[:, lanes] + x[own, lanes].astype(F32)
            part = sigmoid(value)
            silu = value * part
            out[own, lanes] = (silu * mask).astype(BF16)
            slope = part + silu * (1.0 - part)
            back = cot[own, lanes].astype(F32) * mask * slope
            grad[own, lanes] = back
            acc[0, :, lanes] += fold(back)
            acc[1, :, lanes] += fold(back * normed)
        return carry

    lax.fori_loop(0, blocks, step, 0)
    put_row(pay, 0, total(acc[0]))
    put_row(pay, 8, total(acc[1]))
    spread(pay)


def back_terms(stat, gain, shift_sum, gain_sum):
    center, inv, counted = stat[0:1], stat[1:2], stat[2:3]
    a = gain * inv
    d = -a * inv * (gain_sum / counted)
    b = -a * (shift_sum / counted) - d * center
    return a, b, d


def mixture_kernel(
    meta, got, stat3, pre, grad, gain, w, hid, gexp, gmix, top, bottom, gatt, gain_out, shift_out, *, blocks, rows
):
    slab = rows * COLS
    sums = jnp.sum(got[...], 0)
    shift_sum, gain_sum = row_of(sums, 0, 8), row_of(sums, 8, 8)
    shift_out[...] = shift_sum
    gain_out[...] = gain_sum
    a, b, d = back_terms(stat3, gain[...], shift_sum, gain_sum)
    group = 4

    def step(g, carry):
        many = pl.ds(pl.multiple_of(g * group * slab, group * slab), group * slab)
        for j in range(group):
            image = g * group + j
            own = pl.ds(pl.multiple_of(image * slab, slab), slab)
            mask = wide(inside(meta, image, 0, rows), 256)
            for k in range(4):
                lanes = slice(k * 256, k * 256 + 256)
                gexp[own, lanes] = (
                    mask
                    * (
                        a[:, lanes] * grad[own, lanes]
                        + b[:, lanes]
                        + d[:, lanes] * pre[own, lanes].astype(F32)
                    )
                ).astype(BF16)
        value = dot(gexp[many, :], w[...], ((1,), (1,))).astype(BF16)
        gmix[many, :] = value
        value = value.astype(F32)
        for j in range(group):
            image = g * group + j
            own = pl.ds(pl.multiple_of(image * slab, slab), slab)
            edge = pl.ds(pl.multiple_of(image * COLS, COLS), COLS)
            part = value[j * slab : (j + 1) * slab]
            top[edge, :] = part[:COLS]
            bottom[edge, :] = part[slab - COLS :]
            for half in range(2):
                lanes = slice(half * 256, half * 256 + 256)
                gatt[pl.ds(image, 1), lanes] = total(fold(part * hid[own, lanes].astype(F32)))
        return carry

    lax.fori_loop(0, blocks // group, step, 0)


def logits_kernel(meta, gatt, att, we, glog, pay):
    first, second = att[:, :256], att[:, 256:]
    inner = first * gatt[:, :256] + second * gatt[:, 256:]
    logits = jnp.concatenate(
        [first * (gatt[:, :256] - inner), second * (gatt[:, 256:] - inner)], axis=1
    )
    glog[...] = logits
    pay[0] = dot(logits, we[...], ((1,), (1,)), HIGHEST)
    spread(pay)


def expand_grad_kernel(meta, mix, gexp, hsq, glog, keep, send):
    for ref, core in ((send, 1 - meta[2]), (keep, meta[2])):
        for k in range(2):
            lanes = pl.ds(pl.multiple_of(core * 512 + k * 256, 256), 256)
            ref[k * 256 : k * 256 + 256, :] = dot(mix[...], gexp[:, lanes], ((0,), (0,))).astype(ref.dtype)
        lanes = pl.ds(pl.multiple_of(core * 256, 256), 256)
        ref[512:, :] = dot(hsq[...], glog[:, lanes], ((0,), (0,)), HIGHEST).astype(ref.dtype)


def pack_kernel(meta, *refs):
    out = refs[-1]
    start = 0
    for keep, got in zip(refs[:-1:2], refs[1:-1:2]):
        share = keep.shape[0] // out.shape[0]
        for chip in range(out.shape[0]):
            rows = slice(chip * share, chip * share + share)
            out[chip, start : start + share, :] = (keep[rows] + got[rows].astype(F32)).astype(BF16)
        start += share


def share_kernel(meta, shares, out):
    value = shares[0].astype(F32)
    for k in range(1, shares.shape[0]):
        value = value + shares[k].astype(F32)
    out[0] = value.astype(BF16)
    block = out[0]

    def step(k, carry):
        out[k] = block
        return carry

    lax.fori_loop(1, out.shape[0], step, 0)


def hidden_kernel(
    meta, got, znorm, zall, hsq_gain, stat_sq, pooled, wsq, att, gmix, pre, stat2, gain, shift,
    dz, gpool, pay, gain_out, shift_out, acc, full, squeeze, *, blocks, rows, parts
):
    slab = rows * COLS
    bands = got.shape[0] // parts
    for b in range(bands):
        block = got[b * parts]
        for k in range(1, parts):
            block = block + got[b * parts + k]
        full[b * blocks : (b + 1) * blocks, :] = block
    z = zall[...]
    part = jax.nn.sigmoid(z)
    grad_z = full[...] * (part * (1.0 + z * (1.0 - part)))
    full[...] = grad_z
    images = float(bands * blocks)
    shift_sum = total(grad_z)
    gain_sum = total(grad_z * znorm[...])
    shift_out[...] = shift_sum
    gain_out[...] = gain_sum
    mine = pl.ds(pl.multiple_of(meta[1] * blocks, blocks), blocks)
    grad_pre = (
        hsq_gain[...]
        * stat_sq[1:2]
        * (full[mine, :] - shift_sum / images - znorm[mine, :] * (gain_sum / images))
    )
    squeeze[...] = dot(pooled[...], grad_pre, ((0,), (0,)), HIGHEST)
    gpool[...] = dot(grad_pre, wsq[...], ((1,), (1,)), HIGHEST)
    for i in range(blocks):
        gpool[i : i + 1, :] = gpool[i : i + 1, :] / area_of(meta, i)
    center, inv = stat2[0:1], stat2[1:2]
    acc[...] = jnp.zeros_like(acc)

    def step(i, carry):
        own = pl.ds(pl.multiple_of(i * slab, slab), slab)
        mask = wide(inside(meta, i, 0, rows), 256)
        mixed = gmix[own, :].astype(F32)
        pool = gpool[pl.ds(i, 1), :]
        for half in range(2):
            lanes = slice(half * 256, half * 256 + 256)
            normed = (pre[own, lanes] - center[:, lanes]) * inv[:, lanes]
            value = normed * gain[:, lanes] + shift[:, lanes]
            sig = sigmoid(value)
            slope = sig * (1.0 + value * (1.0 - sig))
            hidden = (mixed * att[pl.ds(i, 1), lanes] + pool).astype(BF16).astype(F32)
            back = hidden * mask * slope
            dz[own, lanes] = back
            acc[0, :, lanes] += fold(back)
            acc[1, :, lanes] += fold(back * normed)
        return carry

    lax.fori_loop(0, blocks, step, 0)
    put_row(pay, 0, total(acc[0]))
    put_row(pay, 4, total(acc[1]))
    pay[0, 8:, :] = jnp.zeros((pay.shape[1] - 8, LANES), F32)
    spread(pay)
    share = pay.shape[1] - 8
    for n in range(pay.shape[0]):
        pay[n, 8:, :] = squeeze[n * share : (n + 1) * share, :]


def conv_kernel(
    meta, got, stat2, gain2, shift2, dz, pre2, low2, high2, lowm, highm, att, gpool, w, pre, stat,
    gain, shift, glog, gsplit, out, pay, gain_out, shift_out, tall, acc, *, blocks, rows
):
    slab = rows * COLS
    sums = jnp.sum(got[...], 0)
    shift_sum, gain_sum = row_of(sums, 0, 4), row_of(sums, 4, 4)
    shift_out[...] = shift_sum
    gain_out[...] = gain_sum
    a, b, d = back_terms(stat2, gain2[...], shift_sum, gain_sum)
    center2, inv2 = stat2[0:1], stat2[1:2]

    def prepare(i, carry):
        own = pl.ds(pl.multiple_of(i * slab, slab), slab)
        edge = pl.ds(pl.multiple_of(i * COLS, COLS), COLS)
        mask = inside(meta, i, -1, rows + 2)
        for half in range(2):
            lanes = slice(half * 256, half * 256 + 256)

            def edge_grad(values, mixed, keep):
                z = (values[edge, lanes] - center2[:, lanes]) * inv2[:, lanes]
                z = z * gain2[:, lanes] + shift2[:, lanes]
                sig = sigmoid(z)
                slope = sig * (1.0 + z * (1.0 - sig))
                hidden = (
                    mixed[edge, :] * att[pl.ds(i, 1), lanes] + gpool[pl.ds(i, 1), :]
                ).astype(BF16)
                return hidden.astype(F32) * keep * slope

            keep_low = wide(mask[:COLS], 256)
            keep_high = wide(mask[slab + COLS :], 256)
            grads = jnp.concatenate(
                [edge_grad(low2, lowm, keep_low), dz[own, lanes], edge_grad(high2, highm, keep_high)],
                axis=0,
            )
            values = jnp.concatenate([low2[edge, lanes], pre2[own, lanes], high2[edge, lanes]], axis=0)
            back = wide(mask, 256) * (a[:, lanes] * grads + b[:, lanes] + d[:, lanes] * values)
            left, middle, right = shifted(back)
            tall[0, i, :, lanes] = left
            tall[1, i, :, lanes] = middle
            tall[2, i, :, lanes] = right
            gsplit[own, lanes] = middle[COLS : COLS + slab]
        return carry

    lax.fori_loop(0, blocks, prepare, 0)
    acc[...] = jnp.zeros_like(acc)
    center, inv = stat[0:1], stat[1:2]
    group = 4

    def step(g, carry):
        for half in range(2):
            lanes = slice(half * 256, half * 256 + 256)
            outs = slice(half * 128, half * 128 + 128)
            value = None
            for dy in range(3):
                for dx in range(3):
                    lhs = tall[
                        2 - dx, pl.ds(g * group, group), (2 - dy) * COLS : (2 - dy) * COLS + slab, lanes
                    ].reshape(group * slab, 256)
                    part = dot(lhs, w[dy, dx, half], ((1,), (1,)))
                    value = part if value is None else value + part
            for j in range(group):
                image = g * group + j
                own = pl.ds(pl.multiple_of(image * slab, slab), slab)
                mask = inside(meta, image, 0, rows)
                normed = (pre[own, outs] - center[:, outs]) * inv[:, outs]
                z = normed * gain[:, outs] + shift[:, outs]
                sig = sigmoid(z)
                slope = sig * (1.0 + z * (1.0 - sig))
                back = value[j * slab : (j + 1) * slab] * mask * slope
                out[own, outs] = back
                acc[0, :, outs] += fold(back)
                acc[1, :, outs] += fold(back * normed)
        return carry

    lax.fori_loop(0, blocks // group, step, 0)
    put_row(pay, 0, total(acc[0]))
    put_row(pay, 2, total(acc[1]))
    put_row(pay, 4, total(glog[...]))
    pay[0, 8:, :] = sums[8:]
    spread(pay)


def split_grad_kernel(meta, hid, gsplit, keep, send, *, blocks, rows):
    slab = rows * COLS
    for ref, core in ((send, 1 - meta[2]), (keep, meta[2])):
        lanes = pl.ds(pl.multiple_of(core * 128, 128), 128)
        grads = gsplit[:, pl.ds(pl.multiple_of(core * 256, 256), 256)]
        for dy in range(3):
            lhs = jnp.concatenate(
                [
                    hid[dx, :, dy * COLS : dy * COLS + slab, lanes].reshape(blocks * slab, 128)
                    for dx in range(3)
                ],
                axis=1,
            )
            ref[dy * 384 : dy * 384 + 384, :] = dot(lhs, grads, ((0,), (0,))).astype(ref.dtype)


def reduce_back_kernel(meta, got, stat, gain, dz, pre, x, small, keep, send, gain_out, shift_out, bias_out, squeeze, *, blocks, rows):
    slab = rows * COLS
    sums = jnp.sum(got[:, :8, :], 0)
    share = got.shape[1] - 8
    for n in range(got.shape[0]):
        squeeze[n * share : (n + 1) * share, :] = got[n, 8:, :]
    shift_sum, gain_sum = row_of(sums, 0, 2), row_of(sums, 2, 2)
    shift_out[...] = shift_sum
    gain_out[...] = gain_sum
    bias_out[...] = row_of(sums, 4, 4)
    a, b, d = back_terms(stat, gain[...], shift_sum, gain_sum)

    def step(image, carry):
        own = pl.ds(pl.multiple_of(image * slab, slab), slab)
        mask = wide(inside(meta, image, 0, rows), 256)
        small[own, :] = (mask * (a * dz[own, :] + b + d * pre[own, :])).astype(BF16)
        return carry

    lax.fori_loop(0, blocks, step, 0)
    for ref, core in ((send, 1 - meta[2]), (keep, meta[2])):
        lanes = pl.ds(pl.multiple_of(core * 512, 512), 512)
        ref[...] = dot(x[:, lanes], small[...], ((0,), (0,))).astype(ref.dtype)


def input_kernel(meta, small, w, grad, out, *, blocks, rows):
    slab = rows * COLS
    group = 4

    def step(g, carry):
        many = pl.ds(pl.multiple_of(g * group * slab, group * slab), group * slab)
        for k in range(4):
            lanes = slice(k * 256, k * 256 + 256)
            value = dot(small[many, :], w[lanes, :], ((1,), (1,)))
            for j in range(group):
                image = g * group + j
                own = pl.ds(pl.multiple_of(image * slab, slab), slab)
                mask = wide(inside(meta, image, 0, rows), 256)
                out[own, lanes] = (
                    (value[j * slab : (j + 1) * slab] + grad[own, lanes]) * mask
                ).astype(BF16)
        return carry

    lax.fori_loop(0, blocks // group, step, 0)


def total_kernel(meta, own, other, expand, excite, split, reduce):
    chips = own.shape[0]
    size3, size2, size1 = 640 // chips, 1152 // chips, 512 // chips
    for ref, core in ((own, meta[2]), (other, 1 - meta[2])):

        def part(start, size, first, rows):
            block = ref[:, start : start + size, :].reshape(chips * size, 256)
            return block[first : first + rows].astype(F32)

        for k in range(2):
            lanes = pl.ds(pl.multiple_of(core * 512 + k * 256, 256), 256)
            expand[:, lanes] = part(0, size3, k * 256, 256)
        excite[:, pl.ds(pl.multiple_of(core * 256, 256), 256)] = part(0, size3, 512, 128)
        for tap in range(9):
            split[tap // 3, tap % 3, core] = part(size3, size2, tap * 128, 128)
        reduce[pl.ds(pl.multiple_of(core * 512, 512), 512), :] = part(size3 + size2, size1, 0, 512)


def body(
    inputs,
    image_class,
    weight_reduce,
    gain_reduce,
    shift_reduce,
    weight_split,
    gain_split,
    shift_split,
    weight_squeeze,
    gain_squeeze,
    shift_squeeze,
    weight_excite,
    bias_excite,
    weight_expand,
    gain_expand,
    shift_expand,
    cotangent,
):
    blocks, rows, cols, channels = inputs.shape
    mid = weight_reduce.shape[1]
    inter = weight_squeeze.shape[1]
    parts = lax.axis_size("narrow")
    count = device_count()
    pixels = blocks * rows * cols
    slab = rows * cols
    edge = blocks * cols
    share = mid // count
    images = blocks * lax.axis_size("batch")
    meta = jnp.concatenate(
        [
            (lax.axis_index("narrow") * rows).astype(jnp.int32)[None],
            lax.axis_index("batch").astype(jnp.int32)[None],
            (lax.axis_index("narrow") % 2).astype(jnp.int32)[None],
            image_class,
        ]
    )
    x = inputs.reshape(pixels, channels)
    cot = cotangent.reshape(pixels, channels)
    row = lambda v: v.reshape(1, -1)
    gain1, shift1 = row(gain_reduce), row(shift_reduce)
    gain2, shift2 = row(gain_split), row(shift_split)
    gain3, shift3 = row(gain_expand), row(shift_expand)
    gain_sq, shift_sq = row(gain_squeeze), row(shift_squeeze)
    sizes = dict(blocks=blocks, rows=rows)
    small = 2 * pixels * channels * mid
    large = 2 * pixels * 9 * 128 * 512

    pre1, top, bottom, pay = call(
        reduce_kernel,
        [((pixels, mid), F32), ((edge, mid), F32), ((edge, mid), F32), ((count, 8, LANES), F32)],
        [meta, x, weight_reduce],
        [((3, 8, mid), F32)],
        flops=small,
        local="in out",
        **sizes,
    )
    low, high = halo(top, bottom)
    hid1, pre2, top, bottom, pay, stat1 = call(
        split_kernel,
        [
            ((3, blocks, slab + 2 * cols, mid), BF16),
            ((pixels, 2 * mid), F32),
            ((edge, 2 * mid), F32),
            ((edge, 2 * mid), F32),
            ((count, 8, LANES), F32),
            ((8, mid), F32),
        ],
        [meta, exchange(pay), pre1, low, high, gain1, shift1, weight_split],
        [((2, 8, 2 * mid), F32)],
        flops=large,
        local="in out",
        **sizes,
    )
    low2, high2 = halo(top, bottom)
    hid2, pooled, pay, stat2 = call(
        pool_kernel,
        [
            ((pixels, 2 * mid), BF16),
            ((blocks, mid), F32),
            ((count, blocks, inter), F32),
            ((8, 2 * mid), F32),
        ],
        [meta, exchange(pay), stat1, pre2, gain2, shift2, weight_squeeze],
        local="in out",
        after=(low2, high2),
        **sizes,
    )
    mix, pre3, att, hsq, znorm, zall, pay, stat_sq = call(
        expand_kernel,
        [
            ((pixels, mid), BF16),
            ((pixels, channels), BF16),
            ((blocks, 2 * mid), F32),
            ((blocks, inter), F32),
            ((images, inter), F32),
            ((images, inter), F32),
            ((count, 16, LANES), F32),
            ((8, inter), F32),
        ],
        [
            meta,
            exchange(pay),
            hid2,
            gain_sq,
            shift_sq,
            weight_excite,
            row(bias_excite),
            weight_expand,
        ],
        [((2, 8, channels), F32)],
        flops=small,
        parts=parts,
        local="in out",
        **sizes,
    )
    out, grad_res, pay, stat3 = call(
        residual_kernel,
        [
            ((pixels, channels), BF16),
            ((pixels, channels), F32),
            ((count, 16, LANES), F32),
            ((8, channels), F32),
        ],
        [meta, exchange(pay), stat1, x, pre3, cot, gain3, shift3],
        [((2, 8, channels), F32)],
        local="in out",
        **sizes,
    )
    gexp, gmix, top, bottom, gatt, gain3_grad, shift3_grad = call(
        mixture_kernel,
        [
            ((pixels, channels), BF16),
            ((pixels, mid), BF16),
            ((edge, mid), F32),
            ((edge, mid), F32),
            ((blocks, 2 * mid), F32),
            ((1, channels), F32),
            ((1, channels), F32),
        ],
        [meta, exchange(pay), stat3, pre3, grad_res, gain3, weight_expand, hid2],
        flops=small,
        local="in out",
        **sizes,
    )
    lowm, highm = halo(top, bottom)
    glog, pay = call(
        logits_kernel,
        [((blocks, 2 * mid), F32), ((count, blocks, inter), F32)],
        [meta, gatt, att, weight_excite],
        after=(lowm, highm),
        local="in out",
    )
    dz2, gpool, pay, gain_sq_grad, shift_sq_grad = call(
        hidden_kernel,
        [
            ((pixels, 2 * mid), F32),
            ((blocks, mid), F32),
            ((count, 8 + share, LANES), F32),
            ((1, inter), F32),
            ((1, inter), F32),
        ],
        [
            meta,
            exchange(pay),
            znorm,
            zall,
            gain_sq,
            stat_sq,
            pooled,
            weight_squeeze,
            att,
            gmix,
            pre2,
            stat2,
            gain2,
            shift2,
        ],
        [((2, 8, 2 * mid), F32), ((images, inter), F32), ((mid, inter), F32)],
        parts=parts,
        local="in out",
        **sizes,
    )
    gsplit, dz1, pay, gain2_grad, shift2_grad = call(
        conv_kernel,
        [
            ((pixels, 2 * mid), BF16),
            ((pixels, mid), F32),
            ((count, 8 + share, LANES), F32),
            ((1, 2 * mid), F32),
            ((1, 2 * mid), F32),
        ],
        [
            meta,
            exchange(pay),
            stat2,
            gain2,
            shift2,
            dz2,
            pre2,
            low2,
            high2,
            lowm,
            highm,
            att,
            gpool,
            weight_split,
            pre1,
            stat1,
            gain1,
            shift1,
            glog,
        ],
        [((3, blocks, slab + 2 * cols, 2 * mid), BF16), ((2, 8, mid), F32)],
        flops=large,
        local="in",
        **sizes,
    )
    keep2, send2 = call(
        split_grad_kernel,
        [((9 * 128, 256), F32), ((9 * 128, 256), BF16)],
        [meta, hid1, gsplit],
        flops=large,
        **sizes,
    )
    keep3, send3 = call(
        expand_grad_kernel,
        [((2 * mid + inter, 256), F32), ((2 * mid + inter, 256), BF16)],
        [meta, mix, gexp, hsq, glog],
        flops=small,
        after=(send2,),
    )
    small1, keep1, send1, gain1_grad, shift1_grad, bias_grad, squeeze_total = call(
        reduce_back_kernel,
        [
            ((pixels, mid), BF16),
            ((channels // 2, mid), F32),
            ((channels // 2, mid), BF16),
            ((1, mid), F32),
            ((1, mid), F32),
            ((1, 2 * mid), F32),
            ((mid, inter), F32),
        ],
        [meta, exchange(pay), stat1, gain1, dz1, pre1, x],
        flops=small,
        after=(send2, send3),
        **sizes,
    )
    chips = count // 2
    share_rows = [keep.shape[0] // chips for keep in (keep3, keep2, keep1)]
    (packed,) = call(
        pack_kernel,
        [((chips, sum(share_rows), 256), BF16)],
        [meta, keep3, swap_cores(send3), keep2, swap_cores(send2), keep1, swap_cores(send1)],
    )
    (input_grad,) = call(
        input_kernel,
        [((pixels, channels), BF16)],
        [meta, small1, weight_reduce, grad_res],
        flops=small,
        after=(packed,),
        **sizes,
    )
    (shared,) = call(share_kernel, [(packed.shape, BF16)], [meta, exchange_chips(packed)], after=(input_grad,), local="in out")
    own = exchange_chips(shared)
    expand_total, excite_total, split_total, reduce_total = call(
        total_kernel,
        [
            ((mid, channels), F32),
            ((inter, 2 * mid), F32),
            (weight_split.shape, F32),
            ((channels, mid), F32),
        ],
        [meta, own, swap_cores(own)],
        local="in",
    )
    flat = lambda v: v.reshape(-1)
    return (
        out.reshape(inputs.shape),
        input_grad.reshape(inputs.shape),
        reduce_total,
        flat(gain1_grad),
        flat(shift1_grad),
        split_total,
        flat(gain2_grad),
        flat(shift2_grad),
        squeeze_total,
        flat(gain_sq_grad),
        flat(shift_sq_grad),
        excite_total,
        flat(bias_grad),
        expand_total,
        flat(gain3_grad),
        flat(shift3_grad),
    )


def solution(mesh):
    rows = P("batch", "narrow", None, None)
    return jax.shard_map(
        body,
        mesh=mesh,
        in_specs=(rows, P("batch")) + (P(),) * 14 + (rows,),
        out_specs=(rows, rows) + (P(),) * 14,
        check_vma=False,
    )
```

```python
import functools

import jax
import jax.numpy as jnp
from jax import lax
from jax.experimental import pallas as pl
from jax.experimental.pallas import tpu as pltpu
from jax.sharding import PartitionSpec as P

EPSILON = 1e-05
HIGHEST = lax.Precision.HIGHEST
ALL = ("batch", "narrow")
F32 = jnp.float32
BF16 = jnp.bfloat16
COLS = 16
LANES = 128
TOKEN = ((8, LANES), F32, "hbm")


def device_count():
    return lax.axis_size("batch") * lax.axis_size("narrow")


def halo(top, bottom):
    count = lax.axis_size("narrow")
    low = lax.ppermute(bottom, "narrow", [(i, i + 1) for i in range(count - 1)])
    high = lax.ppermute(top, "narrow", [(i + 1, i) for i in range(count - 1)])
    return low, high


def exchange(block):
    return lax.all_to_all(block, ALL, 0, 0)


def swap(block, bit):
    count = lax.axis_size("narrow")
    return lax.ppermute(block, "narrow", [(i, i ^ bit) for i in range(count)])


def exchange_chips(block):
    count = device_count()
    groups = [[i for i in range(count) if i % 2 == core] for core in range(2)]
    return lax.all_to_all(block, ALL, 0, 0, axis_index_groups=groups)


def sigmoid(values):
    return 0.5 * jnp.tanh(0.5 * values) + 0.5


def wide(mask, width):
    return jnp.concatenate([mask] * (width // LANES), axis=1) if width > LANES else mask


def inside(meta, image, start, count):
    pixel = lax.broadcasted_iota(jnp.int32, (count * COLS, LANES), 0)
    row = (pixel >> 4) + (meta[0] + start)
    col = pixel & (COLS - 1)
    side = 12 + 2 * meta[4 + image]
    return jnp.where((row < side) & (row >= 0) & (col < side), 1.0, 0.0).astype(F32)


def area_of(meta, image):
    side = (12 + 2 * meta[4 + image]).astype(F32)
    return side * side


def row_of(block, first, count):
    return jnp.concatenate([block[first + k : first + k + 1] for k in range(count)], axis=1)


def put_row(ref, first, vector):
    for k in range(vector.shape[1] // LANES):
        ref[0, first + k : first + k + 1, :] = vector[:, k * LANES : (k + 1) * LANES]


def spread(ref):
    block = ref[0]

    def step(k, carry):
        ref[k] = block
        return carry

    lax.fori_loop(1, ref.shape[0], step, 0)


def fold(values):
    return jnp.sum(values.reshape(-1, 8, values.shape[-1]), 0)


def total(block):
    return jnp.sum(block, 0, keepdims=True)


def stats(totals, squares, counted):
    center = totals / counted
    return center, lax.rsqrt(squares / counted - center * center + EPSILON)


def shifted(values):
    count, width = values.shape
    col = lax.broadcasted_iota(jnp.int32, (count, LANES), 0) & (COLS - 1)
    has_left = wide(jnp.where(col > 0, 1.0, 0.0).astype(F32), width)
    has_right = wide(jnp.where(col < COLS - 1, 1.0, 0.0).astype(F32), width)
    left = pltpu.roll(values, 1, 0) * has_left
    right = pltpu.roll(values, count - 1, 0) * has_right
    return left.astype(BF16), values.astype(BF16), right.astype(BF16)


def dot(a, b, dims=((1,), (0,)), precision=None):
    return lax.dot_general(a, b, (dims, ((), ())), precision=precision, preferred_element_type=F32)


def whole(shape):
    return pl.BlockSpec(shape, lambda step: (0,) * len(shape))


def call(
    kernel, outs, args, scratch=(), megabytes=24, flops=0, after=(), local="", raw_in=(), raw_out=(), **sizes
):
    moved = sum(a.size * a.dtype.itemsize for a in args) + sum(
        functools.reduce(lambda x, y: x * y, o[0]) * jnp.dtype(o[1]).itemsize for o in outs
    )
    count = len(args)
    vmem = pl.BlockSpec(memory_space=pltpu.VMEM)
    anywhere = pl.BlockSpec(memory_space=pl.ANY)
    in_hbm = lambda a: pltpu.with_memory_space_constraint(a, pltpu.HBM)
    args = [in_hbm(a) if k in raw_in else a for k, a in enumerate(args)]
    after = [in_hbm(a) if a.shape == TOKEN[0] else a for a in after]

    def run(*refs):
        kernel(*refs[:count], *refs[count + len(after) :], **sizes)

    def spec(place, shape, kept, raws):
        return anywhere if place in raws else vmem if kept else whole(shape)

    return pl.pallas_call(
        run,
        grid=() if local == "in out" else (1,),
        out_shape=[
            pltpu.HBM(o[0], o[1]) if len(o) > 2 else jax.ShapeDtypeStruct(o[0], o[1]) for o in outs
        ],
        in_specs=[pl.BlockSpec(memory_space=pltpu.SMEM)]
        + [spec(k, a.shape, "in" in local, raw_in) for k, a in enumerate(args) if k]
        + [anywhere] * len(after),
        out_specs=[spec(k, o[0], "out" in local, raw_out) for k, o in enumerate(outs)],
        scratch_shapes=[pltpu.VMEM(*entry) if isinstance(entry, tuple) else entry for entry in scratch],
        compiler_params=pltpu.CompilerParams(vmem_limit_bytes=megabytes << 20),
        cost_estimate=pl.CostEstimate(flops=flops, bytes_accessed=moved, transcendentals=0),
    )(*args, *after)


def reduce_kernel(meta, x, w, pre, top, bottom, pay, acc, *, blocks, rows):
    slab = rows * COLS
    acc[...] = jnp.zeros_like(acc)
    group = 4

    def step(g, carry):
        base = pl.multiple_of(g * group * slab, group * slab)
        out = dot(x[pl.ds(base, group * slab), :], w[...])
        for j in range(group):
            image = g * group + j
            mask = inside(meta, image, 0, rows)
            part = out[j * slab : (j + 1) * slab] * wide(mask, out.shape[1])
            pre[pl.ds(pl.multiple_of(image * slab, slab), slab), :] = part
            edge = pl.ds(pl.multiple_of(image * COLS, COLS), COLS)
            top[edge, :] = part[:COLS]
            bottom[edge, :] = part[slab - COLS :]
            acc[0] += fold(part)
            acc[1] += fold(part * part)
            acc[2, :, :LANES] += fold(mask)
        return carry

    lax.fori_loop(0, blocks // group, step, 0)
    put_row(pay, 0, total(acc[0]))
    put_row(pay, 2, total(acc[1]))
    put_row(pay, 4, total(acc[2, :, :LANES]))
    pay[0, 5:8, :] = jnp.zeros((3, LANES), F32)
    spread(pay)


def split_kernel(
    meta, got, pre, low, high, gain, shift, w, hid_out, out, top, bottom, pay, stat, acc, hid, sem, *, blocks, rows
):
    slab = rows * COLS
    sums = jnp.sum(got[...], 0)
    counted = row_of(jnp.concatenate([sums[4:5]] * 2, 0), 0, 2)
    center, inv = stats(row_of(sums, 0, 2), row_of(sums, 2, 2), counted)
    stat[...] = jnp.zeros_like(stat)
    stat[0:1] = center
    stat[1:2] = inv
    stat[2:3] = counted
    scale = inv * gain[...]
    offset = shift[...]

    def prepare(i, carry):
        edge = pl.ds(pl.multiple_of(i * COLS, COLS), COLS)
        own = pl.ds(pl.multiple_of(i * slab, slab), slab)
        tall = jnp.concatenate([low[edge, :], pre[own, :], high[edge, :]], axis=0)
        z = (tall - center) * scale + offset
        mask = wide(inside(meta, i, -1, rows + 2), z.shape[1])
        left, middle, right = shifted(z * sigmoid(z) * mask)
        hid[0, i] = left
        hid[1, i] = middle
        hid[2, i] = right
        return carry

    lax.fori_loop(0, blocks, prepare, 0)
    copy = pltpu.make_async_copy(hid, hid_out, sem)
    copy.start()
    acc[...] = jnp.zeros_like(acc)
    group = 4

    def step(g, carry):
        for half in range(2):
            lanes = slice(half * 128, half * 128 + 128)
            outs = slice(half * 256, half * 256 + 256)
            lhs = jnp.concatenate(
                [
                    hid[dx, pl.ds(g * group, group), dy * COLS : dy * COLS + slab, lanes].reshape(
                        group * slab, 128
                    )
                    for dy in range(3)
                    for dx in range(3)
                ],
                axis=1,
            )
            value = dot(lhs, w[:, :, half].reshape(9 * 128, 256))
            for j in range(group):
                image = g * group + j
                mask = inside(meta, image, 0, rows)
                part = value[j * slab : (j + 1) * slab] * wide(mask, 256)
                out[pl.ds(pl.multiple_of(image * slab, slab), slab), outs] = part
                edge = pl.ds(pl.multiple_of(image * COLS, COLS), COLS)
                top[edge, outs] = part[:COLS]
                bottom[edge, outs] = part[slab - COLS :]
                acc[0, :, outs] += fold(part)
                acc[1, :, outs] += fold(part * part)
        return carry

    lax.fori_loop(0, blocks // group, step, 0)
    put_row(pay, 0, total(acc[0]))
    put_row(pay, 4, total(acc[1]))
    spread(pay)
    copy.wait()


def pool_kernel(
    meta, got, stat, pre, gain, shift, w, hid, pooled, pay, stat2, *, blocks, rows
):
    slab = rows * COLS
    sums = jnp.sum(got[...], 0)
    counted = jnp.concatenate([stat[2:3]] * 2, axis=1)
    center, inv = stats(row_of(sums, 0, 4), row_of(sums, 4, 4), counted)
    stat2[...] = jnp.zeros_like(stat2)
    stat2[0:1] = center
    stat2[1:2] = inv
    stat2[2:3] = counted
    scale = inv * gain[...]
    offset = shift[...]

    def step(i, carry):
        own = pl.ds(pl.multiple_of(i * slab, slab), slab)
        mask = wide(inside(meta, i, 0, rows), 256)
        summed = None
        for half in range(2):
            lanes = slice(half * 256, half * 256 + 256)
            z = (pre[own, lanes] - center[:, lanes]) * scale[:, lanes] + offset[:, lanes]
            value = (z * sigmoid(z) * mask).astype(BF16)
            hid[own, lanes] = value
            part = fold(value.astype(F32))
            summed = part if summed is None else summed + part
        pooled[pl.ds(i, 1), :] = total(summed) / area_of(meta, i)
        return carry

    lax.fori_loop(0, blocks, step, 0)
    pay[0] = dot(pooled[...], w[...], precision=HIGHEST)
    spread(pay)


def squeeze_stats(block):
    return stats(total(block), total(block * block), float(block.shape[0]))


def expand_kernel(
    meta, got, hid, gain, shift, we, bias, w, mix, pre, att, hsq, znorm, zall, pay, stat_sq, acc, *, blocks, rows, parts
):
    slab = rows * COLS
    bands = got.shape[0] // parts
    for b in range(bands):
        block = got[b * parts]
        for k in range(1, parts):
            block = block + got[b * parts + k]
        znorm[b * blocks : (b + 1) * blocks, :] = block
    center, inv = squeeze_stats(znorm[...])
    stat_sq[...] = jnp.zeros_like(stat_sq)
    stat_sq[0:1] = center
    stat_sq[1:2] = inv
    normed = (znorm[...] - center) * inv
    znorm[...] = normed
    zall[...] = normed * gain[...] + shift[...]
    own_z = zall[pl.ds(pl.multiple_of(meta[1] * blocks, blocks), blocks), :]
    hidden = own_z * jax.nn.sigmoid(own_z)
    hsq[...] = hidden
    logits = dot(hidden, we[...], precision=HIGHEST) + bias[...]
    first = logits[:, :256]
    second = logits[:, 256:]
    ceiling = jnp.maximum(first, second)
    exp_first = jnp.exp(first - ceiling)
    exp_second = jnp.exp(second - ceiling)
    att[:, :256] = exp_first / (exp_first + exp_second)
    att[:, 256:] = exp_second / (exp_first + exp_second)
    acc[...] = jnp.zeros_like(acc)
    group = 4

    def step(g, carry):
        for j in range(group):
            image = g * group + j
            own = pl.ds(pl.multiple_of(image * slab, slab), slab)
            weights = att[pl.ds(image, 1), :]
            mix[own, :] = (
                weights[:, :256] * hid[own, :256].astype(F32)
                + weights[:, 256:] * hid[own, 256:].astype(F32)
            ).astype(BF16)
        many = pl.ds(pl.multiple_of(g * group * slab, group * slab), group * slab)
        for k in range(4):
            lanes = slice(k * 256, k * 256 + 256)
            value = dot(mix[many, :], w[:, lanes]).astype(BF16)
            pre[many, lanes] = value
            value = value.astype(F32)
            acc[0, :, lanes] += fold(value)
            acc[1, :, lanes] += fold(value * value)
        return carry

    lax.fori_loop(0, blocks // group, step, 0)
    put_row(pay, 0, total(acc[0]))
    put_row(pay, 8, total(acc[1]))
    spread(pay)


def residual_kernel(
    meta, got, stat, x, pre, cot, gain, shift, out, grad, pay, stat3, acc, *, blocks, rows
):
    slab = rows * COLS
    sums = jnp.sum(got[...], 0)
    counted = jnp.concatenate([stat[2:3]] * 4, axis=1)
    center, inv = stats(row_of(sums, 0, 8), row_of(sums, 8, 8), counted)
    stat3[...] = jnp.zeros_like(stat3)
    stat3[0:1] = center
    stat3[1:2] = inv
    stat3[2:3] = counted
    acc[...] = jnp.zeros_like(acc)

    def step(i, carry):
        own = pl.ds(pl.multiple_of(i * slab, slab), slab)
        mask = wide(inside(meta, i, 0, rows), 256)
        for k in range(4):
            lanes = slice(k * 256, k * 256 + 256)
            normed = (pre[own, lanes].astype(F32) - center[:, lanes]) * inv[:, lanes]
            value = normed * gain[:, lanes] + shift[:, lanes] + x[own, lanes].astype(F32)
            part = sigmoid(value)
            silu = value * part
            out[own, lanes] = (silu * mask).astype(BF16)
            slope = part + silu * (1.0 - part)
            back = cot[own, lanes].astype(F32) * mask * slope
            grad[own, lanes] = back
            acc[0, :, lanes] += fold(back)
            acc[1, :, lanes] += fold(back * normed)
        return carry

    lax.fori_loop(0, blocks, step, 0)
    put_row(pay, 0, total(acc[0]))
    put_row(pay, 8, total(acc[1]))
    spread(pay)


def back_terms(stat, gain, shift_sum, gain_sum):
    center, inv, counted = stat[0:1], stat[1:2], stat[2:3]
    a = gain * inv
    d = -a * inv * (gain_sum / counted)
    b = -a * (shift_sum / counted) - d * center
    return a, b, d


def mixture_kernel(
    meta, got, stat3, pre, grad, gain, w, hid, att, gexp, gmix, top, bottom, glog, gain_out, shift_out, *, blocks, rows
):
    slab = rows * COLS
    sums = jnp.sum(got[...], 0)
    shift_sum, gain_sum = row_of(sums, 0, 8), row_of(sums, 8, 8)
    shift_out[...] = shift_sum
    gain_out[...] = gain_sum
    a, b, d = back_terms(stat3, gain[...], shift_sum, gain_sum)
    group = 4

    def step(g, carry):
        many = pl.ds(pl.multiple_of(g * group * slab, group * slab), group * slab)
        for j in range(group):
            image = g * group + j
            own = pl.ds(pl.multiple_of(image * slab, slab), slab)
            mask = wide(inside(meta, image, 0, rows), 256)
            for k in range(4):
                lanes = slice(k * 256, k * 256 + 256)
                gexp[own, lanes] = (
                    mask
                    * (
                        a[:, lanes] * grad[own, lanes]
                        + b[:, lanes]
                        + d[:, lanes] * pre[own, lanes].astype(F32)
                    )
                ).astype(BF16)
        value = dot(gexp[many, :], w[...], ((1,), (1,))).astype(BF16)
        gmix[many, :] = value
        value = value.astype(F32)
        for j in range(group):
            image = g * group + j
            own = pl.ds(pl.multiple_of(image * slab, slab), slab)
            edge = pl.ds(pl.multiple_of(image * COLS, COLS), COLS)
            part = value[j * slab : (j + 1) * slab]
            top[edge, :] = part[:COLS]
            bottom[edge, :] = part[slab - COLS :]
            for half in range(2):
                lanes = slice(half * 256, half * 256 + 256)
                glog[pl.ds(image, 1), lanes] = total(fold(part * hid[own, lanes].astype(F32)))
        return carry

    lax.fori_loop(0, blocks // group, step, 0)
    first, second = att[:, :256], att[:, 256:]
    inner = first * glog[:, :256] + second * glog[:, 256:]
    glog[...] = jnp.concatenate(
        [first * (glog[:, :256] - inner), second * (glog[:, 256:] - inner)], axis=1
    )


def logits_kernel(meta, glog, we, pay):
    pay[0] = dot(glog[...], we[...], ((1,), (1,)), HIGHEST)
    spread(pay)


def expand_grad_kernel(meta, mix, gexp, hsq, glog, keep, send):
    for ref, core in ((send, 1 - meta[2]), (keep, meta[2])):
        lanes = pl.ds(pl.multiple_of(core * 512, 512), 512)
        value = dot(mix[...], gexp[:, lanes], ((0,), (0,))).astype(ref.dtype)
        lanes = pl.ds(pl.multiple_of(core * 256, 256), 256)
        excite = dot(hsq[...], glog[:, lanes], ((0,), (0,)), HIGHEST).astype(ref.dtype)
        for q in range(2):
            for k in range(2):
                first = k * 256 + q * 128
                ref[q, k * 256 : k * 256 + 256, :] = value[:, first : first + 128]
            ref[q, 512:, :] = excite[:, q * 128 : q * 128 + 128]


def add_kernel(meta, keep2, got2, keep3, got3, keep, send, token):
    first = keep2.shape[1]
    for ref, half in ((send, 1 - meta[3]), (keep, meta[3])):
        ref[:first, :] = (keep2[half] + got2[half].astype(F32)).astype(ref.dtype)
        ref[first:, :] = (keep3[half] + got3[half].astype(F32)).astype(ref.dtype)
    token[...] = jnp.zeros_like(token)


def pack_kernel(meta, keep, got, keep1, got1, out):
    chips = out.shape[0]
    large, small = keep.shape[0] // chips, keep1.shape[0] // chips
    out[:, :large, :] = (keep[...] + got[...].astype(F32)).astype(BF16).reshape(chips, large, LANES)
    out[:, large:, :] = (keep1[...] + got1[...].astype(F32)).astype(BF16).reshape(chips, small, LANES)


def share_kernel(meta, shares, out, *, large):
    chips, rows, _ = shares.shape

    def add(first, last, start, step):
        value = shares[start, first:last, :].astype(F32)
        for k in range(start + step, chips, step):
            value = value + shares[k, first:last, :].astype(F32)
        return value.astype(BF16)

    out[0, :large, :] = add(0, large, 0, 2)
    out[0, large : 2 * large, :] = add(0, large, 1, 2)
    out[0, 2 * large :, :] = add(large, rows, 0, 1)
    block = out[0]

    def step(k, carry):
        out[k] = block
        return carry

    lax.fori_loop(1, out.shape[0], step, 0)


def hidden_kernel(
    meta, got, znorm, zall, hsq_gain, stat_sq, pooled, wsq, att, gmix, pre, stat2, gain, shift,
    dz, gpool, pay, gain_out, shift_out, acc, full, squeeze, *, blocks, rows, parts
):
    slab = rows * COLS
    bands = got.shape[0] // parts
    for b in range(bands):
        block = got[b * parts]
        for k in range(1, parts):
            block = block + got[b * parts + k]
        full[b * blocks : (b + 1) * blocks, :] = block
    z = zall[...]
    part = jax.nn.sigmoid(z)
    grad_z = full[...] * (part * (1.0 + z * (1.0 - part)))
    full[...] = grad_z
    images = float(bands * blocks)
    shift_sum = total(grad_z)
    gain_sum = total(grad_z * znorm[...])
    shift_out[...] = shift_sum
    gain_out[...] = gain_sum
    mine = pl.ds(pl.multiple_of(meta[1] * blocks, blocks), blocks)
    grad_pre = (
        hsq_gain[...]
        * stat_sq[1:2]
        * (full[mine, :] - shift_sum / images - znorm[mine, :] * (gain_sum / images))
    )
    squeeze[...] = dot(pooled[...], grad_pre, ((0,), (0,)), HIGHEST)
    gpool[...] = dot(grad_pre, wsq[...], ((1,), (1,)), HIGHEST)
    for i in range(blocks):
        gpool[i : i + 1, :] = gpool[i : i + 1, :] / area_of(meta, i)
    center, inv = stat2[0:1], stat2[1:2]
    acc[...] = jnp.zeros_like(acc)

    def step(i, carry):
        own = pl.ds(pl.multiple_of(i * slab, slab), slab)
        mask = wide(inside(meta, i, 0, rows), 256)
        mixed = gmix[own, :].astype(F32)
        pool = gpool[pl.ds(i, 1), :]
        for half in range(2):
            lanes = slice(half * 256, half * 256 + 256)
            normed = (pre[own, lanes] - center[:, lanes]) * inv[:, lanes]
            value = normed * gain[:, lanes] + shift[:, lanes]
            sig = sigmoid(value)
            slope = sig * (1.0 + value * (1.0 - sig))
            hidden = (mixed * att[pl.ds(i, 1), lanes] + pool).astype(BF16).astype(F32)
            back = hidden * mask * slope
            dz[own, lanes] = back
            acc[0, :, lanes] += fold(back)
            acc[1, :, lanes] += fold(back * normed)
        return carry

    lax.fori_loop(0, blocks, step, 0)
    put_row(pay, 0, total(acc[0]))
    put_row(pay, 4, total(acc[1]))
    pay[0, 8:, :] = jnp.zeros((pay.shape[1] - 8, LANES), F32)
    spread(pay)
    share = pay.shape[1] - 8
    for n in range(pay.shape[0]):
        pay[n, 8:, :] = squeeze[n * share : (n + 1) * share, :]


def conv_kernel(
    meta, got, stat2, gain2, shift2, dz, pre2, low2, high2, lowm, highm, att, gpool, w, pre, stat,
    gain, shift, glog, hid_in, out_hbm, keep_hbm, send_hbm, pay, gain_out, shift_out, tall, acc,
    hid, out, keep, send, sems, *, blocks, rows
):
    slab = rows * COLS
    fetch = pltpu.make_async_copy(hid_in, hid, sems.at[0])
    fetch.start()
    sums = jnp.sum(got[...], 0)
    shift_sum, gain_sum = row_of(sums, 0, 4), row_of(sums, 4, 4)
    shift_out[...] = shift_sum
    gain_out[...] = gain_sum
    a, b, d = back_terms(stat2, gain2[...], shift_sum, gain_sum)
    center2, inv2 = stat2[0:1], stat2[1:2]

    def prepare(i, carry):
        own = pl.ds(pl.multiple_of(i * slab, slab), slab)
        edge = pl.ds(pl.multiple_of(i * COLS, COLS), COLS)
        mask = inside(meta, i, -1, rows + 2)
        for half in range(2):
            lanes = slice(half * 256, half * 256 + 256)

            def edge_grad(values, mixed, keep):
                z = (values[edge, lanes] - center2[:, lanes]) * inv2[:, lanes]
                z = z * gain2[:, lanes] + shift2[:, lanes]
                sig = sigmoid(z)
                slope = sig * (1.0 + z * (1.0 - sig))
                hidden = (
                    mixed[edge, :] * att[pl.ds(i, 1), lanes] + gpool[pl.ds(i, 1), :]
                ).astype(BF16)
                return hidden.astype(F32) * keep * slope

            keep_low = wide(mask[:COLS], 256)
            keep_high = wide(mask[slab + COLS :], 256)
            grads = jnp.concatenate(
                [edge_grad(low2, lowm, keep_low), dz[own, lanes], edge_grad(high2, highm, keep_high)],
                axis=0,
            )
            values = jnp.concatenate([low2[edge, lanes], pre2[own, lanes], high2[edge, lanes]], axis=0)
            back = wide(mask, 256) * (a[:, lanes] * grads + b[:, lanes] + d[:, lanes] * values)
            left, middle, right = shifted(back)
            tall[0, i, :, lanes] = left
            tall[1, i, :, lanes] = middle
            tall[2, i, :, lanes] = right
        return carry

    lax.fori_loop(0, blocks, prepare, 0)
    fetch.wait()

    def weights(dy, carry):
        rows_at = pl.ds(pl.multiple_of(dy * COLS, COLS), slab)
        for ref, core in ((send, 1 - meta[2]), (keep, meta[2])):
            lanes = pl.ds(pl.multiple_of(core * 128, 128), 128)
            wide_lanes = pl.ds(pl.multiple_of(core * 256, 256), 256)
            grads = tall[1, :, COLS : COLS + slab, wide_lanes].reshape(blocks * slab, 256)
            lhs = jnp.concatenate(
                [hid[dx, :, rows_at, lanes].reshape(blocks * slab, 128) for dx in range(3)], axis=1
            )
            value = dot(lhs, grads, ((0,), (0,))).astype(ref.dtype)
            at = pl.ds(pl.multiple_of(dy * 384, 384), 384)
            for q in range(2):
                ref[q, at, :] = value[:, q * 128 : q * 128 + 128]
        return carry

    lax.fori_loop(0, 3, weights, 0)
    stores = [
        pltpu.make_async_copy(send, send_hbm, sems.at[1]),
        pltpu.make_async_copy(keep, keep_hbm, sems.at[2]),
    ]
    for store in stores:
        store.start()
    acc[...] = jnp.zeros_like(acc)
    center, inv = stat[0:1], stat[1:2]
    group = 4

    def step(g, carry):
        for half in range(2):
            lanes = slice(half * 256, half * 256 + 256)
            outs = slice(half * 128, half * 128 + 128)
            value = None
            for dy in range(3):
                for dx in range(3):
                    lhs = tall[
                        2 - dx, pl.ds(g * group, group), (2 - dy) * COLS : (2 - dy) * COLS + slab, lanes
                    ].reshape(group * slab, 256)
                    part = dot(lhs, w[dy, dx, half], ((1,), (1,)))
                    value = part if value is None else value + part
            for j in range(group):
                image = g * group + j
                own = pl.ds(pl.multiple_of(image * slab, slab), slab)
                mask = inside(meta, image, 0, rows)
                normed = (pre[own, outs] - center[:, outs]) * inv[:, outs]
                z = normed * gain[:, outs] + shift[:, outs]
                sig = sigmoid(z)
                slope = sig * (1.0 + z * (1.0 - sig))
                back = value[j * slab : (j + 1) * slab] * mask * slope
                out[own, outs] = back
                acc[0, :, outs] += fold(back)
                acc[1, :, outs] += fold(back * normed)
        return carry

    lax.fori_loop(0, blocks // group, step, 0)
    stores.append(pltpu.make_async_copy(out, out_hbm, sems.at[3]))
    stores[-1].start()
    put_row(pay, 0, total(acc[0]))
    put_row(pay, 2, total(acc[1]))
    put_row(pay, 4, total(glog[...]))
    pay[0, 8:, :] = sums[8:]
    spread(pay)
    for store in stores:
        store.wait()


def reduce_back_kernel(
    meta, got, stat, gain, dz_in, pre_in, x_in, small_out, keep, send, gain_out, shift_out, bias_out, squeeze,
    dz, pre, x, small, sems, *, blocks, rows
):
    slab = rows * COLS
    fetches = [
        pltpu.make_async_copy(source, target, sems.at[k])
        for k, (source, target) in enumerate(((dz_in, dz), (pre_in, pre), (x_in, x)))
    ]
    for fetch in fetches:
        fetch.start()
    sums = jnp.sum(got[:, :8, :], 0)
    share = got.shape[1] - 8
    for n in range(got.shape[0]):
        squeeze[n * share : (n + 1) * share, :] = got[n, 8:, :]
    shift_sum, gain_sum = row_of(sums, 0, 2), row_of(sums, 2, 2)
    shift_out[...] = shift_sum
    gain_out[...] = gain_sum
    bias_out[...] = row_of(sums, 4, 4)
    a, b, d = back_terms(stat, gain[...], shift_sum, gain_sum)
    fetches[0].wait()
    fetches[1].wait()

    def step(image, carry):
        own = pl.ds(pl.multiple_of(image * slab, slab), slab)
        mask = wide(inside(meta, image, 0, rows), 256)
        small[own, :] = (mask * (a * dz[own, :] + b + d * pre[own, :])).astype(BF16)
        return carry

    lax.fori_loop(0, blocks, step, 0)
    store = pltpu.make_async_copy(small, small_out, sems.at[3])
    store.start()
    fetches[2].wait()
    for ref, core in ((send, 1 - meta[2]), (keep, meta[2])):
        lanes = pl.ds(pl.multiple_of(core * 512, 512), 512)
        value = dot(x[:, lanes], small[...], ((0,), (0,))).astype(ref.dtype)
        for q in range(2):
            ref[q * 512 : q * 512 + 512, :] = value[:, q * 128 : q * 128 + 128]
    store.wait()


def input_kernel(meta, small, w, grad, out, token, *, blocks, rows):
    slab = rows * COLS
    token[...] = jnp.zeros_like(token)
    group = 4

    def step(g, carry):
        many = pl.ds(pl.multiple_of(g * group * slab, group * slab), group * slab)
        for k in range(4):
            lanes = slice(k * 256, k * 256 + 256)
            value = dot(small[many, :], w[lanes, :], ((1,), (1,)))
            for j in range(group):
                image = g * group + j
                own = pl.ds(pl.multiple_of(image * slab, slab), slab)
                mask = wide(inside(meta, image, 0, rows), 256)
                out[own, lanes] = (
                    (value[j * slab : (j + 1) * slab] + grad[own, lanes]) * mask
                ).astype(BF16)
        return carry

    lax.fori_loop(0, blocks // group, step, 0)


def total_kernel(meta, own, other, expand, excite, split, reduce, *, large):
    chips, rows, _ = own.shape
    for ref, core in ((own, meta[2]), (other, 1 - meta[2])):
        for q in range(2):
            lanes = slice(q * 128, q * 128 + 128)
            block = ref[:, q * large : q * large + large, :].reshape(chips * large, LANES)
            for tap in range(9):
                split[tap // 3, tap % 3, core, :, lanes] = block[tap * 128 : tap * 128 + 128].astype(F32)
            for k in range(2):
                first = 1152 + k * 256
                out = pl.ds(pl.multiple_of(core * 512 + (k * 256 + q * 128), 128), 128)
                expand[:, out] = block[first : first + 256].astype(F32)
            out = pl.ds(pl.multiple_of(core * 256 + q * 128, 128), 128)
            excite[:, out] = block[1664:].astype(F32)
        block = ref[:, 2 * large :, :].reshape(chips * (rows - 2 * large), LANES)
        own_rows = pl.ds(pl.multiple_of(core * 512, 512), 512)
        for q in range(2):
            reduce[own_rows, q * 128 : q * 128 + 128] = block[q * 512 : q * 512 + 512].astype(F32)


def body(
    inputs,
    image_class,
    weight_reduce,
    gain_reduce,
    shift_reduce,
    weight_split,
    gain_split,
    shift_split,
    weight_squeeze,
    gain_squeeze,
    shift_squeeze,
    weight_excite,
    bias_excite,
    weight_expand,
    gain_expand,
    shift_expand,
    cotangent,
):
    blocks, rows, cols, channels = inputs.shape
    mid = weight_reduce.shape[1]
    inter = weight_squeeze.shape[1]
    parts = lax.axis_size("narrow")
    count = device_count()
    pixels = blocks * rows * cols
    slab = rows * cols
    edge = blocks * cols
    share = mid // count
    images = blocks * lax.axis_size("batch")
    meta = jnp.concatenate(
        [
            (lax.axis_index("narrow") * rows).astype(jnp.int32)[None],
            lax.axis_index("batch").astype(jnp.int32)[None],
            (lax.axis_index("narrow") % 2).astype(jnp.int32)[None],
            (lax.axis_index("narrow") // 2 % 2).astype(jnp.int32)[None],
            image_class,
        ]
    )
    x = inputs.reshape(pixels, channels)
    cot = cotangent.reshape(pixels, channels)
    row = lambda v: v.reshape(1, -1)
    gain1, shift1 = row(gain_reduce), row(shift_reduce)
    gain2, shift2 = row(gain_split), row(shift_split)
    gain3, shift3 = row(gain_expand), row(shift_expand)
    gain_sq, shift_sq = row(gain_squeeze), row(shift_squeeze)
    sizes = dict(blocks=blocks, rows=rows)
    small = 2 * pixels * channels * mid
    large = 2 * pixels * 9 * 128 * 512

    pre1, top, bottom, pay = call(
        reduce_kernel,
        [((pixels, mid), F32), ((edge, mid), F32), ((edge, mid), F32), ((count, 8, LANES), F32)],
        [meta, x, weight_reduce],
        [((3, 8, mid), F32)],
        flops=small,
        local="in out",
        **sizes,
    )
    low, high = halo(top, bottom)
    hid1, pre2, top, bottom, pay, stat1 = call(
        split_kernel,
        [
            ((3, blocks, slab + 2 * cols, mid), BF16, "hbm"),
            ((pixels, 2 * mid), F32),
            ((edge, 2 * mid), F32),
            ((edge, 2 * mid), F32),
            ((count, 8, LANES), F32),
            ((8, mid), F32),
        ],
        [meta, exchange(pay), pre1, low, high, gain1, shift1, weight_split],
        [((2, 8, 2 * mid), F32), ((3, blocks, slab + 2 * cols, mid), BF16), pltpu.SemaphoreType.DMA],
        raw_out=(0,),
        flops=large,
        local="in out",
        **sizes,
    )
    low2, high2 = halo(top, bottom)
    hid2, pooled, pay, stat2 = call(
        pool_kernel,
        [
            ((pixels, 2 * mid), BF16),
            ((blocks, mid), F32),
            ((count, blocks, inter), F32),
            ((8, 2 * mid), F32),
        ],
        [meta, exchange(pay), stat1, pre2, gain2, shift2, weight_squeeze],
        local="in out",
        after=(low2, high2),
        **sizes,
    )
    mix, pre3, att, hsq, znorm, zall, pay, stat_sq = call(
        expand_kernel,
        [
            ((pixels, mid), BF16),
            ((pixels, channels), BF16),
            ((blocks, 2 * mid), F32),
            ((blocks, inter), F32),
            ((images, inter), F32),
            ((images, inter), F32),
            ((count, 16, LANES), F32),
            ((8, inter), F32),
        ],
        [
            meta,
            exchange(pay),
            hid2,
            gain_sq,
            shift_sq,
            weight_excite,
            row(bias_excite),
            weight_expand,
        ],
        [((2, 8, channels), F32)],
        flops=small,
        parts=parts,
        local="in out",
        **sizes,
    )
    out, grad_res, pay, stat3 = call(
        residual_kernel,
        [
            ((pixels, channels), BF16),
            ((pixels, channels), F32),
            ((count, 16, LANES), F32),
            ((8, channels), F32),
        ],
        [meta, exchange(pay), stat1, x, pre3, cot, gain3, shift3],
        [((2, 8, channels), F32)],
        local="in out",
        **sizes,
    )
    gexp, gmix, top, bottom, glog, gain3_grad, shift3_grad = call(
        mixture_kernel,
        [
            ((pixels, channels), BF16),
            ((pixels, mid), BF16),
            ((edge, mid), F32),
            ((edge, mid), F32),
            ((blocks, 2 * mid), F32),
            ((1, channels), F32),
            ((1, channels), F32),
        ],
        [meta, exchange(pay), stat3, pre3, grad_res, gain3, weight_expand, hid2, att],
        flops=small,
        local="in out",
        **sizes,
    )
    lowm, highm = halo(top, bottom)
    keep3, send3 = call(
        expand_grad_kernel,
        [((2, 2 * mid + inter, LANES), F32), ((2, 2 * mid + inter, LANES), BF16)],
        [meta, mix, gexp, hsq, glog],
        flops=small,
        local="in out",
    )
    (pay,) = call(
        logits_kernel,
        [((count, blocks, inter), F32)],
        [meta, glog, weight_excite],
        after=(lowm, highm, send3),
        local="in out",
    )
    dz2, gpool, pay, gain_sq_grad, shift_sq_grad = call(
        hidden_kernel,
        [
            ((pixels, 2 * mid), F32),
            ((blocks, mid), F32),
            ((count, 8 + share, LANES), F32),
            ((1, inter), F32),
            ((1, inter), F32),
        ],
        [
            meta,
            exchange(pay),
            znorm,
            zall,
            gain_sq,
            stat_sq,
            pooled,
            weight_squeeze,
            att,
            gmix,
            pre2,
            stat2,
            gain2,
            shift2,
        ],
        [((2, 8, 2 * mid), F32), ((images, inter), F32), ((mid, inter), F32)],
        parts=parts,
        local="in out",
        **sizes,
    )
    dz1, keep2, send2, pay, gain2_grad, shift2_grad = call(
        conv_kernel,
        [
            ((pixels, mid), F32, "hbm"),
            ((2, 9 * 128, LANES), F32, "hbm"),
            ((2, 9 * 128, LANES), BF16, "hbm"),
            ((count, 8 + share, LANES), F32, "hbm"),
            ((1, 2 * mid), F32),
            ((1, 2 * mid), F32),
        ],
        [
            meta,
            exchange(pay),
            stat2,
            gain2,
            shift2,
            dz2,
            pre2,
            low2,
            high2,
            lowm,
            highm,
            att,
            gpool,
            weight_split,
            pre1,
            stat1,
            gain1,
            shift1,
            glog,
            hid1,
        ],
        [
            ((3, blocks, slab + 2 * cols, 2 * mid), BF16),
            ((2, 8, mid), F32),
            (hid1.shape, BF16),
            ((pixels, mid), F32),
            ((2, 9 * 128, LANES), F32),
            ((2, 9 * 128, LANES), BF16),
            pltpu.SemaphoreType.DMA((4,)),
        ],
        raw_in=(19,),
        raw_out=(0, 1, 2),
        flops=2 * large,
        local="in",
        **sizes,
    )
    quarter = 9 * 128 + 2 * mid + inter
    keep, send, token = call(
        add_kernel,
        [((quarter, LANES), F32, "hbm"), ((quarter, LANES), BF16, "hbm"), TOKEN],
        [meta, keep2, swap(send2, 1), keep3, swap(send3, 1)],
    )
    small1, keep1, send1, gain1_grad, shift1_grad, bias_grad, squeeze_total = call(
        reduce_back_kernel,
        [
            ((pixels, mid), BF16, "hbm"),
            ((channels, mid // 2), F32),
            ((channels, mid // 2), BF16),
            ((1, mid), F32),
            ((1, mid), F32),
            ((1, 2 * mid), F32),
            ((mid, inter), F32),
        ],
        [meta, exchange(pay), stat1, gain1, dz1, pre1, x],
        [
            ((pixels, mid), F32),
            ((pixels, mid), F32),
            ((pixels, channels), BF16),
            ((pixels, mid), BF16),
            pltpu.SemaphoreType.DMA((4,)),
        ],
        raw_in=(4, 5, 6),
        raw_out=(0,),
        flops=small,
        after=(token,),
        local="in",
        **sizes,
    )
    chips = count // 2
    large = quarter // chips
    (packed,) = call(
        pack_kernel,
        [((chips, large + channels // chips, LANES), BF16, "hbm")],
        [meta, keep, swap(send, 2), keep1, swap(send1, 1)],
    )
    input_grad, token = call(
        input_kernel,
        [((pixels, channels), BF16, "hbm"), TOKEN],
        [meta, small1, weight_reduce, grad_res],
        flops=small,
        after=(packed,),
        **sizes,
    )
    (shared,) = call(
        share_kernel,
        [((chips, 2 * large + channels // chips, LANES), BF16)],
        [meta, exchange_chips(packed)],
        after=(token,),
        local="out",
        large=large,
    )
    own = exchange_chips(shared)
    expand_total, excite_total, split_total, reduce_total = call(
        total_kernel,
        [
            ((mid, channels), F32),
            ((inter, 2 * mid), F32),
            (weight_split.shape, F32),
            ((channels, mid), F32),
        ],
        [meta, own, swap(own, 1)],
        local="in",
        large=large,
    )
    flat = lambda v: v.reshape(-1)
    return (
        out.reshape(inputs.shape),
        input_grad.reshape(inputs.shape),
        reduce_total,
        flat(gain1_grad),
        flat(shift1_grad),
        split_total,
        flat(gain2_grad),
        flat(shift2_grad),
        squeeze_total,
        flat(gain_sq_grad),
        flat(shift_sq_grad),
        excite_total,
        flat(bias_grad),
        expand_total,
        flat(gain3_grad),
        flat(shift3_grad),
    )


def solution(mesh):
    rows = P("batch", "narrow", None, None)
    return jax.shard_map(
        body,
        mesh=mesh,
        in_specs=(rows, P("batch")) + (P(),) * 14 + (rows,),
        out_specs=(rows, rows) + (P(),) * 14,
        check_vma=False,
    )
```

```python
import functools
from itertools import product

import jax
import jax.numpy as jnp
from jax import lax
from jax.experimental import pallas as pl
from jax.experimental.pallas import tpu as pltpu
from jax.sharding import PartitionSpec as P

EPSILON = 1e-05
HIGHEST = lax.Precision.HIGHEST
ALL = ("batch", "narrow")
F32 = jnp.float32
BF16 = jnp.bfloat16
COLS = 16
LANES = 128
TOKEN = ((8, LANES), F32, "hbm")


def device_count():
    return lax.axis_size("batch") * lax.axis_size("narrow")


def halo(top, bottom):
    count = lax.axis_size("narrow")
    low = lax.ppermute(bottom, "narrow", [(i, i + 1) for i in range(count - 1)])
    high = lax.ppermute(top, "narrow", [(i + 1, i) for i in range(count - 1)])
    return low, high


def exchange(block):
    return lax.all_to_all(block, ALL, 0, 0)


def swap(block, bit):
    count = lax.axis_size("narrow")
    return lax.ppermute(block, "narrow", [(i, i ^ bit) for i in range(count)])


def exchange_chips(block):
    count = device_count()
    groups = [[i for i in range(count) if i % 2 == core] for core in range(2)]
    return lax.all_to_all(block, ALL, 0, 0, axis_index_groups=groups)


def gather_chips(share):
    count = device_count()
    bits = list(range(count.bit_length() - 2, 0, -1))
    stages = [bits[k : k + 2] for k in range(0, len(bits), 2)]
    block, places = share[None], [0]
    for stage in stages:
        steps = [sum(bit << stage[k] for k, bit in enumerate(pick)) for pick in product((0, 1), repeat=len(stage))]
        blocks = [block] + [
            lax.ppermute(block, ALL, [(i, i ^ step) for i in range(count)]) for step in steps[1:]
        ]
        lists = [[place ^ (step >> 1) for place in places] for step in steps]
        block, places = jnp.concatenate(blocks), sum(lists, [])
    return blocks, lists


def sigmoid(values):
    return 0.5 * jnp.tanh(0.5 * values) + 0.5


def wide(mask, width):
    return jnp.concatenate([mask] * (width // LANES), axis=1) if width > LANES else mask


def inside(meta, image, start, count):
    pixel = lax.broadcasted_iota(jnp.int32, (count * COLS, LANES), 0)
    row = (pixel >> 4) + (meta[0] + start)
    col = pixel & (COLS - 1)
    side = 12 + 2 * meta[5 + image]
    return jnp.where((row < side) & (row >= 0) & (col < side), 1.0, 0.0).astype(F32)


def area_of(meta, image):
    side = (12 + 2 * meta[5 + image]).astype(F32)
    return side * side


def row_of(block, first, count):
    return jnp.concatenate([block[first + k : first + k + 1] for k in range(count)], axis=1)


def put_row(ref, first, vector):
    for k in range(vector.shape[1] // LANES):
        ref[0, first + k : first + k + 1, :] = vector[:, k * LANES : (k + 1) * LANES]


def spread(ref):
    block = ref[0]

    def step(k, carry):
        ref[k] = block
        return carry

    lax.fori_loop(1, ref.shape[0], step, 0)


def fold(values):
    return jnp.sum(values.reshape(-1, 8, values.shape[-1]), 0)


def clear_from(ref, first):
    if ref.shape[0] > first:
        ref[first:, :] = jnp.zeros((ref.shape[0] - first, LANES), ref.dtype)


def total(block):
    return jnp.sum(block, 0, keepdims=True)


def stats(totals, squares, counted):
    center = totals / counted
    return center, lax.rsqrt(squares / counted - center * center + EPSILON)


def shifted(values):
    count, width = values.shape
    col = lax.broadcasted_iota(jnp.int32, (count, LANES), 0) & (COLS - 1)
    has_left = wide(jnp.where(col > 0, 1.0, 0.0).astype(F32), width)
    has_right = wide(jnp.where(col < COLS - 1, 1.0, 0.0).astype(F32), width)
    left = pltpu.roll(values, 1, 0) * has_left
    right = pltpu.roll(values, count - 1, 0) * has_right
    return left.astype(BF16), values.astype(BF16), right.astype(BF16)


def dot(a, b, dims=((1,), (0,)), precision=None):
    return lax.dot_general(a, b, (dims, ((), ())), precision=precision, preferred_element_type=F32)


def whole(shape):
    return pl.BlockSpec(shape, lambda step: (0,) * len(shape))


def call(
    kernel, outs, args, scratch=(), megabytes=24, flops=0, after=(), local="", raw_in=(), raw_out=(), **sizes
):
    moved = sum(a.size * a.dtype.itemsize for a in args) + sum(
        functools.reduce(lambda x, y: x * y, o[0]) * jnp.dtype(o[1]).itemsize for o in outs
    )
    count = len(args)
    vmem = pl.BlockSpec(memory_space=pltpu.VMEM)
    anywhere = pl.BlockSpec(memory_space=pl.ANY)
    in_hbm = lambda a: pltpu.with_memory_space_constraint(a, pltpu.HBM)
    args = [in_hbm(a) if k in raw_in else a for k, a in enumerate(args)]
    after = [in_hbm(a) if a.shape == TOKEN[0] else a for a in after]

    def run(*refs):
        kernel(*refs[:count], *refs[count + len(after) :], **sizes)

    def spec(place, shape, kept, raws):
        return anywhere if place in raws else vmem if kept else whole(shape)

    return pl.pallas_call(
        run,
        grid=() if local == "in out" else (1,),
        out_shape=[
            pltpu.HBM(o[0], o[1]) if len(o) > 2 else jax.ShapeDtypeStruct(o[0], o[1]) for o in outs
        ],
        in_specs=[pl.BlockSpec(memory_space=pltpu.SMEM)]
        + [spec(k, a.shape, "in" in local, raw_in) for k, a in enumerate(args) if k]
        + [anywhere] * len(after),
        out_specs=[spec(k, o[0], "out" in local, raw_out) for k, o in enumerate(outs)],
        scratch_shapes=[pltpu.VMEM(*entry) if isinstance(entry, tuple) else entry for entry in scratch],
        compiler_params=pltpu.CompilerParams(vmem_limit_bytes=megabytes << 20),
        cost_estimate=pl.CostEstimate(flops=flops, bytes_accessed=moved, transcendentals=0),
    )(*args, *after)


def reduce_kernel(meta, x, w, pre, top, bottom, pay, acc, *, blocks, rows):
    slab = rows * COLS
    acc[...] = jnp.zeros_like(acc)
    group = 4

    def step(g, carry):
        base = pl.multiple_of(g * group * slab, group * slab)
        out = dot(x[pl.ds(base, group * slab), :], w[...])
        for j in range(group):
            image = g * group + j
            mask = inside(meta, image, 0, rows)
            part = out[j * slab : (j + 1) * slab] * wide(mask, out.shape[1])
            pre[pl.ds(pl.multiple_of(image * slab, slab), slab), :] = part
            edge = pl.ds(pl.multiple_of(image * COLS, COLS), COLS)
            top[edge, :] = part[:COLS]
            bottom[edge, :] = part[slab - COLS :]
            acc[0] += fold(part)
            acc[1] += fold(part * part)
            acc[2, :, :LANES] += fold(mask)
        return carry

    lax.fori_loop(0, blocks // group, step, 0)
    put_row(pay, 0, total(acc[0]))
    put_row(pay, 2, total(acc[1]))
    put_row(pay, 4, total(acc[2, :, :LANES]))
    pay[0, 5:8, :] = jnp.zeros((3, LANES), F32)
    spread(pay)


def split_kernel(
    meta, got, pre, low, high, gain, shift, w, hid_out, out, top, bottom, pay, stat, acc, hid, sem, *, blocks, rows
):
    slab = rows * COLS
    sums = jnp.sum(got[...], 0)
    counted = row_of(jnp.concatenate([sums[4:5]] * 2, 0), 0, 2)
    center, inv = stats(row_of(sums, 0, 2), row_of(sums, 2, 2), counted)
    stat[...] = jnp.zeros_like(stat)
    stat[0:1] = center
    stat[1:2] = inv
    stat[2:3] = counted
    scale = inv * gain[...]
    offset = shift[...]

    def prepare(i, carry):
        edge = pl.ds(pl.multiple_of(i * COLS, COLS), COLS)
        own = pl.ds(pl.multiple_of(i * slab, slab), slab)
        tall = jnp.concatenate([low[edge, :], pre[own, :], high[edge, :]], axis=0)
        z = (tall - center) * scale + offset
        mask = wide(inside(meta, i, -1, rows + 2), z.shape[1])
        left, middle, right = shifted(z * sigmoid(z) * mask)
        hid[0, i] = left
        hid[1, i] = middle
        hid[2, i] = right
        return carry

    lax.fori_loop(0, blocks, prepare, 0)
    copy = pltpu.make_async_copy(hid, hid_out, sem)
    copy.start()
    acc[...] = jnp.zeros_like(acc)
    group = 4

    def step(g, carry):
        for half in range(2):
            lanes = slice(half * 128, half * 128 + 128)
            outs = slice(half * 256, half * 256 + 256)
            lhs = jnp.concatenate(
                [
                    hid[dx, pl.ds(g * group, group), dy * COLS : dy * COLS + slab, lanes].reshape(
                        group * slab, 128
                    )
                    for dy in range(3)
                    for dx in range(3)
                ],
                axis=1,
            )
            value = dot(lhs, w[:, :, half].reshape(9 * 128, 256))
            for j in range(group):
                image = g * group + j
                mask = inside(meta, image, 0, rows)
                part = value[j * slab : (j + 1) * slab] * wide(mask, 256)
                out[pl.ds(pl.multiple_of(image * slab, slab), slab), outs] = part
                edge = pl.ds(pl.multiple_of(image * COLS, COLS), COLS)
                top[edge, outs] = part[:COLS]
                bottom[edge, outs] = part[slab - COLS :]
                acc[0, :, outs] += fold(part)
                acc[1, :, outs] += fold(part * part)
        return carry

    lax.fori_loop(0, blocks // group, step, 0)
    put_row(pay, 0, total(acc[0]))
    put_row(pay, 4, total(acc[1]))
    spread(pay)
    copy.wait()


def pool_kernel(
    meta, got, stat, pre, gain, shift, w, hid, pooled, pay, stat2, *, blocks, rows
):
    slab = rows * COLS
    sums = jnp.sum(got[...], 0)
    counted = jnp.concatenate([stat[2:3]] * 2, axis=1)
    center, inv = stats(row_of(sums, 0, 4), row_of(sums, 4, 4), counted)
    stat2[...] = jnp.zeros_like(stat2)
    stat2[0:1] = center
    stat2[1:2] = inv
    stat2[2:3] = counted
    scale = inv * gain[...]
    offset = shift[...]

    def step(i, carry):
        own = pl.ds(pl.multiple_of(i * slab, slab), slab)
        mask = wide(inside(meta, i, 0, rows), 256)
        summed = None
        for half in range(2):
            lanes = slice(half * 256, half * 256 + 256)
            z = (pre[own, lanes] - center[:, lanes]) * scale[:, lanes] + offset[:, lanes]
            value = (z * sigmoid(z) * mask).astype(BF16)
            hid[own, lanes] = value
            part = fold(value.astype(F32))
            summed = part if summed is None else summed + part
        pooled[pl.ds(i, 1), :] = total(summed) / area_of(meta, i)
        return carry

    lax.fori_loop(0, blocks, step, 0)
    pay[0] = dot(pooled[...], w[...], precision=HIGHEST)
    spread(pay)


def squeeze_stats(block):
    return stats(total(block), total(block * block), float(block.shape[0]))


def expand_kernel(
    meta, got, hid, gain, shift, we, bias, w, mix, pre, att, hsq, znorm, zall, pay, stat_sq, acc, *, blocks, rows, parts
):
    slab = rows * COLS
    bands = got.shape[0] // parts
    for b in range(bands):
        block = got[b * parts]
        for k in range(1, parts):
            block = block + got[b * parts + k]
        znorm[b * blocks : (b + 1) * blocks, :] = block
    center, inv = squeeze_stats(znorm[...])
    stat_sq[...] = jnp.zeros_like(stat_sq)
    stat_sq[0:1] = center
    stat_sq[1:2] = inv
    normed = (znorm[...] - center) * inv
    znorm[...] = normed
    zall[...] = normed * gain[...] + shift[...]
    own_z = zall[pl.ds(pl.multiple_of(meta[1] * blocks, blocks), blocks), :]
    hidden = own_z * jax.nn.sigmoid(own_z)
    hsq[...] = hidden
    logits = dot(hidden, we[...], precision=HIGHEST) + bias[...]
    first = logits[:, :256]
    second = logits[:, 256:]
    ceiling = jnp.maximum(first, second)
    exp_first = jnp.exp(first - ceiling)
    exp_second = jnp.exp(second - ceiling)
    att[:, :256] = exp_first / (exp_first + exp_second)
    att[:, 256:] = exp_second / (exp_first + exp_second)
    acc[...] = jnp.zeros_like(acc)
    group = 4

    def step(g, carry):
        for j in range(group):
            image = g * group + j
            own = pl.ds(pl.multiple_of(image * slab, slab), slab)
            weights = att[pl.ds(image, 1), :]
            mix[own, :] = (
                weights[:, :256] * hid[own, :256].astype(F32)
                + weights[:, 256:] * hid[own, 256:].astype(F32)
            ).astype(BF16)
        many = pl.ds(pl.multiple_of(g * group * slab, group * slab), group * slab)
        for k in range(4):
            lanes = slice(k * 256, k * 256 + 256)
            value = dot(mix[many, :], w[:, lanes]).astype(BF16)
            pre[many, lanes] = value
            value = value.astype(F32)
            acc[0, :, lanes] += fold(value)
            acc[1, :, lanes] += fold(value * value)
        return carry

    lax.fori_loop(0, blocks // group, step, 0)
    put_row(pay, 0, total(acc[0]))
    put_row(pay, 8, total(acc[1]))
    spread(pay)


def residual_kernel(
    meta, got, stat, x, pre, cot, gain, shift, out, grad, pay, stat3, acc, *, blocks, rows
):
    slab = rows * COLS
    sums = jnp.sum(got[...], 0)
    counted = jnp.concatenate([stat[2:3]] * 4, axis=1)
    center, inv = stats(row_of(sums, 0, 8), row_of(sums, 8, 8), counted)
    stat3[...] = jnp.zeros_like(stat3)
    stat3[0:1] = center
    stat3[1:2] = inv
    stat3[2:3] = counted
    acc[...] = jnp.zeros_like(acc)

    def step(i, carry):
        own = pl.ds(pl.multiple_of(i * slab, slab), slab)
        mask = wide(inside(meta, i, 0, rows), 256)
        for k in range(4):
            lanes = slice(k * 256, k * 256 + 256)
            normed = (pre[own, lanes].astype(F32) - center[:, lanes]) * inv[:, lanes]
            value = normed * gain[:, lanes] + shift[:, lanes] + x[own, lanes].astype(F32)
            part = sigmoid(value)
            silu = value * part
            out[own, lanes] = (silu * mask).astype(BF16)
            slope = part + silu * (1.0 - part)
            back = cot[own, lanes].astype(F32) * mask * slope
            grad[own, lanes] = back
            acc[0, :, lanes] += fold(back)
            acc[1, :, lanes] += fold(back * normed)
        return carry

    lax.fori_loop(0, blocks, step, 0)
    put_row(pay, 0, total(acc[0]))
    put_row(pay, 8, total(acc[1]))
    spread(pay)


def back_terms(stat, gain, shift_sum, gain_sum):
    center, inv, counted = stat[0:1], stat[1:2], stat[2:3]
    a = gain * inv
    d = -a * inv * (gain_sum / counted)
    b = -a * (shift_sum / counted) - d * center
    return a, b, d


def mixture_kernel(
    meta, got, stat3, pre, grad, gain, w, hid, att, gexp, gmix, top, bottom, glog, gain_out, shift_out, *, blocks, rows
):
    slab = rows * COLS
    sums = jnp.sum(got[...], 0)
    shift_sum, gain_sum = row_of(sums, 0, 8), row_of(sums, 8, 8)
    shift_out[...] = shift_sum
    gain_out[...] = gain_sum
    a, b, d = back_terms(stat3, gain[...], shift_sum, gain_sum)
    group = 4

    def step(g, carry):
        many = pl.ds(pl.multiple_of(g * group * slab, group * slab), group * slab)
        for j in range(group):
            image = g * group + j
            own = pl.ds(pl.multiple_of(image * slab, slab), slab)
            mask = wide(inside(meta, image, 0, rows), 256)
            for k in range(4):
                lanes = slice(k * 256, k * 256 + 256)
                gexp[own, lanes] = (
                    mask
                    * (
                        a[:, lanes] * grad[own, lanes]
                        + b[:, lanes]
                        + d[:, lanes] * pre[own, lanes].astype(F32)
                    )
                ).astype(BF16)
        value = dot(gexp[many, :], w[...], ((1,), (1,))).astype(BF16)
        gmix[many, :] = value
        value = value.astype(F32)
        for j in range(group):
            image = g * group + j
            own = pl.ds(pl.multiple_of(image * slab, slab), slab)
            edge = pl.ds(pl.multiple_of(image * COLS, COLS), COLS)
            part = value[j * slab : (j + 1) * slab]
            top[edge, :] = part[:COLS]
            bottom[edge, :] = part[slab - COLS :]
            for half in range(2):
                lanes = slice(half * 256, half * 256 + 256)
                glog[pl.ds(image, 1), lanes] = total(fold(part * hid[own, lanes].astype(F32)))
        return carry

    lax.fori_loop(0, blocks // group, step, 0)
    first, second = att[:, :256], att[:, 256:]
    inner = first * glog[:, :256] + second * glog[:, 256:]
    glog[...] = jnp.concatenate(
        [first * (glog[:, :256] - inner), second * (glog[:, 256:] - inner)], axis=1
    )


def logits_kernel(meta, glog, we, pay):
    pay[0] = dot(glog[...], we[...], ((1,), (1,)), HIGHEST)
    spread(pay)


def expand_grad_kernel(meta, mix, gexp, hsq, glog, keep, send):
    for ref, core in ((send, 1 - meta[2]), (keep, meta[2])):
        lanes = pl.ds(pl.multiple_of(core * 512, 512), 512)
        value = dot(mix[...], gexp[:, lanes], ((0,), (0,))).astype(ref.dtype)
        lanes = pl.ds(pl.multiple_of(core * 256, 256), 256)
        excite = dot(hsq[...], glog[:, lanes], ((0,), (0,)), HIGHEST).astype(ref.dtype)
        for q in range(2):
            for k in range(2):
                first = k * 256 + q * 128
                ref[q, k * 256 : k * 256 + 256, :] = value[:, first : first + 128]
            ref[q, 512:, :] = excite[:, q * 128 : q * 128 + 128]


def add_kernel(meta, keep2, got2, keep3, got3, keep, send, token):
    first = keep2.shape[1]
    for ref, half in ((send, 1 - meta[3]), (keep, meta[3])):
        ref[:first, :] = (keep2[half] + got2[half].astype(F32)).astype(ref.dtype)
        last = first + keep3.shape[1]
        ref[first:last, :] = (keep3[half] + got3[half].astype(F32)).astype(ref.dtype)
        clear_from(ref, last)
    token[...] = jnp.zeros_like(token)


def pack_kernel(meta, keep, got, keep1, got1, out):
    chips = out.shape[0]
    large, small = keep.shape[0] // chips, keep1.shape[0] // chips
    out[:, :large, :] = (keep[...] + got[...].astype(F32)).astype(BF16).reshape(chips, large, LANES)
    out[:, large:, :] = (keep1[...] + got1[...].astype(F32)).astype(BF16).reshape(chips, small, LANES)


def share_kernel(meta, shares, out, *, large):
    chips, rows, _ = shares.shape

    def add(first, last, start, step):
        value = shares[start, first:last, :].astype(F32)
        for k in range(start + step, chips, step):
            value = value + shares[k, first:last, :].astype(F32)
        return value.astype(BF16)

    out[:large, :] = add(0, large, 0, 2)
    out[large : 2 * large, :] = add(0, large, 1, 2)
    out[2 * large :, :] = add(large, rows, 0, 1)


def hidden_kernel(
    meta, got, znorm, zall, hsq_gain, stat_sq, pooled, wsq, att, gmix, pre, stat2, gain, shift,
    dz, gpool, pay, gain_out, shift_out, acc, full, squeeze, *, blocks, rows, parts
):
    slab = rows * COLS
    bands = got.shape[0] // parts
    for b in range(bands):
        block = got[b * parts]
        for k in range(1, parts):
            block = block + got[b * parts + k]
        full[b * blocks : (b + 1) * blocks, :] = block
    z = zall[...]
    part = jax.nn.sigmoid(z)
    grad_z = full[...] * (part * (1.0 + z * (1.0 - part)))
    full[...] = grad_z
    images = float(bands * blocks)
    shift_sum = total(grad_z)
    gain_sum = total(grad_z * znorm[...])
    shift_out[...] = shift_sum
    gain_out[...] = gain_sum
    mine = pl.ds(pl.multiple_of(meta[1] * blocks, blocks), blocks)
    grad_pre = (
        hsq_gain[...]
        * stat_sq[1:2]
        * (full[mine, :] - shift_sum / images - znorm[mine, :] * (gain_sum / images))
    )
    squeeze[...] = dot(pooled[...], grad_pre, ((0,), (0,)), HIGHEST)
    gpool[...] = dot(grad_pre, wsq[...], ((1,), (1,)), HIGHEST)
    for i in range(blocks):
        gpool[i : i + 1, :] = gpool[i : i + 1, :] / area_of(meta, i)
    center, inv = stat2[0:1], stat2[1:2]
    acc[...] = jnp.zeros_like(acc)

    def step(i, carry):
        own = pl.ds(pl.multiple_of(i * slab, slab), slab)
        mask = wide(inside(meta, i, 0, rows), 256)
        mixed = gmix[own, :].astype(F32)
        pool = gpool[pl.ds(i, 1), :]
        for half in range(2):
            lanes = slice(half * 256, half * 256 + 256)
            normed = (pre[own, lanes] - center[:, lanes]) * inv[:, lanes]
            value = normed * gain[:, lanes] + shift[:, lanes]
            sig = sigmoid(value)
            slope = sig * (1.0 + value * (1.0 - sig))
            hidden = (mixed * att[pl.ds(i, 1), lanes] + pool).astype(BF16).astype(F32)
            back = hidden * mask * slope
            dz[own, lanes] = back
            acc[0, :, lanes] += fold(back)
            acc[1, :, lanes] += fold(back * normed)
        return carry

    lax.fori_loop(0, blocks, step, 0)
    put_row(pay, 0, total(acc[0]))
    put_row(pay, 4, total(acc[1]))
    pay[0, 8:, :] = jnp.zeros((pay.shape[1] - 8, LANES), F32)
    spread(pay)
    share = pay.shape[1] - 8
    for n in range(pay.shape[0]):
        pay[n, 8:, :] = squeeze[n * share : (n + 1) * share, :]


def conv_kernel(
    meta, got, stat2, gain2, shift2, dz, pre2, low2, high2, lowm, highm, att, gpool, w, pre, stat,
    gain, shift, glog, hid_in, out_hbm, keep_hbm, send_hbm, pay, gain_out, shift_out, tall, acc,
    hid, out, keep, send, sems, *, blocks, rows
):
    slab = rows * COLS
    fetch = pltpu.make_async_copy(hid_in, hid, sems.at[0])
    fetch.start()
    sums = jnp.sum(got[...], 0)
    shift_sum, gain_sum = row_of(sums, 0, 4), row_of(sums, 4, 4)
    shift_out[...] = shift_sum
    gain_out[...] = gain_sum
    a, b, d = back_terms(stat2, gain2[...], shift_sum, gain_sum)
    center2, inv2 = stat2[0:1], stat2[1:2]

    def prepare(i, carry):
        own = pl.ds(pl.multiple_of(i * slab, slab), slab)
        edge = pl.ds(pl.multiple_of(i * COLS, COLS), COLS)
        mask = inside(meta, i, -1, rows + 2)
        for half in range(2):
            lanes = slice(half * 256, half * 256 + 256)

            def edge_grad(values, mixed, keep):
                z = (values[edge, lanes] - center2[:, lanes]) * inv2[:, lanes]
                z = z * gain2[:, lanes] + shift2[:, lanes]
                sig = sigmoid(z)
                slope = sig * (1.0 + z * (1.0 - sig))
                hidden = (
                    mixed[edge, :] * att[pl.ds(i, 1), lanes] + gpool[pl.ds(i, 1), :]
                ).astype(BF16)
                return hidden.astype(F32) * keep * slope

            keep_low = wide(mask[:COLS], 256)
            keep_high = wide(mask[slab + COLS :], 256)
            grads = jnp.concatenate(
                [edge_grad(low2, lowm, keep_low), dz[own, lanes], edge_grad(high2, highm, keep_high)],
                axis=0,
            )
            values = jnp.concatenate([low2[edge, lanes], pre2[own, lanes], high2[edge, lanes]], axis=0)
            back = wide(mask, 256) * (a[:, lanes] * grads + b[:, lanes] + d[:, lanes] * values)
            left, middle, right = shifted(back)
            tall[0, i, :, lanes] = left
            tall[1, i, :, lanes] = middle
            tall[2, i, :, lanes] = right
        return carry

    lax.fori_loop(0, blocks, prepare, 0)
    fetch.wait()

    def weights(dy, carry):
        rows_at = pl.ds(pl.multiple_of(dy * COLS, COLS), slab)
        for ref, core in ((send, 1 - meta[2]), (keep, meta[2])):
            lanes = pl.ds(pl.multiple_of(core * 128, 128), 128)
            wide_lanes = pl.ds(pl.multiple_of(core * 256, 256), 256)
            grads = tall[1, :, COLS : COLS + slab, wide_lanes].reshape(blocks * slab, 256)
            lhs = jnp.concatenate(
                [hid[dx, :, rows_at, lanes].reshape(blocks * slab, 128) for dx in range(3)], axis=1
            )
            value = dot(lhs, grads, ((0,), (0,))).astype(ref.dtype)
            at = pl.ds(pl.multiple_of(dy * 384, 384), 384)
            for q in range(2):
                ref[q, at, :] = value[:, q * 128 : q * 128 + 128]
        return carry

    lax.fori_loop(0, 3, weights, 0)
    stores = [
        pltpu.make_async_copy(send, send_hbm, sems.at[1]),
        pltpu.make_async_copy(keep, keep_hbm, sems.at[2]),
    ]
    for store in stores:
        store.start()
    acc[...] = jnp.zeros_like(acc)
    center, inv = stat[0:1], stat[1:2]
    group = 4

    def step(g, carry):
        for half in range(2):
            lanes = slice(half * 256, half * 256 + 256)
            outs = slice(half * 128, half * 128 + 128)
            value = None
            for dy in range(3):
                for dx in range(3):
                    lhs = tall[
                        2 - dx, pl.ds(g * group, group), (2 - dy) * COLS : (2 - dy) * COLS + slab, lanes
                    ].reshape(group * slab, 256)
                    part = dot(lhs, w[dy, dx, half], ((1,), (1,)))
                    value = part if value is None else value + part
            for j in range(group):
                image = g * group + j
                own = pl.ds(pl.multiple_of(image * slab, slab), slab)
                mask = inside(meta, image, 0, rows)
                normed = (pre[own, outs] - center[:, outs]) * inv[:, outs]
                z = normed * gain[:, outs] + shift[:, outs]
                sig = sigmoid(z)
                slope = sig * (1.0 + z * (1.0 - sig))
                back = value[j * slab : (j + 1) * slab] * mask * slope
                out[own, outs] = back
                acc[0, :, outs] += fold(back)
                acc[1, :, outs] += fold(back * normed)
        return carry

    lax.fori_loop(0, blocks // group, step, 0)
    stores.append(pltpu.make_async_copy(out, out_hbm, sems.at[3]))
    stores[-1].start()
    put_row(pay, 0, total(acc[0]))
    put_row(pay, 2, total(acc[1]))
    put_row(pay, 4, total(glog[...]))
    pay[0, 8:, :] = sums[8:]
    spread(pay)
    for store in stores:
        store.wait()


def reduce_back_kernel(
    meta, got, stat, gain, dz_in, pre_in, x_in, small_out, keep, send, gain_out, shift_out, bias_out, squeeze,
    dz, pre, x, small, sems, *, blocks, rows
):
    slab = rows * COLS
    fetches = [
        pltpu.make_async_copy(source, target, sems.at[k])
        for k, (source, target) in enumerate(((dz_in, dz), (pre_in, pre), (x_in, x)))
    ]
    for fetch in fetches:
        fetch.start()
    sums = jnp.sum(got[:, :8, :], 0)
    share = got.shape[1] - 8
    for n in range(got.shape[0]):
        squeeze[n * share : (n + 1) * share, :] = got[n, 8:, :]
    shift_sum, gain_sum = row_of(sums, 0, 2), row_of(sums, 2, 2)
    shift_out[...] = shift_sum
    gain_out[...] = gain_sum
    bias_out[...] = row_of(sums, 4, 4)
    a, b, d = back_terms(stat, gain[...], shift_sum, gain_sum)
    fetches[0].wait()
    fetches[1].wait()

    def step(image, carry):
        own = pl.ds(pl.multiple_of(image * slab, slab), slab)
        mask = wide(inside(meta, image, 0, rows), 256)
        small[own, :] = (mask * (a * dz[own, :] + b + d * pre[own, :])).astype(BF16)
        return carry

    lax.fori_loop(0, blocks, step, 0)
    store = pltpu.make_async_copy(small, small_out, sems.at[3])
    store.start()
    fetches[2].wait()
    for ref, core in ((send, 1 - meta[2]), (keep, meta[2])):
        lanes = pl.ds(pl.multiple_of(core * 512, 512), 512)
        value = dot(x[:, lanes], small[...], ((0,), (0,))).astype(ref.dtype)
        for q in range(2):
            ref[q * 512 : q * 512 + 512, :] = value[:, q * 128 : q * 128 + 128]
        clear_from(ref, 1024)
    store.wait()


def input_kernel(meta, small, w, grad, out, token, *, blocks, rows):
    slab = rows * COLS
    token[...] = jnp.zeros_like(token)
    group = 4

    def step(g, carry):
        many = pl.ds(pl.multiple_of(g * group * slab, group * slab), group * slab)
        for k in range(4):
            lanes = slice(k * 256, k * 256 + 256)
            value = dot(small[many, :], w[lanes, :], ((1,), (1,)))
            for j in range(group):
                image = g * group + j
                own = pl.ds(pl.multiple_of(image * slab, slab), slab)
                mask = wide(inside(meta, image, 0, rows), 256)
                out[own, lanes] = (
                    (value[j * slab : (j + 1) * slab] + grad[own, lanes]) * mask
                ).astype(BF16)
        return carry

    lax.fori_loop(0, blocks // group, step, 0)


def total_kernel(meta, *refs, places, large):
    arrays = len(places)
    expand, excite, split, reduce, wide_part, narrow_part = refs[2 * arrays :]
    small = refs[0].shape[1] - 2 * large
    for parts, core in ((refs[:arrays], meta[2]), (refs[arrays : 2 * arrays], 1 - meta[2])):
        for part, chips in zip(parts, places):
            for k, chip in enumerate(chips):
                at = meta[4] ^ chip
                for q in range(2):
                    wide_part[q, pl.ds(pl.multiple_of(at * large, large), large), :] = part[
                        k, q * large : q * large + large, :
                    ]
                narrow_part[pl.ds(pl.multiple_of(at * small, small), small), :] = part[k, 2 * large :, :]
        for q in range(2):
            lanes = slice(q * 128, q * 128 + 128)
            for tap in range(9):
                split[tap // 3, tap % 3, core, :, lanes] = wide_part[q, tap * 128 : tap * 128 + 128].astype(F32)
            for k in range(2):
                first = 1152 + k * 256
                out = pl.ds(pl.multiple_of(core * 512 + (k * 256 + q * 128), 128), 128)
                expand[:, out] = wide_part[q, first : first + 256].astype(F32)
            out = pl.ds(pl.multiple_of(core * 256 + q * 128, 128), 128)
            excite[:, out] = wide_part[q, 1664:1792].astype(F32)
        own_rows = pl.ds(pl.multiple_of(core * 512, 512), 512)
        for q in range(2):
            reduce[own_rows, q * 128 : q * 128 + 128] = narrow_part[q * 512 : q * 512 + 512].astype(F32)


def body(
    inputs,
    image_class,
    weight_reduce,
    gain_reduce,
    shift_reduce,
    weight_split,
    gain_split,
    shift_split,
    weight_squeeze,
    gain_squeeze,
    shift_squeeze,
    weight_excite,
    bias_excite,
    weight_expand,
    gain_expand,
    shift_expand,
    cotangent,
):
    blocks, rows, cols, channels = inputs.shape
    mid = weight_reduce.shape[1]
    inter = weight_squeeze.shape[1]
    count = device_count()
    pixels = blocks * rows * cols
    slab = rows * cols
    edge = blocks * cols
    share = mid // count
    images = blocks * lax.axis_size("batch")
    meta = jnp.concatenate(
        [
            (lax.axis_index("narrow") * rows).astype(jnp.int32)[None],
            lax.axis_index("batch").astype(jnp.int32)[None],
            (lax.axis_index("narrow") % 2).astype(jnp.int32)[None],
            (lax.axis_index("narrow") // 2 % 2).astype(jnp.int32)[None],
            (lax.axis_index(ALL) // 2).astype(jnp.int32)[None],
            image_class,
        ]
    )
    x = inputs.reshape(pixels, channels)
    cot = cotangent.reshape(pixels, channels)
    row = lambda v: v.reshape(1, -1)
    gain1, shift1 = row(gain_reduce), row(shift_reduce)
    gain2, shift2 = row(gain_split), row(shift_split)
    gain3, shift3 = row(gain_expand), row(shift_expand)
    gain_sq, shift_sq = row(gain_squeeze), row(shift_squeeze)
    sizes = dict(blocks=blocks, rows=rows)
    small = 2 * pixels * channels * mid
    large = 2 * pixels * 9 * 128 * 512

    pre1, top, bottom, pay = call(
        reduce_kernel,
        [((pixels, mid), F32), ((edge, mid), F32), ((edge, mid), F32), ((count, 8, LANES), F32)],
        [meta, x, weight_reduce],
        [((3, 8, mid), F32)],
        flops=small,
        local="in out",
        **sizes,
    )
    low, high = halo(top, bottom)
    hid1, pre2, top, bottom, pay, stat1 = call(
        split_kernel,
        [
            ((3, blocks, slab + 2 * cols, mid), BF16, "hbm"),
            ((pixels, 2 * mid), F32),
            ((edge, 2 * mid), F32),
            ((edge, 2 * mid), F32),
            ((count, 8, LANES), F32),
            ((8, mid), F32),
        ],
        [meta, exchange(pay), pre1, low, high, gain1, shift1, weight_split],
        [((2, 8, 2 * mid), F32), ((3, blocks, slab + 2 * cols, mid), BF16), pltpu.SemaphoreType.DMA],
        raw_out=(0,),
        flops=large,
        local="in out",
        **sizes,
    )
    low2, high2 = halo(top, bottom)
    hid2, pooled, pay, stat2 = call(
        pool_kernel,
        [
            ((pixels, 2 * mid), BF16),
            ((blocks, mid), F32),
            ((count, blocks, inter), F32),
            ((8, 2 * mid), F32),
        ],
        [meta, exchange(pay), stat1, pre2, gain2, shift2, weight_squeeze],
        local="in out",
        after=(low2, high2),
        **sizes,
    )
    mix, pre3, att, hsq, znorm, zall, pay, stat_sq = call(
        expand_kernel,
        [
            ((pixels, mid), BF16),
            ((pixels, channels), BF16),
            ((blocks, 2 * mid), F32),
            ((blocks, inter), F32),
            ((images, inter), F32),
            ((images, inter), F32),
            ((count, 16, LANES), F32),
            ((8, inter), F32),
        ],
        [
            meta,
            exchange(pay),
            hid2,
            gain_sq,
            shift_sq,
            weight_excite,
            row(bias_excite),
            weight_expand,
        ],
        [((2, 8, channels), F32)],
        flops=small,
        parts=lax.axis_size("narrow"),
        local="in out",
        **sizes,
    )
    out, grad_res, pay, stat3 = call(
        residual_kernel,
        [
            ((pixels, channels), BF16),
            ((pixels, channels), F32),
            ((count, 16, LANES), F32),
            ((8, channels), F32),
        ],
        [meta, exchange(pay), stat1, x, pre3, cot, gain3, shift3],
        [((2, 8, channels), F32)],
        local="in out",
        **sizes,
    )
    gexp, gmix, top, bottom, glog, gain3_grad, shift3_grad = call(
        mixture_kernel,
        [
            ((pixels, channels), BF16),
            ((pixels, mid), BF16),
            ((edge, mid), F32),
            ((edge, mid), F32),
            ((blocks, 2 * mid), F32),
            ((1, channels), F32),
            ((1, channels), F32),
        ],
        [meta, exchange(pay), stat3, pre3, grad_res, gain3, weight_expand, hid2, att],
        flops=small,
        local="in out",
        **sizes,
    )
    lowm, highm = halo(top, bottom)
    keep3, send3 = call(
        expand_grad_kernel,
        [((2, 2 * mid + inter, LANES), F32), ((2, 2 * mid + inter, LANES), BF16)],
        [meta, mix, gexp, hsq, glog],
        flops=small,
        local="in out",
    )
    (pay,) = call(
        logits_kernel,
        [((count, blocks, inter), F32)],
        [meta, glog, weight_excite],
        after=(lowm, highm, send3),
        local="in out",
    )
    dz2, gpool, pay, gain_sq_grad, shift_sq_grad = call(
        hidden_kernel,
        [
            ((pixels, 2 * mid), F32),
            ((blocks, mid), F32),
            ((count, 8 + share, LANES), F32),
            ((1, inter), F32),
            ((1, inter), F32),
        ],
        [
            meta,
            exchange(pay),
            znorm,
            zall,
            gain_sq,
            stat_sq,
            pooled,
            weight_squeeze,
            att,
            gmix,
            pre2,
            stat2,
            gain2,
            shift2,
        ],
        [((2, 8, 2 * mid), F32), ((images, inter), F32), ((mid, inter), F32)],
        parts=lax.axis_size("narrow"),
        local="in out",
        **sizes,
    )
    dz1, keep2, send2, pay, gain2_grad, shift2_grad = call(
        conv_kernel,
        [
            ((pixels, mid), F32, "hbm"),
            ((2, 9 * 128, LANES), F32, "hbm"),
            ((2, 9 * 128, LANES), BF16, "hbm"),
            ((count, 8 + share, LANES), F32, "hbm"),
            ((1, 2 * mid), F32),
            ((1, 2 * mid), F32),
        ],
        [
            meta,
            exchange(pay),
            stat2,
            gain2,
            shift2,
            dz2,
            pre2,
            low2,
            high2,
            lowm,
            highm,
            att,
            gpool,
            weight_split,
            pre1,
            stat1,
            gain1,
            shift1,
            glog,
            hid1,
        ],
        [
            ((3, blocks, slab + 2 * cols, 2 * mid), BF16),
            ((2, 8, mid), F32),
            (hid1.shape, BF16),
            ((pixels, mid), F32),
            ((2, 9 * 128, LANES), F32),
            ((2, 9 * 128, LANES), BF16),
            pltpu.SemaphoreType.DMA((4,)),
        ],
        raw_in=(19,),
        raw_out=(0, 1, 2),
        flops=2 * large,
        local="in",
        **sizes,
    )
    chips = count // 2
    large, less = (-(-rows_in // (chips * 16)) * 16 for rows_in in (9 * 128 + 2 * mid + inter, channels))
    keep, send, token = call(
        add_kernel,
        [((chips * large, LANES), F32, "hbm"), ((chips * large, LANES), BF16, "hbm"), TOKEN],
        [meta, keep2, swap(send2, 1), keep3, swap(send3, 1)],
    )
    small1, keep1, send1, gain1_grad, shift1_grad, bias_grad, squeeze_total = call(
        reduce_back_kernel,
        [
            ((pixels, mid), BF16, "hbm"),
            ((chips * less, LANES), F32),
            ((chips * less, LANES), BF16),
            ((1, mid), F32),
            ((1, mid), F32),
            ((1, 2 * mid), F32),
            ((mid, inter), F32),
        ],
        [meta, exchange(pay), stat1, gain1, dz1, pre1, x],
        [
            ((pixels, mid), F32),
            ((pixels, mid), F32),
            ((pixels, channels), BF16),
            ((pixels, mid), BF16),
            pltpu.SemaphoreType.DMA((4,)),
        ],
        raw_in=(4, 5, 6),
        raw_out=(0,),
        flops=small,
        after=(token,),
        local="in",
        **sizes,
    )
    (packed,) = call(
        pack_kernel,
        [((chips, large + less, LANES), BF16, "hbm")],
        [meta, keep, swap(send, 2), keep1, swap(send1, 1)],
    )
    input_grad, token = call(
        input_kernel,
        [((pixels, channels), BF16, "hbm"), TOKEN],
        [meta, small1, weight_reduce, grad_res],
        flops=small,
        after=(packed,),
        **sizes,
    )
    (shared,) = call(
        share_kernel,
        [((2 * large + less, LANES), BF16)],
        [meta, exchange_chips(packed)],
        after=(token,),
        local="out",
        large=large,
    )
    parts, places = gather_chips(shared)
    expand_total, excite_total, split_total, reduce_total = call(
        total_kernel,
        [
            ((mid, channels), F32),
            ((inter, 2 * mid), F32),
            (weight_split.shape, F32),
            ((channels, mid), F32),
        ],
        [meta] + parts + [swap(part, 1) for part in parts],
        [((2, chips * large, LANES), BF16), ((chips * less, LANES), BF16)],
        local="in",
        places=places,
        large=large,
    )
    flat = lambda v: v.reshape(-1)
    return (
        out.reshape(inputs.shape),
        input_grad.reshape(inputs.shape),
        reduce_total,
        flat(gain1_grad),
        flat(shift1_grad),
        split_total,
        flat(gain2_grad),
        flat(shift2_grad),
        squeeze_total,
        flat(gain_sq_grad),
        flat(shift_sq_grad),
        excite_total,
        flat(bias_grad),
        expand_total,
        flat(gain3_grad),
        flat(shift3_grad),
    )


def solution(mesh):
    rows = P("batch", "narrow", None, None)
    return jax.shard_map(
        body,
        mesh=mesh,
        in_specs=(rows, P("batch")) + (P(),) * 14 + (rows,),
        out_specs=(rows, rows) + (P(),) * 14,
        check_vma=False,
    )
```

```python
import functools
from itertools import product

import jax
import jax.numpy as jnp
from jax import lax
from jax.experimental import pallas as pl
from jax.experimental.pallas import tpu as pltpu
from jax.sharding import PartitionSpec as P

EPSILON = 1e-05
HIGHEST = lax.Precision.HIGHEST
ALL = ("batch", "narrow")
F32 = jnp.float32
BF16 = jnp.bfloat16
COLS = 16
LANES = 128
TOKEN = ((8, LANES), F32, "hbm")


def device_count():
    return lax.axis_size("batch") * lax.axis_size("narrow")


def halo(top, bottom):
    count = lax.axis_size("narrow")
    low = lax.ppermute(bottom, "narrow", [(i, i + 1) for i in range(count - 1)])
    high = lax.ppermute(top, "narrow", [(i + 1, i) for i in range(count - 1)])
    return low, high


def exchange(block):
    return lax.all_to_all(block, ALL, 0, 0)


def swap(block, bit):
    count = lax.axis_size("narrow")
    return lax.ppermute(block, "narrow", [(i, i ^ bit) for i in range(count)])


def stages():
    bits = list(range(device_count().bit_length() - 2, 0, -1))
    pairs = [bits[k : k + 2] for k in range(0, len(bits), 2)]
    return [
        [sum(bit << pair[k] for k, bit in enumerate(pick)) for pick in product((0, 1), repeat=len(pair))]
        for pair in pairs
    ]


def partners(blocks, steps):
    count = device_count()
    return [
        lax.ppermute(block, ALL, [(i, i ^ step) for i in range(count)])
        for block, step in zip(blocks[1:], steps[1:])
    ]


def slots():
    order = [0]
    for steps in reversed(stages()):
        order = [place ^ (step >> 1) for place in order for step in steps]
    return order


def scatter_chips(meta, blocks, rows, large, after):
    order = list(reversed(stages()))
    for k, steps in enumerate(order):
        count = 1 if k + 1 == len(order) else len(order[k + 1])
        outs = [((blocks[0].shape[0] // count, rows, LANES), BF16)] * count
        blocks = call(
            sum_kernel,
            outs,
            [meta, blocks[0], *partners(blocks, steps)],
            after=() if k else after,
            large=0 if k else large,
            others=[step >> 1 & 1 for step in steps],
        )
    return blocks[0]


def gather_chips(share):
    block, places = share, [0]
    for steps in stages():
        blocks = [block] + partners([block] * len(steps), steps)
        lists = [[place ^ (step >> 1) for place in places] for step in steps]
        block, places = jnp.concatenate(blocks), sum(lists, [])
    return blocks, lists


def half_terms(center, inv, gain, shift):
    scale = 0.5 * inv * gain
    return scale, 0.5 * shift - scale * center


def silu_of_half(half):
    tanh = jnp.tanh(half)
    more = 1.0 + tanh
    silu = half * more
    return silu, more + silu * (1.0 - tanh)


def wide(mask, width):
    return jnp.concatenate([mask] * (width // LANES), axis=1) if width > LANES else mask


def inside(meta, image, start, count):
    pixel = lax.broadcasted_iota(jnp.int32, (count * COLS, LANES), 0)
    row = (pixel >> 4) + (meta[0] + start)
    col = pixel & (COLS - 1)
    side = 12 + 2 * meta[5 + image]
    return jnp.where((row < side) & (row >= 0) & (col < side), 1.0, 0.0).astype(F32)


def area_of(meta, image):
    side = (12 + 2 * meta[5 + image]).astype(F32)
    return side * side


def row_of(block, first, count):
    return jnp.concatenate([block[first + k : first + k + 1] for k in range(count)], axis=1)


def put_row(ref, first, vector):
    for k in range(vector.shape[1] // LANES):
        ref[0, first + k : first + k + 1, :] = vector[:, k * LANES : (k + 1) * LANES]


def put_sums(ref, rows, acc, center, inv):
    plain = total(acc[0])
    put_row(ref, 0, plain)
    put_row(ref, rows, (total(acc[1]) - center * plain) * inv)


def spread(ref):
    block = ref[0]

    def step(k, carry):
        ref[k] = block
        return carry

    lax.fori_loop(1, ref.shape[0], step, 0)


def fold(values):
    return jnp.sum(values.reshape(-1, 8, values.shape[-1]), 0)


def clear_from(ref, first):
    if ref.shape[0] > first:
        ref[first:, :] = jnp.zeros((ref.shape[0] - first, LANES), ref.dtype)


def total(block):
    return jnp.sum(block, 0, keepdims=True)


def stats(totals, squares, counted):
    center = totals / counted
    return center, lax.rsqrt(squares / counted - center * center + EPSILON)


def shifted(values):
    count, width = values.shape
    col = lax.broadcasted_iota(jnp.int32, (count, LANES), 0) & (COLS - 1)
    has_left = wide(jnp.where(col > 0, 1.0, 0.0).astype(F32), width)
    has_right = wide(jnp.where(col < COLS - 1, 1.0, 0.0).astype(F32), width)
    left = pltpu.roll(values, 1, 0) * has_left
    right = pltpu.roll(values, count - 1, 0) * has_right
    return left.astype(BF16), values.astype(BF16), right.astype(BF16)


def dot(a, b, dims=((1,), (0,)), precision=None):
    return lax.dot_general(a, b, (dims, ((), ())), precision=precision, preferred_element_type=F32)


def whole(shape):
    return pl.BlockSpec(shape, lambda step: (0,) * len(shape))


def call(
    kernel, outs, args, scratch=(), megabytes=24, flops=0, after=(), local="", raw_in=(), raw_out=(), **sizes
):
    moved = sum(a.size * a.dtype.itemsize for a in args) + sum(
        functools.reduce(lambda x, y: x * y, o[0]) * jnp.dtype(o[1]).itemsize for o in outs
    )
    count = len(args)
    vmem = pl.BlockSpec(memory_space=pltpu.VMEM)
    anywhere = pl.BlockSpec(memory_space=pl.ANY)
    in_hbm = lambda a: pltpu.with_memory_space_constraint(a, pltpu.HBM)
    args = [in_hbm(a) if k in raw_in else a for k, a in enumerate(args)]
    after = [in_hbm(a) if a.shape == TOKEN[0] else a for a in after]

    def run(*refs):
        kernel(*refs[:count], *refs[count + len(after) :], **sizes)

    def spec(place, shape, kept, raws):
        return anywhere if place in raws else vmem if kept else whole(shape)

    return pl.pallas_call(
        run,
        grid=() if local == "in out" else (1,),
        out_shape=[
            pltpu.HBM(o[0], o[1]) if len(o) > 2 else jax.ShapeDtypeStruct(o[0], o[1]) for o in outs
        ],
        in_specs=[pl.BlockSpec(memory_space=pltpu.SMEM)]
        + [spec(k, a.shape, "in" in local, raw_in) for k, a in enumerate(args) if k]
        + [anywhere] * len(after),
        out_specs=[spec(k, o[0], "out" in local, raw_out) for k, o in enumerate(outs)],
        scratch_shapes=[pltpu.VMEM(*entry) if isinstance(entry, tuple) else entry for entry in scratch],
        compiler_params=pltpu.CompilerParams(vmem_limit_bytes=megabytes << 20),
        cost_estimate=pl.CostEstimate(flops=flops, bytes_accessed=moved, transcendentals=0),
    )(*args, *after)


def reduce_kernel(meta, x, w, pre, top, bottom, pay, acc, *, blocks, rows):
    slab = rows * COLS
    acc[...] = jnp.zeros_like(acc)
    group = 4

    def step(g, carry):
        base = pl.multiple_of(g * group * slab, group * slab)
        out = dot(x[pl.ds(base, group * slab), :], w[...])
        for j in range(group):
            image = g * group + j
            mask = inside(meta, image, 0, rows)
            part = out[j * slab : (j + 1) * slab] * wide(mask, out.shape[1])
            pre[pl.ds(pl.multiple_of(image * slab, slab), slab), :] = part
            edge = pl.ds(pl.multiple_of(image * COLS, COLS), COLS)
            top[edge, :] = part[:COLS]
            bottom[edge, :] = part[slab - COLS :]
            acc[0] += fold(part)
            acc[1] += fold(part * part)
            acc[2, :, :LANES] += fold(mask)
        return carry

    lax.fori_loop(0, blocks // group, step, 0)
    put_row(pay, 0, total(acc[0]))
    put_row(pay, 2, total(acc[1]))
    put_row(pay, 4, total(acc[2, :, :LANES]))
    pay[0, 5:8, :] = jnp.zeros((3, LANES), F32)
    spread(pay)


def split_kernel(
    meta, got, pre, low, high, gain, shift, w, hid_out, out, top, bottom, pay, stat, acc, hid, sem, *, blocks, rows
):
    slab = rows * COLS
    sums = jnp.sum(got[...], 0)
    counted = row_of(jnp.concatenate([sums[4:5]] * 2, 0), 0, 2)
    center, inv = stats(row_of(sums, 0, 2), row_of(sums, 2, 2), counted)
    stat[...] = jnp.zeros_like(stat)
    stat[0:1] = center
    stat[1:2] = inv
    stat[2:3] = counted
    scale, offset = half_terms(center, inv, gain[...], shift[...])

    def prepare(i, carry):
        edge = pl.ds(pl.multiple_of(i * COLS, COLS), COLS)
        own = pl.ds(pl.multiple_of(i * slab, slab), slab)
        mask = inside(meta, i, -1, rows + 2)
        for k in range(2):
            lanes = slice(k * LANES, k * LANES + LANES)
            tall = jnp.concatenate([low[edge, lanes], pre[own, lanes], high[edge, lanes]], axis=0)
            silu, _ = silu_of_half(tall * scale[:, lanes] + offset[:, lanes])
            left, middle, right = shifted(silu * mask)
            hid[0, i, :, lanes] = left
            hid[1, i, :, lanes] = middle
            hid[2, i, :, lanes] = right
        return carry

    lax.fori_loop(0, blocks, prepare, 0)
    copy = pltpu.make_async_copy(hid, hid_out, sem)
    copy.start()
    acc[...] = jnp.zeros_like(acc)
    group = 4

    def step(g, carry):
        for half in range(2):
            lanes = slice(half * 128, half * 128 + 128)
            outs = slice(half * 256, half * 256 + 256)
            lhs = jnp.concatenate(
                [
                    hid[dx, pl.ds(g * group, group), dy * COLS : dy * COLS + slab, lanes].reshape(
                        group * slab, 128
                    )
                    for dy in range(3)
                    for dx in range(3)
                ],
                axis=1,
            )
            value = dot(lhs, w[:, :, half].reshape(9 * 128, 256))
            for j in range(group):
                image = g * group + j
                mask = inside(meta, image, 0, rows)
                part = value[j * slab : (j + 1) * slab] * wide(mask, 256)
                out[pl.ds(pl.multiple_of(image * slab, slab), slab), outs] = part
                edge = pl.ds(pl.multiple_of(image * COLS, COLS), COLS)
                top[edge, outs] = part[:COLS]
                bottom[edge, outs] = part[slab - COLS :]
                acc[0, :, outs] += fold(part)
                acc[1, :, outs] += fold(part * part)
        return carry

    lax.fori_loop(0, blocks // group, step, 0)
    put_row(pay, 0, total(acc[0]))
    put_row(pay, 4, total(acc[1]))
    spread(pay)
    copy.wait()


def pool_kernel(
    meta, got, stat, pre, gain, shift, w, hid, pooled, pay, stat2, *, blocks, rows
):
    slab = rows * COLS
    sums = jnp.sum(got[...], 0)
    counted = jnp.concatenate([stat[2:3]] * 2, axis=1)
    center, inv = stats(row_of(sums, 0, 4), row_of(sums, 4, 4), counted)
    stat2[...] = jnp.zeros_like(stat2)
    stat2[0:1] = center
    stat2[1:2] = inv
    stat2[2:3] = counted
    scale, offset = half_terms(center, inv, gain[...], shift[...])

    def step(i, carry):
        own = pl.ds(pl.multiple_of(i * slab, slab), slab)
        mask = inside(meta, i, 0, rows)
        summed = [None, None]
        for k in range(4):
            lanes = slice(k * LANES, k * LANES + LANES)
            silu, _ = silu_of_half(pre[own, lanes] * scale[:, lanes] + offset[:, lanes])
            value = (silu * mask).astype(BF16)
            hid[own, lanes] = value
            part = fold(value.astype(F32))
            summed[k % 2] = part if k < 2 else summed[k % 2] + part
        pooled[pl.ds(i, 1), :] = total(jnp.concatenate(summed, axis=1)) / area_of(meta, i)
        return carry

    lax.fori_loop(0, blocks, step, 0)
    pay[0] = dot(pooled[...], w[...], precision=HIGHEST)
    spread(pay)


def squeeze_stats(block):
    return stats(total(block), total(block * block), float(block.shape[0]))


def expand_kernel(
    meta, got, hid, gain, shift, we, bias, w, mix, pre, att, hsq, znorm, zall, pay, stat_sq, acc, *, blocks, rows, parts
):
    slab = rows * COLS
    bands = got.shape[0] // parts
    for b in range(bands):
        block = got[b * parts]
        for k in range(1, parts):
            block = block + got[b * parts + k]
        znorm[b * blocks : (b + 1) * blocks, :] = block
    center, inv = squeeze_stats(znorm[...])
    stat_sq[...] = jnp.zeros_like(stat_sq)
    stat_sq[0:1] = center
    stat_sq[1:2] = inv
    normed = (znorm[...] - center) * inv
    znorm[...] = normed
    zall[...] = normed * gain[...] + shift[...]
    own_z = zall[pl.ds(pl.multiple_of(meta[1] * blocks, blocks), blocks), :]
    hidden = own_z * jax.nn.sigmoid(own_z)
    hsq[...] = hidden
    logits = dot(hidden, we[...], precision=HIGHEST) + bias[...]
    first = logits[:, :256]
    second = logits[:, 256:]
    ceiling = jnp.maximum(first, second)
    exp_first = jnp.exp(first - ceiling)
    exp_second = jnp.exp(second - ceiling)
    att[:, :256] = exp_first / (exp_first + exp_second)
    att[:, 256:] = exp_second / (exp_first + exp_second)
    acc[...] = jnp.zeros_like(acc)
    group = 4

    def step(g, carry):
        for j in range(group):
            image = g * group + j
            own = pl.ds(pl.multiple_of(image * slab, slab), slab)
            weights = att[pl.ds(image, 1), :]
            mix[own, :] = (
                weights[:, :256] * hid[own, :256].astype(F32)
                + weights[:, 256:] * hid[own, 256:].astype(F32)
            ).astype(BF16)
        many = pl.ds(pl.multiple_of(g * group * slab, group * slab), group * slab)
        for k in range(4):
            lanes = slice(k * 256, k * 256 + 256)
            value = dot(mix[many, :], w[:, lanes]).astype(BF16)
            pre[many, lanes] = value
            value = value.astype(F32)
            acc[0, :, lanes] += fold(value)
            acc[1, :, lanes] += fold(value * value)
        return carry

    lax.fori_loop(0, blocks // group, step, 0)
    put_row(pay, 0, total(acc[0]))
    put_row(pay, 8, total(acc[1]))
    spread(pay)


def residual_kernel(
    meta, got, stat, x, pre, cot, gain, shift, out, grad, pay, stat3, acc, *, blocks, rows
):
    slab = rows * COLS
    sums = jnp.sum(got[...], 0)
    counted = jnp.concatenate([stat[2:3]] * 4, axis=1)
    center, inv = stats(row_of(sums, 0, 8), row_of(sums, 8, 8), counted)
    stat3[...] = jnp.zeros_like(stat3)
    stat3[0:1] = center
    stat3[1:2] = inv
    stat3[2:3] = counted
    acc[...] = jnp.zeros_like(acc)
    scale, offset = half_terms(center, inv, gain[...], shift[...])

    def step(i, carry):
        own = pl.ds(pl.multiple_of(i * slab, slab), slab)
        mask = inside(meta, i, 0, rows)
        half_mask = 0.5 * mask
        for k in range(8):
            lanes = slice(k * LANES, k * LANES + LANES)
            values = pre[own, lanes].astype(F32)
            half = values * scale[:, lanes] + offset[:, lanes] + 0.5 * x[own, lanes].astype(F32)
            silu, slope = silu_of_half(half)
            out[own, lanes] = (silu * mask).astype(BF16)
            back = cot[own, lanes].astype(F32) * half_mask * slope
            grad[own, lanes] = back
            acc[0, :, lanes] += fold(back)
            acc[1, :, lanes] += fold(back * values)
        return carry

    lax.fori_loop(0, blocks, step, 0)
    put_sums(pay, 8, acc, center, inv)
    spread(pay)


def back_terms(stat, gain, shift_sum, gain_sum):
    center, inv, counted = stat[0:1], stat[1:2], stat[2:3]
    a = gain * inv
    d = -a * inv * (gain_sum / counted)
    b = -a * (shift_sum / counted) - d * center
    return a, b, d


def mixture_kernel(
    meta, got, stat3, pre, grad, gain, w, hid, att, gexp, gmix, top, bottom, glog, gain_out, shift_out, *, blocks, rows
):
    slab = rows * COLS
    sums = jnp.sum(got[...], 0)
    shift_sum, gain_sum = row_of(sums, 0, 8), row_of(sums, 8, 8)
    shift_out[...] = shift_sum
    gain_out[...] = gain_sum
    a, b, d = back_terms(stat3, gain[...], shift_sum, gain_sum)
    group = 4

    def step(g, carry):
        many = pl.ds(pl.multiple_of(g * group * slab, group * slab), group * slab)
        for j in range(group):
            image = g * group + j
            own = pl.ds(pl.multiple_of(image * slab, slab), slab)
            mask = inside(meta, image, 0, rows)
            for k in range(8):
                lanes = slice(k * LANES, k * LANES + LANES)
                gexp[own, lanes] = (
                    mask
                    * (
                        a[:, lanes] * grad[own, lanes]
                        + b[:, lanes]
                        + d[:, lanes] * pre[own, lanes].astype(F32)
                    )
                ).astype(BF16)
        value = dot(gexp[many, :], w[...], ((1,), (1,))).astype(BF16)
        gmix[many, :] = value
        value = value.astype(F32)
        for j in range(group):
            image = g * group + j
            own = pl.ds(pl.multiple_of(image * slab, slab), slab)
            edge = pl.ds(pl.multiple_of(image * COLS, COLS), COLS)
            part = value[j * slab : (j + 1) * slab]
            top[edge, :] = part[:COLS]
            bottom[edge, :] = part[slab - COLS :]
            for half in range(2):
                lanes = slice(half * 256, half * 256 + 256)
                glog[pl.ds(image, 1), lanes] = total(fold(part * hid[own, lanes].astype(F32)))
        return carry

    lax.fori_loop(0, blocks // group, step, 0)
    first, second = att[:, :256], att[:, 256:]
    inner = first * glog[:, :256] + second * glog[:, 256:]
    glog[...] = jnp.concatenate(
        [first * (glog[:, :256] - inner), second * (glog[:, 256:] - inner)], axis=1
    )


def logits_kernel(meta, glog, we, pay):
    pay[0] = dot(glog[...], we[...], ((1,), (1,)), HIGHEST)
    spread(pay)


def expand_grad_kernel(meta, mix, gexp, hsq, glog, keep, send):
    for ref, core in ((send, 1 - meta[2]), (keep, meta[2])):
        lanes = pl.ds(pl.multiple_of(core * 512, 512), 512)
        value = dot(mix[...], gexp[:, lanes], ((0,), (0,))).astype(ref.dtype)
        lanes = pl.ds(pl.multiple_of(core * 256, 256), 256)
        excite = dot(hsq[...], glog[:, lanes], ((0,), (0,)), HIGHEST).astype(ref.dtype)
        for q in range(2):
            for k in range(2):
                first = k * 256 + q * 128
                ref[q, k * 256 : k * 256 + 256, :] = value[:, first : first + 128]
            ref[q, 512:, :] = excite[:, q * 128 : q * 128 + 128]


def add_kernel(meta, keep2, got2, keep3, got3, keep, send, token):
    first = keep2.shape[1]
    for ref, half in ((send, 1 - meta[3]), (keep, meta[3])):
        ref[:first, :] = (keep2[half] + got2[half].astype(F32)).astype(ref.dtype)
        last = first + keep3.shape[1]
        ref[first:last, :] = (keep3[half] + got3[half].astype(F32)).astype(ref.dtype)
        clear_from(ref, last)
    token[...] = jnp.zeros_like(token)


def pack_kernel(meta, keep, got, keep1, got1, *refs, places):
    *outs, flat, flat1 = refs
    held = outs[0].shape[0]
    large, small = flat.shape[0] // len(places), flat1.shape[0] // len(places)
    flat[...] = (keep[...] + got[...].astype(F32)).astype(BF16)
    flat1[...] = (keep1[...] + got1[...].astype(F32)).astype(BF16)
    for k, place in enumerate(places):
        chip = meta[4] ^ place
        out = outs[k // held]
        out[k % held, :large, :] = flat[pl.ds(pl.multiple_of(chip * large, large), large), :]
        out[k % held, large:, :] = flat1[pl.ds(pl.multiple_of(chip * small, small), small), :]


def sum_kernel(meta, *refs, large, others):
    ins, outs = refs[: len(others)], refs[len(others) :]
    held = outs[0].shape[0]

    def add(pick, first, last):
        value = None
        for ref in pick:
            part = ref[:, first:last, :].astype(F32)
            value = part if value is None else value + part
        return value.astype(BF16)

    def put(value, at, rows):
        for k, out in enumerate(outs):
            out[:, pl.ds(at, rows), :] = value[k * held : k * held + held]

    total_rows = ins[0].shape[1]
    if not large:
        put(add(ins, 0, total_rows), 0, total_rows)
        return
    for other in range(2):
        pick = [ref for ref, side in zip(ins, others) if side == other]
        put(add(pick, 0, large), pl.multiple_of((meta[3] ^ other) * large, large), large)
    put(add(ins, large, total_rows), 2 * large, total_rows - large)


def hidden_kernel(
    meta, got, znorm, zall, hsq_gain, stat_sq, pooled, wsq, att, gmix, pre, stat2, gain, shift,
    dz, gpool, pay, gain_out, shift_out, acc, full, squeeze, *, blocks, rows, parts
):
    slab = rows * COLS
    bands = got.shape[0] // parts
    for b in range(bands):
        block = got[b * parts]
        for k in range(1, parts):
            block = block + got[b * parts + k]
        full[b * blocks : (b + 1) * blocks, :] = block
    z = zall[...]
    part = jax.nn.sigmoid(z)
    grad_z = full[...] * (part * (1.0 + z * (1.0 - part)))
    full[...] = grad_z
    images = float(bands * blocks)
    shift_sum = total(grad_z)
    gain_sum = total(grad_z * znorm[...])
    shift_out[...] = shift_sum
    gain_out[...] = gain_sum
    mine = pl.ds(pl.multiple_of(meta[1] * blocks, blocks), blocks)
    grad_pre = (
        hsq_gain[...]
        * stat_sq[1:2]
        * (full[mine, :] - shift_sum / images - znorm[mine, :] * (gain_sum / images))
    )
    squeeze[...] = dot(pooled[...], grad_pre, ((0,), (0,)), HIGHEST)
    gpool[...] = dot(grad_pre, wsq[...], ((1,), (1,)), HIGHEST)
    for i in range(blocks):
        gpool[i : i + 1, :] = gpool[i : i + 1, :] / area_of(meta, i)
    center, inv = stat2[0:1], stat2[1:2]
    acc[...] = jnp.zeros_like(acc)
    scale, offset = half_terms(center, inv, gain[...], shift[...])

    def step(i, carry):
        own = pl.ds(pl.multiple_of(i * slab, slab), slab)
        half_mask = 0.5 * inside(meta, i, 0, rows)
        weights = att[pl.ds(i, 1), :]
        pool = gpool[pl.ds(i, 1), :]
        for k in range(4):
            lanes = slice(k * LANES, k * LANES + LANES)
            mid = slice(k % 2 * LANES, k % 2 * LANES + LANES)
            mixed = gmix[own, mid].astype(F32)
            values = pre[own, lanes]
            _, slope = silu_of_half(values * scale[:, lanes] + offset[:, lanes])
            hidden = (mixed * weights[:, lanes] + pool[:, mid]).astype(BF16).astype(F32)
            back = hidden * half_mask * slope
            dz[own, lanes] = back
            acc[0, :, lanes] += fold(back)
            acc[1, :, lanes] += fold(back * values)
        return carry

    lax.fori_loop(0, blocks, step, 0)
    put_sums(pay, 4, acc, center, inv)
    pay[0, 8:, :] = jnp.zeros((pay.shape[1] - 8, LANES), F32)
    spread(pay)
    share = pay.shape[1] - 8
    for n in range(pay.shape[0]):
        pay[n, 8:, :] = squeeze[n * share : (n + 1) * share, :]


def conv_kernel(
    meta, got, stat2, gain2, shift2, dz, pre2, low2, high2, lowm, highm, att, gpool, w, pre, stat,
    gain, shift, glog, hid_in, out_hbm, keep_hbm, send_hbm, pay, gain_out, shift_out, tall, acc,
    hid, out, keep, send, sems, *, blocks, rows
):
    slab = rows * COLS
    fetch = pltpu.make_async_copy(hid_in, hid, sems.at[0])
    fetch.start()
    sums = jnp.sum(got[...], 0)
    shift_sum, gain_sum = row_of(sums, 0, 4), row_of(sums, 4, 4)
    shift_out[...] = shift_sum
    gain_out[...] = gain_sum
    a, b, d = back_terms(stat2, gain2[...], shift_sum, gain_sum)
    scale2, offset2 = half_terms(stat2[0:1], stat2[1:2], gain2[...], shift2[...])

    def prepare(i, carry):
        own = pl.ds(pl.multiple_of(i * slab, slab), slab)
        edge = pl.ds(pl.multiple_of(i * COLS, COLS), COLS)
        mask = inside(meta, i, -1, rows + 2)
        weights = att[pl.ds(i, 1), :]
        pool = gpool[pl.ds(i, 1), :]
        for k in range(4):
            lanes = slice(k * LANES, k * LANES + LANES)
            mid = slice(k % 2 * LANES, k % 2 * LANES + LANES)

            def edge_grad(values, mixed, keep):
                _, slope = silu_of_half(values[edge, lanes] * scale2[:, lanes] + offset2[:, lanes])
                hidden = mixed[edge, mid] * weights[:, lanes] + pool[:, mid]
                return hidden.astype(BF16).astype(F32) * (0.5 * keep) * slope

            keep_low, keep_high = mask[:COLS], mask[slab + COLS :]
            grads = jnp.concatenate(
                [edge_grad(low2, lowm, keep_low), dz[own, lanes], edge_grad(high2, highm, keep_high)],
                axis=0,
            )
            values = jnp.concatenate([low2[edge, lanes], pre2[own, lanes], high2[edge, lanes]], axis=0)
            back = mask * (a[:, lanes] * grads + b[:, lanes] + d[:, lanes] * values)
            left, middle, right = shifted(back)
            tall[0, i, :, lanes] = left
            tall[1, i, :, lanes] = middle
            tall[2, i, :, lanes] = right
        return carry

    lax.fori_loop(0, blocks, prepare, 0)
    fetch.wait()

    def weights(dy, carry):
        rows_at = pl.ds(pl.multiple_of(dy * COLS, COLS), slab)
        for ref, core in ((send, 1 - meta[2]), (keep, meta[2])):
            lanes = pl.ds(pl.multiple_of(core * 128, 128), 128)
            wide_lanes = pl.ds(pl.multiple_of(core * 256, 256), 256)
            grads = tall[1, :, COLS : COLS + slab, wide_lanes].reshape(blocks * slab, 256)
            lhs = jnp.concatenate(
                [hid[dx, :, rows_at, lanes].reshape(blocks * slab, 128) for dx in range(3)], axis=1
            )
            value = dot(lhs, grads, ((0,), (0,))).astype(ref.dtype)
            at = pl.ds(pl.multiple_of(dy * 384, 384), 384)
            for q in range(2):
                ref[q, at, :] = value[:, q * 128 : q * 128 + 128]
        return carry

    lax.fori_loop(0, 3, weights, 0)
    stores = [
        pltpu.make_async_copy(send, send_hbm, sems.at[1]),
        pltpu.make_async_copy(keep, keep_hbm, sems.at[2]),
    ]
    for store in stores:
        store.start()
    acc[...] = jnp.zeros_like(acc)
    center, inv = stat[0:1], stat[1:2]
    scale, offset = half_terms(center, inv, gain[...], shift[...])
    group = 4

    def step(g, carry):
        for half in range(2):
            lanes = slice(half * 256, half * 256 + 256)
            outs = slice(half * 128, half * 128 + 128)
            value = None
            for dy in range(3):
                for dx in range(3):
                    lhs = tall[
                        2 - dx, pl.ds(g * group, group), (2 - dy) * COLS : (2 - dy) * COLS + slab, lanes
                    ].reshape(group * slab, 256)
                    part = dot(lhs, w[dy, dx, half], ((1,), (1,)))
                    value = part if value is None else value + part
            for j in range(group):
                image = g * group + j
                own = pl.ds(pl.multiple_of(image * slab, slab), slab)
                values = pre[own, outs]
                _, slope = silu_of_half(values * scale[:, outs] + offset[:, outs])
                back = value[j * slab : (j + 1) * slab] * (0.5 * inside(meta, image, 0, rows)) * slope
                out[own, outs] = back
                acc[0, :, outs] += fold(back)
                acc[1, :, outs] += fold(back * values)
        return carry

    lax.fori_loop(0, blocks // group, step, 0)
    stores.append(pltpu.make_async_copy(out, out_hbm, sems.at[3]))
    stores[-1].start()
    put_sums(pay, 2, acc, center, inv)
    put_row(pay, 4, total(glog[...]))
    pay[0, 8:, :] = sums[8:]
    spread(pay)
    for store in stores:
        store.wait()


def reduce_back_kernel(
    meta, got, stat, gain, dz_in, pre_in, x_in, small, keep, send, gain_out, shift_out, bias_out, squeeze,
    dz, pre, x, sems, *, blocks, rows
):
    slab = rows * COLS
    fetches = [
        pltpu.make_async_copy(source, target, sems.at[k])
        for k, (source, target) in enumerate(((dz_in, dz), (pre_in, pre), (x_in, x)))
    ]
    for fetch in fetches:
        fetch.start()
    sums = jnp.sum(got[:, :8, :], 0)
    share = got.shape[1] - 8
    for n in range(got.shape[0]):
        squeeze[n * share : (n + 1) * share, :] = got[n, 8:, :]
    shift_sum, gain_sum = row_of(sums, 0, 2), row_of(sums, 2, 2)
    shift_out[...] = shift_sum
    gain_out[...] = gain_sum
    bias_out[...] = row_of(sums, 4, 4)
    a, b, d = back_terms(stat, gain[...], shift_sum, gain_sum)
    fetches[0].wait()
    fetches[1].wait()

    def step(image, carry):
        own = pl.ds(pl.multiple_of(image * slab, slab), slab)
        mask = wide(inside(meta, image, 0, rows), 256)
        small[own, :] = (mask * (a * dz[own, :] + b + d * pre[own, :])).astype(BF16)
        return carry

    lax.fori_loop(0, blocks, step, 0)
    fetches[2].wait()
    for ref, core in ((send, 1 - meta[2]), (keep, meta[2])):
        lanes = pl.ds(pl.multiple_of(core * 512, 512), 512)
        value = dot(x[:, lanes], small[...], ((0,), (0,))).astype(ref.dtype)
        for q in range(2):
            ref[q * 512 : q * 512 + 512, :] = value[:, q * 128 : q * 128 + 128]
        clear_from(ref, 1024)


def input_kernel(meta, small, w, grad, out, token, *, blocks, rows):
    slab = rows * COLS
    token[...] = jnp.zeros_like(token)
    group = 4

    def step(g, carry):
        many = pl.ds(pl.multiple_of(g * group * slab, group * slab), group * slab)
        for k in range(4):
            lanes = slice(k * 256, k * 256 + 256)
            value = dot(small[many, :], w[lanes, :], ((1,), (1,)))
            for j in range(group):
                image = g * group + j
                own = pl.ds(pl.multiple_of(image * slab, slab), slab)
                mask = wide(inside(meta, image, 0, rows), 256)
                out[own, lanes] = (
                    (value[j * slab : (j + 1) * slab] + grad[own, lanes]) * mask
                ).astype(BF16)
        return carry

    lax.fori_loop(0, blocks // group, step, 0)


def total_kernel(meta, *refs, places, large):
    arrays = len(places)
    expand, excite, split, reduce, wide_part, narrow_part = refs[2 * arrays :]
    small = refs[0].shape[1] - 2 * large
    for parts, core in ((refs[:arrays], meta[2]), (refs[arrays : 2 * arrays], 1 - meta[2])):
        for part, chips in zip(parts, places):
            for k, chip in enumerate(chips):
                at = meta[4] ^ chip
                for q in range(2):
                    wide_part[q, pl.ds(pl.multiple_of(at * large, large), large), :] = part[
                        k, q * large : q * large + large, :
                    ]
                narrow_part[pl.ds(pl.multiple_of(at * small, small), small), :] = part[k, 2 * large :, :]
        for q in range(2):
            lanes = slice(q * 128, q * 128 + 128)
            for tap in range(9):
                split[tap // 3, tap % 3, core, :, lanes] = wide_part[q, tap * 128 : tap * 128 + 128].astype(F32)
            for k in range(2):
                first = 1152 + k * 256
                out = pl.ds(pl.multiple_of(core * 512 + (k * 256 + q * 128), 128), 128)
                expand[:, out] = wide_part[q, first : first + 256].astype(F32)
            out = pl.ds(pl.multiple_of(core * 256 + q * 128, 128), 128)
            excite[:, out] = wide_part[q, 1664:1792].astype(F32)
        own_rows = pl.ds(pl.multiple_of(core * 512, 512), 512)
        for q in range(2):
            reduce[own_rows, q * 128 : q * 128 + 128] = narrow_part[q * 512 : q * 512 + 512].astype(F32)


def body(
    inputs,
    image_class,
    weight_reduce,
    gain_reduce,
    shift_reduce,
    weight_split,
    gain_split,
    shift_split,
    weight_squeeze,
    gain_squeeze,
    shift_squeeze,
    weight_excite,
    bias_excite,
    weight_expand,
    gain_expand,
    shift_expand,
    cotangent,
):
    blocks, rows, cols, channels = inputs.shape
    mid = weight_reduce.shape[1]
    inter = weight_squeeze.shape[1]
    count = device_count()
    pixels = blocks * rows * cols
    slab = rows * cols
    edge = blocks * cols
    share = mid // count
    images = blocks * lax.axis_size("batch")
    meta = jnp.concatenate(
        [
            (lax.axis_index("narrow") * rows).astype(jnp.int32)[None],
            lax.axis_index("batch").astype(jnp.int32)[None],
            (lax.axis_index("narrow") % 2).astype(jnp.int32)[None],
            (lax.axis_index("narrow") // 2 % 2).astype(jnp.int32)[None],
            (lax.axis_index(ALL) // 2).astype(jnp.int32)[None],
            image_class,
        ]
    )
    x = inputs.reshape(pixels, channels)
    cot = cotangent.reshape(pixels, channels)
    row = lambda v: v.reshape(1, -1)
    gain1, shift1 = row(gain_reduce), row(shift_reduce)
    gain2, shift2 = row(gain_split), row(shift_split)
    gain3, shift3 = row(gain_expand), row(shift_expand)
    gain_sq, shift_sq = row(gain_squeeze), row(shift_squeeze)
    sizes = dict(blocks=blocks, rows=rows)
    small = 2 * pixels * channels * mid
    large = 2 * pixels * 9 * 128 * 512

    pre1, top, bottom, pay = call(
        reduce_kernel,
        [((pixels, mid), F32), ((edge, mid), F32), ((edge, mid), F32), ((count, 8, LANES), F32)],
        [meta, x, weight_reduce],
        [((3, 8, mid), F32)],
        flops=small,
        local="in out",
        **sizes,
    )
    low, high = halo(top, bottom)
    hid1, pre2, top, bottom, pay, stat1 = call(
        split_kernel,
        [
            ((3, blocks, slab + 2 * cols, mid), BF16, "hbm"),
            ((pixels, 2 * mid), F32),
            ((edge, 2 * mid), F32),
            ((edge, 2 * mid), F32),
            ((count, 8, LANES), F32),
            ((8, mid), F32),
        ],
        [meta, exchange(pay), pre1, low, high, gain1, shift1, weight_split],
        [((2, 8, 2 * mid), F32), ((3, blocks, slab + 2 * cols, mid), BF16), pltpu.SemaphoreType.DMA],
        raw_out=(0,),
        flops=large,
        local="in out",
        **sizes,
    )
    low2, high2 = halo(top, bottom)
    hid2, pooled, pay, stat2 = call(
        pool_kernel,
        [
            ((pixels, 2 * mid), BF16),
            ((blocks, mid), F32),
            ((count, blocks, inter), F32),
            ((8, 2 * mid), F32),
        ],
        [meta, exchange(pay), stat1, pre2, gain2, shift2, weight_squeeze],
        local="in out",
        after=(low2, high2),
        **sizes,
    )
    mix, pre3, att, hsq, znorm, zall, pay, stat_sq = call(
        expand_kernel,
        [
            ((pixels, mid), BF16),
            ((pixels, channels), BF16),
            ((blocks, 2 * mid), F32),
            ((blocks, inter), F32),
            ((images, inter), F32),
            ((images, inter), F32),
            ((count, 16, LANES), F32),
            ((8, inter), F32),
        ],
        [
            meta,
            exchange(pay),
            hid2,
            gain_sq,
            shift_sq,
            weight_excite,
            row(bias_excite),
            weight_expand,
        ],
        [((2, 8, channels), F32)],
        flops=small,
        parts=lax.axis_size("narrow"),
        local="in out",
        **sizes,
    )
    out, grad_res, pay, stat3 = call(
        residual_kernel,
        [
            ((pixels, channels), BF16),
            ((pixels, channels), F32),
            ((count, 16, LANES), F32),
            ((8, channels), F32),
        ],
        [meta, exchange(pay), stat1, x, pre3, cot, gain3, shift3],
        [((2, 8, channels), F32)],
        local="in out",
        **sizes,
    )
    gexp, gmix, top, bottom, glog, gain3_grad, shift3_grad = call(
        mixture_kernel,
        [
            ((pixels, channels), BF16),
            ((pixels, mid), BF16),
            ((edge, mid), F32),
            ((edge, mid), F32),
            ((blocks, 2 * mid), F32),
            ((1, channels), F32),
            ((1, channels), F32),
        ],
        [meta, exchange(pay), stat3, pre3, grad_res, gain3, weight_expand, hid2, att],
        flops=small,
        local="in out",
        **sizes,
    )
    lowm, highm = halo(top, bottom)
    keep3, send3 = call(
        expand_grad_kernel,
        [((2, 2 * mid + inter, LANES), F32), ((2, 2 * mid + inter, LANES), BF16)],
        [meta, mix, gexp, hsq, glog],
        flops=small,
        local="in out",
    )
    (pay,) = call(
        logits_kernel,
        [((count, blocks, inter), F32)],
        [meta, glog, weight_excite],
        after=(lowm, highm, send3),
        local="in out",
    )
    dz2, gpool, pay, gain_sq_grad, shift_sq_grad = call(
        hidden_kernel,
        [
            ((pixels, 2 * mid), F32),
            ((blocks, mid), F32),
            ((count, 8 + share, LANES), F32),
            ((1, inter), F32),
            ((1, inter), F32),
        ],
        [
            meta,
            exchange(pay),
            znorm,
            zall,
            gain_sq,
            stat_sq,
            pooled,
            weight_squeeze,
            att,
            gmix,
            pre2,
            stat2,
            gain2,
            shift2,
        ],
        [((2, 8, 2 * mid), F32), ((images, inter), F32), ((mid, inter), F32)],
        parts=lax.axis_size("narrow"),
        local="in out",
        **sizes,
    )
    dz1, keep2, send2, pay, gain2_grad, shift2_grad = call(
        conv_kernel,
        [
            ((pixels, mid), F32, "hbm"),
            ((2, 9 * 128, LANES), F32, "hbm"),
            ((2, 9 * 128, LANES), BF16, "hbm"),
            ((count, 8 + share, LANES), F32, "hbm"),
            ((1, 2 * mid), F32),
            ((1, 2 * mid), F32),
        ],
        [
            meta,
            exchange(pay),
            stat2,
            gain2,
            shift2,
            dz2,
            pre2,
            low2,
            high2,
            lowm,
            highm,
            att,
            gpool,
            weight_split,
            pre1,
            stat1,
            gain1,
            shift1,
            glog,
            hid1,
        ],
        [
            ((3, blocks, slab + 2 * cols, 2 * mid), BF16),
            ((2, 8, mid), F32),
            (hid1.shape, BF16),
            ((pixels, mid), F32),
            ((2, 9 * 128, LANES), F32),
            ((2, 9 * 128, LANES), BF16),
            pltpu.SemaphoreType.DMA((4,)),
        ],
        raw_in=(19,),
        raw_out=(0, 1, 2),
        flops=2 * large,
        local="in",
        **sizes,
    )
    chips = count // 2
    large, less = (-(-rows_in // (chips * 16)) * 16 for rows_in in (9 * 128 + 2 * mid + inter, channels))
    keep, send, token = call(
        add_kernel,
        [((chips * large, LANES), F32), ((chips * large, LANES), BF16), TOKEN],
        [meta, keep2, swap(send2, 1), keep3, swap(send3, 1)],
    )
    small1, keep1, send1, gain1_grad, shift1_grad, bias_grad, squeeze_total = call(
        reduce_back_kernel,
        [
            ((pixels, mid), BF16),
            ((chips * less, LANES), F32),
            ((chips * less, LANES), BF16),
            ((1, mid), F32),
            ((1, mid), F32),
            ((1, 2 * mid), F32),
            ((mid, inter), F32),
        ],
        [meta, exchange(pay), stat1, gain1, dz1, pre1, x],
        [
            ((pixels, mid), F32),
            ((pixels, mid), F32),
            ((pixels, channels), BF16),
            pltpu.SemaphoreType.DMA((3,)),
        ],
        raw_in=(4, 5, 6),
        flops=small,
        after=(token,),
        local="in",
        **sizes,
    )
    first = len(stages()[-1])
    blocks = call(
        pack_kernel,
        [((chips // first, large + less, LANES), BF16)] * first,
        [meta, keep, swap(send, 2), keep1, swap(send1, 1)],
        [((chips * large, LANES), BF16), ((chips * less, LANES), BF16)],
        places=slots(),
    )
    input_grad, token = call(
        input_kernel,
        [((pixels, channels), BF16, "hbm"), TOKEN],
        [meta, small1, weight_reduce, grad_res],
        flops=small,
        **sizes,
    )
    shared = scatter_chips(meta, blocks, 2 * large + less, large, [token])
    parts, places = gather_chips(shared)
    expand_total, excite_total, split_total, reduce_total = call(
        total_kernel,
        [
            ((mid, channels), F32),
            ((inter, 2 * mid), F32),
            (weight_split.shape, F32),
            ((channels, mid), F32),
        ],
        [meta] + parts + [swap(part, 1) for part in parts],
        [((2, chips * large, LANES), BF16), ((chips * less, LANES), BF16)],
        local="in",
        places=places,
        large=large,
    )
    flat = lambda v: v.reshape(-1)
    return (
        out.reshape(inputs.shape),
        input_grad.reshape(inputs.shape),
        reduce_total,
        flat(gain1_grad),
        flat(shift1_grad),
        split_total,
        flat(gain2_grad),
        flat(shift2_grad),
        squeeze_total,
        flat(gain_sq_grad),
        flat(shift_sq_grad),
        excite_total,
        flat(bias_grad),
        expand_total,
        flat(gain3_grad),
        flat(shift3_grad),
    )


def solution(mesh):
    rows = P("batch", "narrow", None, None)
    return jax.shard_map(
        body,
        mesh=mesh,
        in_specs=(rows, P("batch")) + (P(),) * 14 + (rows,),
        out_specs=(rows, rows) + (P(),) * 14,
        check_vma=False,
    )
```

```python
import functools
from itertools import product

import jax
import jax.numpy as jnp
from jax import lax
from jax.experimental import pallas as pl
from jax.experimental.pallas import tpu as pltpu
from jax.sharding import PartitionSpec as P

EPSILON = 1e-05
HIGHEST = lax.Precision.HIGHEST
ALL = ("batch", "narrow")
F32 = jnp.float32
BF16 = jnp.bfloat16
COLS = 16
LANES = 128
TOKEN = ((8, LANES), F32, "hbm")


def device_count():
    return lax.axis_size("batch") * lax.axis_size("narrow")


def halo(top, bottom):
    count = lax.axis_size("narrow")
    low = lax.ppermute(bottom, "narrow", [(i, i + 1) for i in range(count - 1)])
    high = lax.ppermute(top, "narrow", [(i + 1, i) for i in range(count - 1)])
    return low, high


def exchange(block):
    return lax.all_to_all(block, ALL, 0, 0)


def swap(block, bit):
    count = lax.axis_size("narrow")
    return lax.ppermute(block, "narrow", [(i, i ^ bit) for i in range(count)])


def stages():
    bits = list(range(device_count().bit_length() - 2, 0, -1))
    pairs = [bits[k : k + 2] for k in range(0, len(bits), 2)]
    return [
        [sum(bit << pair[k] for k, bit in enumerate(pick)) for pick in product((0, 1), repeat=len(pair))]
        for pair in pairs
    ]


def partners(blocks, steps):
    count = device_count()
    return [
        lax.ppermute(block, ALL, [(i, i ^ step) for i in range(count)])
        for block, step in zip(blocks[1:], steps[1:])
    ]


def slots():
    order = [0]
    for steps in reversed(stages()):
        order = [place ^ (step >> 1) for place in order for step in steps]
    return order


def scatter_chips(meta, blocks, rows, large, extra, after):
    order = list(reversed(stages()))
    for k, steps in enumerate(order):
        last = k + 1 == len(order)
        count = 1 if last else len(order[k + 1])
        out_rows = rows + extra.shape[0] if last else rows
        outs = [((blocks[0].shape[0] // count, out_rows, LANES), BF16)] * count
        blocks = call(
            sum_kernel,
            outs,
            [meta, blocks[0], *partners(blocks, steps)] + ([extra] if last else []),
            after=() if k else after,
            large=0 if k else large,
            others=[step >> 1 & 1 for step in steps],
        )
    return blocks[0]


def gather_chips(share):
    block, places = share, [0]
    for steps in stages():
        blocks = [block] + partners([block] * len(steps), steps)
        lists = [[place ^ (step >> 1) for place in places] for step in steps]
        block, places = jnp.concatenate(blocks), sum(lists, [])
    return blocks, lists


def half_terms(center, inv, gain, shift):
    scale = 0.5 * inv * gain
    return scale, 0.5 * shift - scale * center


def silu_of_half(half):
    tanh = jnp.tanh(half)
    more = 1.0 + tanh
    silu = half * more
    return silu, more + silu * (1.0 - tanh)


def wide(mask, width):
    return jnp.concatenate([mask] * (width // LANES), axis=1) if width > LANES else mask


def inside(meta, image, start, count):
    pixel = lax.broadcasted_iota(jnp.int32, (count * COLS, LANES), 0)
    row = (pixel >> 4) + (meta[0] + start)
    col = pixel & (COLS - 1)
    side = 12 + 2 * meta[5 + image]
    return jnp.where((row < side) & (row >= 0) & (col < side), 1.0, 0.0).astype(F32)


def area_of(meta, image):
    side = (12 + 2 * meta[5 + image]).astype(F32)
    return side * side


def row_of(block, first, count):
    return jnp.concatenate([block[first + k : first + k + 1] for k in range(count)], axis=1)


def put_row(ref, first, vector):
    for k in range(vector.shape[1] // LANES):
        ref[0, first + k : first + k + 1, :] = vector[:, k * LANES : (k + 1) * LANES]


def put_sums(ref, rows, acc, center, inv):
    plain = total(acc[0])
    put_row(ref, 0, plain)
    put_row(ref, rows, (total(acc[1]) - center * plain) * inv)


def spread(ref):
    block = ref[0]

    def step(k, carry):
        ref[k] = block
        return carry

    lax.fori_loop(1, ref.shape[0], step, 0)


def fold(values):
    return jnp.sum(values.reshape(-1, 8, values.shape[-1]), 0)


def clear_from(ref, first):
    if ref.shape[0] > first:
        ref[first:, :] = jnp.zeros((ref.shape[0] - first, LANES), ref.dtype)


def own_of_tall(image, slab):
    return pl.ds(pl.multiple_of(image * (slab + 2 * COLS) + COLS, COLS), slab)


def total(block):
    return jnp.sum(block, 0, keepdims=True)


def stats(totals, squares, counted):
    center = totals / counted
    return center, lax.rsqrt(squares / counted - center * center + EPSILON)


def shifted(values):
    count, width = values.shape
    col = lax.broadcasted_iota(jnp.int32, (count, LANES), 0) & (COLS - 1)
    has_left = wide(jnp.where(col > 0, 1.0, 0.0).astype(F32), width)
    has_right = wide(jnp.where(col < COLS - 1, 1.0, 0.0).astype(F32), width)
    left = pltpu.roll(values, 1, 0) * has_left
    right = pltpu.roll(values, count - 1, 0) * has_right
    return left.astype(BF16), values.astype(BF16), right.astype(BF16)


def dot(a, b, dims=((1,), (0,)), precision=None):
    return lax.dot_general(a, b, (dims, ((), ())), precision=precision, preferred_element_type=F32)


def whole(shape):
    return pl.BlockSpec(shape, lambda step: (0,) * len(shape))


def call(
    kernel, outs, args, scratch=(), megabytes=24, flops=0, after=(), local="", raw_in=(), raw_out=(), **sizes
):
    moved = sum(a.size * a.dtype.itemsize for a in args) + sum(
        functools.reduce(lambda x, y: x * y, o[0]) * jnp.dtype(o[1]).itemsize for o in outs
    )
    count = len(args)
    vmem = pl.BlockSpec(memory_space=pltpu.VMEM)
    anywhere = pl.BlockSpec(memory_space=pl.ANY)
    in_hbm = lambda a: pltpu.with_memory_space_constraint(a, pltpu.HBM)
    args = [in_hbm(a) if k in raw_in else a for k, a in enumerate(args)]
    after = [in_hbm(a) if a.shape == TOKEN[0] else a for a in after]

    def run(*refs):
        kernel(*refs[:count], *refs[count + len(after) :], **sizes)

    def spec(place, shape, kept, raws):
        return anywhere if place in raws else vmem if kept else whole(shape)

    return pl.pallas_call(
        run,
        grid=() if local == "in out" else (1,),
        out_shape=[
            pltpu.HBM(o[0], o[1]) if len(o) > 2 else jax.ShapeDtypeStruct(o[0], o[1]) for o in outs
        ],
        in_specs=[pl.BlockSpec(memory_space=pltpu.SMEM)]
        + [spec(k, a.shape, "in" in local, raw_in) for k, a in enumerate(args) if k]
        + [anywhere] * len(after),
        out_specs=[spec(k, o[0], "out" in local, raw_out) for k, o in enumerate(outs)],
        scratch_shapes=[pltpu.VMEM(*entry) if isinstance(entry, tuple) else entry for entry in scratch],
        compiler_params=pltpu.CompilerParams(vmem_limit_bytes=megabytes << 20),
        cost_estimate=pl.CostEstimate(flops=flops, bytes_accessed=moved, transcendentals=0),
    )(*args, *after)


def reduce_kernel(meta, x, w, pre, top, bottom, pay, acc, *, blocks, rows):
    slab = rows * COLS
    acc[...] = jnp.zeros_like(acc)
    group = 4

    def step(g, carry):
        base = pl.multiple_of(g * group * slab, group * slab)
        out = dot(x[pl.ds(base, group * slab), :], w[...])
        for j in range(group):
            image = g * group + j
            mask = inside(meta, image, 0, rows)
            part = out[j * slab : (j + 1) * slab] * wide(mask, out.shape[1])
            pre[pl.ds(pl.multiple_of(image * slab, slab), slab), :] = part
            edge = pl.ds(pl.multiple_of(image * 2 * COLS, 2 * COLS), 2 * COLS)
            top[edge, :] = part[: 2 * COLS]
            bottom[edge, :] = part[slab - 2 * COLS :]
            acc[0] += fold(part)
            acc[1] += fold(part * part)
            acc[2, :, :LANES] += fold(mask)
        return carry

    lax.fori_loop(0, blocks // group, step, 0)
    put_row(pay, 0, total(acc[0]))
    put_row(pay, 2, total(acc[1]))
    put_row(pay, 4, total(acc[2, :, :LANES]))
    pay[0, 5:8, :] = jnp.zeros((3, LANES), F32)
    spread(pay)


def split_kernel(
    meta, got, pre, low, high, gain, shift, w, hid_out, out, pay, stat, acc, hid, sem, *, blocks, rows
):
    slab = rows * COLS
    sums = jnp.sum(got[...], 0)
    counted = row_of(jnp.concatenate([sums[4:5]] * 2, 0), 0, 2)
    center, inv = stats(row_of(sums, 0, 2), row_of(sums, 2, 2), counted)
    stat[...] = jnp.zeros_like(stat)
    stat[0:1] = center
    stat[1:2] = inv
    stat[2:3] = counted
    scale, offset = half_terms(center, inv, gain[...], shift[...])

    def prepare(i, carry):
        edge = pl.ds(pl.multiple_of(i * 2 * COLS, 2 * COLS), 2 * COLS)
        own = pl.ds(pl.multiple_of(i * slab, slab), slab)
        mask = inside(meta, i, -2, rows + 4)
        for k in range(2):
            lanes = slice(k * LANES, k * LANES + LANES)
            tall = jnp.concatenate([low[edge, lanes], pre[own, lanes], high[edge, lanes]], axis=0)
            silu, _ = silu_of_half(tall * scale[:, lanes] + offset[:, lanes])
            left, middle, right = shifted(silu * mask)
            hid[0, i, :, lanes] = left
            hid[1, i, :, lanes] = middle
            hid[2, i, :, lanes] = right
        return carry

    lax.fori_loop(0, blocks, prepare, 0)
    copy = pltpu.make_async_copy(hid, hid_out, sem)
    copy.start()
    acc[...] = jnp.zeros_like(acc)
    group = 4
    tall = slab + 2 * COLS

    def step(g, carry):
        for half in range(2):
            lanes = slice(half * 128, half * 128 + 128)
            outs = slice(half * 256, half * 256 + 256)
            lhs = jnp.concatenate(
                [
                    hid[dx, pl.ds(g * group, group), dy * COLS : dy * COLS + tall, lanes].reshape(
                        group * tall, 128
                    )
                    for dy in range(3)
                    for dx in range(3)
                ],
                axis=1,
            )
            value = dot(lhs, w[:, :, half].reshape(9 * 128, 256))
            for j in range(group):
                image = g * group + j
                mask = inside(meta, image, -1, rows + 2)
                part = value[j * tall : (j + 1) * tall] * wide(mask, 256)
                out[pl.ds(pl.multiple_of(image * tall, tall), tall), outs] = part
                part = part[COLS : COLS + slab]
                acc[0, :, outs] += fold(part)
                acc[1, :, outs] += fold(part * part)
        return carry

    lax.fori_loop(0, blocks // group, step, 0)
    put_row(pay, 0, total(acc[0]))
    put_row(pay, 4, total(acc[1]))
    spread(pay)
    copy.wait()


def pool_kernel(
    meta, got, stat, pre, gain, shift, w, hid, pooled, pay, stat2, *, blocks, rows
):
    slab = rows * COLS
    sums = jnp.sum(got[...], 0)
    counted = jnp.concatenate([stat[2:3]] * 2, axis=1)
    center, inv = stats(row_of(sums, 0, 4), row_of(sums, 4, 4), counted)
    stat2[...] = jnp.zeros_like(stat2)
    stat2[0:1] = center
    stat2[1:2] = inv
    stat2[2:3] = counted
    scale, offset = half_terms(center, inv, gain[...], shift[...])

    def step(i, carry):
        own = pl.ds(pl.multiple_of(i * slab, slab), slab)
        mask = inside(meta, i, 0, rows)
        summed = [None, None]
        for k in range(4):
            lanes = slice(k * LANES, k * LANES + LANES)
            silu, _ = silu_of_half(pre[own_of_tall(i, slab), lanes] * scale[:, lanes] + offset[:, lanes])
            value = (silu * mask).astype(BF16)
            hid[own, lanes] = value
            part = fold(value.astype(F32))
            summed[k % 2] = part if k < 2 else summed[k % 2] + part
        pooled[pl.ds(i, 1), :] = total(jnp.concatenate(summed, axis=1)) / area_of(meta, i)
        return carry

    lax.fori_loop(0, blocks, step, 0)
    pay[0] = dot(pooled[...], w[...], precision=HIGHEST)
    spread(pay)


def squeeze_stats(block):
    return stats(total(block), total(block * block), float(block.shape[0]))


def expand_kernel(
    meta, got, hid, gain, shift, we, bias, w, mix, pre, att, hsq, znorm, zall, pay, stat_sq, acc, *, blocks, rows, parts
):
    slab = rows * COLS
    bands = got.shape[0] // parts
    for b in range(bands):
        block = got[b * parts]
        for k in range(1, parts):
            block = block + got[b * parts + k]
        znorm[b * blocks : (b + 1) * blocks, :] = block
    center, inv = squeeze_stats(znorm[...])
    stat_sq[...] = jnp.zeros_like(stat_sq)
    stat_sq[0:1] = center
    stat_sq[1:2] = inv
    normed = (znorm[...] - center) * inv
    znorm[...] = normed
    zall[...] = normed * gain[...] + shift[...]
    own_z = zall[pl.ds(pl.multiple_of(meta[1] * blocks, blocks), blocks), :]
    hidden = own_z * jax.nn.sigmoid(own_z)
    hsq[...] = hidden
    logits = dot(hidden, we[...], precision=HIGHEST) + bias[...]
    first = logits[:, :256]
    second = logits[:, 256:]
    ceiling = jnp.maximum(first, second)
    exp_first = jnp.exp(first - ceiling)
    exp_second = jnp.exp(second - ceiling)
    att[:, :256] = exp_first / (exp_first + exp_second)
    att[:, 256:] = exp_second / (exp_first + exp_second)
    acc[...] = jnp.zeros_like(acc)
    group = 4

    def step(g, carry):
        for j in range(group):
            image = g * group + j
            own = pl.ds(pl.multiple_of(image * slab, slab), slab)
            weights = att[pl.ds(image, 1), :]
            mix[own, :] = (
                weights[:, :256] * hid[own, :256].astype(F32)
                + weights[:, 256:] * hid[own, 256:].astype(F32)
            ).astype(BF16)
        many = pl.ds(pl.multiple_of(g * group * slab, group * slab), group * slab)
        for k in range(4):
            lanes = slice(k * 256, k * 256 + 256)
            value = dot(mix[many, :], w[:, lanes]).astype(BF16)
            pre[many, lanes] = value
            value = value.astype(F32)
            acc[0, :, lanes] += fold(value)
            acc[1, :, lanes] += fold(value * value)
        return carry

    lax.fori_loop(0, blocks // group, step, 0)
    put_row(pay, 0, total(acc[0]))
    put_row(pay, 8, total(acc[1]))
    spread(pay)


def residual_kernel(
    meta, got, stat, x, pre, cot, gain, shift, out, grad, pay, stat3, acc, *, blocks, rows
):
    slab = rows * COLS
    sums = jnp.sum(got[...], 0)
    counted = jnp.concatenate([stat[2:3]] * 4, axis=1)
    center, inv = stats(row_of(sums, 0, 8), row_of(sums, 8, 8), counted)
    stat3[...] = jnp.zeros_like(stat3)
    stat3[0:1] = center
    stat3[1:2] = inv
    stat3[2:3] = counted
    acc[...] = jnp.zeros_like(acc)
    scale, offset = half_terms(center, inv, gain[...], shift[...])

    def step(i, carry):
        own = pl.ds(pl.multiple_of(i * slab, slab), slab)
        mask = inside(meta, i, 0, rows)
        half_mask = 0.5 * mask
        for k in range(8):
            lanes = slice(k * LANES, k * LANES + LANES)
            values = pre[own, lanes].astype(F32)
            half = values * scale[:, lanes] + offset[:, lanes] + 0.5 * x[own, lanes].astype(F32)
            silu, slope = silu_of_half(half)
            out[own, lanes] = (silu * mask).astype(BF16)
            back = cot[own, lanes].astype(F32) * half_mask * slope
            grad[own, lanes] = back
            acc[0, :, lanes] += fold(back)
            acc[1, :, lanes] += fold(back * values)
        return carry

    lax.fori_loop(0, blocks, step, 0)
    put_sums(pay, 8, acc, center, inv)
    spread(pay)


def back_terms(stat, gain, shift_sum, gain_sum):
    center, inv, counted = stat[0:1], stat[1:2], stat[2:3]
    a = gain * inv
    d = -a * inv * (gain_sum / counted)
    b = -a * (shift_sum / counted) - d * center
    return a, b, d


def mixture_kernel(
    meta, got, stat3, pre, grad, gain, w, hid, att, we, gexp, gmix, top, bottom, glog, keep, send, gain_out, shift_out, hidden, *, blocks, rows
):
    slab = rows * COLS
    sums = jnp.sum(got[...], 0)
    shift_sum, gain_sum = row_of(sums, 0, 8), row_of(sums, 8, 8)
    shift_out[...] = shift_sum
    gain_out[...] = gain_sum
    a, b, d = back_terms(stat3, gain[...], shift_sum, gain_sum)
    group = 4

    def step(g, carry):
        many = pl.ds(pl.multiple_of(g * group * slab, group * slab), group * slab)
        for j in range(group):
            image = g * group + j
            own = pl.ds(pl.multiple_of(image * slab, slab), slab)
            mask = inside(meta, image, 0, rows)
            for k in range(8):
                lanes = slice(k * LANES, k * LANES + LANES)
                gexp[own, lanes] = (
                    mask
                    * (
                        a[:, lanes] * grad[own, lanes]
                        + b[:, lanes]
                        + d[:, lanes] * pre[own, lanes].astype(F32)
                    )
                ).astype(BF16)
        value = dot(gexp[many, :], w[...], ((1,), (1,))).astype(BF16)
        gmix[many, :] = value
        value = value.astype(F32)
        for j in range(group):
            image = g * group + j
            own = pl.ds(pl.multiple_of(image * slab, slab), slab)
            edge = pl.ds(pl.multiple_of(image * COLS, COLS), COLS)
            part = value[j * slab : (j + 1) * slab]
            top[edge, :] = part[:COLS].astype(BF16)
            bottom[edge, :] = part[slab - COLS :].astype(BF16)
            for half in range(2):
                lanes = slice(half * 256, half * 256 + 256)
                glog[pl.ds(image, 1), lanes] = total(fold(part * hid[own, lanes].astype(F32)))
        return carry

    lax.fori_loop(0, blocks // group, step, 0)
    first, second = att[:, :256], att[:, 256:]
    inner = first * glog[:, :256] + second * glog[:, 256:]
    glog[...] = jnp.concatenate(
        [first * (glog[:, :256] - inner), second * (glog[:, 256:] - inner)], axis=1
    )
    hidden[...] = dot(glog[...], we[...], ((1,), (1,)), HIGHEST)
    many = blocks // 2
    keep[...] = hidden[pl.ds(pl.multiple_of(meta[2] * many, many), many), :]
    send[...] = hidden[pl.ds(pl.multiple_of((1 - meta[2]) * many, many), many), :]


def logits_kernel(meta, keep, got, pay):
    pay[0] = keep[...] + got[...]
    spread(pay)


def expand_grad_kernel(meta, mix, gexp, hsq, glog, keep, send):
    for ref, core in ((send, 1 - meta[2]), (keep, meta[2])):
        lanes = pl.ds(pl.multiple_of(core * 512, 512), 512)
        value = dot(mix[...], gexp[:, lanes], ((0,), (0,))).astype(ref.dtype)
        lanes = pl.ds(pl.multiple_of(core * 256, 256), 256)
        excite = dot(hsq[...], glog[:, lanes], ((0,), (0,)), HIGHEST).astype(ref.dtype)
        for q in range(2):
            for k in range(2):
                first = k * 256 + q * 128
                ref[q, k * 256 : k * 256 + 256, :] = value[:, first : first + 128]
            ref[q, 512:, :] = excite[:, q * 128 : q * 128 + 128]


def add_kernel(meta, keep2, got2, keep3, got3, keep, send, token):
    first = keep2.shape[1]
    for ref, half in ((send, 1 - meta[3]), (keep, meta[3])):
        ref[:first, :] = (keep2[half] + got2[half].astype(F32)).astype(ref.dtype)
        last = first + keep3.shape[1]
        ref[first:last, :] = (keep3[half] + got3[half].astype(F32)).astype(ref.dtype)
        clear_from(ref, last)
    token[...] = jnp.zeros_like(token)


def pack_kernel(meta, keep, got, keep1, got1, *refs, places):
    *outs, flat, flat1 = refs
    held = outs[0].shape[0]
    large, small = flat.shape[0] // len(places), flat1.shape[0] // len(places)
    flat[...] = (keep[...] + got[...].astype(F32)).astype(BF16)
    flat1[...] = (keep1[...] + got1[...].astype(F32)).astype(BF16)
    for k, place in enumerate(places):
        chip = meta[4] ^ place
        out = outs[k // held]
        out[k % held, :large, :] = flat[pl.ds(pl.multiple_of(chip * large, large), large), :]
        out[k % held, large:, :] = flat1[pl.ds(pl.multiple_of(chip * small, small), small), :]


def sum_kernel(meta, *refs, large, others):
    ins, outs = refs[: len(others)], refs[len(others) :]
    if len(outs[0].shape) == 2:
        extra, *outs = outs
        outs[0][0, ins[0].shape[1] :, :] = extra[...].astype(BF16)
    held = outs[0].shape[0]

    def add(pick, first, last):
        value = None
        for ref in pick:
            part = ref[:, first:last, :].astype(F32)
            value = part if value is None else value + part
        return value.astype(BF16)

    def put(value, at, rows):
        for k, out in enumerate(outs):
            out[:, pl.ds(at, rows), :] = value[k * held : k * held + held]

    total_rows = ins[0].shape[1]
    if not large:
        put(add(ins, 0, total_rows), 0, total_rows)
        return
    for other in range(2):
        pick = [ref for ref, side in zip(ins, others) if side == other]
        put(add(pick, 0, large), pl.multiple_of((meta[3] ^ other) * large, large), large)
    put(add(ins, large, total_rows), 2 * large, total_rows - large)


def hidden_kernel(
    meta, got, znorm, zall, hsq_gain, stat_sq, pooled, wsq, att, gmix, pre, stat2, gain, shift,
    dz, gpool, squeeze, pay, gain_out, shift_out, acc, full, *, blocks, rows, parts
):
    slab = rows * COLS
    bands = got.shape[0] // parts
    many = blocks // 2
    for b in range(bands):
        for core in range(2):
            block = got[b * parts + core]
            for k in range(core + 2, parts, 2):
                block = block + got[b * parts + k]
            at = b * blocks + core * many
            full[at : at + many, :] = block
    z = zall[...]
    part = jax.nn.sigmoid(z)
    grad_z = full[...] * (part * (1.0 + z * (1.0 - part)))
    full[...] = grad_z
    images = float(bands * blocks)
    shift_sum = total(grad_z)
    gain_sum = total(grad_z * znorm[...])
    shift_out[...] = shift_sum
    gain_out[...] = gain_sum
    mine = pl.ds(pl.multiple_of(meta[1] * blocks, blocks), blocks)
    grad_pre = (
        hsq_gain[...]
        * stat_sq[1:2]
        * (full[mine, :] - shift_sum / images - znorm[mine, :] * (gain_sum / images))
    )
    squeeze[...] = dot(pooled[...], grad_pre, ((0,), (0,)), HIGHEST)
    gpool[...] = dot(grad_pre, wsq[...], ((1,), (1,)), HIGHEST)
    for i in range(blocks):
        gpool[i : i + 1, :] = gpool[i : i + 1, :] / area_of(meta, i)
    center, inv = stat2[0:1], stat2[1:2]
    acc[...] = jnp.zeros_like(acc)
    scale, offset = half_terms(center, inv, gain[...], shift[...])

    def step(i, carry):
        own = pl.ds(pl.multiple_of(i * slab, slab), slab)
        half_mask = 0.5 * inside(meta, i, 0, rows)
        weights = att[pl.ds(i, 1), :]
        pool = gpool[pl.ds(i, 1), :]
        for k in range(4):
            lanes = slice(k * LANES, k * LANES + LANES)
            mid = slice(k % 2 * LANES, k % 2 * LANES + LANES)
            mixed = gmix[own, mid].astype(F32)
            values = pre[own_of_tall(i, slab), lanes]
            _, slope = silu_of_half(values * scale[:, lanes] + offset[:, lanes])
            hidden = (mixed * weights[:, lanes] + pool[:, mid]).astype(BF16).astype(F32)
            back = hidden * half_mask * slope
            dz[own, lanes] = back
            acc[0, :, lanes] += fold(back)
            acc[1, :, lanes] += fold(back * values)
        return carry

    lax.fori_loop(0, blocks, step, 0)
    put_sums(pay, 4, acc, center, inv)
    spread(pay)


def conv_kernel(
    meta, got, stat2, gain2, shift2, dz, pre2, lowm, highm, att, gpool, w, pre, stat,
    gain, shift, glog, squeeze, hid_in, out_hbm, keep_hbm, send_hbm, pay, gain_out, shift_out, tall, acc,
    hid, out, keep, send, sems, *, blocks, rows
):
    slab = rows * COLS
    fetch = pltpu.make_async_copy(hid_in, hid, sems.at[0])
    fetch.start()
    sums = jnp.sum(got[...], 0)
    shift_sum, gain_sum = row_of(sums, 0, 4), row_of(sums, 4, 4)
    shift_out[...] = shift_sum
    gain_out[...] = gain_sum
    a, b, d = back_terms(stat2, gain2[...], shift_sum, gain_sum)
    scale2, offset2 = half_terms(stat2[0:1], stat2[1:2], gain2[...], shift2[...])

    def prepare(i, carry):
        own = pl.ds(pl.multiple_of(i * slab, slab), slab)
        edge = pl.ds(pl.multiple_of(i * COLS, COLS), COLS)
        whole_image = pl.ds(pl.multiple_of(i * (slab + 2 * COLS), COLS), slab + 2 * COLS)
        mask = inside(meta, i, -1, rows + 2)
        weights = att[pl.ds(i, 1), :]
        pool = gpool[pl.ds(i, 1), :]
        for k in range(4):
            lanes = slice(k * LANES, k * LANES + LANES)
            mid = slice(k % 2 * LANES, k % 2 * LANES + LANES)

            def edge_grad(values, mixed, keep):
                _, slope = silu_of_half(values * scale2[:, lanes] + offset2[:, lanes])
                hidden = mixed[edge, mid].astype(F32) * weights[:, lanes] + pool[:, mid]
                return hidden.astype(BF16).astype(F32) * (0.5 * keep) * slope

            keep_low, keep_high = mask[:COLS], mask[slab + COLS :]
            values = pre2[whole_image, lanes]
            grads = jnp.concatenate(
                [
                    edge_grad(values[:COLS], lowm, keep_low),
                    dz[own, lanes],
                    edge_grad(values[slab + COLS :], highm, keep_high),
                ],
                axis=0,
            )
            back = mask * (a[:, lanes] * grads + b[:, lanes] + d[:, lanes] * values)
            left, middle, right = shifted(back)
            tall[0, i, :, lanes] = left
            tall[1, i, :, lanes] = middle
            tall[2, i, :, lanes] = right
        return carry

    lax.fori_loop(0, blocks, prepare, 0)
    fetch.wait()

    def weights(dy, carry):
        rows_at = pl.ds(pl.multiple_of((dy + 1) * COLS, COLS), slab)
        for ref, core in ((send, 1 - meta[2]), (keep, meta[2])):
            lanes = pl.ds(pl.multiple_of(core * 128, 128), 128)
            wide_lanes = pl.ds(pl.multiple_of(core * 256, 256), 256)
            grads = tall[1, :, COLS : COLS + slab, wide_lanes].reshape(blocks * slab, 256)
            lhs = jnp.concatenate(
                [hid[dx, :, rows_at, lanes].reshape(blocks * slab, 128) for dx in range(3)], axis=1
            )
            value = dot(lhs, grads, ((0,), (0,))).astype(ref.dtype)
            at = pl.ds(pl.multiple_of(dy * 384, 384), 384)
            for q in range(2):
                ref[q, at, :] = value[:, q * 128 : q * 128 + 128]
        return carry

    lax.fori_loop(0, 3, weights, 0)
    stores = [
        pltpu.make_async_copy(send, send_hbm, sems.at[1]),
        pltpu.make_async_copy(keep, keep_hbm, sems.at[2]),
    ]
    for store in stores:
        store.start()
    acc[...] = jnp.zeros_like(acc)
    center, inv = stat[0:1], stat[1:2]
    scale, offset = half_terms(center, inv, gain[...], shift[...])
    group = 4

    def step(g, carry):
        for half in range(2):
            lanes = slice(half * 256, half * 256 + 256)
            outs = slice(half * 128, half * 128 + 128)
            value = None
            for dy in range(3):
                for dx in range(3):
                    lhs = tall[
                        2 - dx, pl.ds(g * group, group), (2 - dy) * COLS : (2 - dy) * COLS + slab, lanes
                    ].reshape(group * slab, 256)
                    part = dot(lhs, w[dy, dx, half], ((1,), (1,)))
                    value = part if value is None else value + part
            for j in range(group):
                image = g * group + j
                own = pl.ds(pl.multiple_of(image * slab, slab), slab)
                values = pre[own, outs]
                _, slope = silu_of_half(values * scale[:, outs] + offset[:, outs])
                back = value[j * slab : (j + 1) * slab] * (0.5 * inside(meta, image, 0, rows)) * slope
                out[own, outs] = back
                acc[0, :, outs] += fold(back)
                acc[1, :, outs] += fold(back * values)
        return carry

    lax.fori_loop(0, blocks // group, step, 0)
    stores.append(pltpu.make_async_copy(out, out_hbm, sems.at[3]))
    stores[-1].start()
    put_sums(pay, 2, acc, center, inv)
    put_row(pay, 4, total(glog[...]))
    pay[0, 8:, :] = jnp.zeros((pay.shape[1] - 8, LANES), F32)
    spread(pay)
    share = pay.shape[1] - 8
    for n in range(pay.shape[0]):
        pay[n, 8:, :] = squeeze[n * share : (n + 1) * share, :]
    for store in stores:
        store.wait()


def reduce_back_kernel(
    meta, got, stat, gain, dz_in, pre_in, x_in, small, keep, send, gain_out, shift_out, bias_out, squeeze,
    dz, pre, x, sems, *, blocks, rows
):
    slab = rows * COLS
    fetches = [
        pltpu.make_async_copy(source, target, sems.at[k])
        for k, (source, target) in enumerate(((dz_in, dz), (pre_in, pre), (x_in, x)))
    ]
    for fetch in fetches:
        fetch.start()
    sums = jnp.sum(got[...], 0)
    share = got.shape[1] - 8
    squeeze[...] = jnp.zeros_like(squeeze)
    squeeze[:share, :] = sums[8:]
    shift_sum, gain_sum = row_of(sums, 0, 2), row_of(sums, 2, 2)
    shift_out[...] = shift_sum
    gain_out[...] = gain_sum
    bias_out[...] = row_of(sums, 4, 4)
    a, b, d = back_terms(stat, gain[...], shift_sum, gain_sum)
    fetches[0].wait()
    fetches[1].wait()

    def step(image, carry):
        own = pl.ds(pl.multiple_of(image * slab, slab), slab)
        mask = wide(inside(meta, image, 0, rows), 256)
        small[own, :] = (mask * (a * dz[own, :] + b + d * pre[own, :])).astype(BF16)
        return carry

    lax.fori_loop(0, blocks, step, 0)
    fetches[2].wait()
    for ref, core in ((send, 1 - meta[2]), (keep, meta[2])):
        lanes = pl.ds(pl.multiple_of(core * 512, 512), 512)
        value = dot(x[:, lanes], small[...], ((0,), (0,))).astype(ref.dtype)
        for q in range(2):
            ref[q * 512 : q * 512 + 512, :] = value[:, q * 128 : q * 128 + 128]
        clear_from(ref, 1024)


def input_kernel(meta, small, w, grad, out, token, *, blocks, rows):
    slab = rows * COLS
    token[...] = jnp.zeros_like(token)
    group = 4

    def step(g, carry):
        many = pl.ds(pl.multiple_of(g * group * slab, group * slab), group * slab)
        for k in range(4):
            lanes = slice(k * 256, k * 256 + 256)
            value = dot(small[many, :], w[lanes, :], ((1,), (1,)))
            for j in range(group):
                image = g * group + j
                own = pl.ds(pl.multiple_of(image * slab, slab), slab)
                mask = wide(inside(meta, image, 0, rows), 256)
                out[own, lanes] = (
                    (value[j * slab : (j + 1) * slab] + grad[own, lanes]) * mask
                ).astype(BF16)
        return carry

    lax.fori_loop(0, blocks // group, step, 0)


def total_kernel(meta, *refs, places, large, less):
    arrays = len(places)
    expand, excite, split, reduce, squeeze, wide_part, narrow_part = refs[2 * arrays :]
    chips_in_all = wide_part.shape[1] // large
    share = squeeze.shape[0] // (2 * chips_in_all)
    behind = 2 * large + less
    for parts, core in ((refs[:arrays], meta[2]), (refs[arrays : 2 * arrays], 1 - meta[2])):
        for part, chips in zip(parts, places):
            for k, chip in enumerate(chips):
                at = meta[4] ^ chip
                for q in range(2):
                    wide_part[q, pl.ds(pl.multiple_of(at * large, large), large), :] = part[
                        k, q * large : q * large + large, :
                    ]
                narrow_part[pl.ds(pl.multiple_of(at * less, less), less), :] = part[k, 2 * large : behind, :]
                device = pl.multiple_of((2 * at + core) * share, share)
                squeeze[pl.ds(device, share), :] = part[k, behind:, :].astype(F32)[:share]
        for q in range(2):
            lanes = slice(q * 128, q * 128 + 128)
            for tap in range(9):
                split[tap // 3, tap % 3, core, :, lanes] = wide_part[q, tap * 128 : tap * 128 + 128].astype(F32)
            for k in range(2):
                first = 1152 + k * 256
                out = pl.ds(pl.multiple_of(core * 512 + (k * 256 + q * 128), 128), 128)
                expand[:, out] = wide_part[q, first : first + 256].astype(F32)
            out = pl.ds(pl.multiple_of(core * 256 + q * 128, 128), 128)
            excite[:, out] = wide_part[q, 1664:1792].astype(F32)
        own_rows = pl.ds(pl.multiple_of(core * 512, 512), 512)
        for q in range(2):
            reduce[own_rows, q * 128 : q * 128 + 128] = narrow_part[q * 512 : q * 512 + 512].astype(F32)


def body(
    inputs,
    image_class,
    weight_reduce,
    gain_reduce,
    shift_reduce,
    weight_split,
    gain_split,
    shift_split,
    weight_squeeze,
    gain_squeeze,
    shift_squeeze,
    weight_excite,
    bias_excite,
    weight_expand,
    gain_expand,
    shift_expand,
    cotangent,
):
    blocks, rows, cols, channels = inputs.shape
    mid = weight_reduce.shape[1]
    inter = weight_squeeze.shape[1]
    count = device_count()
    pixels = blocks * rows * cols
    slab = rows * cols
    edge = blocks * cols
    share = mid // count
    images = blocks * lax.axis_size("batch")
    meta = jnp.concatenate(
        [
            (lax.axis_index("narrow") * rows).astype(jnp.int32)[None],
            lax.axis_index("batch").astype(jnp.int32)[None],
            (lax.axis_index("narrow") % 2).astype(jnp.int32)[None],
            (lax.axis_index("narrow") // 2 % 2).astype(jnp.int32)[None],
            (lax.axis_index(ALL) // 2).astype(jnp.int32)[None],
            image_class,
        ]
    )
    x = inputs.reshape(pixels, channels)
    cot = cotangent.reshape(pixels, channels)
    row = lambda v: v.reshape(1, -1)
    gain1, shift1 = row(gain_reduce), row(shift_reduce)
    gain2, shift2 = row(gain_split), row(shift_split)
    gain3, shift3 = row(gain_expand), row(shift_expand)
    gain_sq, shift_sq = row(gain_squeeze), row(shift_squeeze)
    sizes = dict(blocks=blocks, rows=rows)
    small = 2 * pixels * channels * mid
    large = 2 * pixels * 9 * 128 * 512

    pre1, top, bottom, pay = call(
        reduce_kernel,
        [((pixels, mid), F32), ((2 * edge, mid), F32), ((2 * edge, mid), F32), ((count, 8, LANES), F32)],
        [meta, x, weight_reduce],
        [((3, 8, mid), F32)],
        flops=small,
        local="in out",
        **sizes,
    )
    low, high = halo(top, bottom)
    hid1, pre2, pay, stat1 = call(
        split_kernel,
        [
            ((3, blocks, slab + 4 * cols, mid), BF16, "hbm"),
            ((pixels + 2 * edge, 2 * mid), F32),
            ((count, 8, LANES), F32),
            ((8, mid), F32),
        ],
        [meta, exchange(pay), pre1, low, high, gain1, shift1, weight_split],
        [((2, 8, 2 * mid), F32), ((3, blocks, slab + 4 * cols, mid), BF16), pltpu.SemaphoreType.DMA],
        raw_out=(0,),
        flops=large,
        local="in out",
        **sizes,
    )
    hid2, pooled, pay, stat2 = call(
        pool_kernel,
        [
            ((pixels, 2 * mid), BF16),
            ((blocks, mid), F32),
            ((count, blocks, inter), F32),
            ((8, 2 * mid), F32),
        ],
        [meta, exchange(pay), stat1, pre2, gain2, shift2, weight_squeeze],
        local="in out",
        **sizes,
    )
    mix, pre3, att, hsq, znorm, zall, pay, stat_sq = call(
        expand_kernel,
        [
            ((pixels, mid), BF16),
            ((pixels, channels), BF16),
            ((blocks, 2 * mid), F32),
            ((blocks, inter), F32),
            ((images, inter), F32),
            ((images, inter), F32),
            ((count, 16, LANES), F32),
            ((8, inter), F32),
        ],
        [
            meta,
            exchange(pay),
            hid2,
            gain_sq,
            shift_sq,
            weight_excite,
            row(bias_excite),
            weight_expand,
        ],
        [((2, 8, channels), F32)],
        flops=small,
        parts=lax.axis_size("narrow"),
        local="in out",
        **sizes,
    )
    out, grad_res, pay, stat3 = call(
        residual_kernel,
        [
            ((pixels, channels), BF16),
            ((pixels, channels), F32),
            ((count, 16, LANES), F32),
            ((8, channels), F32),
        ],
        [meta, exchange(pay), stat1, x, pre3, cot, gain3, shift3],
        [((2, 8, channels), F32)],
        local="in out",
        **sizes,
    )
    gexp, gmix, top, bottom, glog, keep6, send6, gain3_grad, shift3_grad = call(
        mixture_kernel,
        [
            ((pixels, channels), BF16),
            ((pixels, mid), BF16),
            ((edge, mid), BF16),
            ((edge, mid), BF16),
            ((blocks, 2 * mid), F32),
            ((blocks // 2, inter), F32),
            ((blocks // 2, inter), F32),
            ((1, channels), F32),
            ((1, channels), F32),
        ],
        [meta, exchange(pay), stat3, pre3, grad_res, gain3, weight_expand, hid2, att, weight_excite],
        [((blocks, inter), F32)],
        flops=small,
        local="in out",
        **sizes,
    )
    lowm, highm = halo(top, bottom)
    keep3, send3 = call(
        expand_grad_kernel,
        [((2, 2 * mid + inter, LANES), F32), ((2, 2 * mid + inter, LANES), BF16)],
        [meta, mix, gexp, hsq, glog],
        flops=small,
        local="in out",
    )
    (pay,) = call(
        logits_kernel,
        [((count, blocks // 2, inter), F32)],
        [meta, keep6, swap(send6, 1)],
        after=(lowm, highm, send3),
        local="in out",
    )
    dz2, gpool, squeeze_part, pay, gain_sq_grad, shift_sq_grad = call(
        hidden_kernel,
        [
            ((pixels, 2 * mid), F32),
            ((blocks, mid), F32),
            ((mid, inter), F32),
            ((count, 8, LANES), F32),
            ((1, inter), F32),
            ((1, inter), F32),
        ],
        [
            meta,
            exchange(pay),
            znorm,
            zall,
            gain_sq,
            stat_sq,
            pooled,
            weight_squeeze,
            att,
            gmix,
            pre2,
            stat2,
            gain2,
            shift2,
        ],
        [((2, 8, 2 * mid), F32), ((images, inter), F32)],
        parts=lax.axis_size("narrow"),
        local="in out",
        **sizes,
    )
    dz1, keep2, send2, pay, gain2_grad, shift2_grad = call(
        conv_kernel,
        [
            ((pixels, mid), F32, "hbm"),
            ((2, 9 * 128, LANES), F32, "hbm"),
            ((2, 9 * 128, LANES), BF16, "hbm"),
            ((count, 8 + share, LANES), F32, "hbm"),
            ((1, 2 * mid), F32),
            ((1, 2 * mid), F32),
        ],
        [
            meta,
            exchange(pay),
            stat2,
            gain2,
            shift2,
            dz2,
            pre2,
            lowm,
            highm,
            att,
            gpool,
            weight_split,
            pre1,
            stat1,
            gain1,
            shift1,
            glog,
            squeeze_part,
            hid1,
        ],
        [
            ((3, blocks, slab + 2 * cols, 2 * mid), BF16),
            ((2, 8, mid), F32),
            (hid1.shape, BF16),
            ((pixels, mid), F32),
            ((2, 9 * 128, LANES), F32),
            ((2, 9 * 128, LANES), BF16),
            pltpu.SemaphoreType.DMA((4,)),
        ],
        raw_in=(18,),
        raw_out=(0, 1, 2),
        flops=2 * large,
        local="in",
        **sizes,
    )
    chips = count // 2
    large, less = (-(-rows_in // (chips * 16)) * 16 for rows_in in (9 * 128 + 2 * mid + inter, channels))
    keep, send, token = call(
        add_kernel,
        [((chips * large, LANES), F32), ((chips * large, LANES), BF16), TOKEN],
        [meta, keep2, swap(send2, 1), keep3, swap(send3, 1)],
    )
    small1, keep1, send1, gain1_grad, shift1_grad, bias_grad, squeeze_share = call(
        reduce_back_kernel,
        [
            ((pixels, mid), BF16),
            ((chips * less, LANES), F32),
            ((chips * less, LANES), BF16),
            ((1, mid), F32),
            ((1, mid), F32),
            ((1, 2 * mid), F32),
            ((16, inter), F32),
        ],
        [meta, exchange(pay), stat1, gain1, dz1, pre1, x],
        [
            ((pixels, mid), F32),
            ((pixels, mid), F32),
            ((pixels, channels), BF16),
            pltpu.SemaphoreType.DMA((3,)),
        ],
        raw_in=(4, 5, 6),
        flops=small,
        after=(token,),
        local="in",
        **sizes,
    )
    first = len(stages()[-1])
    blocks = call(
        pack_kernel,
        [((chips // first, large + less, LANES), BF16)] * first,
        [meta, keep, swap(send, 2), keep1, swap(send1, 1)],
        [((chips * large, LANES), BF16), ((chips * less, LANES), BF16)],
        places=slots(),
    )
    input_grad, token = call(
        input_kernel,
        [((pixels, channels), BF16, "hbm"), TOKEN],
        [meta, small1, weight_reduce, grad_res],
        flops=small,
        **sizes,
    )
    shared = scatter_chips(meta, blocks, 2 * large + less, large, squeeze_share, [token])
    parts, places = gather_chips(shared)
    expand_total, excite_total, split_total, reduce_total, squeeze_total = call(
        total_kernel,
        [
            ((mid, channels), F32),
            ((inter, 2 * mid), F32),
            (weight_split.shape, F32),
            ((channels, mid), F32),
            ((mid, inter), F32),
        ],
        [meta] + parts + [swap(part, 1) for part in parts],
        [((2, chips * large, LANES), BF16), ((chips * less, LANES), BF16)],
        local="in",
        places=places,
        large=large,
        less=less,
    )
    flat = lambda v: v.reshape(-1)
    return (
        out.reshape(inputs.shape),
        input_grad.reshape(inputs.shape),
        reduce_total,
        flat(gain1_grad),
        flat(shift1_grad),
        split_total,
        flat(gain2_grad),
        flat(shift2_grad),
        squeeze_total,
        flat(gain_sq_grad),
        flat(shift_sq_grad),
        excite_total,
        flat(bias_grad),
        expand_total,
        flat(gain3_grad),
        flat(shift3_grad),
    )


def solution(mesh):
    rows = P("batch", "narrow", None, None)
    return jax.shard_map(
        body,
        mesh=mesh,
        in_specs=(rows, P("batch")) + (P(),) * 14 + (rows,),
        out_specs=(rows, rows) + (P(),) * 14,
        check_vma=False,
    )
```

```python
import functools
from itertools import product

import jax
import jax.numpy as jnp
from jax import lax
from jax.experimental import pallas as pl
from jax.experimental.pallas import tpu as pltpu
from jax.sharding import PartitionSpec as P

EPSILON = 1e-05
HIGHEST = lax.Precision.HIGHEST
ALL = ("batch", "narrow")
F32 = jnp.float32
BF16 = jnp.bfloat16
COLS = 16
LANES = 128
TOKEN = ((8, LANES), F32, "hbm")


def device_count():
    return lax.axis_size("batch") * lax.axis_size("narrow")


def halo(top, bottom):
    count = lax.axis_size("narrow")
    low = lax.ppermute(bottom, "narrow", [(i, i + 1) for i in range(count - 1)])
    high = lax.ppermute(top, "narrow", [(i + 1, i) for i in range(count - 1)])
    return low, high


def exchange(block):
    return lax.all_to_all(block, ALL, 0, 0)


def swap(block, bit):
    count = lax.axis_size("narrow")
    return lax.ppermute(block, "narrow", [(i, i ^ bit) for i in range(count)])


def stages():
    bits = list(range(device_count().bit_length() - 2, 0, -1))
    pairs = [bits[k : k + 2] for k in range(0, len(bits), 2)]
    return [
        [sum(bit << pair[k] for k, bit in enumerate(pick)) for pick in product((0, 1), repeat=len(pair))]
        for pair in pairs
    ]


def partners(blocks, steps):
    count = device_count()
    return [
        lax.ppermute(block, ALL, [(i, i ^ step) for i in range(count)])
        for block, step in zip(blocks[1:], steps[1:])
    ]


def slots():
    order = [0]
    for steps in reversed(stages()):
        order = [place ^ (step >> 1) for place in order for step in steps]
    return order


def scatter_chips(meta, blocks, rows, large, extra, after):
    order = list(reversed(stages()))
    for k, steps in enumerate(order):
        last = k + 1 == len(order)
        count = 1 if last else len(order[k + 1])
        out_rows = rows + extra.shape[0] if last else rows
        outs = [((blocks[0].shape[0] // count, out_rows, LANES), BF16)] * count
        blocks = call(
            sum_kernel,
            outs,
            [meta, blocks[0], *partners(blocks, steps)] + ([extra] if last else []),
            after=() if k else after,
            large=0 if k else large,
            others=[step >> 1 & 1 for step in steps],
        )
    return blocks[0]


def gather_chips(share):
    block, places = share, [0]
    for steps in stages():
        blocks = [block] + partners([block] * len(steps), steps)
        lists = [[place ^ (step >> 1) for place in places] for step in steps]
        block, places = jnp.concatenate(blocks), sum(lists, [])
    return blocks, lists


def half_terms(center, inv, gain, shift):
    scale = 0.5 * inv * gain
    return scale, 0.5 * shift - scale * center


def silu_of_half(half):
    tanh = jnp.tanh(half)
    more = 1.0 + tanh
    silu = half * more
    return silu, more + silu * (1.0 - tanh)


def wide(mask, width):
    return jnp.concatenate([mask] * (width // LANES), axis=1) if width > LANES else mask


def inside(meta, image, start, count):
    pixel = lax.broadcasted_iota(jnp.int32, (count * COLS, LANES), 0)
    row = (pixel >> 4) + (meta[0] + start)
    col = pixel & (COLS - 1)
    side = 12 + 2 * meta[5 + image]
    return jnp.where((row < side) & (row >= 0) & (col < side), 1.0, 0.0).astype(F32)


def area_of(meta, image):
    side = (12 + 2 * meta[5 + image]).astype(F32)
    return side * side


def row_of(block, first, count):
    return jnp.concatenate([block[first + k : first + k + 1] for k in range(count)], axis=1)


def put_row(ref, first, vector):
    for k in range(vector.shape[1] // LANES):
        ref[0, first + k : first + k + 1, :] = vector[:, k * LANES : (k + 1) * LANES]


def put_sums(ref, rows, acc, center, inv):
    plain = total(acc[0])
    put_row(ref, 0, plain)
    put_row(ref, rows, (total(acc[1]) - center * plain) * inv)


def spread(ref):
    block = ref[0]

    def step(k, carry):
        ref[k] = block
        return carry

    lax.fori_loop(1, ref.shape[0], step, 0)


def fold(values):
    return jnp.sum(values.reshape(-1, 8, values.shape[-1]), 0)


def clear_from(ref, first):
    if ref.shape[0] > first:
        ref[first:, :] = jnp.zeros((ref.shape[0] - first, LANES), ref.dtype)


def own_of_tall(image, slab):
    return pl.ds(pl.multiple_of(image * (slab + 2 * COLS) + COLS, COLS), slab)


def total(block):
    return jnp.sum(block, 0, keepdims=True)


def stats(totals, squares, counted):
    center = totals / counted
    return center, lax.rsqrt(squares / counted - center * center + EPSILON)


def shifted(values):
    count, width = values.shape
    col = lax.broadcasted_iota(jnp.int32, (count, LANES), 0) & (COLS - 1)
    has_left = wide(jnp.where(col > 0, 1.0, 0.0).astype(F32), width)
    has_right = wide(jnp.where(col < COLS - 1, 1.0, 0.0).astype(F32), width)
    left = pltpu.roll(values, 1, 0) * has_left
    right = pltpu.roll(values, count - 1, 0) * has_right
    return left.astype(BF16), values.astype(BF16), right.astype(BF16)


def dot(a, b, dims=((1,), (0,)), precision=None):
    return lax.dot_general(a, b, (dims, ((), ())), precision=precision, preferred_element_type=F32)


def whole(shape):
    return pl.BlockSpec(shape, lambda step: (0,) * len(shape))


def call(
    kernel, outs, args, scratch=(), megabytes=24, flops=0, after=(), local="", raw_in=(), raw_out=(), aliases=None, **sizes
):
    moved = sum(a.size * a.dtype.itemsize for a in args) + sum(
        functools.reduce(lambda x, y: x * y, o[0]) * jnp.dtype(o[1]).itemsize for o in outs
    )
    count = len(args)
    vmem = pl.BlockSpec(memory_space=pltpu.VMEM)
    anywhere = pl.BlockSpec(memory_space=pl.ANY)
    in_hbm = lambda a: pltpu.with_memory_space_constraint(a, pltpu.HBM)
    args = [in_hbm(a) if k in raw_in else a for k, a in enumerate(args)]
    after = [in_hbm(a) if a.shape == TOKEN[0] else a for a in after]

    def run(*refs):
        kernel(*refs[:count], *refs[count + len(after) :], **sizes)

    def spec(place, shape, kept, raws):
        return anywhere if place in raws else vmem if kept else whole(shape)

    return pl.pallas_call(
        run,
        grid=() if local == "in out" else (1,),
        out_shape=[
            pltpu.HBM(o[0], o[1]) if len(o) > 2 else jax.ShapeDtypeStruct(o[0], o[1]) for o in outs
        ],
        in_specs=[pl.BlockSpec(memory_space=pltpu.SMEM)]
        + [spec(k, a.shape, "in" in local, raw_in) for k, a in enumerate(args) if k]
        + [anywhere] * len(after),
        out_specs=[spec(k, o[0], "out" in local, raw_out) for k, o in enumerate(outs)],
        input_output_aliases=aliases or {},
        scratch_shapes=[pltpu.VMEM(*entry) if isinstance(entry, tuple) else entry for entry in scratch],
        compiler_params=pltpu.CompilerParams(vmem_limit_bytes=megabytes << 20),
        cost_estimate=pl.CostEstimate(flops=flops, bytes_accessed=moved, transcendentals=0),
    )(*args, *after)


def reduce_kernel(meta, x, w, pre, top, bottom, pay, acc, *, blocks, rows):
    slab = rows * COLS
    acc[...] = jnp.zeros_like(acc)
    group = 4

    def step(g, carry):
        base = pl.multiple_of(g * group * slab, group * slab)
        out = dot(x[pl.ds(base, group * slab), :], w[...])
        for j in range(group):
            image = g * group + j
            mask = inside(meta, image, 0, rows)
            part = out[j * slab : (j + 1) * slab] * wide(mask, out.shape[1])
            pre[pl.ds(pl.multiple_of(image * slab, slab), slab), :] = part
            edge = pl.ds(pl.multiple_of(image * 2 * COLS, 2 * COLS), 2 * COLS)
            top[edge, :] = part[: 2 * COLS]
            bottom[edge, :] = part[slab - 2 * COLS :]
            acc[0] += fold(part)
            acc[1] += fold(part * part)
            acc[2, :, :LANES] += fold(mask)
        return carry

    lax.fori_loop(0, blocks // group, step, 0, unroll=True)
    put_row(pay, 0, total(acc[0]))
    put_row(pay, 2, total(acc[1]))
    put_row(pay, 4, total(acc[2, :, :LANES]))
    pay[0, 5:8, :] = jnp.zeros((3, LANES), F32)
    spread(pay)


def split_kernel(
    meta, got, pre, low, high, gain, shift, w, hid_out, out, pay, stat, acc, hid, sem, *, blocks, rows
):
    slab = rows * COLS
    sums = jnp.sum(got[...], 0)
    counted = row_of(jnp.concatenate([sums[4:5]] * 2, 0), 0, 2)
    center, inv = stats(row_of(sums, 0, 2), row_of(sums, 2, 2), counted)
    stat[...] = jnp.zeros_like(stat)
    stat[0:1] = center
    stat[1:2] = inv
    stat[2:3] = counted
    scale, offset = half_terms(center, inv, gain[...], shift[...])

    def prepare(i, carry):
        edge = pl.ds(pl.multiple_of(i * 2 * COLS, 2 * COLS), 2 * COLS)
        own = pl.ds(pl.multiple_of(i * slab, slab), slab)
        mask = inside(meta, i, -2, rows + 4)
        for k in range(2):
            lanes = slice(k * LANES, k * LANES + LANES)
            tall = jnp.concatenate([low[edge, lanes], pre[own, lanes], high[edge, lanes]], axis=0)
            silu, _ = silu_of_half(tall * scale[:, lanes] + offset[:, lanes])
            left, middle, right = shifted(silu * mask)
            hid[0, i, :, lanes] = left
            hid[1, i, :, lanes] = middle
            hid[2, i, :, lanes] = right
        return carry

    lax.fori_loop(0, blocks, prepare, 0, unroll=4)
    copy = pltpu.make_async_copy(hid, hid_out, sem)
    copy.start()
    acc[...] = jnp.zeros_like(acc)
    group = 4
    tall = slab + 2 * COLS

    def step(g, carry):
        for half in range(2):
            lanes = slice(half * 128, half * 128 + 128)
            outs = slice(half * 256, half * 256 + 256)
            lhs = jnp.concatenate(
                [
                    hid[dx, pl.ds(g * group, group), dy * COLS : dy * COLS + tall, lanes].reshape(
                        group * tall, 128
                    )
                    for dy in range(3)
                    for dx in range(3)
                ],
                axis=1,
            )
            value = dot(lhs, w[:, :, half].reshape(9 * 128, 256))
            for j in range(group):
                image = g * group + j
                mask = inside(meta, image, -1, rows + 2)
                part = value[j * tall : (j + 1) * tall] * wide(mask, 256)
                out[pl.ds(pl.multiple_of(image * tall, tall), tall), outs] = part
                part = part[COLS : COLS + slab]
                acc[0, :, outs] += fold(part)
                acc[1, :, outs] += fold(part * part)
        return carry

    lax.fori_loop(0, blocks // group, step, 0, unroll=2)
    put_row(pay, 0, total(acc[0]))
    put_row(pay, 4, total(acc[1]))
    spread(pay)
    copy.wait()


def pool_kernel(
    meta, got, stat, pre, gain, shift, w, hid, pooled, pay, stat2, *, blocks, rows
):
    slab = rows * COLS
    sums = jnp.sum(got[...], 0)
    counted = jnp.concatenate([stat[2:3]] * 2, axis=1)
    center, inv = stats(row_of(sums, 0, 4), row_of(sums, 4, 4), counted)
    stat2[...] = jnp.zeros_like(stat2)
    stat2[0:1] = center
    stat2[1:2] = inv
    stat2[2:3] = counted
    scale, offset = half_terms(center, inv, gain[...], shift[...])

    def step(i, carry):
        own = pl.ds(pl.multiple_of(i * slab, slab), slab)
        mask = inside(meta, i, 0, rows)
        summed = [None, None]
        for k in range(4):
            lanes = slice(k * LANES, k * LANES + LANES)
            silu, _ = silu_of_half(pre[own_of_tall(i, slab), lanes] * scale[:, lanes] + offset[:, lanes])
            value = (silu * mask).astype(BF16)
            hid[own, lanes] = value
            part = fold(value.astype(F32))
            summed[k % 2] = part if k < 2 else summed[k % 2] + part
        pooled[pl.ds(i, 1), :] = total(jnp.concatenate(summed, axis=1)) / area_of(meta, i)
        return carry

    lax.fori_loop(0, blocks, step, 0, unroll=4)
    pay[0] = dot(pooled[...], w[...], precision=HIGHEST)
    spread(pay)


def squeeze_stats(block):
    return stats(total(block), total(block * block), float(block.shape[0]))


def expand_kernel(
    meta, got, hid, gain, shift, we, bias, w, mix, pre, att, hsq, znorm, zall, pay, stat_sq, acc, *, blocks, rows, parts
):
    slab = rows * COLS
    bands = got.shape[0] // parts
    for b in range(bands):
        block = got[b * parts]
        for k in range(1, parts):
            block = block + got[b * parts + k]
        znorm[b * blocks : (b + 1) * blocks, :] = block
    center, inv = squeeze_stats(znorm[...])
    stat_sq[...] = jnp.zeros_like(stat_sq)
    stat_sq[0:1] = center
    stat_sq[1:2] = inv
    normed = (znorm[...] - center) * inv
    znorm[...] = normed
    zall[...] = normed * gain[...] + shift[...]
    own_z = zall[pl.ds(pl.multiple_of(meta[1] * blocks, blocks), blocks), :]
    hidden = own_z * jax.nn.sigmoid(own_z)
    hsq[...] = hidden
    logits = dot(hidden, we[...], precision=HIGHEST) + bias[...]
    first = logits[:, :256]
    second = logits[:, 256:]
    ceiling = jnp.maximum(first, second)
    exp_first = jnp.exp(first - ceiling)
    exp_second = jnp.exp(second - ceiling)
    att[:, :256] = exp_first / (exp_first + exp_second)
    att[:, 256:] = exp_second / (exp_first + exp_second)
    acc[...] = jnp.zeros_like(acc)
    group = 4

    def step(g, carry):
        for j in range(group):
            image = g * group + j
            own = pl.ds(pl.multiple_of(image * slab, slab), slab)
            weights = att[pl.ds(image, 1), :]
            mix[own, :] = (
                weights[:, :256] * hid[own, :256].astype(F32)
                + weights[:, 256:] * hid[own, 256:].astype(F32)
            ).astype(BF16)
        many = pl.ds(pl.multiple_of(g * group * slab, group * slab), group * slab)
        for k in range(4):
            lanes = slice(k * 256, k * 256 + 256)
            value = dot(mix[many, :], w[:, lanes]).astype(BF16)
            pre[many, lanes] = value
            value = value.astype(F32)
            acc[0, :, lanes] += fold(value)
            acc[1, :, lanes] += fold(value * value)
        return carry

    lax.fori_loop(0, blocks // group, step, 0, unroll=True)
    put_row(pay, 0, total(acc[0]))
    put_row(pay, 8, total(acc[1]))
    spread(pay)


def residual_kernel(
    meta, got, stat, x, pre, cot, gain, shift, out, grad, pay, stat3, acc, *, blocks, rows
):
    slab = rows * COLS
    sums = jnp.sum(got[...], 0)
    counted = jnp.concatenate([stat[2:3]] * 4, axis=1)
    center, inv = stats(row_of(sums, 0, 8), row_of(sums, 8, 8), counted)
    stat3[...] = jnp.zeros_like(stat3)
    stat3[0:1] = center
    stat3[1:2] = inv
    stat3[2:3] = counted
    acc[...] = jnp.zeros_like(acc)
    scale, offset = half_terms(center, inv, gain[...], shift[...])

    def step(i, carry):
        own = pl.ds(pl.multiple_of(i * slab, slab), slab)
        mask = inside(meta, i, 0, rows)
        half_mask = 0.5 * mask
        for k in range(8):
            lanes = slice(k * LANES, k * LANES + LANES)
            values = pre[own, lanes].astype(F32)
            half = values * scale[:, lanes] + offset[:, lanes] + 0.5 * x[own, lanes].astype(F32)
            silu, slope = silu_of_half(half)
            out[own, lanes] = (silu * mask).astype(BF16)
            back = cot[own, lanes].astype(F32) * half_mask * slope
            grad[own, lanes] = back
            acc[0, :, lanes] += fold(back)
            acc[1, :, lanes] += fold(back * values)
        return carry

    lax.fori_loop(0, blocks, step, 0)
    put_sums(pay, 8, acc, center, inv)
    spread(pay)


def back_terms(stat, gain, shift_sum, gain_sum):
    center, inv, counted = stat[0:1], stat[1:2], stat[2:3]
    a = gain * inv
    d = -a * inv * (gain_sum / counted)
    b = -a * (shift_sum / counted) - d * center
    return a, b, d


def mixture_kernel(
    meta, got, stat3, pre, grad, gain, w, hid, att, we, gexp, gmix, top, bottom, glog, keep, send, gain_out, shift_out, hidden, *, blocks, rows
):
    slab = rows * COLS
    sums = jnp.sum(got[...], 0)
    shift_sum, gain_sum = row_of(sums, 0, 8), row_of(sums, 8, 8)
    shift_out[...] = shift_sum
    gain_out[...] = gain_sum
    a, b, d = back_terms(stat3, gain[...], shift_sum, gain_sum)
    group = 4

    def step(g, carry):
        many = pl.ds(pl.multiple_of(g * group * slab, group * slab), group * slab)
        for j in range(group):
            image = g * group + j
            own = pl.ds(pl.multiple_of(image * slab, slab), slab)
            mask = inside(meta, image, 0, rows)
            for k in range(8):
                lanes = slice(k * LANES, k * LANES + LANES)
                gexp[own, lanes] = (
                    mask
                    * (
                        a[:, lanes] * grad[own, lanes]
                        + b[:, lanes]
                        + d[:, lanes] * pre[own, lanes].astype(F32)
                    )
                ).astype(BF16)
        value = dot(gexp[many, :], w[...], ((1,), (1,))).astype(BF16)
        gmix[many, :] = value
        value = value.astype(F32)
        for j in range(group):
            image = g * group + j
            own = pl.ds(pl.multiple_of(image * slab, slab), slab)
            edge = pl.ds(pl.multiple_of(image * COLS, COLS), COLS)
            part = value[j * slab : (j + 1) * slab]
            top[edge, :] = part[:COLS].astype(BF16)
            bottom[edge, :] = part[slab - COLS :].astype(BF16)
            for half in range(2):
                lanes = slice(half * 256, half * 256 + 256)
                glog[pl.ds(image, 1), lanes] = total(fold(part * hid[own, lanes].astype(F32)))
        return carry

    lax.fori_loop(0, blocks // group, step, 0, unroll=2)
    first, second = att[:, :256], att[:, 256:]
    inner = first * glog[:, :256] + second * glog[:, 256:]
    glog[...] = jnp.concatenate(
        [first * (glog[:, :256] - inner), second * (glog[:, 256:] - inner)], axis=1
    )
    hidden[...] = dot(glog[...], we[...], ((1,), (1,)), HIGHEST)
    many = blocks // 2
    keep[...] = hidden[pl.ds(pl.multiple_of(meta[2] * many, many), many), :]
    send[...] = hidden[pl.ds(pl.multiple_of((1 - meta[2]) * many, many), many), :]


def logits_kernel(meta, keep, got, pay):
    pay[0] = keep[...] + got[...]
    spread(pay)


def expand_grad_kernel(meta, mix, gexp, hsq, glog, keep, send):
    for ref, core in ((send, 1 - meta[2]), (keep, meta[2])):
        lanes = pl.ds(pl.multiple_of(core * 512, 512), 512)
        value = dot(mix[...], gexp[:, lanes], ((0,), (0,))).astype(ref.dtype)
        lanes = pl.ds(pl.multiple_of(core * 256, 256), 256)
        excite = dot(hsq[...], glog[:, lanes], ((0,), (0,)), HIGHEST).astype(ref.dtype)
        for q in range(2):
            for k in range(2):
                first = k * 256 + q * 128
                ref[q, k * 256 : k * 256 + 256, :] = value[:, first : first + 128]
            ref[q, 512:, :] = excite[:, q * 128 : q * 128 + 128]


def add_kernel(meta, keep2, got2, keep3, got3, keep, send, token):
    first = keep2.shape[1]
    for ref, half in ((send, 1 - meta[3]), (keep, meta[3])):
        ref[:first, :] = (keep2[half] + got2[half].astype(F32)).astype(ref.dtype)
        last = first + keep3.shape[1]
        ref[first:last, :] = (keep3[half] + got3[half].astype(F32)).astype(ref.dtype)
        clear_from(ref, last)
    token[...] = jnp.zeros_like(token)


def pack_kernel(meta, keep, got, keep1, got1, *refs, places):
    *outs, flat, flat1 = refs
    held = outs[0].shape[0]
    large, small = flat.shape[0] // len(places), flat1.shape[0] // len(places)
    flat[...] = (keep[...] + got[...].astype(F32)).astype(BF16)
    flat1[...] = (keep1[...] + got1[...].astype(F32)).astype(BF16)
    for k, place in enumerate(places):
        chip = meta[4] ^ place
        out = outs[k // held]
        out[k % held, :large, :] = flat[pl.ds(pl.multiple_of(chip * large, large), large), :]
        out[k % held, large:, :] = flat1[pl.ds(pl.multiple_of(chip * small, small), small), :]


def sum_kernel(meta, *refs, large, others):
    ins, outs = refs[: len(others)], refs[len(others) :]
    if len(outs[0].shape) == 2:
        extra, *outs = outs
        outs[0][0, ins[0].shape[1] :, :] = extra[...].astype(BF16)
    held = outs[0].shape[0]

    def add(pick, first, last):
        value = None
        for ref in pick:
            part = ref[:, first:last, :].astype(F32)
            value = part if value is None else value + part
        return value.astype(BF16)

    def put(value, at, rows):
        for k, out in enumerate(outs):
            out[:, pl.ds(at, rows), :] = value[k * held : k * held + held]

    total_rows = ins[0].shape[1]
    if not large:
        put(add(ins, 0, total_rows), 0, total_rows)
        return
    for other in range(2):
        pick = [ref for ref, side in zip(ins, others) if side == other]
        put(add(pick, 0, large), pl.multiple_of((meta[3] ^ other) * large, large), large)
    put(add(ins, large, total_rows), 2 * large, total_rows - large)


def hidden_kernel(
    meta, got, znorm, zall, hsq_gain, stat_sq, pooled, wsq, att, gmix, pre, stat2, gain, shift,
    dz, gpool, squeeze, pay, gain_out, shift_out, acc, full, *, blocks, rows, parts
):
    slab = rows * COLS
    bands = got.shape[0] // parts
    many = blocks // 2
    for b in range(bands):
        for core in range(2):
            block = got[b * parts + core]
            for k in range(core + 2, parts, 2):
                block = block + got[b * parts + k]
            at = b * blocks + core * many
            full[at : at + many, :] = block
    z = zall[...]
    part = jax.nn.sigmoid(z)
    grad_z = full[...] * (part * (1.0 + z * (1.0 - part)))
    full[...] = grad_z
    images = float(bands * blocks)
    shift_sum = total(grad_z)
    gain_sum = total(grad_z * znorm[...])
    shift_out[...] = shift_sum
    gain_out[...] = gain_sum
    mine = pl.ds(pl.multiple_of(meta[1] * blocks, blocks), blocks)
    grad_pre = (
        hsq_gain[...]
        * stat_sq[1:2]
        * (full[mine, :] - shift_sum / images - znorm[mine, :] * (gain_sum / images))
    )
    squeeze[...] = dot(pooled[...], grad_pre, ((0,), (0,)), HIGHEST)
    gpool[...] = dot(grad_pre, wsq[...], ((1,), (1,)), HIGHEST)
    for i in range(blocks):
        gpool[i : i + 1, :] = gpool[i : i + 1, :] / area_of(meta, i)
    center, inv = stat2[0:1], stat2[1:2]
    acc[...] = jnp.zeros_like(acc)
    scale, offset = half_terms(center, inv, gain[...], shift[...])

    def step(i, carry):
        own = pl.ds(pl.multiple_of(i * slab, slab), slab)
        half_mask = 0.5 * inside(meta, i, 0, rows)
        weights = att[pl.ds(i, 1), :]
        pool = gpool[pl.ds(i, 1), :]
        for k in range(4):
            lanes = slice(k * LANES, k * LANES + LANES)
            mid = slice(k % 2 * LANES, k % 2 * LANES + LANES)
            mixed = gmix[own, mid].astype(F32)
            values = pre[own_of_tall(i, slab), lanes]
            _, slope = silu_of_half(values * scale[:, lanes] + offset[:, lanes])
            hidden = (mixed * weights[:, lanes] + pool[:, mid]).astype(BF16).astype(F32)
            back = hidden * half_mask * slope
            dz[own, lanes] = back
            acc[0, :, lanes] += fold(back)
            acc[1, :, lanes] += fold(back * values)
        return carry

    lax.fori_loop(0, blocks, step, 0, unroll=4)
    put_sums(pay, 4, acc, center, inv)
    spread(pay)


def conv_kernel(
    meta, got, stat2, gain2, shift2, dz, pre2, lowm, highm, att, gpool, w, pre, stat,
    gain, shift, glog, squeeze, hid, out_hbm, keep_hbm, send_hbm, pay_hbm, gain_out, shift_out, tall, acc,
    out, keep, send, pay, sems, *, blocks, rows
):
    slab = rows * COLS
    sums = jnp.sum(got[...], 0)
    shift_sum, gain_sum = row_of(sums, 0, 4), row_of(sums, 4, 4)
    shift_out[...] = shift_sum
    gain_out[...] = gain_sum
    a, b, d = back_terms(stat2, gain2[...], shift_sum, gain_sum)
    scale2, offset2 = half_terms(stat2[0:1], stat2[1:2], gain2[...], shift2[...])

    def prepare(i, carry):
        own = pl.ds(pl.multiple_of(i * slab, slab), slab)
        edge = pl.ds(pl.multiple_of(i * COLS, COLS), COLS)
        whole_image = pl.ds(pl.multiple_of(i * (slab + 2 * COLS), COLS), slab + 2 * COLS)
        mask = inside(meta, i, -1, rows + 2)
        weights = att[pl.ds(i, 1), :]
        pool = gpool[pl.ds(i, 1), :]
        for k in range(4):
            lanes = slice(k * LANES, k * LANES + LANES)
            mid = slice(k % 2 * LANES, k % 2 * LANES + LANES)

            def edge_grad(values, mixed, keep):
                _, slope = silu_of_half(values * scale2[:, lanes] + offset2[:, lanes])
                hidden = mixed[edge, mid].astype(F32) * weights[:, lanes] + pool[:, mid]
                return hidden.astype(BF16).astype(F32) * (0.5 * keep) * slope

            keep_low, keep_high = mask[:COLS], mask[slab + COLS :]
            values = pre2[whole_image, lanes]
            grads = jnp.concatenate(
                [
                    edge_grad(values[:COLS], lowm, keep_low),
                    dz[own, lanes],
                    edge_grad(values[slab + COLS :], highm, keep_high),
                ],
                axis=0,
            )
            back = mask * (a[:, lanes] * grads + b[:, lanes] + d[:, lanes] * values)
            left, middle, right = shifted(back)
            tall[0, i, :, lanes] = left
            tall[1, i, :, lanes] = middle
            tall[2, i, :, lanes] = right
        return carry

    lax.fori_loop(0, blocks, prepare, 0, unroll=4)

    def weights(dy, carry):
        rows_at = pl.ds(pl.multiple_of((dy + 1) * COLS, COLS), slab)
        for ref, core in ((send, 1 - meta[2]), (keep, meta[2])):
            lanes = pl.ds(pl.multiple_of(core * 128, 128), 128)
            wide_lanes = pl.ds(pl.multiple_of(core * 256, 256), 256)
            grads = tall[1, :, COLS : COLS + slab, wide_lanes].reshape(blocks * slab, 256)
            lhs = jnp.concatenate(
                [hid[dx, :, rows_at, lanes].reshape(blocks * slab, 128) for dx in range(3)], axis=1
            )
            value = dot(lhs, grads, ((0,), (0,))).astype(ref.dtype)
            at = pl.ds(pl.multiple_of(dy * 384, 384), 384)
            for q in range(2):
                ref[q, at, :] = value[:, q * 128 : q * 128 + 128]
        return carry

    lax.fori_loop(0, 3, weights, 0)
    stores = [
        pltpu.make_async_copy(send, send_hbm, sems.at[1]),
        pltpu.make_async_copy(keep, keep_hbm, sems.at[2]),
    ]
    for store in stores:
        store.start()
    acc[...] = jnp.zeros_like(acc)
    center, inv = stat[0:1], stat[1:2]
    scale, offset = half_terms(center, inv, gain[...], shift[...])
    group = 4

    def store_group(g):
        many = pl.ds(pl.multiple_of(g * group * slab, group * slab), group * slab)
        return pltpu.make_async_copy(out.at[many], out_hbm.at[many], sems.at[3 + g])

    def step(g, carry):
        for half in range(2):
            lanes = slice(half * 256, half * 256 + 256)
            outs = slice(half * 128, half * 128 + 128)
            taps = [(dy, dx) for dy in range(3) for dx in range(3)]
            lhs = jnp.concatenate(
                [
                    tall[
                        2 - dx, pl.ds(g * group, group), (2 - dy) * COLS : (2 - dy) * COLS + slab, lanes
                    ].reshape(group * slab, 256)
                    for dy, dx in taps
                ],
                axis=1,
            )
            rhs = jnp.concatenate([w[dy, dx, half] for dy, dx in taps], axis=1)
            value = dot(lhs, rhs, ((1,), (1,)))
            for j in range(group):
                image = g * group + j
                own = pl.ds(pl.multiple_of(image * slab, slab), slab)
                values = pre[own, outs]
                _, slope = silu_of_half(values * scale[:, outs] + offset[:, outs])
                back = value[j * slab : (j + 1) * slab] * (0.5 * inside(meta, image, 0, rows)) * slope
                out[own, outs] = back
                acc[0, :, outs] += fold(back)
                acc[1, :, outs] += fold(back * values)
        store_group(g).start()
        return carry

    lax.fori_loop(0, blocks // group, step, 0, unroll=2)
    put_sums(pay, 2, acc, center, inv)
    put_row(pay, 4, total(glog[...]))
    pay[0, 8:, :] = jnp.zeros((pay.shape[1] - 8, LANES), F32)
    spread(pay)
    share = pay.shape[1] - 8
    for n in range(pay.shape[0]):
        pay[n, 8:, :] = squeeze[n * share : (n + 1) * share, :]
    stores.append(pltpu.make_async_copy(pay, pay_hbm, sems.at[0]))
    stores[-1].start()
    stores += [store_group(g) for g in range(blocks // group)]
    for store in stores:
        store.wait()


def reduce_back_kernel(
    meta, got, stat, gain, dz_in, pre_in, x_in, small, keep, send, gain_out, shift_out, bias_out, squeeze,
    dz, pre, x, sems, *, blocks, rows
):
    slab = rows * COLS
    fetches = [
        pltpu.make_async_copy(source, target, sems.at[k])
        for k, (source, target) in enumerate(((dz_in, dz), (pre_in, pre), (x_in, x)))
    ]
    for fetch in fetches:
        fetch.start()
    sums = jnp.sum(got[...], 0)
    share = got.shape[1] - 8
    squeeze[...] = jnp.zeros_like(squeeze)
    squeeze[:share, :] = sums[8:]
    shift_sum, gain_sum = row_of(sums, 0, 2), row_of(sums, 2, 2)
    shift_out[...] = shift_sum
    gain_out[...] = gain_sum
    bias_out[...] = row_of(sums, 4, 4)
    a, b, d = back_terms(stat, gain[...], shift_sum, gain_sum)
    fetches[0].wait()
    fetches[1].wait()

    def step(image, carry):
        own = pl.ds(pl.multiple_of(image * slab, slab), slab)
        mask = wide(inside(meta, image, 0, rows), 256)
        small[own, :] = (mask * (a * dz[own, :] + b + d * pre[own, :])).astype(BF16)
        return carry

    lax.fori_loop(0, blocks, step, 0)
    fetches[2].wait()
    for ref, core in ((send, 1 - meta[2]), (keep, meta[2])):
        lanes = pl.ds(pl.multiple_of(core * 512, 512), 512)
        value = dot(x[:, lanes], small[...], ((0,), (0,))).astype(ref.dtype)
        for q in range(2):
            ref[q * 512 : q * 512 + 512, :] = value[:, q * 128 : q * 128 + 128]
        clear_from(ref, 1024)


def input_kernel(meta, small, w, grad, out, token, *, blocks, rows):
    slab = rows * COLS
    token[...] = jnp.zeros_like(token)
    group = 4

    def step(g, carry):
        many = pl.ds(pl.multiple_of(g * group * slab, group * slab), group * slab)
        for k in range(4):
            lanes = slice(k * 256, k * 256 + 256)
            value = dot(small[many, :], w[lanes, :], ((1,), (1,)))
            for j in range(group):
                image = g * group + j
                own = pl.ds(pl.multiple_of(image * slab, slab), slab)
                mask = wide(inside(meta, image, 0, rows), 256)
                out[own, lanes] = (
                    (value[j * slab : (j + 1) * slab] + grad[own, lanes]) * mask
                ).astype(BF16)
        return carry

    lax.fori_loop(0, blocks // group, step, 0)


def total_kernel(meta, *refs, places, large, less, other):
    arrays = len(places)
    *outs, wide_part, narrow_part, expand, excite, split, reduce, squeeze, sems = refs[arrays + 5 * other :]
    share = squeeze.shape[1]
    behind = 2 * large + less
    core = meta[2] ^ other
    for part, chips in zip(refs[:arrays], places):
        for k, chip in enumerate(chips):
            at = meta[4] ^ chip
            for q in range(2):
                wide_part[q, pl.ds(pl.multiple_of(at * large, large), large), :] = part[
                    k, q * large : q * large + large, :
                ]
            narrow_part[pl.ds(pl.multiple_of(at * less, less), less), :] = part[k, 2 * large : behind, :]
            squeeze[at] = part[k, behind:, :].astype(F32)[:share]
    expand_out, excite_out, split_out, reduce_out, squeeze_out = outs
    copies = []

    def send(source, target):
        copies.append(pltpu.make_async_copy(source, target, sems.at[len(copies)]))
        copies[-1].start()

    send(squeeze, squeeze_out.at[:, core])
    for q in range(2):
        reduce[:, q * 128 : q * 128 + 128] = narrow_part[q * 512 : q * 512 + 512].astype(F32)
    send(reduce, reduce_out.at[pl.ds(pl.multiple_of(core * 512, 512), 512)])
    for dy in range(3):
        for dx in range(3):
            first = (3 * dy + dx) * 128
            for q in range(2):
                split[dy, dx, :, q * 128 : q * 128 + 128] = wide_part[q, first : first + 128].astype(F32)
        send(split.at[dy], split_out.at[dy, :, core])
    for q in range(2):
        for k in range(2):
            first = 1152 + k * 256
            at = k * 256 + q * 128
            expand[:, at : at + 128] = wide_part[q, first : first + 256].astype(F32)
        excite[:, q * 128 : q * 128 + 128] = wide_part[q, 1664:1792].astype(F32)
    send(expand, expand_out.at[:, pl.ds(pl.multiple_of(core * 512, 512), 512)])
    send(excite, excite_out.at[:, pl.ds(pl.multiple_of(core * 256, 256), 256)])
    for copy in copies:
        copy.wait()


def body(
    inputs,
    image_class,
    weight_reduce,
    gain_reduce,
    shift_reduce,
    weight_split,
    gain_split,
    shift_split,
    weight_squeeze,
    gain_squeeze,
    shift_squeeze,
    weight_excite,
    bias_excite,
    weight_expand,
    gain_expand,
    shift_expand,
    cotangent,
):
    blocks, rows, cols, channels = inputs.shape
    mid = weight_reduce.shape[1]
    inter = weight_squeeze.shape[1]
    count = device_count()
    pixels = blocks * rows * cols
    slab = rows * cols
    edge = blocks * cols
    share = mid // count
    images = blocks * lax.axis_size("batch")
    meta = jnp.concatenate(
        [
            (lax.axis_index("narrow") * rows).astype(jnp.int32)[None],
            lax.axis_index("batch").astype(jnp.int32)[None],
            (lax.axis_index("narrow") % 2).astype(jnp.int32)[None],
            (lax.axis_index("narrow") // 2 % 2).astype(jnp.int32)[None],
            (lax.axis_index(ALL) // 2).astype(jnp.int32)[None],
            image_class,
        ]
    )
    x = inputs.reshape(pixels, channels)
    cot = cotangent.reshape(pixels, channels)
    row = lambda v: v.reshape(1, -1)
    gain1, shift1 = row(gain_reduce), row(shift_reduce)
    gain2, shift2 = row(gain_split), row(shift_split)
    gain3, shift3 = row(gain_expand), row(shift_expand)
    gain_sq, shift_sq = row(gain_squeeze), row(shift_squeeze)
    sizes = dict(blocks=blocks, rows=rows)
    small = 2 * pixels * channels * mid
    large = 2 * pixels * 9 * 128 * 512

    pre1, top, bottom, pay = call(
        reduce_kernel,
        [((pixels, mid), F32), ((2 * edge, mid), F32), ((2 * edge, mid), F32), ((count, 8, LANES), F32)],
        [meta, x, weight_reduce],
        [((3, 8, mid), F32)],
        flops=small,
        local="in out",
        **sizes,
    )
    low, high = halo(top, bottom)
    hid1, pre2, pay, stat1 = call(
        split_kernel,
        [
            ((3, blocks, slab + 4 * cols, mid), BF16, "hbm"),
            ((pixels + 2 * edge, 2 * mid), F32),
            ((count, 8, LANES), F32),
            ((8, mid), F32),
        ],
        [meta, exchange(pay), pre1, low, high, gain1, shift1, weight_split],
        [((2, 8, 2 * mid), F32), ((3, blocks, slab + 4 * cols, mid), BF16), pltpu.SemaphoreType.DMA],
        raw_out=(0,),
        flops=large,
        local="in out",
        **sizes,
    )
    hid2, pooled, pay, stat2 = call(
        pool_kernel,
        [
            ((pixels, 2 * mid), BF16),
            ((blocks, mid), F32),
            ((count, blocks, inter), F32),
            ((8, 2 * mid), F32),
        ],
        [meta, exchange(pay), stat1, pre2, gain2, shift2, weight_squeeze],
        local="in out",
        **sizes,
    )
    mix, pre3, att, hsq, znorm, zall, pay, stat_sq = call(
        expand_kernel,
        [
            ((pixels, mid), BF16),
            ((pixels, channels), BF16),
            ((blocks, 2 * mid), F32),
            ((blocks, inter), F32),
            ((images, inter), F32),
            ((images, inter), F32),
            ((count, 16, LANES), F32),
            ((8, inter), F32),
        ],
        [
            meta,
            exchange(pay),
            hid2,
            gain_sq,
            shift_sq,
            weight_excite,
            row(bias_excite),
            weight_expand,
        ],
        [((2, 8, channels), F32)],
        flops=small,
        parts=lax.axis_size("narrow"),
        local="in out",
        **sizes,
    )
    out, grad_res, pay, stat3 = call(
        residual_kernel,
        [
            ((pixels, channels), BF16),
            ((pixels, channels), F32),
            ((count, 16, LANES), F32),
            ((8, channels), F32),
        ],
        [meta, exchange(pay), stat1, x, pre3, cot, gain3, shift3],
        [((2, 8, channels), F32)],
        local="in out",
        **sizes,
    )
    gexp, gmix, top, bottom, glog, keep6, send6, gain3_grad, shift3_grad = call(
        mixture_kernel,
        [
            ((pixels, channels), BF16),
            ((pixels, mid), BF16),
            ((edge, mid), BF16),
            ((edge, mid), BF16),
            ((blocks, 2 * mid), F32),
            ((blocks // 2, inter), F32),
            ((blocks // 2, inter), F32),
            ((1, channels), F32),
            ((1, channels), F32),
        ],
        [meta, exchange(pay), stat3, pre3, grad_res, gain3, weight_expand, hid2, att, weight_excite],
        [((blocks, inter), F32)],
        flops=small,
        local="in out",
        **sizes,
    )
    lowm, highm = halo(top, bottom)
    keep3, send3 = call(
        expand_grad_kernel,
        [((2, 2 * mid + inter, LANES), F32), ((2, 2 * mid + inter, LANES), BF16)],
        [meta, mix, gexp, hsq, glog],
        flops=small,
        local="in out",
    )
    (pay,) = call(
        logits_kernel,
        [((count, blocks // 2, inter), F32)],
        [meta, keep6, swap(send6, 1)],
        after=(lowm, highm, send3),
        local="in out",
    )
    dz2, gpool, squeeze_part, pay, gain_sq_grad, shift_sq_grad = call(
        hidden_kernel,
        [
            ((pixels, 2 * mid), F32),
            ((blocks, mid), F32),
            ((mid, inter), F32),
            ((count, 8, LANES), F32),
            ((1, inter), F32),
            ((1, inter), F32),
        ],
        [
            meta,
            exchange(pay),
            znorm,
            zall,
            gain_sq,
            stat_sq,
            pooled,
            weight_squeeze,
            att,
            gmix,
            pre2,
            stat2,
            gain2,
            shift2,
        ],
        [((2, 8, 2 * mid), F32), ((images, inter), F32)],
        parts=lax.axis_size("narrow"),
        local="in out",
        **sizes,
    )
    dz1, keep2, send2, pay, gain2_grad, shift2_grad = call(
        conv_kernel,
        [
            ((pixels, mid), F32, "hbm"),
            ((2, 9 * 128, LANES), F32, "hbm"),
            ((2, 9 * 128, LANES), BF16, "hbm"),
            ((count, 8 + share, LANES), F32, "hbm"),
            ((1, 2 * mid), F32),
            ((1, 2 * mid), F32),
        ],
        [
            meta,
            exchange(pay),
            stat2,
            gain2,
            shift2,
            dz2,
            pre2,
            lowm,
            highm,
            att,
            gpool,
            weight_split,
            pre1,
            stat1,
            gain1,
            shift1,
            glog,
            squeeze_part,
            hid1,
        ],
        [
            ((3, blocks, slab + 2 * cols, 2 * mid), BF16),
            ((2, 8, mid), F32),
            ((pixels, mid), F32),
            ((2, 9 * 128, LANES), F32),
            ((2, 9 * 128, LANES), BF16),
            ((count, 8 + share, LANES), F32),
            pltpu.SemaphoreType.DMA((3 + blocks // 4,)),
        ],
        raw_out=(0, 1, 2, 3),
        flops=2 * large,
        local="in",
        **sizes,
    )
    chips = count // 2
    large, less = (-(-rows_in // (chips * 16)) * 16 for rows_in in (9 * 128 + 2 * mid + inter, channels))
    keep, send, token = call(
        add_kernel,
        [((chips * large, LANES), F32), ((chips * large, LANES), BF16), TOKEN],
        [meta, keep2, swap(send2, 1), keep3, swap(send3, 1)],
    )
    small1, keep1, send1, gain1_grad, shift1_grad, bias_grad, squeeze_share = call(
        reduce_back_kernel,
        [
            ((pixels, mid), BF16),
            ((chips * less, LANES), F32),
            ((chips * less, LANES), BF16),
            ((1, mid), F32),
            ((1, mid), F32),
            ((1, 2 * mid), F32),
            ((16, inter), F32),
        ],
        [meta, exchange(pay), stat1, gain1, dz1, pre1, x],
        [
            ((pixels, mid), F32),
            ((pixels, mid), F32),
            ((pixels, channels), BF16),
            pltpu.SemaphoreType.DMA((3,)),
        ],
        raw_in=(4, 5, 6),
        flops=small,
        after=(token,),
        local="in out",
        **sizes,
    )
    first = len(stages()[-1])
    blocks = call(
        pack_kernel,
        [((chips // first, large + less, LANES), BF16)] * first,
        [meta, keep, swap(send, 2), keep1, swap(send1, 1)],
        [((chips * large, LANES), BF16), ((chips * less, LANES), BF16)],
        places=slots(),
    )
    input_grad, token = call(
        input_kernel,
        [((pixels, channels), BF16, "hbm"), TOKEN],
        [meta, small1, weight_reduce, grad_res],
        flops=small,
        **sizes,
    )
    shared = scatter_chips(meta, blocks, 2 * large + less, large, squeeze_share, [token])
    parts, places = gather_chips(shared)
    swapped = [swap(part, 1) for part in parts]
    totals = ()
    for other, half in enumerate((parts, swapped)):
        args = [meta, *half, *totals]
        totals = call(
            total_kernel,
            [
                ((mid, channels), F32, "hbm"),
                ((inter, 2 * mid), F32, "hbm"),
                (weight_split.shape, F32, "hbm"),
                ((channels, mid), F32, "hbm"),
                ((chips, 2, share, inter), F32, "hbm"),
            ],
            args,
            [
                ((2, chips * large, LANES), BF16),
                ((chips * less, LANES), BF16),
                ((mid, channels // 2), F32),
                ((inter, mid), F32),
                ((3, 3, 128, mid), F32),
                ((channels // 2, mid), F32),
                ((chips, share, inter), F32),
                pltpu.SemaphoreType.DMA((7,)),
            ],
            local="in",
            raw_in=range(1 + len(half), len(args)),
            raw_out=range(5),
            aliases={1 + len(half) + k: k for k in range(len(totals))},
            places=places,
            large=large,
            less=less,
            other=other,
        )
    expand_total, excite_total, split_total, reduce_total, squeeze_total = totals
    squeeze_total = squeeze_total.reshape(mid, inter)
    flat = lambda v: v.reshape(-1)
    return (
        out.reshape(inputs.shape),
        input_grad.reshape(inputs.shape),
        reduce_total,
        flat(gain1_grad),
        flat(shift1_grad),
        split_total,
        flat(gain2_grad),
        flat(shift2_grad),
        squeeze_total,
        flat(gain_sq_grad),
        flat(shift_sq_grad),
        excite_total,
        flat(bias_grad),
        expand_total,
        flat(gain3_grad),
        flat(shift3_grad),
    )


def solution(mesh):
    rows = P("batch", "narrow", None, None)
    return jax.shard_map(
        body,
        mesh=mesh,
        in_specs=(rows, P("batch")) + (P(),) * 14 + (rows,),
        out_specs=(rows, rows) + (P(),) * 14,
        check_vma=False,
    )
```

```python
import functools
from itertools import product

import jax
import jax.numpy as jnp
from jax import lax
from jax.experimental import pallas as pl
from jax.experimental.pallas import tpu as pltpu
from jax.sharding import PartitionSpec as P

EPSILON = 1e-05
HIGHEST = lax.Precision.HIGHEST
ALL = ("batch", "narrow")
F32 = jnp.float32
BF16 = jnp.bfloat16
COLS = 16
LANES = 128
TOKEN = ((8, LANES), F32, "hbm")


def device_count():
    return lax.axis_size("batch") * lax.axis_size("narrow")


def halo(top, bottom):
    count = lax.axis_size("narrow")
    low = lax.ppermute(bottom, "narrow", [(i, i + 1) for i in range(count - 1)])
    high = lax.ppermute(top, "narrow", [(i + 1, i) for i in range(count - 1)])
    return low, high


def exchange(block):
    return lax.all_to_all(block, ALL, 0, 0)


def swap(block, bit):
    count = lax.axis_size("narrow")
    return lax.ppermute(block, "narrow", [(i, i ^ bit) for i in range(count)])


def stages():
    bits = list(range(device_count().bit_length() - 2, 0, -1))
    pairs = [bits[k : k + 2] for k in range(0, len(bits), 2)]
    return [
        [sum(bit << pair[k] for k, bit in enumerate(pick)) for pick in product((0, 1), repeat=len(pair))]
        for pair in pairs
    ]


def partners(blocks, steps):
    count = device_count()
    return [
        lax.ppermute(block, ALL, [(i, i ^ step) for i in range(count)])
        for block, step in zip(blocks[1:], steps[1:])
    ]


def slots():
    order = [0]
    for steps in reversed(stages()):
        order = [place ^ (step >> 1) for place in order for step in steps]
    return order


def scatter_chips(meta, blocks, rows, large, extra, after):
    order = list(reversed(stages()))
    for k, steps in enumerate(order):
        last = k + 1 == len(order)
        count = 1 if last else len(order[k + 1])
        out_rows = rows + extra.shape[0] if last else rows
        outs = [((blocks[0].shape[0] // count, out_rows, LANES), BF16)] * count
        blocks = call(
            sum_kernel,
            outs,
            [meta, blocks[0], *partners(blocks, steps)] + ([extra] if last else []),
            after=() if k else after,
            large=0 if k else large,
            others=[step >> 1 & 1 for step in steps],
        )
    return blocks[0]


def gather_chips(share):
    block, places = share, [0]
    for steps in stages():
        blocks = [block] + partners([block] * len(steps), steps)
        lists = [[place ^ (step >> 1) for place in places] for step in steps]
        block, places = jnp.concatenate(blocks), sum(lists, [])
    return blocks, lists


def half_terms(center, inv, gain, shift):
    scale = 0.5 * inv * gain
    return scale, 0.5 * shift - scale * center


def silu_of_half(half):
    tanh = jnp.tanh(half)
    more = 1.0 + tanh
    silu = half * more
    return silu, more + silu * (1.0 - tanh)


def wide(mask, width):
    return jnp.concatenate([mask] * (width // LANES), axis=1) if width > LANES else mask


def inside(meta, image, start, count):
    pixel = lax.broadcasted_iota(jnp.int32, (count * COLS, LANES), 0)
    row = (pixel >> 4) + (meta[0] + start)
    col = pixel & (COLS - 1)
    side = 12 + 2 * meta[5 + image]
    return jnp.where((row < side) & (row >= 0) & (col < side), 1.0, 0.0).astype(F32)


def area_of(meta, image):
    side = (12 + 2 * meta[5 + image]).astype(F32)
    return side * side


def row_of(block, first, count):
    return jnp.concatenate([block[first + k : first + k + 1] for k in range(count)], axis=1)


def put_row(ref, first, vector):
    for k in range(vector.shape[1] // LANES):
        ref[0, first + k : first + k + 1, :] = vector[:, k * LANES : (k + 1) * LANES]


def put_sums(ref, rows, acc, center, inv):
    plain = total(acc[0])
    put_row(ref, 0, plain)
    put_row(ref, rows, (total(acc[1]) - center * plain) * inv)


def spread(ref):
    block = ref[0]

    def step(k, carry):
        ref[k] = block
        return carry

    lax.fori_loop(1, ref.shape[0], step, 0, unroll=31)


def fold(values):
    return jnp.sum(values.reshape(-1, 8, values.shape[-1]), 0)


def clear_from(ref, first):
    if ref.shape[0] > first:
        ref[first:, :] = jnp.zeros((ref.shape[0] - first, LANES), ref.dtype)


def own_of_tall(image, slab):
    return pl.ds(pl.multiple_of(image * (slab + 2 * COLS) + COLS, COLS), slab)


def total(block):
    return jnp.sum(block, 0, keepdims=True)


def stats(totals, squares, counted):
    center = totals / counted
    return center, lax.rsqrt(squares / counted - center * center + EPSILON)


def shifted(values):
    count, width = values.shape
    col = lax.broadcasted_iota(jnp.int32, (count, LANES), 0) & (COLS - 1)
    has_left = wide(jnp.where(col > 0, 1.0, 0.0).astype(F32), width)
    has_right = wide(jnp.where(col < COLS - 1, 1.0, 0.0).astype(F32), width)
    left = pltpu.roll(values, 1, 0) * has_left
    right = pltpu.roll(values, count - 1, 0) * has_right
    return left.astype(BF16), values.astype(BF16), right.astype(BF16)


def dot(a, b, dims=((1,), (0,)), precision=None):
    return lax.dot_general(a, b, (dims, ((), ())), precision=precision, preferred_element_type=F32)


def whole(shape):
    return pl.BlockSpec(shape, lambda step: (0,) * len(shape))


def call(
    kernel, outs, args, scratch=(), megabytes=24, flops=0, after=(), local="", raw_in=(), raw_out=(), aliases=None, **sizes
):
    moved = sum(a.size * a.dtype.itemsize for a in args) + sum(
        functools.reduce(lambda x, y: x * y, o[0]) * jnp.dtype(o[1]).itemsize for o in outs
    )
    count = len(args)
    vmem = pl.BlockSpec(memory_space=pltpu.VMEM)
    anywhere = pl.BlockSpec(memory_space=pl.ANY)
    in_hbm = lambda a: pltpu.with_memory_space_constraint(a, pltpu.HBM)
    args = [in_hbm(a) if k in raw_in else a for k, a in enumerate(args)]
    after = [in_hbm(a) if a.shape == TOKEN[0] else a for a in after]

    def run(*refs):
        kernel(*refs[:count], *refs[count + len(after) :], **sizes)

    def spec(place, shape, kept, raws):
        return anywhere if place in raws else vmem if kept else whole(shape)

    return pl.pallas_call(
        run,
        grid=() if local == "in out" else (1,),
        out_shape=[
            pltpu.HBM(o[0], o[1]) if len(o) > 2 else jax.ShapeDtypeStruct(o[0], o[1]) for o in outs
        ],
        in_specs=[pl.BlockSpec(memory_space=pltpu.SMEM)]
        + [spec(k, a.shape, "in" in local, raw_in) for k, a in enumerate(args) if k]
        + [anywhere] * len(after),
        out_specs=[spec(k, o[0], "out" in local, raw_out) for k, o in enumerate(outs)],
        input_output_aliases=aliases or {},
        scratch_shapes=[pltpu.VMEM(*entry) if isinstance(entry, tuple) else entry for entry in scratch],
        compiler_params=pltpu.CompilerParams(vmem_limit_bytes=megabytes << 20),
        cost_estimate=pl.CostEstimate(flops=flops, bytes_accessed=moved, transcendentals=0),
    )(*args, *after)


def reduce_kernel(meta, x, w, pre, top, bottom, pay, acc, *, blocks, rows):
    slab = rows * COLS
    acc[...] = jnp.zeros_like(acc)
    group = 4

    def step(g, carry):
        base = pl.multiple_of(g * group * slab, group * slab)
        out = dot(x[pl.ds(base, group * slab), :], w[...])
        for j in range(group):
            image = g * group + j
            mask = inside(meta, image, 0, rows)
            part = out[j * slab : (j + 1) * slab] * wide(mask, out.shape[1])
            pre[pl.ds(pl.multiple_of(image * slab, slab), slab), :] = part
            edge = pl.ds(pl.multiple_of(image * 2 * COLS, 2 * COLS), 2 * COLS)
            top[edge, :] = part[: 2 * COLS]
            bottom[edge, :] = part[slab - 2 * COLS :]
            acc[0] += fold(part)
            acc[1] += fold(part * part)
            acc[2, :, :LANES] += fold(mask)
        return carry

    lax.fori_loop(0, blocks // group, step, 0, unroll=True)
    put_row(pay, 0, total(acc[0]))
    put_row(pay, 2, total(acc[1]))
    put_row(pay, 4, total(acc[2, :, :LANES]))
    pay[0, 5:8, :] = jnp.zeros((3, LANES), F32)
    spread(pay)


def split_kernel(
    meta, got, pre, low, high, gain, shift, w, hid_out, out, pay, stat, acc, hid, sem, *, blocks, rows
):
    slab = rows * COLS
    sums = jnp.sum(got[...], 0)
    counted = row_of(jnp.concatenate([sums[4:5]] * 2, 0), 0, 2)
    center, inv = stats(row_of(sums, 0, 2), row_of(sums, 2, 2), counted)
    stat[...] = jnp.zeros_like(stat)
    stat[0:1] = center
    stat[1:2] = inv
    stat[2:3] = counted
    scale, offset = half_terms(center, inv, gain[...], shift[...])

    def prepare(i, carry):
        edge = pl.ds(pl.multiple_of(i * 2 * COLS, 2 * COLS), 2 * COLS)
        own = pl.ds(pl.multiple_of(i * slab, slab), slab)
        mask = inside(meta, i, -2, rows + 4)
        for k in range(2):
            lanes = slice(k * LANES, k * LANES + LANES)
            tall = jnp.concatenate([low[edge, lanes], pre[own, lanes], high[edge, lanes]], axis=0)
            silu, _ = silu_of_half(tall * scale[:, lanes] + offset[:, lanes])
            left, middle, right = shifted(silu * mask)
            hid[0, i, :, lanes] = left
            hid[1, i, :, lanes] = middle
            hid[2, i, :, lanes] = right
        return carry

    lax.fori_loop(0, blocks, prepare, 0, unroll=4)
    copy = pltpu.make_async_copy(hid, hid_out, sem)
    copy.start()
    acc[...] = jnp.zeros_like(acc)
    group = 4
    tall = slab + 2 * COLS

    def step(g, carry):
        for half in range(2):
            lanes = slice(half * 128, half * 128 + 128)
            outs = slice(half * 256, half * 256 + 256)
            lhs = jnp.concatenate(
                [
                    hid[dx, pl.ds(g * group, group), dy * COLS : dy * COLS + tall, lanes].reshape(
                        group * tall, 128
                    )
                    for dy in range(3)
                    for dx in range(3)
                ],
                axis=1,
            )
            value = dot(lhs, w[:, :, half].reshape(9 * 128, 256))
            for j in range(group):
                image = g * group + j
                mask = inside(meta, image, -1, rows + 2)
                part = value[j * tall : (j + 1) * tall] * wide(mask, 256)
                out[pl.ds(pl.multiple_of(image * tall, tall), tall), outs] = part
                part = part[COLS : COLS + slab]
                acc[0, :, outs] += fold(part)
                acc[1, :, outs] += fold(part * part)
        return carry

    lax.fori_loop(0, blocks // group, step, 0, unroll=2)
    put_row(pay, 0, total(acc[0]))
    put_row(pay, 4, total(acc[1]))
    spread(pay)
    copy.wait()


def pool_kernel(
    meta, got, stat, pre, gain, shift, w, hid, pooled, pay, stat2, *, blocks, rows
):
    slab = rows * COLS
    sums = jnp.sum(got[...], 0)
    counted = jnp.concatenate([stat[2:3]] * 2, axis=1)
    center, inv = stats(row_of(sums, 0, 4), row_of(sums, 4, 4), counted)
    stat2[...] = jnp.zeros_like(stat2)
    stat2[0:1] = center
    stat2[1:2] = inv
    stat2[2:3] = counted
    scale, offset = half_terms(center, inv, gain[...], shift[...])

    def step(i, carry):
        own = pl.ds(pl.multiple_of(i * slab, slab), slab)
        mask = inside(meta, i, 0, rows)
        summed = [None, None]
        for k in range(4):
            lanes = slice(k * LANES, k * LANES + LANES)
            silu, _ = silu_of_half(pre[own_of_tall(i, slab), lanes] * scale[:, lanes] + offset[:, lanes])
            value = (silu * mask).astype(BF16)
            hid[own, lanes] = value
            part = fold(value.astype(F32))
            summed[k % 2] = part if k < 2 else summed[k % 2] + part
        pooled[pl.ds(i, 1), :] = total(jnp.concatenate(summed, axis=1)) / area_of(meta, i)
        return carry

    lax.fori_loop(0, blocks, step, 0, unroll=4)
    pay[0] = dot(pooled[...], w[...], precision=HIGHEST)
    spread(pay)


def squeeze_stats(block):
    return stats(total(block), total(block * block), float(block.shape[0]))


def expand_kernel(
    meta, got, hid, gain, shift, we, bias, w, mix, pre, att, hsq, znorm, zall, pay, stat_sq, acc, *, blocks, rows, parts
):
    slab = rows * COLS
    bands = got.shape[0] // parts
    for b in range(bands):
        block = got[b * parts]
        for k in range(1, parts):
            block = block + got[b * parts + k]
        znorm[b * blocks : (b + 1) * blocks, :] = block
    center, inv = squeeze_stats(znorm[...])
    stat_sq[...] = jnp.zeros_like(stat_sq)
    stat_sq[0:1] = center
    stat_sq[1:2] = inv
    normed = (znorm[...] - center) * inv
    znorm[...] = normed
    zall[...] = normed * gain[...] + shift[...]
    own_z = zall[pl.ds(pl.multiple_of(meta[1] * blocks, blocks), blocks), :]
    hidden = own_z * jax.nn.sigmoid(own_z)
    hsq[...] = hidden
    logits = dot(hidden, we[...], precision=HIGHEST) + bias[...]
    first = logits[:, :256]
    second = logits[:, 256:]
    ceiling = jnp.maximum(first, second)
    exp_first = jnp.exp(first - ceiling)
    exp_second = jnp.exp(second - ceiling)
    att[:, :256] = exp_first / (exp_first + exp_second)
    att[:, 256:] = exp_second / (exp_first + exp_second)
    acc[...] = jnp.zeros_like(acc)
    group = 4

    def step(g, carry):
        for j in range(group):
            image = g * group + j
            own = pl.ds(pl.multiple_of(image * slab, slab), slab)
            weights = att[pl.ds(image, 1), :]
            mix[own, :] = (
                weights[:, :256] * hid[own, :256].astype(F32)
                + weights[:, 256:] * hid[own, 256:].astype(F32)
            ).astype(BF16)
        many = pl.ds(pl.multiple_of(g * group * slab, group * slab), group * slab)
        for k in range(4):
            lanes = slice(k * 256, k * 256 + 256)
            value = dot(mix[many, :], w[:, lanes]).astype(BF16)
            pre[many, lanes] = value
            value = value.astype(F32)
            acc[0, :, lanes] += fold(value)
            acc[1, :, lanes] += fold(value * value)
        return carry

    lax.fori_loop(0, blocks // group, step, 0, unroll=True)
    put_row(pay, 0, total(acc[0]))
    put_row(pay, 8, total(acc[1]))
    spread(pay)


def residual_kernel(
    meta, got, stat, x, pre, cot, gain, shift, out, grad, pay, stat3, acc, *, blocks, rows
):
    slab = rows * COLS
    sums = jnp.sum(got[...], 0)
    counted = jnp.concatenate([stat[2:3]] * 4, axis=1)
    center, inv = stats(row_of(sums, 0, 8), row_of(sums, 8, 8), counted)
    stat3[...] = jnp.zeros_like(stat3)
    stat3[0:1] = center
    stat3[1:2] = inv
    stat3[2:3] = counted
    acc[...] = jnp.zeros_like(acc)
    scale, offset = half_terms(center, inv, gain[...], shift[...])

    def step(i, carry):
        own = pl.ds(pl.multiple_of(i * slab, slab), slab)
        mask = inside(meta, i, 0, rows)
        half_mask = 0.5 * mask
        for k in range(8):
            lanes = slice(k * LANES, k * LANES + LANES)
            values = pre[own, lanes].astype(F32)
            half = values * scale[:, lanes] + offset[:, lanes] + 0.5 * x[own, lanes].astype(F32)
            silu, slope = silu_of_half(half)
            out[own, lanes] = (silu * mask).astype(BF16)
            back = cot[own, lanes].astype(F32) * half_mask * slope
            grad[own, lanes] = back
            acc[0, :, lanes] += fold(back)
            acc[1, :, lanes] += fold(back * values)
        return carry

    lax.fori_loop(0, blocks, step, 0)
    put_sums(pay, 8, acc, center, inv)
    spread(pay)


def back_terms(stat, gain, shift_sum, gain_sum):
    center, inv, counted = stat[0:1], stat[1:2], stat[2:3]
    a = gain * inv
    d = -a * inv * (gain_sum / counted)
    b = -a * (shift_sum / counted) - d * center
    return a, b, d


def mixture_kernel(
    meta, got, stat3, pre, grad, gain, w, hid, att, we, gexp, gmix, top, bottom, glog, keep, send, gain_out, shift_out, hidden, *, blocks, rows
):
    slab = rows * COLS
    sums = jnp.sum(got[...], 0)
    shift_sum, gain_sum = row_of(sums, 0, 8), row_of(sums, 8, 8)
    shift_out[...] = shift_sum
    gain_out[...] = gain_sum
    a, b, d = back_terms(stat3, gain[...], shift_sum, gain_sum)
    group = 4

    def step(g, carry):
        many = pl.ds(pl.multiple_of(g * group * slab, group * slab), group * slab)
        for j in range(group):
            image = g * group + j
            own = pl.ds(pl.multiple_of(image * slab, slab), slab)
            mask = inside(meta, image, 0, rows)
            for k in range(8):
                lanes = slice(k * LANES, k * LANES + LANES)
                gexp[own, lanes] = (
                    mask
                    * (
                        a[:, lanes] * grad[own, lanes]
                        + b[:, lanes]
                        + d[:, lanes] * pre[own, lanes].astype(F32)
                    )
                ).astype(BF16)
        value = dot(gexp[many, :], w[...], ((1,), (1,))).astype(BF16)
        gmix[many, :] = value
        value = value.astype(F32)
        for j in range(group):
            image = g * group + j
            own = pl.ds(pl.multiple_of(image * slab, slab), slab)
            edge = pl.ds(pl.multiple_of(image * COLS, COLS), COLS)
            part = value[j * slab : (j + 1) * slab]
            top[edge, :] = part[:COLS].astype(BF16)
            bottom[edge, :] = part[slab - COLS :].astype(BF16)
            for half in range(2):
                lanes = slice(half * 256, half * 256 + 256)
                glog[pl.ds(image, 1), lanes] = total(fold(part * hid[own, lanes].astype(F32)))
        return carry

    lax.fori_loop(0, blocks // group, step, 0, unroll=2)
    first, second = att[:, :256], att[:, 256:]
    inner = first * glog[:, :256] + second * glog[:, 256:]
    glog[...] = jnp.concatenate(
        [first * (glog[:, :256] - inner), second * (glog[:, 256:] - inner)], axis=1
    )
    hidden[...] = dot(glog[...], we[...], ((1,), (1,)), HIGHEST)
    many = blocks // 2
    keep[...] = hidden[pl.ds(pl.multiple_of(meta[2] * many, many), many), :]
    send[...] = hidden[pl.ds(pl.multiple_of((1 - meta[2]) * many, many), many), :]


def logits_kernel(meta, keep, got, pay):
    pay[0] = keep[...] + got[...]
    spread(pay)


def expand_grad_kernel(meta, mix, gexp, hsq, glog, keep, send):
    for ref, core in ((send, 1 - meta[2]), (keep, meta[2])):
        lanes = pl.ds(pl.multiple_of(core * 512, 512), 512)
        value = dot(mix[...], gexp[:, lanes], ((0,), (0,))).astype(ref.dtype)
        lanes = pl.ds(pl.multiple_of(core * 256, 256), 256)
        excite = dot(hsq[...], glog[:, lanes], ((0,), (0,)), HIGHEST).astype(ref.dtype)
        for q in range(2):
            for k in range(2):
                first = k * 256 + q * 128
                ref[q, k * 256 : k * 256 + 256, :] = value[:, first : first + 128]
            ref[q, 512:, :] = excite[:, q * 128 : q * 128 + 128]


def add_kernel(meta, keep2, got2, keep3, got3, keep, send, token):
    first = keep2.shape[1]
    for ref, half in ((send, 1 - meta[3]), (keep, meta[3])):
        ref[:first, :] = (keep2[half] + got2[half].astype(F32)).astype(ref.dtype)
        last = first + keep3.shape[1]
        ref[first:last, :] = (keep3[half] + got3[half].astype(F32)).astype(ref.dtype)
        clear_from(ref, last)
    token[...] = jnp.zeros_like(token)


def pack_kernel(meta, keep, got, keep1, got1, *refs, places):
    *outs, flat, flat1 = refs
    held = outs[0].shape[0]
    large, small = flat.shape[0] // len(places), flat1.shape[0] // len(places)
    flat[...] = (keep[...] + got[...].astype(F32)).astype(BF16)
    flat1[...] = (keep1[...] + got1[...].astype(F32)).astype(BF16)
    for k, place in enumerate(places):
        chip = meta[4] ^ place
        out = outs[k // held]
        out[k % held, :large, :] = flat[pl.ds(pl.multiple_of(chip * large, large), large), :]
        out[k % held, large:, :] = flat1[pl.ds(pl.multiple_of(chip * small, small), small), :]


def sum_kernel(meta, *refs, large, others):
    ins, outs = refs[: len(others)], refs[len(others) :]
    if len(outs[0].shape) == 2:
        extra, *outs = outs
        outs[0][0, ins[0].shape[1] :, :] = extra[...].astype(BF16)
    held = outs[0].shape[0]

    def add(pick, first, last):
        value = None
        for ref in pick:
            part = ref[:, first:last, :].astype(F32)
            value = part if value is None else value + part
        return value.astype(BF16)

    def put(value, at, rows):
        for k, out in enumerate(outs):
            out[:, pl.ds(at, rows), :] = value[k * held : k * held + held]

    total_rows = ins[0].shape[1]
    if not large:
        put(add(ins, 0, total_rows), 0, total_rows)
        return
    for other in range(2):
        pick = [ref for ref, side in zip(ins, others) if side == other]
        put(add(pick, 0, large), pl.multiple_of((meta[3] ^ other) * large, large), large)
    put(add(ins, large, total_rows), 2 * large, total_rows - large)


def hidden_kernel(
    meta, got, znorm, zall, hsq_gain, stat_sq, pooled, wsq, att, gmix, pre, stat2, gain, shift,
    dz, gpool, squeeze, pay, gain_out, shift_out, acc, full, *, blocks, rows, parts
):
    slab = rows * COLS
    bands = got.shape[0] // parts
    many = blocks // 2
    for b in range(bands):
        for core in range(2):
            block = got[b * parts + core]
            for k in range(core + 2, parts, 2):
                block = block + got[b * parts + k]
            at = b * blocks + core * many
            full[at : at + many, :] = block
    z = zall[...]
    part = jax.nn.sigmoid(z)
    grad_z = full[...] * (part * (1.0 + z * (1.0 - part)))
    full[...] = grad_z
    images = float(bands * blocks)
    shift_sum = total(grad_z)
    gain_sum = total(grad_z * znorm[...])
    shift_out[...] = shift_sum
    gain_out[...] = gain_sum
    mine = pl.ds(pl.multiple_of(meta[1] * blocks, blocks), blocks)
    grad_pre = (
        hsq_gain[...]
        * stat_sq[1:2]
        * (full[mine, :] - shift_sum / images - znorm[mine, :] * (gain_sum / images))
    )
    squeeze[...] = dot(pooled[...], grad_pre, ((0,), (0,)), HIGHEST)
    gpool[...] = dot(grad_pre, wsq[...], ((1,), (1,)), HIGHEST)
    for i in range(blocks):
        gpool[i : i + 1, :] = gpool[i : i + 1, :] / area_of(meta, i)
    center, inv = stat2[0:1], stat2[1:2]
    acc[...] = jnp.zeros_like(acc)
    scale, offset = half_terms(center, inv, gain[...], shift[...])

    def step(i, carry):
        own = pl.ds(pl.multiple_of(i * slab, slab), slab)
        half_mask = 0.5 * inside(meta, i, 0, rows)
        weights = att[pl.ds(i, 1), :]
        pool = gpool[pl.ds(i, 1), :]
        for k in range(4):
            lanes = slice(k * LANES, k * LANES + LANES)
            mid = slice(k % 2 * LANES, k % 2 * LANES + LANES)
            mixed = gmix[own, mid].astype(F32)
            values = pre[own_of_tall(i, slab), lanes]
            _, slope = silu_of_half(values * scale[:, lanes] + offset[:, lanes])
            hidden = (mixed * weights[:, lanes] + pool[:, mid]).astype(BF16).astype(F32)
            back = hidden * half_mask * slope
            dz[own, lanes] = back
            acc[0, :, lanes] += fold(back)
            acc[1, :, lanes] += fold(back * values)
        return carry

    lax.fori_loop(0, blocks, step, 0, unroll=4)
    put_sums(pay, 4, acc, center, inv)
    spread(pay)


def conv_kernel(
    meta, got, stat2, gain2, shift2, dz, pre2, lowm, highm, att, gpool, w, pre, stat,
    gain, shift, glog, squeeze, hid, out_hbm, keep_hbm, send_hbm, pay_hbm, gain_hbm, shift_hbm, tall, acc,
    out, keep, send, pay, gain_out, shift_out, sems, *, blocks, rows
):
    slab = rows * COLS
    sums = jnp.sum(got[...], 0)
    shift_sum, gain_sum = row_of(sums, 0, 4), row_of(sums, 4, 4)
    shift_out[...] = shift_sum
    gain_out[...] = gain_sum
    a, b, d = back_terms(stat2, gain2[...], shift_sum, gain_sum)
    scale2, offset2 = half_terms(stat2[0:1], stat2[1:2], gain2[...], shift2[...])

    def prepare(i, carry):
        own = pl.ds(pl.multiple_of(i * slab, slab), slab)
        edge = pl.ds(pl.multiple_of(i * COLS, COLS), COLS)
        whole_image = pl.ds(pl.multiple_of(i * (slab + 2 * COLS), COLS), slab + 2 * COLS)
        mask = inside(meta, i, -1, rows + 2)
        weights = att[pl.ds(i, 1), :]
        pool = gpool[pl.ds(i, 1), :]
        for k in range(4):
            lanes = slice(k * LANES, k * LANES + LANES)
            mid = slice(k % 2 * LANES, k % 2 * LANES + LANES)

            def edge_grad(values, mixed, keep):
                _, slope = silu_of_half(values * scale2[:, lanes] + offset2[:, lanes])
                hidden = mixed[edge, mid].astype(F32) * weights[:, lanes] + pool[:, mid]
                return hidden.astype(BF16).astype(F32) * (0.5 * keep) * slope

            keep_low, keep_high = mask[:COLS], mask[slab + COLS :]
            values = pre2[whole_image, lanes]
            grads = jnp.concatenate(
                [
                    edge_grad(values[:COLS], lowm, keep_low),
                    dz[own, lanes],
                    edge_grad(values[slab + COLS :], highm, keep_high),
                ],
                axis=0,
            )
            back = mask * (a[:, lanes] * grads + b[:, lanes] + d[:, lanes] * values)
            left, middle, right = shifted(back)
            tall[0, i, :, lanes] = left
            tall[1, i, :, lanes] = middle
            tall[2, i, :, lanes] = right
        return carry

    lax.fori_loop(0, blocks, prepare, 0, unroll=4)

    def weights(dy, carry):
        rows_at = pl.ds(pl.multiple_of((dy + 1) * COLS, COLS), slab)
        for ref, core in ((send, 1 - meta[2]), (keep, meta[2])):
            lanes = pl.ds(pl.multiple_of(core * 128, 128), 128)
            wide_lanes = pl.ds(pl.multiple_of(core * 256, 256), 256)
            grads = tall[1, :, COLS : COLS + slab, wide_lanes].reshape(blocks * slab, 256)
            lhs = jnp.concatenate(
                [hid[dx, :, rows_at, lanes].reshape(blocks * slab, 128) for dx in range(3)], axis=1
            )
            value = dot(lhs, grads, ((0,), (0,))).astype(ref.dtype)
            at = pl.ds(pl.multiple_of(dy * 384, 384), 384)
            for q in range(2):
                ref[q, at, :] = value[:, q * 128 : q * 128 + 128]
        return carry

    lax.fori_loop(0, 3, weights, 0)
    stores = [
        pltpu.make_async_copy(send, send_hbm, sems.at[1]),
        pltpu.make_async_copy(keep, keep_hbm, sems.at[2]),
        pltpu.make_async_copy(gain_out, gain_hbm, sems.at[3]),
        pltpu.make_async_copy(shift_out, shift_hbm, sems.at[4]),
    ]
    for store in stores:
        store.start()
    acc[...] = jnp.zeros_like(acc)
    center, inv = stat[0:1], stat[1:2]
    scale, offset = half_terms(center, inv, gain[...], shift[...])
    group = 4

    def store_group(g):
        many = pl.ds(pl.multiple_of(g * group * slab, group * slab), group * slab)
        return pltpu.make_async_copy(out.at[many], out_hbm.at[many], sems.at[5 + g])

    def step(g, carry):
        for half in range(2):
            lanes = slice(half * 256, half * 256 + 256)
            outs = slice(half * 128, half * 128 + 128)
            taps = [(dy, dx) for dy in range(3) for dx in range(3)]
            lhs = jnp.concatenate(
                [
                    tall[
                        2 - dx, pl.ds(g * group, group), (2 - dy) * COLS : (2 - dy) * COLS + slab, lanes
                    ].reshape(group * slab, 256)
                    for dy, dx in taps
                ],
                axis=1,
            )
            rhs = jnp.concatenate([w[dy, dx, half] for dy, dx in taps], axis=1)
            value = dot(lhs, rhs, ((1,), (1,)))
            for j in range(group):
                image = g * group + j
                own = pl.ds(pl.multiple_of(image * slab, slab), slab)
                values = pre[own, outs]
                _, slope = silu_of_half(values * scale[:, outs] + offset[:, outs])
                back = value[j * slab : (j + 1) * slab] * (0.5 * inside(meta, image, 0, rows)) * slope
                out[own, outs] = back
                acc[0, :, outs] += fold(back)
                acc[1, :, outs] += fold(back * values)
        store_group(g).start()
        return carry

    lax.fori_loop(0, blocks // group, step, 0, unroll=2)
    put_sums(pay, 2, acc, center, inv)
    put_row(pay, 4, total(glog[...]))
    pay[0, 8:, :] = jnp.zeros((pay.shape[1] - 8, LANES), F32)
    spread(pay)
    share = pay.shape[1] - 8
    for n in range(pay.shape[0]):
        pay[n, 8:, :] = squeeze[n * share : (n + 1) * share, :]
    stores.append(pltpu.make_async_copy(pay, pay_hbm, sems.at[0]))
    stores[-1].start()
    stores += [store_group(g) for g in range(blocks // group)]
    for store in stores:
        store.wait()


def reduce_back_kernel(
    meta, got, stat, gain, dz_in, pre_in, x_in, small, keep, send, gain_out, shift_out, bias_out, squeeze,
    dz, pre, x, sems, *, blocks, rows
):
    slab = rows * COLS
    fetches = [
        pltpu.make_async_copy(source, target, sems.at[k])
        for k, (source, target) in enumerate(((dz_in, dz), (pre_in, pre), (x_in, x)))
    ]
    for fetch in fetches:
        fetch.start()
    sums = jnp.sum(got[...], 0)
    share = got.shape[1] - 8
    squeeze[...] = jnp.zeros_like(squeeze)
    squeeze[:share, :] = sums[8:]
    shift_sum, gain_sum = row_of(sums, 0, 2), row_of(sums, 2, 2)
    shift_out[...] = shift_sum
    gain_out[...] = gain_sum
    bias_out[...] = row_of(sums, 4, 4)
    a, b, d = back_terms(stat, gain[...], shift_sum, gain_sum)
    fetches[0].wait()
    fetches[1].wait()

    def step(image, carry):
        own = pl.ds(pl.multiple_of(image * slab, slab), slab)
        mask = wide(inside(meta, image, 0, rows), 256)
        small[own, :] = (mask * (a * dz[own, :] + b + d * pre[own, :])).astype(BF16)
        return carry

    lax.fori_loop(0, blocks, step, 0)
    fetches[2].wait()
    for ref, core in ((send, 1 - meta[2]), (keep, meta[2])):
        lanes = pl.ds(pl.multiple_of(core * 512, 512), 512)
        value = dot(x[:, lanes], small[...], ((0,), (0,))).astype(ref.dtype)
        for q in range(2):
            ref[q * 512 : q * 512 + 512, :] = value[:, q * 128 : q * 128 + 128]
        clear_from(ref, 1024)


def input_kernel(meta, small, w, grad, out, token, *, blocks, rows):
    slab = rows * COLS
    token[...] = jnp.zeros_like(token)
    group = 4

    def step(g, carry):
        many = pl.ds(pl.multiple_of(g * group * slab, group * slab), group * slab)
        for k in range(4):
            lanes = slice(k * 256, k * 256 + 256)
            value = dot(small[many, :], w[lanes, :], ((1,), (1,)))
            for j in range(group):
                image = g * group + j
                own = pl.ds(pl.multiple_of(image * slab, slab), slab)
                mask = wide(inside(meta, image, 0, rows), 256)
                out[own, lanes] = (
                    (value[j * slab : (j + 1) * slab] + grad[own, lanes]) * mask
                ).astype(BF16)
        return carry

    lax.fori_loop(0, blocks // group, step, 0)


def total_kernel(meta, *refs, places, large, less, other):
    arrays = len(places)
    *outs, wide_part, narrow_part, expand, excite, split, reduce, squeeze, sems = refs[arrays + 5 * other :]
    share = squeeze.shape[1]
    behind = 2 * large + less
    core = meta[2] ^ other
    for part, chips in zip(refs[:arrays], places):
        for k, chip in enumerate(chips):
            at = meta[4] ^ chip
            for q in range(2):
                wide_part[q, pl.ds(pl.multiple_of(at * large, large), large), :] = part[
                    k, q * large : q * large + large, :
                ]
            narrow_part[pl.ds(pl.multiple_of(at * less, less), less), :] = part[k, 2 * large : behind, :]
            squeeze[at] = part[k, behind:, :].astype(F32)[:share]
    expand_out, excite_out, split_out, reduce_out, squeeze_out = outs
    copies = []

    def send(source, target):
        copies.append(pltpu.make_async_copy(source, target, sems.at[len(copies)]))
        copies[-1].start()

    send(squeeze, squeeze_out.at[:, core])
    for q in range(2):
        reduce[:, q * 128 : q * 128 + 128] = narrow_part[q * 512 : q * 512 + 512].astype(F32)
    send(reduce, reduce_out.at[pl.ds(pl.multiple_of(core * 512, 512), 512)])
    for dy in range(3):
        for dx in range(3):
            first = (3 * dy + dx) * 128
            for q in range(2):
                split[dy, dx, :, q * 128 : q * 128 + 128] = wide_part[q, first : first + 128].astype(F32)
        send(split.at[dy], split_out.at[dy, :, core])
    for q in range(2):
        for k in range(2):
            first = 1152 + k * 256
            at = k * 256 + q * 128
            expand[:, at : at + 128] = wide_part[q, first : first + 256].astype(F32)
        excite[:, q * 128 : q * 128 + 128] = wide_part[q, 1664:1792].astype(F32)
    send(expand, expand_out.at[:, pl.ds(pl.multiple_of(core * 512, 512), 512)])
    send(excite, excite_out.at[:, pl.ds(pl.multiple_of(core * 256, 256), 256)])
    for copy in copies:
        copy.wait()


def body(
    inputs,
    image_class,
    weight_reduce,
    gain_reduce,
    shift_reduce,
    weight_split,
    gain_split,
    shift_split,
    weight_squeeze,
    gain_squeeze,
    shift_squeeze,
    weight_excite,
    bias_excite,
    weight_expand,
    gain_expand,
    shift_expand,
    cotangent,
):
    blocks, rows, cols, channels = inputs.shape
    mid = weight_reduce.shape[1]
    inter = weight_squeeze.shape[1]
    count = device_count()
    pixels = blocks * rows * cols
    slab = rows * cols
    edge = blocks * cols
    share = mid // count
    images = blocks * lax.axis_size("batch")
    meta = jnp.concatenate(
        [
            (lax.axis_index("narrow") * rows).astype(jnp.int32)[None],
            lax.axis_index("batch").astype(jnp.int32)[None],
            (lax.axis_index("narrow") % 2).astype(jnp.int32)[None],
            (lax.axis_index("narrow") // 2 % 2).astype(jnp.int32)[None],
            (lax.axis_index(ALL) // 2).astype(jnp.int32)[None],
            image_class,
        ]
    )
    x = inputs.reshape(pixels, channels)
    cot = cotangent.reshape(pixels, channels)
    row = lambda v: v.reshape(1, -1)
    gain1, shift1 = row(gain_reduce), row(shift_reduce)
    gain2, shift2 = row(gain_split), row(shift_split)
    gain3, shift3 = row(gain_expand), row(shift_expand)
    gain_sq, shift_sq = row(gain_squeeze), row(shift_squeeze)
    sizes = dict(blocks=blocks, rows=rows)
    small = 2 * pixels * channels * mid
    large = 2 * pixels * 9 * 128 * 512

    pre1, top, bottom, pay = call(
        reduce_kernel,
        [((pixels, mid), F32), ((2 * edge, mid), F32), ((2 * edge, mid), F32), ((count, 8, LANES), F32)],
        [meta, x, weight_reduce],
        [((3, 8, mid), F32)],
        flops=small,
        local="in out",
        **sizes,
    )
    low, high = halo(top, bottom)
    hid1, pre2, pay, stat1 = call(
        split_kernel,
        [
            ((3, blocks, slab + 4 * cols, mid), BF16, "hbm"),
            ((pixels + 2 * edge, 2 * mid), F32),
            ((count, 8, LANES), F32),
            ((8, mid), F32),
        ],
        [meta, exchange(pay), pre1, low, high, gain1, shift1, weight_split],
        [((2, 8, 2 * mid), F32), ((3, blocks, slab + 4 * cols, mid), BF16), pltpu.SemaphoreType.DMA],
        raw_out=(0,),
        flops=large,
        local="in out",
        **sizes,
    )
    hid2, pooled, pay, stat2 = call(
        pool_kernel,
        [
            ((pixels, 2 * mid), BF16),
            ((blocks, mid), F32),
            ((count, blocks, inter), F32),
            ((8, 2 * mid), F32),
        ],
        [meta, exchange(pay), stat1, pre2, gain2, shift2, weight_squeeze],
        local="in out",
        **sizes,
    )
    mix, pre3, att, hsq, znorm, zall, pay, stat_sq = call(
        expand_kernel,
        [
            ((pixels, mid), BF16),
            ((pixels, channels), BF16),
            ((blocks, 2 * mid), F32),
            ((blocks, inter), F32),
            ((images, inter), F32),
            ((images, inter), F32),
            ((count, 16, LANES), F32),
            ((8, inter), F32),
        ],
        [
            meta,
            exchange(pay),
            hid2,
            gain_sq,
            shift_sq,
            weight_excite,
            row(bias_excite),
            weight_expand,
        ],
        [((2, 8, channels), F32)],
        flops=small,
        parts=lax.axis_size("narrow"),
        local="in out",
        **sizes,
    )
    out, grad_res, pay, stat3 = call(
        residual_kernel,
        [
            ((pixels, channels), BF16),
            ((pixels, channels), F32),
            ((count, 16, LANES), F32),
            ((8, channels), F32),
        ],
        [meta, exchange(pay), stat1, x, pre3, cot, gain3, shift3],
        [((2, 8, channels), F32)],
        local="in out",
        **sizes,
    )
    gexp, gmix, top, bottom, glog, keep6, send6, gain3_grad, shift3_grad = call(
        mixture_kernel,
        [
            ((pixels, channels), BF16),
            ((pixels, mid), BF16),
            ((edge, mid), BF16),
            ((edge, mid), BF16),
            ((blocks, 2 * mid), F32),
            ((blocks // 2, inter), F32),
            ((blocks // 2, inter), F32),
            ((1, channels), F32),
            ((1, channels), F32),
        ],
        [meta, exchange(pay), stat3, pre3, grad_res, gain3, weight_expand, hid2, att, weight_excite],
        [((blocks, inter), F32)],
        flops=small,
        local="in out",
        **sizes,
    )
    lowm, highm = halo(top, bottom)
    keep3, send3 = call(
        expand_grad_kernel,
        [((2, 2 * mid + inter, LANES), F32), ((2, 2 * mid + inter, LANES), BF16)],
        [meta, mix, gexp, hsq, glog],
        flops=small,
        local="in out",
    )
    (pay,) = call(
        logits_kernel,
        [((count, blocks // 2, inter), F32)],
        [meta, keep6, swap(send6, 1)],
        after=(lowm, highm, send3),
        local="in out",
    )
    dz2, gpool, squeeze_part, pay, gain_sq_grad, shift_sq_grad = call(
        hidden_kernel,
        [
            ((pixels, 2 * mid), F32),
            ((blocks, mid), F32),
            ((mid, inter), F32),
            ((count, 8, LANES), F32),
            ((1, inter), F32),
            ((1, inter), F32),
        ],
        [
            meta,
            exchange(pay),
            znorm,
            zall,
            gain_sq,
            stat_sq,
            pooled,
            weight_squeeze,
            att,
            gmix,
            pre2,
            stat2,
            gain2,
            shift2,
        ],
        [((2, 8, 2 * mid), F32), ((images, inter), F32)],
        parts=lax.axis_size("narrow"),
        local="in out",
        **sizes,
    )
    dz1, keep2, send2, pay, gain2_grad, shift2_grad = call(
        conv_kernel,
        [
            ((pixels, mid), F32, "hbm"),
            ((2, 9 * 128, LANES), F32, "hbm"),
            ((2, 9 * 128, LANES), BF16, "hbm"),
            ((count, 8 + share, LANES), F32, "hbm"),
            ((1, 2 * mid), F32, "hbm"),
            ((1, 2 * mid), F32, "hbm"),
        ],
        [
            meta,
            exchange(pay),
            stat2,
            gain2,
            shift2,
            dz2,
            pre2,
            lowm,
            highm,
            att,
            gpool,
            weight_split,
            pre1,
            stat1,
            gain1,
            shift1,
            glog,
            squeeze_part,
            hid1,
        ],
        [
            ((3, blocks, slab + 2 * cols, 2 * mid), BF16),
            ((2, 8, mid), F32),
            ((pixels, mid), F32),
            ((2, 9 * 128, LANES), F32),
            ((2, 9 * 128, LANES), BF16),
            ((count, 8 + share, LANES), F32),
            ((1, 2 * mid), F32),
            ((1, 2 * mid), F32),
            pltpu.SemaphoreType.DMA((5 + blocks // 4,)),
        ],
        raw_out=range(6),
        flops=2 * large,
        local="in out",
        **sizes,
    )
    chips = count // 2
    large, less = (-(-rows_in // (chips * 16)) * 16 for rows_in in (9 * 128 + 2 * mid + inter, channels))
    keep, send, token = call(
        add_kernel,
        [((chips * large, LANES), F32), ((chips * large, LANES), BF16), TOKEN],
        [meta, keep2, swap(send2, 1), keep3, swap(send3, 1)],
    )
    small1, keep1, send1, gain1_grad, shift1_grad, bias_grad, squeeze_share = call(
        reduce_back_kernel,
        [
            ((pixels, mid), BF16),
            ((chips * less, LANES), F32),
            ((chips * less, LANES), BF16),
            ((1, mid), F32),
            ((1, mid), F32),
            ((1, 2 * mid), F32),
            ((16, inter), F32),
        ],
        [meta, exchange(pay), stat1, gain1, dz1, pre1, x],
        [
            ((pixels, mid), F32),
            ((pixels, mid), F32),
            ((pixels, channels), BF16),
            pltpu.SemaphoreType.DMA((3,)),
        ],
        raw_in=(4, 5, 6),
        flops=small,
        after=(token,),
        local="in out",
        **sizes,
    )
    first = len(stages()[-1])
    blocks = call(
        pack_kernel,
        [((chips // first, large + less, LANES), BF16)] * first,
        [meta, keep, swap(send, 2), keep1, swap(send1, 1)],
        [((chips * large, LANES), BF16), ((chips * less, LANES), BF16)],
        places=slots(),
    )
    input_grad, token = call(
        input_kernel,
        [((pixels, channels), BF16, "hbm"), TOKEN],
        [meta, small1, weight_reduce, grad_res],
        flops=small,
        **sizes,
    )
    shared = scatter_chips(meta, blocks, 2 * large + less, large, squeeze_share, [token])
    parts, places = gather_chips(shared)
    swapped = [swap(part, 1) for part in parts]
    totals = ()
    for other, half in enumerate((parts, swapped)):
        args = [meta, *half, *totals]
        totals = call(
            total_kernel,
            [
                ((mid, channels), F32, "hbm"),
                ((inter, 2 * mid), F32, "hbm"),
                (weight_split.shape, F32, "hbm"),
                ((channels, mid), F32, "hbm"),
                ((chips, 2, share, inter), F32, "hbm"),
            ],
            args,
            [
                ((2, chips * large, LANES), BF16),
                ((chips * less, LANES), BF16),
                ((mid, channels // 2), F32),
                ((inter, mid), F32),
                ((3, 3, 128, mid), F32),
                ((channels // 2, mid), F32),
                ((chips, share, inter), F32),
                pltpu.SemaphoreType.DMA((7,)),
            ],
            local="in",
            raw_in=range(1 + len(half), len(args)),
            raw_out=range(5),
            aliases={1 + len(half) + k: k for k in range(len(totals))},
            places=places,
            large=large,
            less=less,
            other=other,
        )
    expand_total, excite_total, split_total, reduce_total, squeeze_total = totals
    squeeze_total = squeeze_total.reshape(mid, inter)
    flat = lambda v: v.reshape(-1)
    return (
        out.reshape(inputs.shape),
        input_grad.reshape(inputs.shape),
        reduce_total,
        flat(gain1_grad),
        flat(shift1_grad),
        split_total,
        flat(gain2_grad),
        flat(shift2_grad),
        squeeze_total,
        flat(gain_sq_grad),
        flat(shift_sq_grad),
        excite_total,
        flat(bias_grad),
        expand_total,
        flat(gain3_grad),
        flat(shift3_grad),
    )


def solution(mesh):
    rows = P("batch", "narrow", None, None)
    return jax.shard_map(
        body,
        mesh=mesh,
        in_specs=(rows, P("batch")) + (P(),) * 14 + (rows,),
        out_specs=(rows, rows) + (P(),) * 14,
        check_vma=False,
    )
```

```python
import functools
from itertools import product

import jax
import jax.numpy as jnp
from jax import lax
from jax.experimental import pallas as pl
from jax.experimental.pallas import tpu as pltpu
from jax.sharding import PartitionSpec as P

EPSILON = 1e-05
HIGHEST = lax.Precision.HIGHEST
ALL = ("batch", "narrow")
F32 = jnp.float32
BF16 = jnp.bfloat16
COLS = 16
LANES = 128
TOKEN = ((8, LANES), F32, "hbm")


def device_count():
    return lax.axis_size("batch") * lax.axis_size("narrow")


def halo(top, bottom):
    count = lax.axis_size("narrow")
    low = lax.ppermute(bottom, "narrow", [(i, i + 1) for i in range(count - 1)])
    high = lax.ppermute(top, "narrow", [(i + 1, i) for i in range(count - 1)])
    return low, high


def exchange(block):
    return lax.all_to_all(block, ALL, 0, 0)


def swap(block, bit):
    count = lax.axis_size("narrow")
    return lax.ppermute(block, "narrow", [(i, i ^ bit) for i in range(count)])


def stages():
    bits = list(range(device_count().bit_length() - 2, 0, -1))
    pairs = [bits[k : k + 2] for k in range(0, len(bits), 2)]
    return [
        [sum(bit << pair[k] for k, bit in enumerate(pick)) for pick in product((0, 1), repeat=len(pair))]
        for pair in pairs
    ]


def partners(blocks, steps):
    count = device_count()
    return [
        lax.ppermute(block, ALL, [(i, i ^ step) for i in range(count)])
        for block, step in zip(blocks[1:], steps[1:])
    ]


def slots():
    order = [0]
    for steps in reversed(stages()):
        order = [place ^ (step >> 1) for place in order for step in steps]
    return order


def scatter_chips(meta, blocks, rows, large, extra, after):
    order = list(reversed(stages()))
    for k, steps in enumerate(order):
        last = k + 1 == len(order)
        count = 1 if last else len(order[k + 1])
        out_rows = rows + extra.shape[0] if last else rows
        outs = [((blocks[0].shape[0] // count, out_rows, LANES), BF16)] * count
        blocks = call(
            sum_kernel,
            outs,
            [meta, blocks[0], *partners(blocks, steps)] + ([extra] if last else []),
            after=() if k else after,
            large=0 if k else large,
            others=[step >> 1 & 1 for step in steps],
        )
    return blocks[0]


def gather_chips(share):
    block, places = share, [0]
    for steps in stages():
        blocks = [block] + partners([block] * len(steps), steps)
        lists = [[place ^ (step >> 1) for place in places] for step in steps]
        block, places = jnp.concatenate(blocks), sum(lists, [])
    return blocks, lists


def half_terms(center, inv, gain, shift):
    scale = 0.5 * inv * gain
    return scale, 0.5 * shift - scale * center


def silu_of_half(half):
    tanh = jnp.tanh(half)
    more = 1.0 + tanh
    silu = half * more
    return silu, more + silu * (1.0 - tanh)


def wide(mask, width):
    return jnp.concatenate([mask] * (width // LANES), axis=1) if width > LANES else mask


def inside(meta, image, start, count):
    pixel = lax.broadcasted_iota(jnp.int32, (count * COLS, LANES), 0)
    row = (pixel >> 4) + (meta[0] + start)
    col = pixel & (COLS - 1)
    side = 12 + 2 * meta[5 + image]
    return jnp.where((row < side) & (row >= 0) & (col < side), 1.0, 0.0).astype(F32)


def area_of(meta, image):
    side = (12 + 2 * meta[5 + image]).astype(F32)
    return side * side


def row_of(block, first, count):
    return jnp.concatenate([block[first + k : first + k + 1] for k in range(count)], axis=1)


def put_row(ref, first, vector):
    for k in range(vector.shape[1] // LANES):
        ref[0, first + k : first + k + 1, :] = vector[:, k * LANES : (k + 1) * LANES]


def put_sums(ref, rows, acc, center, inv):
    plain = total(acc[0])
    put_row(ref, 0, plain)
    put_row(ref, rows, (total(acc[1]) - center * plain) * inv)


def spread(ref):
    block = ref[0]

    def step(k, carry):
        ref[k] = block
        return carry

    lax.fori_loop(1, ref.shape[0], step, 0, unroll=31)


def fold(values):
    return jnp.sum(values.reshape(-1, 8, values.shape[-1]), 0)


def clear_from(ref, first):
    if ref.shape[0] > first:
        ref[first:, :] = jnp.zeros((ref.shape[0] - first, LANES), ref.dtype)


def own_of_tall(image, slab):
    return pl.ds(pl.multiple_of(image * (slab + 2 * COLS) + COLS, COLS), slab)


def total(block):
    return jnp.sum(block, 0, keepdims=True)


def stats(totals, squares, counted):
    center = totals / counted
    return center, lax.rsqrt(squares / counted - center * center + EPSILON)


def shifted(values):
    count, width = values.shape
    col = lax.broadcasted_iota(jnp.int32, (count, LANES), 0) & (COLS - 1)
    has_left = wide(jnp.where(col > 0, 1.0, 0.0).astype(F32), width)
    has_right = wide(jnp.where(col < COLS - 1, 1.0, 0.0).astype(F32), width)
    left = pltpu.roll(values, 1, 0) * has_left
    right = pltpu.roll(values, count - 1, 0) * has_right
    return left.astype(BF16), values.astype(BF16), right.astype(BF16)


def dot(a, b, dims=((1,), (0,)), precision=None):
    return lax.dot_general(a, b, (dims, ((), ())), precision=precision, preferred_element_type=F32)


def whole(shape):
    return pl.BlockSpec(shape, lambda step: (0,) * len(shape))


def call(
    kernel, outs, args, scratch=(), megabytes=24, flops=0, after=(), local="", raw_in=(), raw_out=(), aliases=None, **sizes
):
    moved = sum(a.size * a.dtype.itemsize for a in args) + sum(
        functools.reduce(lambda x, y: x * y, o[0]) * jnp.dtype(o[1]).itemsize for o in outs
    )
    count = len(args)
    vmem = pl.BlockSpec(memory_space=pltpu.VMEM)
    anywhere = pl.BlockSpec(memory_space=pl.ANY)
    in_hbm = lambda a: pltpu.with_memory_space_constraint(a, pltpu.HBM)
    args = [in_hbm(a) if k in raw_in else a for k, a in enumerate(args)]
    after = [in_hbm(a) if a.shape == TOKEN[0] else a for a in after]

    def run(*refs):
        kernel(*refs[:count], *refs[count + len(after) :], **sizes)

    def spec(place, shape, kept, raws):
        return anywhere if place in raws else vmem if kept else whole(shape)

    return pl.pallas_call(
        run,
        grid=() if local == "in out" else (1,),
        out_shape=[
            pltpu.HBM(o[0], o[1]) if len(o) > 2 else jax.ShapeDtypeStruct(o[0], o[1]) for o in outs
        ],
        in_specs=[pl.BlockSpec(memory_space=pltpu.SMEM)]
        + [spec(k, a.shape, "in" in local, raw_in) for k, a in enumerate(args) if k]
        + [anywhere] * len(after),
        out_specs=[spec(k, o[0], "out" in local, raw_out) for k, o in enumerate(outs)],
        input_output_aliases=aliases or {},
        scratch_shapes=[pltpu.VMEM(*entry) if isinstance(entry, tuple) else entry for entry in scratch],
        compiler_params=pltpu.CompilerParams(vmem_limit_bytes=megabytes << 20),
        cost_estimate=pl.CostEstimate(flops=flops, bytes_accessed=moved, transcendentals=0),
    )(*args, *after)


def reduce_kernel(meta, x, w, pre, top, bottom, pay, acc, *, blocks, rows):
    slab = rows * COLS
    acc[...] = jnp.zeros_like(acc)
    group = 4

    def step(g, carry):
        base = pl.multiple_of(g * group * slab, group * slab)
        out = dot(x[pl.ds(base, group * slab), :], w[...])
        for j in range(group):
            image = g * group + j
            mask = inside(meta, image, 0, rows)
            part = out[j * slab : (j + 1) * slab] * wide(mask, out.shape[1])
            pre[pl.ds(pl.multiple_of(image * slab, slab), slab), :] = part
            edge = pl.ds(pl.multiple_of(image * 2 * COLS, 2 * COLS), 2 * COLS)
            top[edge, :] = part[: 2 * COLS]
            bottom[edge, :] = part[slab - 2 * COLS :]
            acc[0] += fold(part)
            acc[1] += fold(part * part)
            acc[2, :, :LANES] += fold(mask)
        return carry

    lax.fori_loop(0, blocks // group, step, 0, unroll=True)
    put_row(pay, 0, total(acc[0]))
    put_row(pay, 2, total(acc[1]))
    put_row(pay, 4, total(acc[2, :, :LANES]))
    pay[0, 5:8, :] = jnp.zeros((3, LANES), F32)
    spread(pay)


def split_kernel(
    meta, got, pre, low, high, gain, shift, w, hid_out, out, pay, stat, acc, hid, sem, *, blocks, rows
):
    slab = rows * COLS
    sums = jnp.sum(got[...], 0)
    counted = row_of(jnp.concatenate([sums[4:5]] * 2, 0), 0, 2)
    center, inv = stats(row_of(sums, 0, 2), row_of(sums, 2, 2), counted)
    stat[...] = jnp.zeros_like(stat)
    stat[0:1] = center
    stat[1:2] = inv
    stat[2:3] = counted
    scale, offset = half_terms(center, inv, gain[...], shift[...])

    def prepare(i, carry):
        edge = pl.ds(pl.multiple_of(i * 2 * COLS, 2 * COLS), 2 * COLS)
        own = pl.ds(pl.multiple_of(i * slab, slab), slab)
        mask = inside(meta, i, -2, rows + 4)
        for k in range(2):
            lanes = slice(k * LANES, k * LANES + LANES)
            tall = jnp.concatenate([low[edge, lanes], pre[own, lanes], high[edge, lanes]], axis=0)
            silu, _ = silu_of_half(tall * scale[:, lanes] + offset[:, lanes])
            left, middle, right = shifted(silu * mask)
            hid[0, i, :, lanes] = left
            hid[1, i, :, lanes] = middle
            hid[2, i, :, lanes] = right
        return carry

    lax.fori_loop(0, blocks, prepare, 0, unroll=4)
    copy = pltpu.make_async_copy(hid, hid_out, sem)
    copy.start()
    acc[...] = jnp.zeros_like(acc)
    group = 4
    tall = slab + 2 * COLS

    def step(g, carry):
        for half in range(2):
            lanes = slice(half * 128, half * 128 + 128)
            outs = slice(half * 256, half * 256 + 256)
            lhs = jnp.concatenate(
                [
                    hid[dx, pl.ds(g * group, group), dy * COLS : dy * COLS + tall, lanes].reshape(
                        group * tall, 128
                    )
                    for dy in range(3)
                    for dx in range(3)
                ],
                axis=1,
            )
            value = dot(lhs, w[:, :, half].reshape(9 * 128, 256))
            for j in range(group):
                image = g * group + j
                mask = inside(meta, image, -1, rows + 2)
                part = value[j * tall : (j + 1) * tall] * wide(mask, 256)
                out[pl.ds(pl.multiple_of(image * tall, tall), tall), outs] = part
                part = part[COLS : COLS + slab]
                acc[0, :, outs] += fold(part)
                acc[1, :, outs] += fold(part * part)
        return carry

    lax.fori_loop(0, blocks // group, step, 0, unroll=True)
    put_row(pay, 0, total(acc[0]))
    put_row(pay, 4, total(acc[1]))
    spread(pay)
    copy.wait()


def pool_kernel(
    meta, got, stat, pre, gain, shift, w, hid, pooled, pay, stat2, *, blocks, rows
):
    slab = rows * COLS
    sums = jnp.sum(got[...], 0)
    counted = jnp.concatenate([stat[2:3]] * 2, axis=1)
    center, inv = stats(row_of(sums, 0, 4), row_of(sums, 4, 4), counted)
    stat2[...] = jnp.zeros_like(stat2)
    stat2[0:1] = center
    stat2[1:2] = inv
    stat2[2:3] = counted
    scale, offset = half_terms(center, inv, gain[...], shift[...])

    def step(i, carry):
        own = pl.ds(pl.multiple_of(i * slab, slab), slab)
        mask = inside(meta, i, 0, rows)
        summed = [None, None]
        for k in range(4):
            lanes = slice(k * LANES, k * LANES + LANES)
            silu, _ = silu_of_half(pre[own_of_tall(i, slab), lanes] * scale[:, lanes] + offset[:, lanes])
            value = (silu * mask).astype(BF16)
            hid[own, lanes] = value
            part = fold(value.astype(F32))
            summed[k % 2] = part if k < 2 else summed[k % 2] + part
        pooled[pl.ds(i, 1), :] = total(jnp.concatenate(summed, axis=1)) / area_of(meta, i)
        return carry

    lax.fori_loop(0, blocks, step, 0, unroll=4)
    pay[0] = dot(pooled[...], w[...], precision=HIGHEST)
    spread(pay)


def squeeze_stats(block):
    return stats(total(block), total(block * block), float(block.shape[0]))


def expand_kernel(
    meta, got, hid, gain, shift, we, bias, w, mix, pre, att, hsq, znorm, zall, pay, stat_sq, acc, *, blocks, rows, parts
):
    slab = rows * COLS
    bands = got.shape[0] // parts
    for b in range(bands):
        block = got[b * parts]
        for k in range(1, parts):
            block = block + got[b * parts + k]
        znorm[b * blocks : (b + 1) * blocks, :] = block
    center, inv = squeeze_stats(znorm[...])
    stat_sq[...] = jnp.zeros_like(stat_sq)
    stat_sq[0:1] = center
    stat_sq[1:2] = inv
    normed = (znorm[...] - center) * inv
    znorm[...] = normed
    zall[...] = normed * gain[...] + shift[...]
    own_z = zall[pl.ds(pl.multiple_of(meta[1] * blocks, blocks), blocks), :]
    hidden = own_z * jax.nn.sigmoid(own_z)
    hsq[...] = hidden
    logits = dot(hidden, we[...], precision=HIGHEST) + bias[...]
    first = logits[:, :256]
    second = logits[:, 256:]
    ceiling = jnp.maximum(first, second)
    exp_first = jnp.exp(first - ceiling)
    exp_second = jnp.exp(second - ceiling)
    att[:, :256] = exp_first / (exp_first + exp_second)
    att[:, 256:] = exp_second / (exp_first + exp_second)
    acc[...] = jnp.zeros_like(acc)
    group = 4

    def step(g, carry):
        for j in range(group):
            image = g * group + j
            own = pl.ds(pl.multiple_of(image * slab, slab), slab)
            weights = att[pl.ds(image, 1), :]
            mix[own, :] = (
                weights[:, :256] * hid[own, :256].astype(F32)
                + weights[:, 256:] * hid[own, 256:].astype(F32)
            ).astype(BF16)
        many = pl.ds(pl.multiple_of(g * group * slab, group * slab), group * slab)
        for k in range(4):
            lanes = slice(k * 256, k * 256 + 256)
            value = dot(mix[many, :], w[:, lanes]).astype(BF16)
            pre[many, lanes] = value
            value = value.astype(F32)
            acc[0, :, lanes] += fold(value)
            acc[1, :, lanes] += fold(value * value)
        return carry

    lax.fori_loop(0, blocks // group, step, 0, unroll=True)
    put_row(pay, 0, total(acc[0]))
    put_row(pay, 8, total(acc[1]))
    spread(pay)


def residual_kernel(
    meta, got, stat, x, pre, cot, gain, shift, out, grad, pay, stat3, acc, *, blocks, rows
):
    slab = rows * COLS
    sums = jnp.sum(got[...], 0)
    counted = jnp.concatenate([stat[2:3]] * 4, axis=1)
    center, inv = stats(row_of(sums, 0, 8), row_of(sums, 8, 8), counted)
    stat3[...] = jnp.zeros_like(stat3)
    stat3[0:1] = center
    stat3[1:2] = inv
    stat3[2:3] = counted
    acc[...] = jnp.zeros_like(acc)
    scale, offset = half_terms(center, inv, gain[...], shift[...])

    def step(i, carry):
        own = pl.ds(pl.multiple_of(i * slab, slab), slab)
        mask = inside(meta, i, 0, rows)
        half_mask = 0.5 * mask
        for k in range(8):
            lanes = slice(k * LANES, k * LANES + LANES)
            values = pre[own, lanes].astype(F32)
            half = values * scale[:, lanes] + offset[:, lanes] + 0.5 * x[own, lanes].astype(F32)
            silu, slope = silu_of_half(half)
            out[own, lanes] = (silu * mask).astype(BF16)
            back = cot[own, lanes].astype(F32) * half_mask * slope
            grad[own, lanes] = back
            acc[0, :, lanes] += fold(back)
            acc[1, :, lanes] += fold(back * values)
        return carry

    lax.fori_loop(0, blocks, step, 0)
    put_sums(pay, 8, acc, center, inv)
    spread(pay)


def back_terms(stat, gain, shift_sum, gain_sum):
    center, inv, counted = stat[0:1], stat[1:2], stat[2:3]
    a = gain * inv
    d = -a * inv * (gain_sum / counted)
    b = -a * (shift_sum / counted) - d * center
    return a, b, d


def mixture_kernel(
    meta, got, stat3, pre, grad, gain, w, hid, att, we, gexp, gmix, top, bottom, glog, keep, send, gain_out, shift_out, hidden, *, blocks, rows
):
    slab = rows * COLS
    sums = jnp.sum(got[...], 0)
    shift_sum, gain_sum = row_of(sums, 0, 8), row_of(sums, 8, 8)
    shift_out[...] = shift_sum
    gain_out[...] = gain_sum
    a, b, d = back_terms(stat3, gain[...], shift_sum, gain_sum)
    group = 4

    def step(g, carry):
        many = pl.ds(pl.multiple_of(g * group * slab, group * slab), group * slab)
        for j in range(group):
            image = g * group + j
            own = pl.ds(pl.multiple_of(image * slab, slab), slab)
            mask = inside(meta, image, 0, rows)
            for k in range(8):
                lanes = slice(k * LANES, k * LANES + LANES)
                gexp[own, lanes] = (
                    mask
                    * (
                        a[:, lanes] * grad[own, lanes]
                        + b[:, lanes]
                        + d[:, lanes] * pre[own, lanes].astype(F32)
                    )
                ).astype(BF16)
        value = dot(gexp[many, :], w[...], ((1,), (1,))).astype(BF16)
        gmix[many, :] = value
        value = value.astype(F32)
        for j in range(group):
            image = g * group + j
            own = pl.ds(pl.multiple_of(image * slab, slab), slab)
            edge = pl.ds(pl.multiple_of(image * COLS, COLS), COLS)
            part = value[j * slab : (j + 1) * slab]
            top[edge, :] = part[:COLS].astype(BF16)
            bottom[edge, :] = part[slab - COLS :].astype(BF16)
            for half in range(2):
                lanes = slice(half * 256, half * 256 + 256)
                glog[pl.ds(image, 1), lanes] = total(fold(part * hid[own, lanes].astype(F32)))
        return carry

    lax.fori_loop(0, blocks // group, step, 0, unroll=True)
    first, second = att[:, :256], att[:, 256:]
    inner = first * glog[:, :256] + second * glog[:, 256:]
    glog[...] = jnp.concatenate(
        [first * (glog[:, :256] - inner), second * (glog[:, 256:] - inner)], axis=1
    )
    hidden[...] = dot(glog[...], we[...], ((1,), (1,)), HIGHEST)
    many = blocks // 2
    keep[...] = hidden[pl.ds(pl.multiple_of(meta[2] * many, many), many), :]
    send[...] = hidden[pl.ds(pl.multiple_of((1 - meta[2]) * many, many), many), :]


def logits_kernel(meta, keep, got, pay):
    pay[0] = keep[...] + got[...]
    spread(pay)


def expand_grad_kernel(meta, mix, gexp, hsq, glog, keep, send):
    for ref, core in ((send, 1 - meta[2]), (keep, meta[2])):
        lanes = pl.ds(pl.multiple_of(core * 512, 512), 512)
        value = dot(mix[...], gexp[:, lanes], ((0,), (0,))).astype(ref.dtype)
        lanes = pl.ds(pl.multiple_of(core * 256, 256), 256)
        excite = dot(hsq[...], glog[:, lanes], ((0,), (0,)), HIGHEST).astype(ref.dtype)
        for q in range(2):
            for k in range(2):
                first = k * 256 + q * 128
                ref[q, k * 256 : k * 256 + 256, :] = value[:, first : first + 128]
            ref[q, 512:, :] = excite[:, q * 128 : q * 128 + 128]


def add_kernel(meta, keep2, got2, keep3, got3, keep, send, token):
    first = keep2.shape[1]
    for ref, half in ((send, 1 - meta[3]), (keep, meta[3])):
        ref[:first, :] = (keep2[half] + got2[half].astype(F32)).astype(ref.dtype)
        last = first + keep3.shape[1]
        ref[first:last, :] = (keep3[half] + got3[half].astype(F32)).astype(ref.dtype)
        clear_from(ref, last)
    token[...] = jnp.zeros_like(token)


def pack_kernel(meta, keep, got, keep1, got1, *refs, places):
    *outs, flat, flat1 = refs
    held = outs[0].shape[0]
    large, small = flat.shape[0] // len(places), flat1.shape[0] // len(places)
    flat[...] = (keep[...] + got[...].astype(F32)).astype(BF16)
    flat1[...] = (keep1[...] + got1[...].astype(F32)).astype(BF16)
    for k, place in enumerate(places):
        chip = meta[4] ^ place
        out = outs[k // held]
        out[k % held, :large, :] = flat[pl.ds(pl.multiple_of(chip * large, large), large), :]
        out[k % held, large:, :] = flat1[pl.ds(pl.multiple_of(chip * small, small), small), :]


def sum_kernel(meta, *refs, large, others):
    ins, outs = refs[: len(others)], refs[len(others) :]
    if len(outs[0].shape) == 2:
        extra, *outs = outs
        outs[0][0, ins[0].shape[1] :, :] = extra[...].astype(BF16)
    held = outs[0].shape[0]

    def add(pick, first, last):
        value = None
        for ref in pick:
            part = ref[:, first:last, :].astype(F32)
            value = part if value is None else value + part
        return value.astype(BF16)

    def put(value, at, rows):
        for k, out in enumerate(outs):
            out[:, pl.ds(at, rows), :] = value[k * held : k * held + held]

    total_rows = ins[0].shape[1]
    if not large:
        put(add(ins, 0, total_rows), 0, total_rows)
        return
    for other in range(2):
        pick = [ref for ref, side in zip(ins, others) if side == other]
        put(add(pick, 0, large), pl.multiple_of((meta[3] ^ other) * large, large), large)
    put(add(ins, large, total_rows), 2 * large, total_rows - large)


def hidden_kernel(
    meta, got, znorm, zall, hsq_gain, stat_sq, pooled, wsq, att, gmix, pre, stat2, gain, shift,
    dz, gpool, squeeze, pay, gain_out, shift_out, acc, full, *, blocks, rows, parts
):
    slab = rows * COLS
    bands = got.shape[0] // parts
    many = blocks // 2
    for b in range(bands):
        for core in range(2):
            block = got[b * parts + core]
            for k in range(core + 2, parts, 2):
                block = block + got[b * parts + k]
            at = b * blocks + core * many
            full[at : at + many, :] = block
    z = zall[...]
    part = jax.nn.sigmoid(z)
    grad_z = full[...] * (part * (1.0 + z * (1.0 - part)))
    full[...] = grad_z
    images = float(bands * blocks)
    shift_sum = total(grad_z)
    gain_sum = total(grad_z * znorm[...])
    shift_out[...] = shift_sum
    gain_out[...] = gain_sum
    mine = pl.ds(pl.multiple_of(meta[1] * blocks, blocks), blocks)
    grad_pre = (
        hsq_gain[...]
        * stat_sq[1:2]
        * (full[mine, :] - shift_sum / images - znorm[mine, :] * (gain_sum / images))
    )
    squeeze[...] = dot(pooled[...], grad_pre, ((0,), (0,)), HIGHEST)
    gpool[...] = dot(grad_pre, wsq[...], ((1,), (1,)), HIGHEST)
    for i in range(blocks):
        gpool[i : i + 1, :] = gpool[i : i + 1, :] / area_of(meta, i)
    center, inv = stat2[0:1], stat2[1:2]
    acc[...] = jnp.zeros_like(acc)
    scale, offset = half_terms(center, inv, gain[...], shift[...])

    def step(i, carry):
        own = pl.ds(pl.multiple_of(i * slab, slab), slab)
        half_mask = 0.5 * inside(meta, i, 0, rows)
        weights = att[pl.ds(i, 1), :]
        pool = gpool[pl.ds(i, 1), :]
        for k in range(4):
            lanes = slice(k * LANES, k * LANES + LANES)
            mid = slice(k % 2 * LANES, k % 2 * LANES + LANES)
            mixed = gmix[own, mid].astype(F32)
            values = pre[own_of_tall(i, slab), lanes]
            _, slope = silu_of_half(values * scale[:, lanes] + offset[:, lanes])
            hidden = (mixed * weights[:, lanes] + pool[:, mid]).astype(BF16).astype(F32)
            back = hidden * half_mask * slope
            dz[own, lanes] = back
            acc[0, :, lanes] += fold(back)
            acc[1, :, lanes] += fold(back * values)
        return carry

    lax.fori_loop(0, blocks, step, 0, unroll=4)
    put_sums(pay, 4, acc, center, inv)
    spread(pay)


def conv_kernel(
    meta, got, stat2, gain2, shift2, dz, pre2, lowm, highm, att, gpool, w, pre, stat,
    gain, shift, glog, squeeze, hid, out_hbm, keep_hbm, send_hbm, pay_hbm, gain_hbm, shift_hbm, tall, acc,
    out, keep, send, pay, gain_out, shift_out, sems, *, blocks, rows
):
    slab = rows * COLS
    sums = jnp.sum(got[...], 0)
    shift_sum, gain_sum = row_of(sums, 0, 4), row_of(sums, 4, 4)
    shift_out[...] = shift_sum
    gain_out[...] = gain_sum
    a, b, d = back_terms(stat2, gain2[...], shift_sum, gain_sum)
    scale2, offset2 = half_terms(stat2[0:1], stat2[1:2], gain2[...], shift2[...])

    def prepare(i, carry):
        own = pl.ds(pl.multiple_of(i * slab, slab), slab)
        edge = pl.ds(pl.multiple_of(i * COLS, COLS), COLS)
        whole_image = pl.ds(pl.multiple_of(i * (slab + 2 * COLS), COLS), slab + 2 * COLS)
        mask = inside(meta, i, -1, rows + 2)
        weights = att[pl.ds(i, 1), :]
        pool = gpool[pl.ds(i, 1), :]
        for k in range(4):
            lanes = slice(k * LANES, k * LANES + LANES)
            mid = slice(k % 2 * LANES, k % 2 * LANES + LANES)

            def edge_grad(values, mixed, keep):
                _, slope = silu_of_half(values * scale2[:, lanes] + offset2[:, lanes])
                hidden = mixed[edge, mid].astype(F32) * weights[:, lanes] + pool[:, mid]
                return hidden.astype(BF16).astype(F32) * (0.5 * keep) * slope

            keep_low, keep_high = mask[:COLS], mask[slab + COLS :]
            values = pre2[whole_image, lanes]
            grads = jnp.concatenate(
                [
                    edge_grad(values[:COLS], lowm, keep_low),
                    dz[own, lanes],
                    edge_grad(values[slab + COLS :], highm, keep_high),
                ],
                axis=0,
            )
            back = mask * (a[:, lanes] * grads + b[:, lanes] + d[:, lanes] * values)
            left, middle, right = shifted(back)
            tall[0, i, :, lanes] = left
            tall[1, i, :, lanes] = middle
            tall[2, i, :, lanes] = right
        return carry

    lax.fori_loop(0, blocks, prepare, 0, unroll=4)

    def weights(dy, carry):
        rows_at = pl.ds(pl.multiple_of((dy + 1) * COLS, COLS), slab)
        for ref, core in ((send, 1 - meta[2]), (keep, meta[2])):
            lanes = pl.ds(pl.multiple_of(core * 128, 128), 128)
            wide_lanes = pl.ds(pl.multiple_of(core * 256, 256), 256)
            grads = tall[1, :, COLS : COLS + slab, wide_lanes].reshape(blocks * slab, 256)
            lhs = jnp.concatenate(
                [hid[dx, :, rows_at, lanes].reshape(blocks * slab, 128) for dx in range(3)], axis=1
            )
            value = dot(lhs, grads, ((0,), (0,))).astype(ref.dtype)
            at = pl.ds(pl.multiple_of(dy * 384, 384), 384)
            for q in range(2):
                ref[q, at, :] = value[:, q * 128 : q * 128 + 128]
        return carry

    lax.fori_loop(0, 3, weights, 0)
    stores = [
        pltpu.make_async_copy(send, send_hbm, sems.at[1]),
        pltpu.make_async_copy(keep, keep_hbm, sems.at[2]),
        pltpu.make_async_copy(gain_out, gain_hbm, sems.at[3]),
        pltpu.make_async_copy(shift_out, shift_hbm, sems.at[4]),
    ]
    for store in stores:
        store.start()
    acc[...] = jnp.zeros_like(acc)
    center, inv = stat[0:1], stat[1:2]
    scale, offset = half_terms(center, inv, gain[...], shift[...])
    group = 4

    def store_group(g):
        many = pl.ds(pl.multiple_of(g * group * slab, group * slab), group * slab)
        return pltpu.make_async_copy(out.at[many], out_hbm.at[many], sems.at[5 + g])

    def step(g, carry):
        for half in range(2):
            lanes = slice(half * 256, half * 256 + 256)
            outs = slice(half * 128, half * 128 + 128)
            taps = [(dy, dx) for dy in range(3) for dx in range(3)]
            lhs = jnp.concatenate(
                [
                    tall[
                        2 - dx, pl.ds(g * group, group), (2 - dy) * COLS : (2 - dy) * COLS + slab, lanes
                    ].reshape(group * slab, 256)
                    for dy, dx in taps
                ],
                axis=1,
            )
            rhs = jnp.concatenate([w[dy, dx, half] for dy, dx in taps], axis=1)
            value = dot(lhs, rhs, ((1,), (1,)))
            for j in range(group):
                image = g * group + j
                own = pl.ds(pl.multiple_of(image * slab, slab), slab)
                values = pre[own, outs]
                _, slope = silu_of_half(values * scale[:, outs] + offset[:, outs])
                back = value[j * slab : (j + 1) * slab] * (0.5 * inside(meta, image, 0, rows)) * slope
                out[own, outs] = back
                acc[0, :, outs] += fold(back)
                acc[1, :, outs] += fold(back * values)
        store_group(g).start()
        return carry

    lax.fori_loop(0, blocks // group, step, 0, unroll=True)
    put_sums(pay, 2, acc, center, inv)
    put_row(pay, 4, total(glog[...]))
    pay[0, 8:, :] = jnp.zeros((pay.shape[1] - 8, LANES), F32)
    spread(pay)
    share = pay.shape[1] - 8
    for n in range(pay.shape[0]):
        pay[n, 8:, :] = squeeze[n * share : (n + 1) * share, :]
    stores.append(pltpu.make_async_copy(pay, pay_hbm, sems.at[0]))
    stores[-1].start()
    stores += [store_group(g) for g in range(blocks // group)]
    for store in stores:
        store.wait()


def reduce_back_kernel(
    meta, got, stat, gain, dz_in, pre_in, x, small, keep, send, gain_out, shift_out, bias_out, squeeze,
    dz, pre, sems, *, blocks, rows
):
    slab = rows * COLS
    fetches = [
        pltpu.make_async_copy(source, target, sems.at[k])
        for k, (source, target) in enumerate(((dz_in, dz), (pre_in, pre)))
    ]
    for fetch in fetches:
        fetch.start()
    sums = jnp.sum(got[...], 0)
    share = got.shape[1] - 8
    squeeze[...] = jnp.zeros_like(squeeze)
    squeeze[:share, :] = sums[8:]
    shift_sum, gain_sum = row_of(sums, 0, 2), row_of(sums, 2, 2)
    shift_out[...] = shift_sum
    gain_out[...] = gain_sum
    bias_out[...] = row_of(sums, 4, 4)
    a, b, d = back_terms(stat, gain[...], shift_sum, gain_sum)
    fetches[0].wait()
    fetches[1].wait()

    def step(image, carry):
        own = pl.ds(pl.multiple_of(image * slab, slab), slab)
        mask = wide(inside(meta, image, 0, rows), 256)
        small[own, :] = (mask * (a * dz[own, :] + b + d * pre[own, :])).astype(BF16)
        return carry

    lax.fori_loop(0, blocks, step, 0, unroll=4)
    for ref, core in ((send, 1 - meta[2]), (keep, meta[2])):
        lanes = pl.ds(pl.multiple_of(core * 512, 512), 512)
        value = dot(x[:, lanes], small[...], ((0,), (0,))).astype(ref.dtype)
        for q in range(2):
            ref[q * 512 : q * 512 + 512, :] = value[:, q * 128 : q * 128 + 128]
        clear_from(ref, 1024)


def input_kernel(meta, small, w, grad, out, token, *, blocks, rows):
    slab = rows * COLS
    token[...] = jnp.zeros_like(token)
    group = 4

    def step(g, carry):
        many = pl.ds(pl.multiple_of(g * group * slab, group * slab), group * slab)
        for k in range(4):
            lanes = slice(k * 256, k * 256 + 256)
            value = dot(small[many, :], w[lanes, :], ((1,), (1,)))
            for j in range(group):
                image = g * group + j
                own = pl.ds(pl.multiple_of(image * slab, slab), slab)
                mask = wide(inside(meta, image, 0, rows), 256)
                out[own, lanes] = (
                    (value[j * slab : (j + 1) * slab] + grad[own, lanes]) * mask
                ).astype(BF16)
        return carry

    lax.fori_loop(0, blocks // group, step, 0)


def total_kernel(meta, *refs, places, large, less, other):
    arrays = len(places)
    *outs, wide_part, narrow_part, expand, excite, split, reduce, squeeze, sems = refs[arrays + 5 * other :]
    share = squeeze.shape[1]
    behind = 2 * large + less
    core = meta[2] ^ other
    for part, chips in zip(refs[:arrays], places):
        for k, chip in enumerate(chips):
            at = meta[4] ^ chip
            for q in range(2):
                wide_part[q, pl.ds(pl.multiple_of(at * large, large), large), :] = part[
                    k, q * large : q * large + large, :
                ]
            narrow_part[pl.ds(pl.multiple_of(at * less, less), less), :] = part[k, 2 * large : behind, :]
            squeeze[at] = part[k, behind:, :].astype(F32)[:share]
    expand_out, excite_out, split_out, reduce_out, squeeze_out = outs
    copies = []

    def send(source, target):
        copies.append(pltpu.make_async_copy(source, target, sems.at[len(copies)]))
        copies[-1].start()

    send(squeeze, squeeze_out.at[:, core])
    for q in range(2):
        reduce[:, q * 128 : q * 128 + 128] = narrow_part[q * 512 : q * 512 + 512].astype(F32)
    send(reduce, reduce_out.at[pl.ds(pl.multiple_of(core * 512, 512), 512)])
    for dy in range(3):
        for dx in range(3):
            first = (3 * dy + dx) * 128
            for q in range(2):
                split[dy, dx, :, q * 128 : q * 128 + 128] = wide_part[q, first : first + 128].astype(F32)
        send(split.at[dy], split_out.at[dy, :, core])
    for q in range(2):
        for k in range(2):
            first = 1152 + k * 256
            at = k * 256 + q * 128
            expand[:, at : at + 128] = wide_part[q, first : first + 256].astype(F32)
        excite[:, q * 128 : q * 128 + 128] = wide_part[q, 1664:1792].astype(F32)
    send(expand, expand_out.at[:, pl.ds(pl.multiple_of(core * 512, 512), 512)])
    send(excite, excite_out.at[:, pl.ds(pl.multiple_of(core * 256, 256), 256)])
    for copy in copies:
        copy.wait()


def body(
    inputs,
    image_class,
    weight_reduce,
    gain_reduce,
    shift_reduce,
    weight_split,
    gain_split,
    shift_split,
    weight_squeeze,
    gain_squeeze,
    shift_squeeze,
    weight_excite,
    bias_excite,
    weight_expand,
    gain_expand,
    shift_expand,
    cotangent,
):
    blocks, rows, cols, channels = inputs.shape
    mid = weight_reduce.shape[1]
    inter = weight_squeeze.shape[1]
    count = device_count()
    pixels = blocks * rows * cols
    slab = rows * cols
    edge = blocks * cols
    share = mid // count
    images = blocks * lax.axis_size("batch")
    meta = jnp.concatenate(
        [
            (lax.axis_index("narrow") * rows).astype(jnp.int32)[None],
            lax.axis_index("batch").astype(jnp.int32)[None],
            (lax.axis_index("narrow") % 2).astype(jnp.int32)[None],
            (lax.axis_index("narrow") // 2 % 2).astype(jnp.int32)[None],
            (lax.axis_index(ALL) // 2).astype(jnp.int32)[None],
            image_class,
        ]
    )
    x = inputs.reshape(pixels, channels)
    cot = cotangent.reshape(pixels, channels)
    row = lambda v: v.reshape(1, -1)
    gain1, shift1 = row(gain_reduce), row(shift_reduce)
    gain2, shift2 = row(gain_split), row(shift_split)
    gain3, shift3 = row(gain_expand), row(shift_expand)
    gain_sq, shift_sq = row(gain_squeeze), row(shift_squeeze)
    sizes = dict(blocks=blocks, rows=rows)
    small = 2 * pixels * channels * mid
    large = 2 * pixels * 9 * 128 * 512

    pre1, top, bottom, pay = call(
        reduce_kernel,
        [((pixels, mid), F32), ((2 * edge, mid), F32), ((2 * edge, mid), F32), ((count, 8, LANES), F32)],
        [meta, x, weight_reduce],
        [((3, 8, mid), F32)],
        flops=small,
        local="in out",
        **sizes,
    )
    low, high = halo(top, bottom)
    hid1, pre2, pay, stat1 = call(
        split_kernel,
        [
            ((3, blocks, slab + 4 * cols, mid), BF16, "hbm"),
            ((pixels + 2 * edge, 2 * mid), F32),
            ((count, 8, LANES), F32),
            ((8, mid), F32),
        ],
        [meta, exchange(pay), pre1, low, high, gain1, shift1, weight_split],
        [((2, 8, 2 * mid), F32), ((3, blocks, slab + 4 * cols, mid), BF16), pltpu.SemaphoreType.DMA],
        raw_out=(0,),
        flops=large,
        local="in out",
        **sizes,
    )
    hid2, pooled, pay, stat2 = call(
        pool_kernel,
        [
            ((pixels, 2 * mid), BF16),
            ((blocks, mid), F32),
            ((count, blocks, inter), F32),
            ((8, 2 * mid), F32),
        ],
        [meta, exchange(pay), stat1, pre2, gain2, shift2, weight_squeeze],
        local="in out",
        **sizes,
    )
    mix, pre3, att, hsq, znorm, zall, pay, stat_sq = call(
        expand_kernel,
        [
            ((pixels, mid), BF16),
            ((pixels, channels), BF16),
            ((blocks, 2 * mid), F32),
            ((blocks, inter), F32),
            ((images, inter), F32),
            ((images, inter), F32),
            ((count, 16, LANES), F32),
            ((8, inter), F32),
        ],
        [
            meta,
            exchange(pay),
            hid2,
            gain_sq,
            shift_sq,
            weight_excite,
            row(bias_excite),
            weight_expand,
        ],
        [((2, 8, channels), F32)],
        flops=small,
        parts=lax.axis_size("narrow"),
        local="in out",
        **sizes,
    )
    out, grad_res, pay, stat3 = call(
        residual_kernel,
        [
            ((pixels, channels), BF16),
            ((pixels, channels), F32),
            ((count, 16, LANES), F32),
            ((8, channels), F32),
        ],
        [meta, exchange(pay), stat1, x, pre3, cot, gain3, shift3],
        [((2, 8, channels), F32)],
        local="in out",
        **sizes,
    )
    gexp, gmix, top, bottom, glog, keep6, send6, gain3_grad, shift3_grad = call(
        mixture_kernel,
        [
            ((pixels, channels), BF16),
            ((pixels, mid), BF16),
            ((edge, mid), BF16),
            ((edge, mid), BF16),
            ((blocks, 2 * mid), F32),
            ((blocks // 2, inter), F32),
            ((blocks // 2, inter), F32),
            ((1, channels), F32),
            ((1, channels), F32),
        ],
        [meta, exchange(pay), stat3, pre3, grad_res, gain3, weight_expand, hid2, att, weight_excite],
        [((blocks, inter), F32)],
        flops=small,
        local="in out",
        **sizes,
    )
    lowm, highm = halo(top, bottom)
    keep3, send3 = call(
        expand_grad_kernel,
        [((2, 2 * mid + inter, LANES), F32), ((2, 2 * mid + inter, LANES), BF16)],
        [meta, mix, gexp, hsq, glog],
        flops=small,
        local="in out",
    )
    (pay,) = call(
        logits_kernel,
        [((count, blocks // 2, inter), F32)],
        [meta, keep6, swap(send6, 1)],
        after=(lowm, highm, send3),
        local="in out",
    )
    dz2, gpool, squeeze_part, pay, gain_sq_grad, shift_sq_grad = call(
        hidden_kernel,
        [
            ((pixels, 2 * mid), F32),
            ((blocks, mid), F32),
            ((mid, inter), F32),
            ((count, 8, LANES), F32),
            ((1, inter), F32),
            ((1, inter), F32),
        ],
        [
            meta,
            exchange(pay),
            znorm,
            zall,
            gain_sq,
            stat_sq,
            pooled,
            weight_squeeze,
            att,
            gmix,
            pre2,
            stat2,
            gain2,
            shift2,
        ],
        [((2, 8, 2 * mid), F32), ((images, inter), F32)],
        parts=lax.axis_size("narrow"),
        local="in out",
        **sizes,
    )
    dz1, keep2, send2, pay, gain2_grad, shift2_grad = call(
        conv_kernel,
        [
            ((pixels, mid), F32, "hbm"),
            ((2, 9 * 128, LANES), F32, "hbm"),
            ((2, 9 * 128, LANES), BF16, "hbm"),
            ((count, 8 + share, LANES), F32, "hbm"),
            ((1, 2 * mid), F32, "hbm"),
            ((1, 2 * mid), F32, "hbm"),
        ],
        [
            meta,
            exchange(pay),
            stat2,
            gain2,
            shift2,
            dz2,
            pre2,
            lowm,
            highm,
            att,
            gpool,
            weight_split,
            pre1,
            stat1,
            gain1,
            shift1,
            glog,
            squeeze_part,
            hid1,
        ],
        [
            ((3, blocks, slab + 2 * cols, 2 * mid), BF16),
            ((2, 8, mid), F32),
            ((pixels, mid), F32),
            ((2, 9 * 128, LANES), F32),
            ((2, 9 * 128, LANES), BF16),
            ((count, 8 + share, LANES), F32),
            ((1, 2 * mid), F32),
            ((1, 2 * mid), F32),
            pltpu.SemaphoreType.DMA((5 + blocks // 4,)),
        ],
        raw_out=range(6),
        flops=2 * large,
        local="in out",
        **sizes,
    )
    chips = count // 2
    large, less = (-(-rows_in // (chips * 16)) * 16 for rows_in in (9 * 128 + 2 * mid + inter, channels))
    keep, send, token = call(
        add_kernel,
        [((chips * large, LANES), F32), ((chips * large, LANES), BF16), TOKEN],
        [meta, keep2, swap(send2, 1), keep3, swap(send3, 1)],
    )
    small1, keep1, send1, gain1_grad, shift1_grad, bias_grad, squeeze_share = call(
        reduce_back_kernel,
        [
            ((pixels, mid), BF16),
            ((chips * less, LANES), F32),
            ((chips * less, LANES), BF16),
            ((1, mid), F32),
            ((1, mid), F32),
            ((1, 2 * mid), F32),
            ((16, inter), F32),
        ],
        [meta, exchange(pay), stat1, gain1, dz1, pre1, x],
        [
            ((pixels, mid), F32),
            ((pixels, mid), F32),
            pltpu.SemaphoreType.DMA((2,)),
        ],
        raw_in=(4, 5),
        flops=small,
        after=(token,),
        local="in out",
        **sizes,
    )
    first = len(stages()[-1])
    blocks = call(
        pack_kernel,
        [((chips // first, large + less, LANES), BF16)] * first,
        [meta, keep, swap(send, 2), keep1, swap(send1, 1)],
        [((chips * large, LANES), BF16), ((chips * less, LANES), BF16)],
        places=slots(),
    )
    input_grad, token = call(
        input_kernel,
        [((pixels, channels), BF16, "hbm"), TOKEN],
        [meta, small1, weight_reduce, grad_res],
        flops=small,
        **sizes,
    )
    shared = scatter_chips(meta, blocks, 2 * large + less, large, squeeze_share, [token])
    parts, places = gather_chips(shared)
    swapped = [swap(part, 1) for part in parts]
    totals = ()
    for other, half in enumerate((parts, swapped)):
        args = [meta, *half, *totals]
        totals = call(
            total_kernel,
            [
                ((mid, channels), F32, "hbm"),
                ((inter, 2 * mid), F32, "hbm"),
                (weight_split.shape, F32, "hbm"),
                ((channels, mid), F32, "hbm"),
                ((chips, 2, share, inter), F32, "hbm"),
            ],
            args,
            [
                ((2, chips * large, LANES), BF16),
                ((chips * less, LANES), BF16),
                ((mid, channels // 2), F32),
                ((inter, mid), F32),
                ((3, 3, 128, mid), F32),
                ((channels // 2, mid), F32),
                ((chips, share, inter), F32),
                pltpu.SemaphoreType.DMA((7,)),
            ],
            local="in",
            raw_in=range(1 + len(half), len(args)),
            raw_out=range(5),
            aliases={1 + len(half) + k: k for k in range(len(totals))},
            places=places,
            large=large,
            less=less,
            other=other,
        )
    expand_total, excite_total, split_total, reduce_total, squeeze_total = totals
    squeeze_total = squeeze_total.reshape(mid, inter)
    flat = lambda v: v.reshape(-1)
    return (
        out.reshape(inputs.shape),
        input_grad.reshape(inputs.shape),
        reduce_total,
        flat(gain1_grad),
        flat(shift1_grad),
        split_total,
        flat(gain2_grad),
        flat(shift2_grad),
        squeeze_total,
        flat(gain_sq_grad),
        flat(shift_sq_grad),
        excite_total,
        flat(bias_grad),
        expand_total,
        flat(gain3_grad),
        flat(shift3_grad),
    )


def solution(mesh):
    rows = P("batch", "narrow", None, None)
    return jax.shard_map(
        body,
        mesh=mesh,
        in_specs=(rows, P("batch")) + (P(),) * 14 + (rows,),
        out_specs=(rows, rows) + (P(),) * 14,
        check_vma=False,
    )
```
